32 devices in a mesh: seq: 8 (over y, x, core), head: 4 (over z).
Axes of the slice: x: 2, y: 2, z: 4, core: 2. Of those that a mesh axis runs over, the one named last changes fastest.
Arguments:
- inputs: bfloat16 [4, 4096, 1024], P(None, 'seq'), may hold values from -6 to 6
- lengths: int32 [4], replicated, may hold values from 1024 to 4096, as said below
- decays: float32 [2, 4, 8, 8], P(None, None, 'seq'), may hold values from 0 to 1
- norm_gain: float32 [1024], replicated, may hold values from 0.5 to 1.5
- query_proj: bfloat16 [1024, 1024], P(None, 'head'), may hold values from -0.1875 to 0.1875
- key_proj: bfloat16 [1024, 1024], P(None, 'head'), may hold values from -0.1875 to 0.1875
- value_proj: bfloat16 [1024, 1024], P(None, 'head'), may hold values from -0.1875 to 0.1875
- gate_proj: bfloat16 [1024, 1024], P(None, 'head'), may hold values from -0.1875 to 0.1875
- conv_taps: bfloat16 [3, 4, 1024], P(None, None, 'head'), may hold values from -3 to 3
- pers_keys: bfloat16 [16, 1024], P(None, 'head'), may hold values from -6 to 6
- pers_values: bfloat16 [16, 1024], P(None, 'head'), may hold values from -6 to 6
- out_proj: bfloat16 [1024, 1024], P('head'), may hold values from -0.375 to 0.375
- ffn_gain: float32 [1024], replicated, may hold values from 0.5 to 1.5
- ffn_gate: bfloat16 [1024, 2816], P(None, 'head'), may hold values from -0.1875 to 0.1875
- ffn_up: bfloat16 [1024, 2816], P(None, 'head'), may hold values from -0.1875 to 0.1875
- ffn_down: bfloat16 [2816, 1024], P('head'), may hold values from -0.15625 to 0.15625
- cotangent: bfloat16 [4, 4096, 1024], P(None, 'seq'), may hold values from -6 to 6
Outputs:
- output: bfloat16 [4, 4096, 1024], P(None, 'seq')
- input_grad: bfloat16 [4, 4096, 1024], P(None, 'seq')
- grad_norm_gain: float32 [1024], replicated
- grad_query: float32 [1024, 1024], P('seq', 'head')
- grad_key: float32 [1024, 1024], P('seq', 'head')
- grad_value: float32 [1024, 1024], P('seq', 'head')
- grad_gate: float32 [1024, 1024], P('seq', 'head')
- grad_conv: float32 [3, 4, 1024], P(None, None, 'head')
- grad_pers_keys: float32 [16, 1024], P(None, 'head')
- grad_pers_values: float32 [16, 1024], P(None, 'head')
- grad_out_proj: float32 [1024, 1024], P('head', 'seq')
- grad_ffn_gain: float32 [1024], replicated
- grad_ffn_gate: float32 [1024, 2816], P('seq', 'head')
- grad_ffn_up: float32 [1024, 2816], P('seq', 'head')
- grad_ffn_down: float32 [2816, 1024], P('head', 'seq')
The draws below stay inside these ranges and needn't reach their ends.
Inputs may be any that keep to these rules, and one draw needn't show every extreme that they name: `lengths`: one sequence, chosen by the seed, is 4096 long.
All inputs are finite; a program needn't handle non-finite values.
Results may differ from the reference program's by a relative error of at most 0.02.
Values may be sent and summed in bfloat16 or wider, within the bound.
A program may use at most 320 MiB of HBM per device.

```python
import math
import jax
import jax.numpy as jnp
from jax import lax

D = 1024
H = 8
DH = 128
FF = 2816
P_SIZE = 16
KW = 4
SEG = 512
SEQS = 4
SEGMENTS = 8
SLOTS = 4096


def draw_decays(key, part):
    first, second, tertiary_term, quarter_term = jax.random.split(jax.random.fold_in(key, 11), 4)
    upper = 3.0
    lower = 0.05 / SEGMENTS
    complete_dims = (2, SEQS, SEGMENTS, H)
    starting_level = jnp.exp(jax.random.uniform(first, (2, 1, 1, H), minval=math.log(lower), maxval=math.log(max(upper, 2.0 * lower))))
    noise_offset = jax.random.uniform(second, complete_dims, minval=0.5, maxval=2.0)
    spike_size = jnp.where(jax.random.uniform(tertiary_term, complete_dims) < 0.1, jax.random.uniform(quarter_term, complete_dims, minval=0.5, maxval=0.8), 1.0)
    multiplier_coeff = jnp.array([1.0, 0.95], jnp.float32).reshape(2, 1, 1, 1)
    return (jnp.exp(-starting_level * noise_offset) * spike_size * multiplier_coeff).astype(jnp.float32)


def draw_lengths(key, part):
    first, second = jax.random.split(jax.random.fold_in(key, 23))
    longest = jax.random.randint(first, (), 0, SEQS)
    drawn = jax.random.randint(second, (SEQS,), SLOTS // 4, SLOTS + 1)
    return jnp.where(jnp.arange(SEQS) == longest, SLOTS, drawn).astype(jnp.int32)


def levels(stream_key, shape, cuts, smallest, top_value):
    gain = 1.0
    for axis_at, blocks in cuts:
        steps = jax.random.uniform(jax.random.fold_in(jax.random.fold_in(stream_key, 6), axis_at), (blocks,), jnp.float32, smallest / len(cuts), top_value / len(cuts))
        gain = gain * jnp.repeat(jnp.exp(steps), shape[axis_at] // blocks).reshape((-1,) + (1,) * (len(shape) - 1 - axis_at))
    return gain


def normal_values(stream_key, extent, spread, bound, cuts=(), kind=jnp.bfloat16):
    values = jax.random.normal(stream_key, extent, jnp.float32) * spread
    if len(cuts) > 0:
        values = levels(stream_key, extent, cuts, -0.22, 0.18) * values
    return jnp.clip(values, min=-bound, max=bound).astype(kind)


def setup_inputs(seed: int = 0) -> dict:
    streams_of = jax.random.split(jax.random.key(seed), 18)
    return {
        "inputs": normal_values(streams_of[0], (SEQS, SLOTS, D), 1.0, 6.0, ((1, 8),)),
        "lengths": draw_lengths(jax.random.fold_in(streams_of[17], 71), 0),
        "decays": draw_decays(jax.random.fold_in(streams_of[17], 71), 0),
        "norm_gain": jnp.clip(1.0 + 0.1 * jax.random.normal(streams_of[3], (D,), jnp.float32), 0.5, 1.5),
        "query_proj": normal_values(streams_of[4], (D, H * DH), D ** -0.5, 0.1875, ((1, 4),)),
        "key_proj": normal_values(streams_of[5], (D, H * DH), D ** -0.5, 0.1875, ((1, 4),)),
        "value_proj": normal_values(streams_of[6], (D, H * DH), D ** -0.5, 0.1875, ((1, 4),)),
        "gate_proj": normal_values(streams_of[7], (D, H * DH), D ** -0.5, 0.1875, ((1, 4),)),
        "conv_taps": normal_values(streams_of[8], (3, KW, H * DH), 0.6, 3.0, ((2, 4),)),
        "pers_keys": normal_values(streams_of[9], (P_SIZE, H * DH), 1.0, 6.0, ((1, 4),)),
        "pers_values": normal_values(streams_of[10], (P_SIZE, H * DH), 1.0, 6.0, ((1, 4),)),
        "out_proj": normal_values(streams_of[11], (H * DH, D), (H * DH // 4) ** -0.5, 0.375, ((0, 4),)),
        "ffn_gain": jnp.clip(1.0 + 0.1 * jax.random.normal(streams_of[12], (D,), jnp.float32), 0.5, 1.5),
        "ffn_gate": normal_values(streams_of[13], (D, FF), D ** -0.5, 0.1875, ((1, 4),)),
        "ffn_up": normal_values(streams_of[14], (D, FF), D ** -0.5, 0.1875, ((1, 4),)),
        "ffn_down": normal_values(streams_of[15], (FF, D), (FF // 2) ** -0.5, 0.15625, ((0, 4),)),
        "cotangent": normal_values(streams_of[16], (SEQS, SLOTS, D), 1.0, 6.0, ((1, 8),)),
    }


EPSILON = 1e-06
HIGHEST = lax.Precision.HIGHEST

@jax.custom_vjp
def low(v):
    return lax.optimization_barrier(v.astype(jnp.bfloat16)).astype(jnp.float32)

@jax.custom_vjp
def low_back(v):
    return v

def low_keep(v):
    return (low(v), None)

def low_pass(kept, grad):
    return (grad,)

def back_keep(v):
    return (v, None)

def back_low(kept, grad):
    return (low(grad),)
low.defvjp(low_keep, low_pass)
low_back.defvjp(back_keep, back_low)

def norm_rows(values):
    return values * lax.rsqrt(lax.optimization_barrier(jnp.mean(values * values, axis=-1, keepdims=True)) + EPSILON)

def head_norm(values):
    shaped = values.reshape(values.shape[:-1] + (H, DH))
    return norm_rows(shaped).reshape(values.shape)

def causal_conv(series, taps):
    length = series.shape[1]
    padded = jnp.pad(series, ((0, 0), (KW - 1, 0), (0, 0)))
    total = taps[0] * padded[:, KW - 1:KW - 1 + length]
    for lag in range(1, KW):
        total = total + taps[lag] * padded[:, KW - 1 - lag:KW - 1 - lag + length]
    return total

def block_attention(blocks, pers_k, pers_v):
    query, keyed, valued, valid_rows = blocks
    keys_all = jnp.concatenate([pers_k, keyed], axis=0)
    values_all = jnp.concatenate([pers_v, valued], axis=0)
    score = jnp.einsum('thd,uhd->htu', query, keys_all, precision=HIGHEST) * DH ** (-0.5)
    score = low_back(score)
    rows_index = jnp.arange(SEG)[:, None]
    column = jnp.arange(P_SIZE + SEG)[None, :] - P_SIZE
    key_valid = jnp.concatenate([jnp.ones((P_SIZE,), valid_rows.dtype), valid_rows])
    allowed = (column < 0) | (column <= rows_index) & (key_valid[None, :] > 0.5)
    score = jnp.where(allowed[None], score, -1e+30)
    top_score = lax.optimization_barrier(jnp.max(score, axis=-1, keepdims=True))
    log_total = top_score + jnp.log(lax.optimization_barrier(jnp.sum(jnp.exp(score - top_score), axis=-1, keepdims=True)))
    prob = low(jnp.exp(score - log_total))
    return jnp.einsum('htu,uhd->thd', prob, values_all, precision=HIGHEST)

def layer(inputs, norm_gain, query_proj, key_proj, value_proj, gate_proj, conv_taps, pers_keys, pers_values, out_proj, ffn_gain, ffn_gate, ffn_up, ffn_down, live, alpha, eta):
    h_one = low(norm_rows(inputs) * norm_gain)
    flat_one = h_one.reshape(-1, D)

    def project(matrix):
        return jnp.dot(flat_one, matrix, precision=HIGHEST).reshape(SEQS, SLOTS, H * DH)
    pres = [low_back(low(project(matrix))) for matrix in (query_proj, key_proj, value_proj)]
    gate_pre = low_back(project(gate_proj))
    acts = [jax.nn.silu(causal_conv(pres[index], conv_taps[index])) for index in range(3)]
    query = low(head_norm(acts[0]))
    keyed = low(head_norm(acts[1]))
    valued = low(acts[2])
    shape_five = (SEQS, SEGMENTS, SEG, H, DH)
    query_five = query.reshape(shape_five)
    key_five = keyed.reshape(shape_five)
    value_five = valued.reshape(shape_five)
    masked_five = (valued * live[:, :, None]).reshape(shape_five)
    write = low_back(jnp.einsum('sctha,scthb->schab', masked_five, key_five, precision=HIGHEST) / SEG)

    def advance(carry, step_in):
        memory, moment = carry
        written, keep_mem, keep_mom = step_in
        new_mom = keep_mom[..., None, None] * moment + written
        new_mem = keep_mem[..., None, None] * memory + new_mom
        return ((new_mem, new_mom), memory)
    zero_state = jnp.zeros((SEQS, H, DH, DH), jnp.float32)
    _, reads = lax.scan(advance, (zero_state, zero_state), (jnp.moveaxis(write, 1, 0), jnp.moveaxis(alpha, 1, 0), jnp.moveaxis(eta, 1, 0)))
    reads = jnp.moveaxis(reads, 0, 1)
    raw_read = low_back(jnp.einsum('schab,scthb->sctha', low(reads), query_five, precision=HIGHEST))
    readout = norm_rows(raw_read).reshape(SEQS, SLOTS, H * DH)
    pers_k = pers_keys.reshape(P_SIZE, H, DH)
    pers_v = pers_values.reshape(P_SIZE, H, DH)

    def one_block(blocks):
        return block_attention(blocks, pers_k, pers_v)
    count = SEQS * SEGMENTS
    attended = lax.map(jax.checkpoint(one_block), (query_five.reshape(count, SEG, H, DH), key_five.reshape(count, SEG, H, DH), value_five.reshape(count, SEG, H, DH), live.reshape(count, SEG)))
    attended = low_back(attended.reshape(SEQS, SLOTS, H * DH))
    mixed = low(attended + jax.nn.sigmoid(gate_pre) * readout)
    attn_out = low_back(jnp.dot(mixed.reshape(-1, H * DH), out_proj, precision=HIGHEST).reshape(SEQS, SLOTS, D))
    middle = inputs + live[:, :, None] * attn_out
    h_two = low(norm_rows(middle) * ffn_gain).reshape(-1, D)
    gate_value = low_back(jnp.dot(h_two, ffn_gate, precision=HIGHEST))
    up_value = low_back(jnp.dot(h_two, ffn_up, precision=HIGHEST))
    hidden = low(jax.nn.silu(gate_value) * up_value)
    ffn_out = jnp.dot(hidden, ffn_down, precision=HIGHEST).reshape(SEQS, SLOTS, D)
    return middle + live[:, :, None] * ffn_out

def reference(inputs, lengths, decays, norm_gain, query_proj, key_proj, value_proj, gate_proj, conv_taps, pers_keys, pers_values, out_proj, ffn_gain, ffn_gate, ffn_up, ffn_down, cotangent):
    positions = jnp.arange(SLOTS, dtype=jnp.int32)
    live = (positions[None, :] < lengths[:, None].astype(jnp.int32)).astype(jnp.float32)
    floats = [array.astype(jnp.float32) for array in (inputs, norm_gain, query_proj, key_proj, value_proj, gate_proj, conv_taps, pers_keys, pers_values, out_proj, ffn_gain, ffn_gate, ffn_up, ffn_down)]
    alpha = decays[0].astype(jnp.float32)
    eta = decays[1].astype(jnp.float32)

    def forward(*params):
        return layer(*params, live, alpha, eta)
    result, pull = jax.vjp(forward, *floats)
    grads = pull(cotangent.astype(jnp.float32))
    return (result.astype(jnp.bfloat16), grads[0].astype(jnp.bfloat16), grads[1], grads[2], grads[3], grads[4], grads[5], grads[6], grads[7], grads[8], grads[9], grads[10], grads[11], grads[12], grads[13])
```

```python
import jax
import jax.numpy as jnp
from jax import lax
from jax.sharding import PartitionSpec as P

DH = 128
KW = 4
HALO = 8
EPSILON = 1e-06
BF = jnp.bfloat16
F32 = jnp.float32


def custom_mesh():
    return lax.axis_size("seq") == 8 and lax.axis_size("head") == 4


def along_seq(value, flip):
    return lax.ppermute(value, "seq", [(i, i ^ flip) for i in range(8)])


def along_head(value, pairs):
    return lax.ppermute(value, "head", pairs)


def slot_owner(k):
    return lax.axis_index("head") ^ k if custom_mesh() else k


def gather_head(value):
    z = lax.axis_index("head")
    middle = (z == 1) | (z == 2)
    one = along_head(value, [(0, 1), (1, 0), (2, 3), (3, 2)])
    inner = along_head(value, [(1, 2), (2, 1)])
    two_inner = along_head(one, [(1, 2), (2, 1)])
    two_outer = along_head(inner, [(2, 3), (1, 0)])
    three_outer = along_head(two_inner, [(2, 3), (1, 0)])
    two = jnp.where(middle, two_inner, two_outer)
    three = jnp.where(middle, inner, three_outer)
    return [value, one, two, three]


def gather_plane(value, x_first):
    near, far = (2, 4) if x_first else (4, 2)
    pieces = {0: value, near: along_seq(value, near), far: along_seq(value, far)}
    pieces[6] = along_seq(pieces[near], far)
    for j in (0, 2, 4, 6):
        pieces[j + 1] = along_seq(pieces[j], 1)
    return [pieces[j] for j in range(8)]


def gather_weights(own):
    if not custom_mesh():
        whole = lax.all_gather(own, "head")
        return [whole[k] for k in range(lax.axis_size("head"))]
    p = lax.axis_index("seq")
    matrices, depth, width = own.shape
    block = depth // 8
    mine = lax.dynamic_slice_in_dim(own, p * block, block, 1)
    slots = [own]
    for k, piece in enumerate(gather_head(mine)[1:]):
        if k < 2:
            parts = gather_plane(piece, k == 0)
        else:
            half = block // 2
            upper = gather_plane(piece[:, :half], True)
            lower = gather_plane(piece[:, half:], False)
            parts = [jnp.concatenate([u, v], axis=1) for u, v in zip(upper, lower)]
        full = jnp.zeros((matrices, depth, width), own.dtype)
        for j, part in enumerate(parts):
            full = lax.dynamic_update_slice_in_dim(full, part, (p ^ j) * block, 1)
        slots.append(full)
    return slots


def gather_small(own):
    if not custom_mesh():
        whole = lax.all_gather(own, "head")
        return [whole[k] for k in range(lax.axis_size("head"))]
    return [own] + [along_head(own, [(i, i ^ k) for i in range(4)]) for k in (1, 2, 3)]


def gather_states(value):
    p = lax.axis_index("seq")
    if not custom_mesh():
        whole = lax.all_gather(value, "seq")
        count = lax.axis_size("seq")
        return [whole[i] for i in range(count)], list(range(count))
    half = value.shape[0] // 2
    upper = gather_plane(value[:half], True)
    lower = gather_plane(value[half:], False)
    pieces = [jnp.concatenate([u, v]) for u, v in zip(upper, lower)]
    return pieces, [p ^ j for j in range(8)]


def gather_rows(own):
    if not custom_mesh():
        return lax.all_gather(own, "head")
    z = lax.axis_index("head")
    full = jnp.zeros((4,) + own.shape, own.dtype)
    for k, slot in enumerate(gather_head(own)):
        full = lax.dynamic_update_slice_in_dim(full, slot[None], z ^ k, 0)
    return full


def weight_grads(pairs, x_first):
    dot = lambda a, b: lax.dot_general(a, b, (((0,), (0,)), ((), ())), preferred_element_type=F32)
    if not custom_mesh():
        out = []
        for a, b in pairs:
            full = jnp.stack([dot(a, one) for one in b]).astype(BF)
            part = lax.psum_scatter(full, "head", scatter_dimension=0, tiled=True)[0]
            out.append(lax.psum_scatter(part, "seq", scatter_dimension=0, tiled=True).astype(F32))
        return out
    p, z = lax.axis_index("seq"), lax.axis_index("head")
    block = pairs[0][0].shape[1] // 8
    stacks = [[] for _ in range(4)]
    for a, b in pairs:
        cut = lambda j: lax.dynamic_slice_in_dim(a, (p ^ j) * block, block, 1)
        even = jnp.concatenate([cut(j) for j in (0, 2, 4, 6)], axis=1)
        odd = jnp.concatenate([cut(j) for j in (1, 3, 5, 7)], axis=1)
        peer_a = along_seq(odd, 1)
        for k in range(4):
            peer_b = along_seq(b[k], 1)
            stacks[k].append(
                (dot(even, b[k]) + dot(peer_a, peer_b)).astype(BF).reshape(4, block, -1)
            )
    near, far = (2, 4) if x_first else (4, 2)
    slots = []
    for k in range(4):
        g = jnp.stack(stacks[k])
        y_zero, y_one = g[:, :2], g[:, 2:]
        if x_first:
            keep = jnp.stack([g[:, 0], g[:, 2]], 1)
            away = jnp.stack([g[:, 1], g[:, 3]], 1)
        else:
            keep, away = y_zero, y_one
        summed = (keep.astype(F32) + along_seq(away, near).astype(F32)).astype(BF)
        slots.append(
            (summed[:, 0].astype(F32) + along_seq(summed[:, 1], far).astype(F32)).astype(BF)
        )
    return list(reduce_head(slots))


def add(a, b):
    return (a.astype(F32) + b.astype(F32)).astype(BF)


def reduce_head(slots):
    outer, inner, back = [(0, 1), (3, 2)], [(1, 2), (2, 1)], [(2, 3), (1, 0)]
    own, one, two, three = slots
    far = add(two, along_head(three, outer))
    far = add(one, along_head(far, inner))
    far = along_head(far, back)
    mid = add(three, along_head(two, outer))
    mid = along_head(mid, inner)
    near = along_head(one, outer)
    return own.astype(F32) + far.astype(F32) + mid.astype(F32) + near.astype(F32)


def sum_small(slots, gains):
    if not custom_mesh():
        part = lax.psum_scatter(jnp.stack(slots), "head", scatter_dimension=0, tiled=True)[0]
        return lax.psum(part, "seq"), lax.psum(gains, ("seq", "head"))
    part = slots[0]
    for k in (1, 2, 3):
        part = part + along_head(slots[k], [(i, i ^ k) for i in range(4)])
    for k in (1, 2):
        gains = gains + along_head(gains, [(i, i ^ k) for i in range(4)])
    count = part.shape[0]
    total = jnp.concatenate([part, gains])
    for flip in (1, 2, 4):
        total = total + along_seq(total, flip)
    return total[:count], total[count:]


def norm_keep(values):
    inverse = lax.rsqrt(jnp.mean(values * values, axis=-1, keepdims=True) + EPSILON)
    return (values * inverse, inverse)


def norm_back(grad, normed, inverse):
    return inverse * (grad - normed * jnp.mean(grad * normed, axis=-1, keepdims=True))


def silu_slope(values):
    sigma = jax.nn.sigmoid(values)
    return sigma * (1.0 + values * (1.0 - sigma))


def carry_coefficients(alpha, eta):
    count, heads = alpha.shape
    place = jnp.arange(count)[:, None]
    mem = jnp.zeros((count, heads), F32)
    mom = jnp.zeros((count, heads), F32)
    rows = []
    for c in range(count):
        rows.append(mem)
        mom = eta[c] * mom + (place == c).astype(F32)
        mem = alpha[c] * mem + mom
    return jnp.stack(rows)


def dot(a, b):
    return jnp.dot(a, b, preferred_element_type=F32)


def dot_t(a, b):
    return lax.dot_general(a, b, (((1,), (1,)), ((), ())), preferred_element_type=F32)


def local(
    inputs,
    lengths,
    decays,
    norm_gain,
    query_proj,
    key_proj,
    value_proj,
    gate_proj,
    conv_taps,
    pers_keys,
    pers_values,
    out_proj,
    ffn_gain,
    ffn_gate,
    ffn_up,
    ffn_down,
    cotangent,
):
    seqs, seg, features = inputs.shape
    segments = lax.axis_size("seq")
    shards = lax.axis_size("head")
    p, z = lax.axis_index("seq"), lax.axis_index("head")
    width = query_proj.shape[1]
    heads_here = width // DH
    heads = heads_here * shards
    rim = KW - 1
    persistent = pers_keys.shape[0]

    attn_slots = gather_weights(jnp.stack([query_proj, key_proj, value_proj, gate_proj, out_proj.T]))
    ffn_slots = gather_weights(jnp.stack([ffn_gate, ffn_up, ffn_down.T]))
    small = gather_small(
        jnp.concatenate([conv_taps.reshape(3 * KW, width), pers_keys, pers_values])
    )
    small = jnp.concatenate(small, axis=1)
    taps = small[: 3 * KW].reshape(3, KW, heads * DH).astype(F32)
    pers_k = small[3 * KW : 3 * KW + persistent].reshape(persistent, heads, DH)
    pers_v = small[3 * KW + persistent :].reshape(persistent, heads, DH)
    q_mat, k_mat, v_mat, g_mat, o_mat = [
        jnp.concatenate([slot[i] for slot in attn_slots], axis=1) for i in range(5)
    ]

    mine = lax.dynamic_index_in_dim(decays, z, 1, False)[:, 0]
    mine = jnp.concatenate(
        [lax.dynamic_slice_in_dim(mine, slot_owner(k) * heads_here, heads_here, 1) for k in range(shards)],
        axis=1,
    )
    every = lax.all_gather(mine, "seq")
    carry = carry_coefficients(every[:, 0], every[:, 1])

    x = lax.dynamic_index_in_dim(inputs, z, 0, False).astype(F32)
    cot = lax.dynamic_index_in_dim(cotangent, z, 0, False).astype(F32)
    length = lax.dynamic_index_in_dim(lengths, z, 0, False)
    live = ((p * seg + jnp.arange(seg, dtype=jnp.int32)) < length).astype(F32)
    live_two = live[:, None]
    tail = lax.dynamic_index_in_dim(inputs, z, 0, False)[seg - HALO :]
    before = lax.ppermute(tail, "seq", [(i, i + 1) for i in range(segments - 1)]).astype(F32)
    x_long = jnp.concatenate([before, x])
    n_long, inv_long = norm_keep(x_long)
    h_long = (n_long * norm_gain).astype(BF)
    n_one, inv_one, h_one = n_long[HALO:], inv_long[HALO:], h_long[HALO:]

    pre = jnp.stack([dot(h_long, m) for m in (q_mat, k_mat, v_mat)]).astype(BF)
    zgate = dot(h_one, g_mat)
    wide_pre = pre.astype(F32)
    conv_sum = sum(
        taps[:, lag][:, None, :] * wide_pre[:, HALO - lag : HALO - lag + seg] for lag in range(KW)
    )
    acts = jax.nn.silu(conv_sum).reshape(3, seg, heads, DH)
    q_normed, q_inverse = norm_keep(acts[0])
    k_normed, k_inverse = norm_keep(acts[1])
    query, keyed, valued = q_normed.astype(BF), k_normed.astype(BF), acts[2].astype(BF)
    live_three = live[:, None, None]
    masked_value = valued * live_three.astype(BF)
    write = jnp.einsum("tha,thb->hab", masked_value, keyed, preferred_element_type=F32) / seg

    def mix_states(values, coefficients):
        pieces, places = gather_states(values.astype(BF))
        total = 0.0
        for piece, place in zip(pieces, places):
            coefficient = lax.dynamic_index_in_dim(coefficients, place, 0, False)
            total = total + coefficient[:, None, None] * piece.astype(F32)
        return total.astype(BF)

    prior = mix_states(write, lax.dynamic_index_in_dim(carry, p, 0, False))
    raw_read = jnp.einsum("hab,thb->tha", prior, query, preferred_element_type=F32)
    readout, read_inverse = norm_keep(raw_read)

    keys_all = jnp.concatenate([pers_k, keyed])
    values_all = jnp.concatenate([pers_v, valued])
    valid = jnp.concatenate([jnp.ones((persistent,), F32), live])
    rows_index = jnp.arange(seg)[:, None]
    column = jnp.arange(persistent + seg)[None, :] - persistent
    allowed = (column < 0) | (column <= rows_index) & (valid[None, :] > 0.5)
    scale = DH ** (-0.5)
    score = jnp.einsum("thd,uhd->htu", query, keys_all, preferred_element_type=F32) * scale
    score = jnp.where(allowed[None], score, -1e30)
    top = jnp.max(score, axis=-1, keepdims=True)
    log_total = top + jnp.log(jnp.sum(jnp.exp(score - top), axis=-1, keepdims=True))
    prob = jnp.exp(score - log_total)
    prob_low = prob.astype(BF)
    attended = jnp.einsum("htu,uhd->thd", prob_low, values_all, preferred_element_type=F32)

    sigma = jax.nn.sigmoid(zgate)
    read_flat = readout.reshape(seg, -1)
    mixed = (attended.reshape(seg, -1) + sigma * read_flat).astype(BF)
    middle = x + live_two * dot_t(mixed, o_mat)
    n_two, inv_two = norm_keep(middle)
    h_two = (n_two * ffn_gain).astype(BF)

    gffn = (live_two * cot).astype(BF)
    ffn_out = 0.0
    dh_two = 0.0
    hidden_slots, gate_slots, up_slots = [], [], []
    for slot in ffn_slots:
        gate_value = dot(h_two, slot[0])
        up_value = dot(h_two, slot[1])
        silu_gate = jax.nn.silu(gate_value)
        hidden = (silu_gate * up_value).astype(BF)
        ffn_out = ffn_out + dot_t(hidden, slot[2])
        dhidden = dot(gffn, slot[2])
        dgate = (dhidden * up_value * silu_slope(gate_value)).astype(BF)
        dup = (dhidden * silu_gate).astype(BF)
        dh_two = dh_two + dot_t(dgate, slot[0]) + dot_t(dup, slot[1])
        hidden_slots.append(hidden)
        gate_slots.append(dgate)
        up_slots.append(dup)
    output = gather_rows((middle + live_two * ffn_out).astype(BF))
    g_gate, g_up, g_down = weight_grads(
        [(h_two, gate_slots), (h_two, up_slots), (gffn, hidden_slots)], True
    )

    grad_ffn_gain = jnp.sum(dh_two * n_two, axis=0)
    dmiddle = cot + norm_back(dh_two * ffn_gain, n_two, inv_two)
    gattn = (live_two * dmiddle).astype(BF)
    dmixed = dot(gattn, o_mat)
    datt = dmixed.astype(BF).reshape(seg, heads, DH)
    dzgate = (dmixed * read_flat * sigma * (1.0 - sigma)).astype(BF)
    dread = norm_back((dmixed * sigma).reshape(seg, heads, DH), readout, read_inverse).astype(BF)
    dprior = jnp.einsum("tha,thb->hab", dread, query, preferred_element_type=F32)
    dwrite = mix_states(dprior, lax.dynamic_index_in_dim(carry, p, 1, False))
    dquery_mem = jnp.einsum("hab,tha->thb", prior, dread, preferred_element_type=F32)
    dprob = jnp.einsum("thd,uhd->htu", datt, values_all, preferred_element_type=F32)
    row_dot = jnp.sum(prob * dprob, axis=-1, keepdims=True)
    dscore = (prob * (dprob - row_dot)).astype(BF)
    dquery = (
        jnp.einsum("htu,uhd->thd", dscore, keys_all, preferred_element_type=F32) * scale
        + dquery_mem
    )
    dkeys = jnp.einsum("htu,thd->uhd", dscore, query, preferred_element_type=F32) * scale
    dvalues = jnp.einsum("htu,thd->uhd", prob_low, datt, preferred_element_type=F32)
    dvals = (
        dvalues[persistent:]
        + live_three * jnp.einsum("hab,thb->tha", dwrite, keyed, preferred_element_type=F32) / seg
    )
    dkey = (
        dkeys[persistent:]
        + jnp.einsum("hab,tha->thb", dwrite, masked_value, preferred_element_type=F32) / seg
    )
    dact = jnp.stack(
        [norm_back(dquery, q_normed, q_inverse), norm_back(dkey, k_normed, k_inverse), dvals]
    ).reshape(3, seg, -1)
    dconv = dact * silu_slope(conv_sum)
    longer = jnp.pad(dconv, ((0, 0), (rim, rim), (0, 0)))
    spread = sum(
        taps[:, lag][:, None, :] * longer[:, lag : lag + seg + rim] for lag in range(KW)
    )
    grad_conv = jnp.stack(
        [
            jnp.sum(dconv * wide_pre[:, HALO - lag : HALO - lag + seg], axis=1)
            for lag in range(KW)
        ],
        axis=1,
    )
    back = lax.ppermute(
        spread[:, :rim].astype(BF), "seq", [(i + 1, i) for i in range(segments - 1)]
    ).astype(F32)
    dpre = spread[:, rim:] + jnp.pad(back, ((0, 0), (seg - rim, 0), (0, 0)))
    dpre = dpre.astype(BF)

    dh_one = (
        dot_t(dpre[0], q_mat) + dot_t(dpre[1], k_mat) + dot_t(dpre[2], v_mat) + dot_t(dzgate, g_mat)
    )
    grad_norm_gain = jnp.sum(dh_one * n_one, axis=0)
    input_grad = gather_rows(
        (dmiddle + norm_back(dh_one * norm_gain, n_one, inv_one)).astype(BF)
    )

    def by_slot(value):
        return [value[..., k * width : (k + 1) * width] for k in range(shards)]

    g_query, g_key, g_value, g_zgate, g_out = weight_grads(
        [(h_one, by_slot(d)) for d in (dpre[0], dpre[1], dpre[2], dzgate)]
        + [(gattn, by_slot(mixed))],
        False,
    )
    rows = jnp.concatenate(
        [
            grad_conv.reshape(3 * KW, -1),
            dkeys[:persistent].reshape(persistent, -1),
            dvalues[:persistent].reshape(persistent, -1),
        ]
    )
    gains = jnp.concatenate([grad_norm_gain, grad_ffn_gain]).reshape(-1, width)
    rows, gains = sum_small(by_slot(rows), gains)
    gains = gains.reshape(2, features)
    return (
        output,
        input_grad,
        gains[0],
        g_query,
        g_key,
        g_value,
        g_zgate,
        rows[: 3 * KW].reshape(3, KW, width),
        rows[3 * KW : 3 * KW + persistent],
        rows[3 * KW + persistent :],
        g_out.T,
        gains[1],
        g_gate,
        g_up,
        g_down.T,
    )


def solution(mesh):
    in_specs = (
        P(None, "seq", None),
        P(),
        P(None, None, "seq", None),
        P(),
        P(None, "head"),
        P(None, "head"),
        P(None, "head"),
        P(None, "head"),
        P(None, None, "head"),
        P(None, "head"),
        P(None, "head"),
        P("head", None),
        P(),
        P(None, "head"),
        P(None, "head"),
        P("head", None),
        P(None, "seq", None),
    )
    out_specs = (
        P(None, "seq", None),
        P(None, "seq", None),
        P(),
        P("seq", "head"),
        P("seq", "head"),
        P("seq", "head"),
        P("seq", "head"),
        P(None, None, "head"),
        P(None, "head"),
        P(None, "head"),
        P("head", "seq"),
        P(),
        P("seq", "head"),
        P("seq", "head"),
        P("head", "seq"),
    )
    return jax.shard_map(local, mesh=mesh, in_specs=in_specs, out_specs=out_specs, check_vma=False)
```

```python
import functools

import jax
import jax.numpy as jnp
from jax import lax
from jax.experimental import pallas as pl
from jax.experimental.pallas import tpu as pltpu
from jax.sharding import PartitionSpec as P

DH = 128
KW = 4
HALO = 8
EPSILON = 1e-06
BF = jnp.bfloat16
F32 = jnp.float32


def custom_mesh():
    return lax.axis_size("seq") == 8 and lax.axis_size("head") == 4


def along_seq(value, flip):
    return lax.ppermute(value, "seq", [(i, i ^ flip) for i in range(8)])


def along_head(value, pairs):
    return lax.ppermute(value, "head", pairs)


def slot_owner(k):
    return lax.axis_index("head") ^ k if custom_mesh() else k


def gather_head(value):
    z = lax.axis_index("head")
    middle = (z == 1) | (z == 2)
    one = along_head(value, [(0, 1), (1, 0), (2, 3), (3, 2)])
    inner = along_head(value, [(1, 2), (2, 1)])
    two_inner = along_head(one, [(1, 2), (2, 1)])
    two_outer = along_head(inner, [(2, 3), (1, 0)])
    three_outer = along_head(two_inner, [(2, 3), (1, 0)])
    two = jnp.where(middle, two_inner, two_outer)
    three = jnp.where(middle, inner, three_outer)
    return [value, one, two, three]


def gather_plane(value, x_first):
    near, far = (2, 4) if x_first else (4, 2)
    pieces = {0: value, near: along_seq(value, near), far: along_seq(value, far)}
    pieces[6] = along_seq(pieces[near], far)
    for j in (0, 2, 4, 6):
        pieces[j + 1] = along_seq(pieces[j], 1)
    return [pieces[j] for j in range(8)]


def gather_weights(own):
    if not custom_mesh():
        whole = lax.all_gather(own, "head")
        return [whole[k] for k in range(lax.axis_size("head"))]
    p = lax.axis_index("seq")
    matrices, depth, width = own.shape
    block = depth // 8
    mine = lax.dynamic_slice_in_dim(own, p * block, block, 1)
    slots = [own]
    for k, piece in enumerate(gather_head(mine)[1:]):
        if k < 2:
            parts = gather_plane(piece, k == 0)
        else:
            half = block // 2
            upper = gather_plane(piece[:, :half], True)
            lower = gather_plane(piece[:, half:], False)
            parts = [jnp.concatenate([u, v], axis=1) for u, v in zip(upper, lower)]
        full = jnp.zeros((matrices, depth, width), own.dtype)
        for j, part in enumerate(parts):
            full = lax.dynamic_update_slice_in_dim(full, part, (p ^ j) * block, 1)
        slots.append(full)
    return slots


def gather_small(own):
    if not custom_mesh():
        whole = lax.all_gather(own, "head")
        return [whole[k] for k in range(lax.axis_size("head"))]
    return [own] + [along_head(own, [(i, i ^ k) for i in range(4)]) for k in (1, 2, 3)]


def gather_states(value):
    p = lax.axis_index("seq")
    if not custom_mesh():
        whole = lax.all_gather(value, "seq")
        count = lax.axis_size("seq")
        return [whole[i] for i in range(count)], list(range(count))
    half = value.shape[0] // 2
    upper = gather_plane(value[:half], True)
    lower = gather_plane(value[half:], False)
    pieces = [jnp.concatenate([u, v]) for u, v in zip(upper, lower)]
    return pieces, [p ^ j for j in range(8)]


def gather_rows(own):
    if not custom_mesh():
        return lax.all_gather(own, "head")
    z = lax.axis_index("head")
    full = jnp.zeros((4,) + own.shape, own.dtype)
    for k, slot in enumerate(gather_head(own)):
        full = lax.dynamic_update_slice_in_dim(full, slot[None], z ^ k, 0)
    return full


def weight_grads(pairs, x_first):
    dot = lambda a, b: lax.dot_general(a, b, (((0,), (0,)), ((), ())), preferred_element_type=F32)
    if not custom_mesh():
        out = []
        for a, b in pairs:
            full = jnp.stack([dot(a, one) for one in b]).astype(BF)
            part = lax.psum_scatter(full, "head", scatter_dimension=0, tiled=True)[0]
            out.append(lax.psum_scatter(part, "seq", scatter_dimension=0, tiled=True).astype(F32))
        return out
    p, z = lax.axis_index("seq"), lax.axis_index("head")
    block = pairs[0][0].shape[1] // 8
    stacks = [[] for _ in range(4)]
    for a, b in pairs:
        cut = lambda j: lax.dynamic_slice_in_dim(a, (p ^ j) * block, block, 1)
        even = jnp.concatenate([cut(j) for j in (0, 2, 4, 6)], axis=1)
        odd = jnp.concatenate([cut(j) for j in (1, 3, 5, 7)], axis=1)
        peer_a = along_seq(odd, 1)
        for k in range(4):
            peer_b = along_seq(b[k], 1)
            stacks[k].append(
                (dot(even, b[k]) + dot(peer_a, peer_b)).astype(BF).reshape(4, block, -1)
            )
    near, far = (2, 4) if x_first else (4, 2)
    slots = []
    for k in range(4):
        g = jnp.stack(stacks[k])
        y_zero, y_one = g[:, :2], g[:, 2:]
        if x_first:
            keep = jnp.stack([g[:, 0], g[:, 2]], 1)
            away = jnp.stack([g[:, 1], g[:, 3]], 1)
        else:
            keep, away = y_zero, y_one
        summed = (keep.astype(F32) + along_seq(away, near).astype(F32)).astype(BF)
        slots.append(
            (summed[:, 0].astype(F32) + along_seq(summed[:, 1], far).astype(F32)).astype(BF)
        )
    return list(reduce_head(slots))


def add(a, b):
    return (a.astype(F32) + b.astype(F32)).astype(BF)


def reduce_head(slots):
    outer, inner, back = [(0, 1), (3, 2)], [(1, 2), (2, 1)], [(2, 3), (1, 0)]
    own, one, two, three = slots
    far = add(two, along_head(three, outer))
    far = add(one, along_head(far, inner))
    far = along_head(far, back)
    mid = add(three, along_head(two, outer))
    mid = along_head(mid, inner)
    near = along_head(one, outer)
    return own.astype(F32) + far.astype(F32) + mid.astype(F32) + near.astype(F32)


def sum_small(slots, gains):
    if not custom_mesh():
        part = lax.psum_scatter(jnp.stack(slots), "head", scatter_dimension=0, tiled=True)[0]
        return lax.psum(part, "seq"), lax.psum(gains, ("seq", "head"))
    part = slots[0]
    for k in (1, 2, 3):
        part = part + along_head(slots[k], [(i, i ^ k) for i in range(4)])
    for k in (1, 2):
        gains = gains + along_head(gains, [(i, i ^ k) for i in range(4)])
    count = part.shape[0]
    total = jnp.concatenate([part, gains])
    for flip in (1, 2, 4):
        total = total + along_seq(total, flip)
    return total[:count], total[count:]


def norm_keep(values):
    inverse = lax.rsqrt(jnp.mean(values * values, axis=-1, keepdims=True) + EPSILON)
    return (values * inverse, inverse)


def norm_back(grad, normed, inverse):
    return inverse * (grad - normed * jnp.mean(grad * normed, axis=-1, keepdims=True))


def silu_slope(values):
    sigma = jax.nn.sigmoid(values)
    return sigma * (1.0 + values * (1.0 - sigma))


def carry_coefficients(alpha, eta):
    count, heads = alpha.shape
    place = jnp.arange(count)[:, None]
    mem = jnp.zeros((count, heads), F32)
    mom = jnp.zeros((count, heads), F32)
    rows = []
    for c in range(count):
        rows.append(mem)
        mom = eta[c] * mom + (place == c).astype(F32)
        mem = alpha[c] * mem + mom
    return jnp.stack(rows)


def dot(a, b):
    return jnp.dot(a, b, preferred_element_type=F32)


def dot_t(a, b):
    return lax.dot_general(a, b, (((1,), (1,)), ((), ())), preferred_element_type=F32)


def local_plain(
    inputs,
    lengths,
    decays,
    norm_gain,
    query_proj,
    key_proj,
    value_proj,
    gate_proj,
    conv_taps,
    pers_keys,
    pers_values,
    out_proj,
    ffn_gain,
    ffn_gate,
    ffn_up,
    ffn_down,
    cotangent,
):
    seqs, seg, features = inputs.shape
    segments = lax.axis_size("seq")
    shards = lax.axis_size("head")
    p, z = lax.axis_index("seq"), lax.axis_index("head")
    width = query_proj.shape[1]
    heads_here = width // DH
    heads = heads_here * shards
    rim = KW - 1
    persistent = pers_keys.shape[0]

    attn_slots = gather_weights(jnp.stack([query_proj, key_proj, value_proj, gate_proj, out_proj.T]))
    ffn_slots = gather_weights(jnp.stack([ffn_gate, ffn_up, ffn_down.T]))
    small = gather_small(
        jnp.concatenate([conv_taps.reshape(3 * KW, width), pers_keys, pers_values])
    )
    small = jnp.concatenate(small, axis=1)
    taps = small[: 3 * KW].reshape(3, KW, heads * DH).astype(F32)
    pers_k = small[3 * KW : 3 * KW + persistent].reshape(persistent, heads, DH)
    pers_v = small[3 * KW + persistent :].reshape(persistent, heads, DH)
    q_mat, k_mat, v_mat, g_mat, o_mat = [
        jnp.concatenate([slot[i] for slot in attn_slots], axis=1) for i in range(5)
    ]

    mine = lax.dynamic_index_in_dim(decays, z, 1, False)[:, 0]
    mine = jnp.concatenate(
        [lax.dynamic_slice_in_dim(mine, slot_owner(k) * heads_here, heads_here, 1) for k in range(shards)],
        axis=1,
    )
    every = lax.all_gather(mine, "seq")
    carry = carry_coefficients(every[:, 0], every[:, 1])

    x = lax.dynamic_index_in_dim(inputs, z, 0, False).astype(F32)
    cot = lax.dynamic_index_in_dim(cotangent, z, 0, False).astype(F32)
    length = lax.dynamic_index_in_dim(lengths, z, 0, False)
    live = ((p * seg + jnp.arange(seg, dtype=jnp.int32)) < length).astype(F32)
    live_two = live[:, None]
    tail = lax.dynamic_index_in_dim(inputs, z, 0, False)[seg - HALO :]
    before = lax.ppermute(tail, "seq", [(i, i + 1) for i in range(segments - 1)]).astype(F32)
    x_long = jnp.concatenate([before, x])
    n_long, inv_long = norm_keep(x_long)
    h_long = (n_long * norm_gain).astype(BF)
    n_one, inv_one, h_one = n_long[HALO:], inv_long[HALO:], h_long[HALO:]

    pre = jnp.stack([dot(h_long, m) for m in (q_mat, k_mat, v_mat)]).astype(BF)
    zgate = dot(h_one, g_mat)
    wide_pre = pre.astype(F32)
    conv_sum = sum(
        taps[:, lag][:, None, :] * wide_pre[:, HALO - lag : HALO - lag + seg] for lag in range(KW)
    )
    acts = jax.nn.silu(conv_sum).reshape(3, seg, heads, DH)
    q_normed, q_inverse = norm_keep(acts[0])
    k_normed, k_inverse = norm_keep(acts[1])
    query, keyed, valued = q_normed.astype(BF), k_normed.astype(BF), acts[2].astype(BF)
    live_three = live[:, None, None]
    masked_value = valued * live_three.astype(BF)
    write = jnp.einsum("tha,thb->hab", masked_value, keyed, preferred_element_type=F32) / seg

    def mix_states(values, coefficients):
        pieces, places = gather_states(values.astype(BF))
        total = 0.0
        for piece, place in zip(pieces, places):
            coefficient = lax.dynamic_index_in_dim(coefficients, place, 0, False)
            total = total + coefficient[:, None, None] * piece.astype(F32)
        return total.astype(BF)

    prior = mix_states(write, lax.dynamic_index_in_dim(carry, p, 0, False))
    raw_read = jnp.einsum("hab,thb->tha", prior, query, preferred_element_type=F32)
    readout, read_inverse = norm_keep(raw_read)

    keys_all = jnp.concatenate([pers_k, keyed])
    values_all = jnp.concatenate([pers_v, valued])
    valid = jnp.concatenate([jnp.ones((persistent,), F32), live])
    rows_index = jnp.arange(seg)[:, None]
    column = jnp.arange(persistent + seg)[None, :] - persistent
    allowed = (column < 0) | (column <= rows_index) & (valid[None, :] > 0.5)
    scale = DH ** (-0.5)
    score = jnp.einsum("thd,uhd->htu", query, keys_all, preferred_element_type=F32) * scale
    score = jnp.where(allowed[None], score, -1e30)
    top = jnp.max(score, axis=-1, keepdims=True)
    log_total = top + jnp.log(jnp.sum(jnp.exp(score - top), axis=-1, keepdims=True))
    prob = jnp.exp(score - log_total)
    prob_low = prob.astype(BF)
    attended = jnp.einsum("htu,uhd->thd", prob_low, values_all, preferred_element_type=F32)

    sigma = jax.nn.sigmoid(zgate)
    read_flat = readout.reshape(seg, -1)
    mixed = (attended.reshape(seg, -1) + sigma * read_flat).astype(BF)
    middle = x + live_two * dot_t(mixed, o_mat)
    n_two, inv_two = norm_keep(middle)
    h_two = (n_two * ffn_gain).astype(BF)

    gffn = (live_two * cot).astype(BF)
    ffn_out = 0.0
    dh_two = 0.0
    hidden_slots, gate_slots, up_slots = [], [], []
    for slot in ffn_slots:
        gate_value = dot(h_two, slot[0])
        up_value = dot(h_two, slot[1])
        silu_gate = jax.nn.silu(gate_value)
        hidden = (silu_gate * up_value).astype(BF)
        ffn_out = ffn_out + dot_t(hidden, slot[2])
        dhidden = dot(gffn, slot[2])
        dgate = (dhidden * up_value * silu_slope(gate_value)).astype(BF)
        dup = (dhidden * silu_gate).astype(BF)
        dh_two = dh_two + dot_t(dgate, slot[0]) + dot_t(dup, slot[1])
        hidden_slots.append(hidden)
        gate_slots.append(dgate)
        up_slots.append(dup)
    output = gather_rows((middle + live_two * ffn_out).astype(BF))
    g_gate, g_up, g_down = weight_grads(
        [(h_two, gate_slots), (h_two, up_slots), (gffn, hidden_slots)], True
    )

    grad_ffn_gain = jnp.sum(dh_two * n_two, axis=0)
    dmiddle = cot + norm_back(dh_two * ffn_gain, n_two, inv_two)
    gattn = (live_two * dmiddle).astype(BF)
    dmixed = dot(gattn, o_mat)
    datt = dmixed.astype(BF).reshape(seg, heads, DH)
    dzgate = (dmixed * read_flat * sigma * (1.0 - sigma)).astype(BF)
    dread = norm_back((dmixed * sigma).reshape(seg, heads, DH), readout, read_inverse).astype(BF)
    dprior = jnp.einsum("tha,thb->hab", dread, query, preferred_element_type=F32)
    dwrite = mix_states(dprior, lax.dynamic_index_in_dim(carry, p, 1, False))
    dquery_mem = jnp.einsum("hab,tha->thb", prior, dread, preferred_element_type=F32)
    dprob = jnp.einsum("thd,uhd->htu", datt, values_all, preferred_element_type=F32)
    row_dot = jnp.sum(prob * dprob, axis=-1, keepdims=True)
    dscore = (prob * (dprob - row_dot)).astype(BF)
    dquery = (
        jnp.einsum("htu,uhd->thd", dscore, keys_all, preferred_element_type=F32) * scale
        + dquery_mem
    )
    dkeys = jnp.einsum("htu,thd->uhd", dscore, query, preferred_element_type=F32) * scale
    dvalues = jnp.einsum("htu,thd->uhd", prob_low, datt, preferred_element_type=F32)
    dvals = (
        dvalues[persistent:]
        + live_three * jnp.einsum("hab,thb->tha", dwrite, keyed, preferred_element_type=F32) / seg
    )
    dkey = (
        dkeys[persistent:]
        + jnp.einsum("hab,tha->thb", dwrite, masked_value, preferred_element_type=F32) / seg
    )
    dact = jnp.stack(
        [norm_back(dquery, q_normed, q_inverse), norm_back(dkey, k_normed, k_inverse), dvals]
    ).reshape(3, seg, -1)
    dconv = dact * silu_slope(conv_sum)
    longer = jnp.pad(dconv, ((0, 0), (rim, rim), (0, 0)))
    spread = sum(
        taps[:, lag][:, None, :] * longer[:, lag : lag + seg + rim] for lag in range(KW)
    )
    grad_conv = jnp.stack(
        [
            jnp.sum(dconv * wide_pre[:, HALO - lag : HALO - lag + seg], axis=1)
            for lag in range(KW)
        ],
        axis=1,
    )
    back = lax.ppermute(
        spread[:, :rim].astype(BF), "seq", [(i + 1, i) for i in range(segments - 1)]
    ).astype(F32)
    dpre = spread[:, rim:] + jnp.pad(back, ((0, 0), (seg - rim, 0), (0, 0)))
    dpre = dpre.astype(BF)

    dh_one = (
        dot_t(dpre[0], q_mat) + dot_t(dpre[1], k_mat) + dot_t(dpre[2], v_mat) + dot_t(dzgate, g_mat)
    )
    grad_norm_gain = jnp.sum(dh_one * n_one, axis=0)
    input_grad = gather_rows(
        (dmiddle + norm_back(dh_one * norm_gain, n_one, inv_one)).astype(BF)
    )

    def by_slot(value):
        return [value[..., k * width : (k + 1) * width] for k in range(shards)]

    g_query, g_key, g_value, g_zgate, g_out = weight_grads(
        [(h_one, by_slot(d)) for d in (dpre[0], dpre[1], dpre[2], dzgate)]
        + [(gattn, by_slot(mixed))],
        False,
    )
    rows = jnp.concatenate(
        [
            grad_conv.reshape(3 * KW, -1),
            dkeys[:persistent].reshape(persistent, -1),
            dvalues[:persistent].reshape(persistent, -1),
        ]
    )
    gains = jnp.concatenate([grad_norm_gain, grad_ffn_gain]).reshape(-1, width)
    rows, gains = sum_small(by_slot(rows), gains)
    gains = gains.reshape(2, features)
    return (
        output,
        input_grad,
        gains[0],
        g_query,
        g_key,
        g_value,
        g_zgate,
        rows[: 3 * KW].reshape(3, KW, width),
        rows[3 * KW : 3 * KW + persistent],
        rows[3 * KW + persistent :],
        g_out.T,
        gains[1],
        g_gate,
        g_up,
        g_down.T,
    )


ROWS = 16
BLOCK = 128
SCALE = DH ** (-0.5)


def shift_sum(source, taps, first, rows, step):
    total = taps[0:1] * source[pl.ds(first, rows)]
    for lag in range(1, KW):
        total = total + taps[lag : lag + 1] * source[pl.ds(first + step * lag, rows)]
    return total


def live_rows(first, rows, length, segment_start):
    place = segment_start + first + lax.broadcasted_iota(jnp.int32, (rows, 1), 0)
    return (place < length).astype(F32)


def live_columns(columns, length, segment_start):
    return segment_start + lax.broadcasted_iota(jnp.int32, (1, columns), 1) < length


def masked_scores(query, keys, pers_k, index, columns_live):
    width = keys.shape[0]
    raw = dot_t(query, keys) * SCALE
    row = index * BLOCK + lax.broadcasted_iota(jnp.int32, (BLOCK, width), 0)
    column = lax.broadcasted_iota(jnp.int32, (BLOCK, width), 1)
    keep = (column <= row) & columns_live[:, :width]
    return jnp.where(keep, raw, -1e30), dot_t(query, pers_k) * SCALE


def forward_slot(k, refs, length, segment_start):
    h_long, weights, taps, pers_k, pers_v, pre, zgate, query, keyed, valued, att, lse, write, wide = refs
    seg = query.shape[1]
    heads = query.shape[2] // DH
    for i in range(3):
        rounded = dot(h_long[...], weights[k, i]).astype(BF)
        pre[i, k] = rounded
        wide[i] = rounded.astype(F32)
    zgate[k] = dot(h_long[pl.ds(ROWS, seg)], weights[k, 3])
    for first in range(0, seg, BLOCK):
        rows = pl.ds(first, BLOCK)
        for i in range(3):
            conv = shift_sum(wide.at[i], taps[k, i].astype(F32), ROWS + first, BLOCK, -1)
            act = conv * jax.nn.sigmoid(conv)
            if i == 2:
                valued[k, rows] = act.astype(BF)
                continue
            target = (query, keyed)[i]
            for head in range(heads):
                lanes = slice(head * DH, (head + 1) * DH)
                target[k, rows, lanes] = norm_keep(act[:, lanes])[0].astype(BF)
    seg_live = live_rows(0, seg, length, segment_start).astype(BF)
    columns_live = live_columns(seg, length, segment_start)
    for head in range(heads):
        lanes = slice(head * DH, (head + 1) * DH)
        masked = valued[k, :, lanes] * seg_live
        write[k, head] = (
            lax.dot_general(
                masked, keyed[k, :, lanes], (((0,), (0,)), ((), ())), preferred_element_type=F32
            )
            / seg
        ).astype(BF)
        for index in range(seg // BLOCK):
            rows = pl.ds(index * BLOCK, BLOCK)
            upto = pl.ds(0, (index + 1) * BLOCK)
            score, pers = masked_scores(
                query[k, rows, lanes], keyed[k, upto, lanes], pers_k[k, :, lanes], index, columns_live
            )
            top = jnp.maximum(
                jnp.max(score, axis=-1, keepdims=True), jnp.max(pers, axis=-1, keepdims=True)
            )
            score, pers = jnp.exp(score - top), jnp.exp(pers - top)
            total = jnp.sum(score, axis=-1, keepdims=True) + jnp.sum(pers, axis=-1, keepdims=True)
            inverse = 1.0 / total
            lse[k, head, rows] = top + jnp.log(total)
            att[k, rows, lanes] = dot((score * inverse).astype(BF), valued[k, upto, lanes]) + dot(
                (pers * inverse).astype(BF), pers_v[k, :, lanes]
            )


def forward_kernel(
    place, x_long, gain, weights, taps, pers_k, pers_v,
    h_long, pre, zgate, query, keyed, valued, att, lse, write, wide,
):
    for first in range(0, x_long.shape[0], 176):
        rows = pl.ds(first, 176)
        normed, _ = norm_keep(x_long[rows].astype(F32))
        h_long[rows] = (normed * gain[...]).astype(BF)
    refs = (h_long, weights, taps, pers_k, pers_v, pre, zgate, query, keyed, valued, att, lse, write, wide)

    @pl.loop(0, 4)
    def _(k):
        forward_slot(k, refs, place[0], place[1])


def read_slot(k, refs):
    prior, query, zgate, att, readout, rinv, mixed = refs
    seg = query.shape[1]
    for head in range(query.shape[2] // DH):
        lanes = slice(head * DH, (head + 1) * DH)
        normed, inverse = norm_keep(dot_t(query[k, :, lanes], prior[k, head]))
        readout[k, :, lanes] = normed
        rinv[k, head] = inverse
        mixed[k, :, lanes] = (
            att[k, :, lanes] + jax.nn.sigmoid(zgate[k, :, lanes]) * normed
        ).astype(BF)


def mix_kernel(
    place, x_long, cot, ffn_gain, prior, query, zgate, att, out_w,
    h_two, gffn, mixed, middle, readout, rinv, acc,
):
    seg = cot.shape[0]
    length, start = place[0], place[1]
    refs = (prior, query, zgate, att, readout, rinv, mixed)

    @pl.loop(0, 4)
    def _(k):
        read_slot(k, refs)
        part = dot(mixed[k], out_w[k])

        @pl.when(k == 0)
        def _():
            acc[...] = part

        @pl.when(k > 0)
        def _():
            acc[...] += part

    for first in range(0, seg, BLOCK):
        rows = pl.ds(first, BLOCK)
        live = live_rows(first, BLOCK, length, start)
        value = x_long[pl.ds(ROWS + first, BLOCK)].astype(F32) + live * acc[rows]
        middle[rows] = value
        normed, _ = norm_keep(value)
        h_two[rows] = (normed * ffn_gain[...]).astype(BF)
        gffn[rows] = (live * cot[rows].astype(F32)).astype(BF)


def ffn_kernel(h_two, gffn, gate_up, down, hidden, dgate, dup, out_acc, grad_acc):
    @pl.when(pl.program_id(0) == 0)
    def _():
        out_acc[...] = jnp.zeros_like(out_acc)
        grad_acc[...] = jnp.zeros_like(grad_acc)

    gate_w, up_w, down_w = gate_up[0, 0], gate_up[0, 1], down[0]
    rows_at_once = 256

    @pl.loop(0, h_two.shape[0] // rows_at_once)
    def _(part):
        rows = pl.ds(pl.multiple_of(part * rows_at_once, rows_at_once), rows_at_once)
        gate = dot(h_two[rows], gate_w)
        up = dot(h_two[rows], up_w)
        sigma = jax.nn.sigmoid(gate)
        silu = gate * sigma
        low = (silu * up).astype(BF)
        hidden[0, rows] = low
        out_acc[rows] += dot(low, down_w)
        back = dot_t(gffn[rows], down_w)
        low_gate = (back * up * (sigma * (1.0 + gate * (1.0 - sigma)))).astype(BF)
        low_up = (back * silu).astype(BF)
        dgate[0, rows] = low_gate
        dup[0, rows] = low_up
        grad_acc[rows] += dot_t(low_gate, gate_w) + dot_t(low_up, up_w)


def tail_kernel(
    place, cot, ffn_gain, query, zgate, out_w, middle, readout, rinv, out_acc, grad_acc,
    output, dmiddle, gattn, datt, dzgate, dread, dprior, gain_grad,
):
    seg = cot.shape[0]
    length, start = place[0], place[1]
    gain_sum = jnp.zeros((1, cot.shape[1]), F32)
    for first in range(0, seg, BLOCK):
        rows = pl.ds(first, BLOCK)
        live = live_rows(first, BLOCK, length, start)
        value = middle[rows]
        output[rows] = (value + live * out_acc[rows]).astype(BF)
        normed, inverse = norm_keep(value)
        grad = grad_acc[rows]
        gain_sum = gain_sum + jnp.sum(grad * normed, axis=0, keepdims=True)
        result = cot[rows].astype(F32) + norm_back(grad * ffn_gain[...], normed, inverse)
        dmiddle[rows] = result
        gattn[rows] = (live * result).astype(BF)
    gain_grad[...] = gain_sum

    @pl.loop(0, 4)
    def _(k):
        dmixed = dot_t(gattn[...], out_w[k])
        datt[k] = dmixed.astype(BF)
        sigma = jax.nn.sigmoid(zgate[k])
        dzgate[k] = (dmixed * readout[k] * sigma * (1.0 - sigma)).astype(BF)
        grad = dmixed * sigma
        for head in range(dmixed.shape[1] // DH):
            lanes = slice(head * DH, (head + 1) * DH)
            low = norm_back(grad[:, lanes], readout[k, :, lanes], rinv[k, head]).astype(BF)
            dread[k, :, lanes] = low
            dprior[k, head] = lax.dot_general(
                low, query[k, :, lanes], (((0,), (0,)), ((), ())), preferred_element_type=F32
            ).astype(BF)


def attention_back_slot(k, refs, length, segment_start):
    query, keyed, valued, lse, datt, dread, prior, pers_k, pers_v, dqkv, dpers_k, dpers_v = refs
    seg = query.shape[1]
    columns_live = live_columns(seg, length, segment_start)
    turn = lambda a, b: lax.dot_general(a, b, (((0,), (0,)), ((), ())), preferred_element_type=F32)
    for head in range(query.shape[2] // DH):
        lanes = slice(head * DH, (head + 1) * DH)
        pers_keys_sum = jnp.zeros((pers_k.shape[1], DH), F32)
        pers_values_sum = jnp.zeros((pers_k.shape[1], DH), F32)
        dqkv[1, :, lanes] = jnp.zeros((seg, DH), F32)
        dqkv[2, :, lanes] = jnp.zeros((seg, DH), F32)
        dqkv[0, :, lanes] = dot(dread[k, :, lanes], prior[k, head])
        for index in range(seg // BLOCK):
            rows = pl.ds(index * BLOCK, BLOCK)
            upto = pl.ds(0, (index + 1) * BLOCK)
            q, d = query[k, rows, lanes], datt[k, rows, lanes]
            keys, pk = keyed[k, upto, lanes], pers_k[k, :, lanes]
            score, pers = masked_scores(q, keys, pk, index, columns_live)
            log_total = lse[k, head, rows]
            prob, prob_p = jnp.exp(score - log_total), jnp.exp(pers - log_total)
            grad = dot_t(d, valued[k, upto, lanes])
            grad_p = dot_t(d, pers_v[k, :, lanes])
            row_dot = jnp.sum(prob * grad, axis=-1, keepdims=True) + jnp.sum(
                prob_p * grad_p, axis=-1, keepdims=True
            )
            dscore = (prob * (grad - row_dot)).astype(BF)
            dscore_p = (prob_p * (grad_p - row_dot)).astype(BF)
            dqkv[0, rows, lanes] += (dot(dscore, keys) + dot(dscore_p, pk)) * SCALE
            dqkv[1, upto, lanes] += turn(dscore, q) * SCALE
            dqkv[2, upto, lanes] += turn(prob.astype(BF), d)
            pers_keys_sum = pers_keys_sum + turn(dscore_p, q)
            pers_values_sum = pers_values_sum + turn(prob_p.astype(BF), d)
        dpers_k[k, :, lanes] = pers_keys_sum * SCALE
        dpers_v[k, :, lanes] = pers_values_sum


def conv_back_slot(k, refs, length, segment_start):
    pre, taps, keyed, valued, dwrite, dqkv, dconv, grad_conv, wide = refs
    seg = keyed.shape[1]
    heads = keyed.shape[2] // DH
    for i in range(3):
        wide[i] = pre[i, k].astype(F32)
    sums = [[jnp.zeros((1, heads * DH), F32) for _ in range(KW)] for _ in range(3)]
    for first in range(0, seg, BLOCK):
        rows = pl.ds(first, BLOCK)
        live = live_rows(first, BLOCK, length, segment_start)
        for i in range(3):
            conv = shift_sum(wide.at[i], taps[k, i].astype(F32), ROWS + first, BLOCK, -1)
            sigma = jax.nn.sigmoid(conv)
            act = conv * sigma
            parts = []
            for head in range(heads):
                lanes = slice(head * DH, (head + 1) * DH)
                grad = dqkv[i, rows, lanes]
                if i == 1:
                    masked = valued[k, rows, lanes] * live.astype(BF)
                    grad = grad + dot(masked, dwrite[k, head]) / seg
                if i == 2:
                    grad = grad + live * dot_t(keyed[k, rows, lanes], dwrite[k, head]) / seg
                else:
                    grad = norm_back(grad, *norm_keep(act[:, lanes]))
                parts.append(grad)
            result = jnp.concatenate(parts, axis=1) * (sigma * (1.0 + conv * (1.0 - sigma)))
            dconv[i, k, rows] = result
            for lag in range(KW):
                sums[i][lag] = sums[i][lag] + jnp.sum(
                    result * wide[i, pl.ds(ROWS + first - lag, BLOCK)], axis=0, keepdims=True
                )
    for i in range(3):
        for lag in range(KW):
            grad_conv[k, i, lag : lag + 1] = sums[i][lag]


def back_kernel(
    place, query, keyed, valued, lse, datt, dread, prior, pers_k, pers_v, pre, taps, dwrite,
    dconv, dpers_k, dpers_v, grad_conv, dqkv, wide,
):
    length, start = place[0], place[1]
    one = (query, keyed, valued, lse, datt, dread, prior, pers_k, pers_v, dqkv, dpers_k, dpers_v)
    two = (pre, taps, keyed, valued, dwrite, dqkv, dconv, grad_conv, wide)

    @pl.loop(0, 4)
    def _(k):
        attention_back_slot(k, one, length, start)
        conv_back_slot(k, two, length, start)


def input_kernel(
    x_long, gain, dconv, after, taps, weights, dzgate, dmiddle,
    dpre, input_grad, gain_grad, longer, acc,
):
    seg = dmiddle.shape[0]
    acc[...] = jnp.zeros_like(acc)

    @pl.loop(0, 4)
    def _(k):
        for i in range(3):
            longer[pl.ds(0, seg)] = dconv[i, k]
            longer[pl.ds(seg, 8)] = after[i, k]
            for first in range(0, seg, BLOCK):
                dpre[i, k, pl.ds(first, BLOCK)] = shift_sum(
                    longer, taps[k, i].astype(F32), first, BLOCK, 1
                ).astype(BF)
        total = dot_t(dpre[0, k], weights[k, 0])
        for i in (1, 2):
            total = total + dot_t(dpre[i, k], weights[k, i])
        acc[...] += total + dot_t(dzgate[k], weights[k, 3])

    gain_sum = jnp.zeros((1, acc.shape[1]), F32)
    for first in range(0, seg, BLOCK):
        rows = pl.ds(first, BLOCK)
        normed, inverse = norm_keep(x_long[pl.ds(ROWS + first, BLOCK)].astype(F32))
        grad = acc[rows]
        gain_sum = gain_sum + jnp.sum(grad * normed, axis=0, keepdims=True)
        input_grad[rows] = (
            dmiddle[rows] + norm_back(grad * gain[...], normed, inverse)
        ).astype(BF)
    gain_grad[...] = gain_sum


SHAPE = jax.ShapeDtypeStruct
VMEM_LIMIT = 60 * 1024 * 1024


def call(kernel, outs, scratch, smem, *args):
    specs = [pl.BlockSpec(memory_space=pltpu.SMEM)] * smem
    specs += [pl.BlockSpec(memory_space=pltpu.VMEM)] * (len(args) - smem)
    return pl.pallas_call(
        kernel,
        out_shape=outs,
        in_specs=specs,
        out_specs=[pl.BlockSpec(memory_space=pltpu.VMEM)] * len(outs),
        scratch_shapes=scratch,
        compiler_params=pltpu.CompilerParams(vmem_limit_bytes=VMEM_LIMIT),
    )(*args)


MESH = pl.DeviceIdType.MESH
SKEW_ONE, SKEW_TWO = 2, 4


class Links:
    def __init__(self, send, recv):
        self.send, self.recv = send, recv
        self.sent = 0
        self.names = {}
        self.always, self.middles = [], []
        self.p, self.z = lax.axis_index("seq"), lax.axis_index("head")
        self.middle = (self.z == 1) | (self.z == 2)

    def greet(self):
        barrier = pltpu.get_barrier_semaphore()
        for flip in (1, 2, 4):
            pl.semaphore_signal(barrier, device_id=(self.p ^ flip, self.z), device_id_type=MESH)
        for flip in (1, 3):
            pl.semaphore_signal(barrier, device_id=(self.p, self.z ^ flip), device_id_type=MESH)
        pl.semaphore_wait(barrier, 5)

    def place(self, name):
        return self.recv.at[self.names.setdefault(name, len(self.names))]

    def copy(self, source, target, name, device):
        index = self.sent
        self.sent += 1
        return pltpu.make_async_remote_copy(
            src_ref=source, dst_ref=target, send_sem=self.send.at[index], recv_sem=self.place(name),
            device_id=device, device_id_type=MESH,
        )

    def along_seq(self, source, target, name, flip):
        copy = self.copy(source, target, name, (self.p ^ flip, self.z))
        copy.start()
        self.always.append((lambda: source, self.sent - 1))

    def along_head(self, source, target, name, flip, waits):
        index = self.sent
        copy = self.copy(source(), target(), name, (self.p, self.z ^ flip))
        copy.start()
        waits.append((source, index))

    def arrived(self, target, name):
        pltpu.make_async_remote_copy(
            src_ref=target, dst_ref=target, send_sem=self.send.at[0], recv_sem=self.place(name),
            device_id=(self.p, self.z ^ 1), device_id_type=MESH,
        ).wait_recv()

    def gone(self, source, index):
        pltpu.make_async_remote_copy(
            src_ref=source(), dst_ref=source(), send_sem=self.send.at[index], recv_sem=self.recv.at[0],
            device_id=(self.p, self.z ^ 1), device_id_type=MESH,
        ).wait_send()

    def finish(self):
        for source, index in self.always:
            self.gone(source, index)

        @pl.when(self.middle)
        def _():
            for source, index in self.middles:
                self.gone(source, index)


class LineGather:
    def __init__(self, links, name, view):
        self.links, self.name, self.view = links, name, view

    def start(self, sources):
        links = self.links
        for source, view in sources:
            links.along_head(source, lambda: view(1), (self.name, 1), 1, links.always)

        @pl.when(links.middle)
        def _():
            for source, view in sources:
                links.along_head(source, lambda: view(3), (self.name, 3), 3, links.middles)

    def step(self, k):
        links, name, view = self.links, self.name, self.view
        if k == 1:
            links.arrived(view(1), (name, 1))

            @pl.when(links.middle)
            def _():
                links.along_head(lambda: view(1), lambda: view(2), (name, 2), 3, links.middles)
                links.arrived(view(3), (name, 3))
                links.along_head(lambda: view(3), lambda: view(2), (name, 2), 1, links.middles)

        if k == 2:
            links.arrived(view(2), (name, 2))

            @pl.when(links.middle)
            def _():
                links.along_head(lambda: view(2), lambda: view(3), (name, 3), 1, links.middles)

        if k == 3:

            @pl.when(~links.middle)
            def _():
                links.arrived(view(3), (name, 3))


class PlaneGather:
    def __init__(self, links, name, view, x_first):
        self.links, self.name, self.view = links, name, view
        self.near, self.far = (2, 4) if x_first else (4, 2)

    def send(self, j, flip):
        links = self.links
        block = self.view(links.p ^ j)
        links.along_seq(block, block, (self.name, j ^ flip), flip)

    def wait(self, j):
        self.links.arrived(self.view(self.links.p ^ j), (self.name, j))

    def start(self):
        self.send(0, self.near)
        self.send(0, self.far)
        self.send(0, 1)

    def step(self):
        self.wait(self.near)
        self.send(self.near, self.far)
        self.send(self.near, 1)
        self.wait(self.far)
        self.send(self.far, 1)

    def last(self):
        self.wait(6)
        self.send(6, 1)

    def end(self):
        for j in (1, 3, 5, 7):
            self.wait(j)


def weight_pieces(links, weights, out_w, gate_up, down):
    block = lambda q: pl.ds(pl.multiple_of(q * 128, 128), 128)
    views = {
        "proj": (lambda k, q: weights.at[k, :, block(q), :], True),
        "out": (lambda k, q: out_w.at[k, :, block(q)], False),
        "ffn": (lambda k, q: gate_up.at[k, :, block(q), :], False),
        "down": (lambda k, q: down.at[k, :, block(q)], True),
    }
    pieces = {}
    for name, (view, x_first) in views.items():
        line = LineGather(links, name, lambda k, view=view: view(k, links.p))
        planes = [
            PlaneGather(links, (name, k), lambda q, view=view, k=k: view(k, q), x_first)
            for k in (1, 2, 3)
        ]
        pieces[name] = (line, planes)
    return pieces


def weight_events(links, own, weights, out_w, gate_up, down):
    q_own, k_own, v_own, g_own, o_own, gate_own, up_own, down_own = own
    mine = pl.ds(pl.multiple_of(links.p * 128, 128), 128)
    pieces = weight_pieces(links, weights, out_w, gate_up, down)
    starts = {
        "proj": [
            (lambda ref=ref: ref.at[mine, :], lambda k, i=i: weights.at[k, i, mine, :])
            for i, ref in enumerate((q_own, k_own, v_own, g_own))
        ],
        "out": [(lambda: o_own.at[:, mine], lambda k: out_w.at[k, :, mine])],
        "ffn": [
            (lambda ref=ref: ref.at[mine, :], lambda k, i=i: gate_up.at[k, i, mine, :])
            for i, ref in enumerate((gate_own, up_own))
        ],
        "down": [(lambda: down_own.at[:, mine], lambda k: down.at[k, :, mine])],
    }
    begin = lambda name: pieces[name][0].start(starts[name])
    units = [("proj", k) for k in (1, 2, 3)] + [("out", k) for k in (1, 2, 3)]
    units += [(name, k) for k in (1, 2, 3) for name in ("ffn", "down")]
    when = {0: ["proj"], 1: ["out"], 2: ["ffn"], 3: ["down"]}
    count = len(units)
    events = []
    for i in range(count + SKEW_TWO):
        for name in when.get(i, []):
            events.append((None, lambda name=name: begin(name)))
        if i < count:
            name, k = units[i]

            def first(name=name, k=k):
                pieces[name][0].step(k)
                pieces[name][1][k - 1].start()

            events.append((None, first))
        if 0 <= i - SKEW_ONE < count:
            name, k = units[i - SKEW_ONE]
            events.append((None, pieces[name][1][k - 1].step))
        if 0 <= i - SKEW_TWO < count:
            name, k = units[i - SKEW_TWO]
            events.append(((name, k), pieces[name][1][k - 1].last))
    return events, pieces


def gather_kernel(
    q_own, k_own, v_own, g_own, o_own, gate_own, up_own, down_own,
    weights, out_w, gate_up, down, send, recv,
):
    links = Links(send, recv)
    links.greet()
    own = (q_own, k_own, v_own, g_own, o_own, gate_own, up_own, down_own)
    events, pieces = weight_events(links, own, weights, out_w, gate_up, down)
    for _, step in events:
        step()
    for line, planes in pieces.values():
        for plane in planes:
            plane.end()
    links.finish()


def gather_all(own):
    features, width = own[0].shape
    hidden_width = own[5].shape[1]
    anywhere = pl.BlockSpec(memory_space=pl.ANY)
    low = lambda *shape: jax.ShapeDtypeStruct(shape, BF)
    return pl.pallas_call(
        gather_kernel,
        out_shape=[
            low(4, 4, features, width), low(4, width, features), low(4, 2, features, hidden_width),
            low(4, hidden_width, features),
        ],
        in_specs=[anywhere] * 8,
        out_specs=[anywhere] * 4,
        scratch_shapes=[
            pltpu.SemaphoreType.DMA((128,)), pltpu.SemaphoreType.DMA((128,)),
        ],
        compiler_params=pltpu.CompilerParams(collective_id=0, has_side_effects=True),
    )(*own)


def local_fast(
    inputs, lengths, decays, norm_gain, query_proj, key_proj, value_proj, gate_proj, conv_taps,
    pers_keys, pers_values, out_proj, ffn_gain, ffn_gate, ffn_up, ffn_down, cotangent,
):
    seqs, seg, features = inputs.shape
    segments, shards = lax.axis_size("seq"), lax.axis_size("head")
    p, z = lax.axis_index("seq"), lax.axis_index("head")
    width, hidden_width = query_proj.shape[1], ffn_gate.shape[1]
    heads_here = width // DH
    heads = heads_here * shards
    persistent = pers_keys.shape[0]

    weights, out_w, gate_up, down_w = gather_all(
        (query_proj, key_proj, value_proj, gate_proj, out_proj, ffn_gate, ffn_up, ffn_down)
    )
    weights = weights.at[0].set(jnp.stack([query_proj, key_proj, value_proj, gate_proj]))
    out_w = out_w.at[0].set(out_proj)
    gate_up = gate_up.at[0].set(jnp.stack([ffn_gate, ffn_up]))
    down_w = down_w.at[0].set(ffn_down)
    small = jnp.stack(
        gather_small(jnp.concatenate([conv_taps.reshape(3 * KW, width), pers_keys, pers_values]))
    )
    taps = small[:, : 3 * KW].reshape(shards, 3, KW, width)
    pers_k = small[:, 3 * KW : 3 * KW + persistent]
    pers_v = small[:, 3 * KW + persistent :]

    mine = lax.dynamic_index_in_dim(decays, z, 1, False)[:, 0]
    mine = jnp.concatenate(
        [lax.dynamic_slice_in_dim(mine, slot_owner(k) * heads_here, heads_here, 1) for k in range(shards)],
        axis=1,
    )
    every = lax.all_gather(mine, "seq")
    carry = carry_coefficients(every[:, 0], every[:, 1])

    x = lax.dynamic_index_in_dim(inputs, z, 0, False)
    cot = lax.dynamic_index_in_dim(cotangent, z, 0, False)
    length = lax.dynamic_index_in_dim(lengths, z, 0, False)
    place = jnp.stack([length, p * seg]).astype(jnp.int32)
    before = lax.ppermute(x[seg - ROWS :], "seq", [(i, i + 1) for i in range(segments - 1)])
    x_long = jnp.concatenate([before, x])
    gain = norm_gain[None]
    ffn_gain = ffn_gain[None]
    low = lambda *shape: SHAPE(shape, BF)
    full = lambda *shape: SHAPE(shape, F32)
    rows_low = low(shards, seg, width)
    rows_full = full(shards, seg, width)
    state = low(shards, heads_here, DH, DH)
    wide = pltpu.VMEM((3, seg + ROWS, width), F32)

    h_long, pre, zgate, query, keyed, valued, att, lse, write = call(
        forward_kernel,
        [
            low(seg + ROWS, features), low(3, shards, seg + ROWS, width), rows_full,
            rows_low, rows_low, rows_low, rows_full, full(shards, heads_here, seg, 1), state,
        ],
        [wide],
        1,
        place, x_long, gain, weights, taps, pers_k, pers_v,
    )

    def mix_states(values, coefficients):
        pieces, places = gather_states(values)
        total = 0.0
        coefficients = coefficients.reshape(segments, shards, heads_here)
        for piece, at in zip(pieces, places):
            coefficient = lax.dynamic_index_in_dim(coefficients, at, 0, False)
            total = total + coefficient[:, :, None, None] * piece.astype(F32)
        return total.astype(BF)

    prior = mix_states(write, lax.dynamic_index_in_dim(carry, p, 0, False))
    h_two, gffn, mixed, middle, readout, rinv = call(
        mix_kernel,
        [
            low(seg, features), low(seg, features), rows_low, full(seg, features), rows_full,
            full(shards, heads_here, seg, 1),
        ],
        [pltpu.VMEM((seg, features), F32)],
        1,
        place, x_long, cot, ffn_gain, prior, query, zgate, att, out_w,
    )
    hid = low(shards, seg, hidden_width)
    whole = pl.BlockSpec((seg, features), lambda k: (0, 0))
    part = pl.BlockSpec((1, seg, hidden_width), lambda k: (k, 0, 0))
    hidden, dgate, dup, out_acc, grad_acc = pl.pallas_call(
        ffn_kernel,
        grid=(shards,),
        out_shape=[hid, hid, hid, full(seg, features), full(seg, features)],
        in_specs=[
            whole, whole,
            pl.BlockSpec((1, 2, features, hidden_width), lambda k: (k, 0, 0, 0)),
            pl.BlockSpec((1, hidden_width, features), lambda k: (k, 0, 0)),
        ],
        out_specs=[part, part, part, whole, whole],
        compiler_params=pltpu.CompilerParams(vmem_limit_bytes=VMEM_LIMIT),
    )(h_two, gffn, gate_up, down_w)
    output, dmiddle, gattn, datt, dzgate, dread, dprior, g_ffn_gain = call(
        tail_kernel,
        [
            low(seg, features), full(seg, features), low(seg, features), rows_low, rows_low, rows_low,
            state, full(1, features),
        ],
        [],
        1,
        place, cot, ffn_gain, query, zgate, out_w, middle, readout, rinv, out_acc, grad_acc,
    )
    output = gather_rows(output)
    split = lambda value: [value[k] for k in range(shards)]
    g_gate, g_up, g_down = weight_grads(
        [(h_two, split(dgate)), (h_two, split(dup)), (gffn, split(hidden))], True
    )
    dwrite = mix_states(dprior, lax.dynamic_index_in_dim(carry, p, 1, False))
    dconv, dpers_k, dpers_v, grad_conv = call(
        back_kernel,
        [
            full(3, shards, seg, width), full(shards, persistent, width), full(shards, persistent, width),
            full(shards, 3, KW, width),
        ],
        [pltpu.VMEM((3, seg, width), F32), wide],
        1,
        place, query, keyed, valued, lse, datt, dread, prior, pers_k, pers_v, pre, taps, dwrite,
    )
    after = lax.ppermute(dconv[:, :, :8], "seq", [(i + 1, i) for i in range(segments - 1)])
    dpre, input_grad, g_norm_gain = call(
        input_kernel,
        [low(3, shards, seg, width), low(seg, features), full(1, features)],
        [pltpu.VMEM((seg + 8, width), F32), pltpu.VMEM((seg, features), F32)],
        0,
        x_long, gain, dconv, after, taps, weights, dzgate, dmiddle,
    )
    input_grad = gather_rows(input_grad)
    h_one = h_long[ROWS:]
    g_query, g_key, g_value, g_zgate, g_out = weight_grads(
        [(h_one, split(d)) for d in (dpre[0], dpre[1], dpre[2], dzgate)] + [(gattn, split(mixed))],
        False,
    )
    rows = jnp.concatenate([grad_conv.reshape(shards, 3 * KW, width), dpers_k, dpers_v], axis=1)
    gains = jnp.concatenate([g_norm_gain, g_ffn_gain]).reshape(-1, width)
    rows, gains = sum_small(split(rows), gains)
    gains = gains.reshape(2, features)
    return (
        output, input_grad, gains[0], g_query, g_key, g_value, g_zgate,
        rows[: 3 * KW].reshape(3, KW, width), rows[3 * KW : 3 * KW + persistent], rows[3 * KW + persistent :],
        g_out.T, gains[1], g_gate, g_up, g_down.T,
    )


def local(*args):
    return local_fast(*args) if custom_mesh() else local_plain(*args)


def solution(mesh):
    in_specs = (
        P(None, "seq", None),
        P(),
        P(None, None, "seq", None),
        P(),
        P(None, "head"),
        P(None, "head"),
        P(None, "head"),
        P(None, "head"),
        P(None, None, "head"),
        P(None, "head"),
        P(None, "head"),
        P("head", None),
        P(),
        P(None, "head"),
        P(None, "head"),
        P("head", None),
        P(None, "seq", None),
    )
    out_specs = (
        P(None, "seq", None),
        P(None, "seq", None),
        P(),
        P("seq", "head"),
        P("seq", "head"),
        P("seq", "head"),
        P("seq", "head"),
        P(None, None, "head"),
        P(None, "head"),
        P(None, "head"),
        P("head", "seq"),
        P(),
        P("seq", "head"),
        P("seq", "head"),
        P("head", "seq"),
    )
    return jax.shard_map(local, mesh=mesh, in_specs=in_specs, out_specs=out_specs, check_vma=False)
```

```python
import functools

import jax
import jax.numpy as jnp
from jax import lax
from jax.experimental import pallas as pl
from jax.experimental.pallas import tpu as pltpu
from jax.sharding import PartitionSpec as P

DH = 128
KW = 4
HALO = 8
EPSILON = 1e-06
BF = jnp.bfloat16
F32 = jnp.float32


def custom_mesh():
    return lax.axis_size("seq") == 8 and lax.axis_size("head") == 4


def along_seq(value, flip):
    return lax.ppermute(value, "seq", [(i, i ^ flip) for i in range(8)])


def along_head(value, pairs):
    return lax.ppermute(value, "head", pairs)


def slot_owner(k):
    return lax.axis_index("head") ^ k if custom_mesh() else k


def gather_head(value):
    z = lax.axis_index("head")
    middle = (z == 1) | (z == 2)
    one = along_head(value, [(0, 1), (1, 0), (2, 3), (3, 2)])
    inner = along_head(value, [(1, 2), (2, 1)])
    two_inner = along_head(one, [(1, 2), (2, 1)])
    two_outer = along_head(inner, [(2, 3), (1, 0)])
    three_outer = along_head(two_inner, [(2, 3), (1, 0)])
    two = jnp.where(middle, two_inner, two_outer)
    three = jnp.where(middle, inner, three_outer)
    return [value, one, two, three]


def gather_plane(value, x_first):
    near, far = (2, 4) if x_first else (4, 2)
    pieces = {0: value, near: along_seq(value, near), far: along_seq(value, far)}
    pieces[6] = along_seq(pieces[near], far)
    for j in (0, 2, 4, 6):
        pieces[j + 1] = along_seq(pieces[j], 1)
    return [pieces[j] for j in range(8)]


def gather_weights(own):
    if not custom_mesh():
        whole = lax.all_gather(own, "head")
        return [whole[k] for k in range(lax.axis_size("head"))]
    p = lax.axis_index("seq")
    matrices, depth, width = own.shape
    block = depth // 8
    mine = lax.dynamic_slice_in_dim(own, p * block, block, 1)
    slots = [own]
    for k, piece in enumerate(gather_head(mine)[1:]):
        if k < 2:
            parts = gather_plane(piece, k == 0)
        else:
            half = block // 2
            upper = gather_plane(piece[:, :half], True)
            lower = gather_plane(piece[:, half:], False)
            parts = [jnp.concatenate([u, v], axis=1) for u, v in zip(upper, lower)]
        full = jnp.zeros((matrices, depth, width), own.dtype)
        for j, part in enumerate(parts):
            full = lax.dynamic_update_slice_in_dim(full, part, (p ^ j) * block, 1)
        slots.append(full)
    return slots


def gather_small(own):
    if not custom_mesh():
        whole = lax.all_gather(own, "head")
        return [whole[k] for k in range(lax.axis_size("head"))]
    return [own] + [along_head(own, [(i, i ^ k) for i in range(4)]) for k in (1, 2, 3)]


def gather_states(value):
    p = lax.axis_index("seq")
    if not custom_mesh():
        whole = lax.all_gather(value, "seq")
        count = lax.axis_size("seq")
        return [whole[i] for i in range(count)], list(range(count))
    half = value.shape[0] // 2
    upper = gather_plane(value[:half], True)
    lower = gather_plane(value[half:], False)
    pieces = [jnp.concatenate([u, v]) for u, v in zip(upper, lower)]
    return pieces, [p ^ j for j in range(8)]


def gather_rows(own):
    if not custom_mesh():
        return lax.all_gather(own, "head")
    z = lax.axis_index("head")
    full = jnp.zeros((4,) + own.shape, own.dtype)
    for k, slot in enumerate(gather_head(own)):
        full = lax.dynamic_update_slice_in_dim(full, slot[None], z ^ k, 0)
    return full


def weight_grads(pairs, x_first):
    dot = lambda a, b: lax.dot_general(a, b, (((0,), (0,)), ((), ())), preferred_element_type=F32)
    if not custom_mesh():
        out = []
        for a, b in pairs:
            full = jnp.stack([dot(a, one) for one in b]).astype(BF)
            part = lax.psum_scatter(full, "head", scatter_dimension=0, tiled=True)[0]
            out.append(lax.psum_scatter(part, "seq", scatter_dimension=0, tiled=True).astype(F32))
        return out
    p, z = lax.axis_index("seq"), lax.axis_index("head")
    block = pairs[0][0].shape[1] // 8
    stacks = [[] for _ in range(4)]
    for a, b in pairs:
        cut = lambda j: lax.dynamic_slice_in_dim(a, (p ^ j) * block, block, 1)
        even = jnp.concatenate([cut(j) for j in (0, 2, 4, 6)], axis=1)
        odd = jnp.concatenate([cut(j) for j in (1, 3, 5, 7)], axis=1)
        peer_a = along_seq(odd, 1)
        for k in range(4):
            peer_b = along_seq(b[k], 1)
            stacks[k].append(
                (dot(even, b[k]) + dot(peer_a, peer_b)).astype(BF).reshape(4, block, -1)
            )
    near, far = (2, 4) if x_first else (4, 2)
    slots = []
    for k in range(4):
        g = jnp.stack(stacks[k])
        y_zero, y_one = g[:, :2], g[:, 2:]
        if x_first:
            keep = jnp.stack([g[:, 0], g[:, 2]], 1)
            away = jnp.stack([g[:, 1], g[:, 3]], 1)
        else:
            keep, away = y_zero, y_one
        summed = (keep.astype(F32) + along_seq(away, near).astype(F32)).astype(BF)
        slots.append(
            (summed[:, 0].astype(F32) + along_seq(summed[:, 1], far).astype(F32)).astype(BF)
        )
    return list(reduce_head(slots))


def add(a, b):
    return (a.astype(F32) + b.astype(F32)).astype(BF)


def reduce_head(slots):
    outer, inner, back = [(0, 1), (3, 2)], [(1, 2), (2, 1)], [(2, 3), (1, 0)]
    own, one, two, three = slots
    far = add(two, along_head(three, outer))
    far = add(one, along_head(far, inner))
    far = along_head(far, back)
    mid = add(three, along_head(two, outer))
    mid = along_head(mid, inner)
    near = along_head(one, outer)
    return own.astype(F32) + far.astype(F32) + mid.astype(F32) + near.astype(F32)


def sum_small(slots, gains):
    if not custom_mesh():
        part = lax.psum_scatter(jnp.stack(slots), "head", scatter_dimension=0, tiled=True)[0]
        return lax.psum(part, "seq"), lax.psum(gains, ("seq", "head"))
    part = slots[0]
    for k in (1, 2, 3):
        part = part + along_head(slots[k], [(i, i ^ k) for i in range(4)])
    for k in (1, 2):
        gains = gains + along_head(gains, [(i, i ^ k) for i in range(4)])
    count = part.shape[0]
    total = jnp.concatenate([part, gains])
    for flip in (1, 2, 4):
        total = total + along_seq(total, flip)
    return total[:count], total[count:]


def norm_keep(values):
    inverse = lax.rsqrt(jnp.mean(values * values, axis=-1, keepdims=True) + EPSILON)
    return (values * inverse, inverse)


def norm_back(grad, normed, inverse):
    return inverse * (grad - normed * jnp.mean(grad * normed, axis=-1, keepdims=True))


def silu_slope(values):
    sigma = jax.nn.sigmoid(values)
    return sigma * (1.0 + values * (1.0 - sigma))


def carry_coefficients(alpha, eta):
    count, heads = alpha.shape
    place = jnp.arange(count)[:, None]
    mem = jnp.zeros((count, heads), F32)
    mom = jnp.zeros((count, heads), F32)
    rows = []
    for c in range(count):
        rows.append(mem)
        mom = eta[c] * mom + (place == c).astype(F32)
        mem = alpha[c] * mem + mom
    return jnp.stack(rows)


def dot(a, b):
    return jnp.dot(a, b, preferred_element_type=F32)


def dot_t(a, b):
    return lax.dot_general(a, b, (((1,), (1,)), ((), ())), preferred_element_type=F32)


def local_plain(
    inputs,
    lengths,
    decays,
    norm_gain,
    query_proj,
    key_proj,
    value_proj,
    gate_proj,
    conv_taps,
    pers_keys,
    pers_values,
    out_proj,
    ffn_gain,
    ffn_gate,
    ffn_up,
    ffn_down,
    cotangent,
):
    seqs, seg, features = inputs.shape
    segments = lax.axis_size("seq")
    shards = lax.axis_size("head")
    p, z = lax.axis_index("seq"), lax.axis_index("head")
    width = query_proj.shape[1]
    heads_here = width // DH
    heads = heads_here * shards
    rim = KW - 1
    persistent = pers_keys.shape[0]

    attn_slots = gather_weights(jnp.stack([query_proj, key_proj, value_proj, gate_proj, out_proj.T]))
    ffn_slots = gather_weights(jnp.stack([ffn_gate, ffn_up, ffn_down.T]))
    small = gather_small(
        jnp.concatenate([conv_taps.reshape(3 * KW, width), pers_keys, pers_values])
    )
    small = jnp.concatenate(small, axis=1)
    taps = small[: 3 * KW].reshape(3, KW, heads * DH).astype(F32)
    pers_k = small[3 * KW : 3 * KW + persistent].reshape(persistent, heads, DH)
    pers_v = small[3 * KW + persistent :].reshape(persistent, heads, DH)
    q_mat, k_mat, v_mat, g_mat, o_mat = [
        jnp.concatenate([slot[i] for slot in attn_slots], axis=1) for i in range(5)
    ]

    mine = lax.dynamic_index_in_dim(decays, z, 1, False)[:, 0]
    mine = jnp.concatenate(
        [lax.dynamic_slice_in_dim(mine, slot_owner(k) * heads_here, heads_here, 1) for k in range(shards)],
        axis=1,
    )
    every = lax.all_gather(mine, "seq")
    carry = carry_coefficients(every[:, 0], every[:, 1])

    x = lax.dynamic_index_in_dim(inputs, z, 0, False).astype(F32)
    cot = lax.dynamic_index_in_dim(cotangent, z, 0, False).astype(F32)
    length = lax.dynamic_index_in_dim(lengths, z, 0, False)
    live = ((p * seg + jnp.arange(seg, dtype=jnp.int32)) < length).astype(F32)
    live_two = live[:, None]
    tail = lax.dynamic_index_in_dim(inputs, z, 0, False)[seg - HALO :]
    before = lax.ppermute(tail, "seq", [(i, i + 1) for i in range(segments - 1)]).astype(F32)
    x_long = jnp.concatenate([before, x])
    n_long, inv_long = norm_keep(x_long)
    h_long = (n_long * norm_gain).astype(BF)
    n_one, inv_one, h_one = n_long[HALO:], inv_long[HALO:], h_long[HALO:]

    pre = jnp.stack([dot(h_long, m) for m in (q_mat, k_mat, v_mat)]).astype(BF)
    zgate = dot(h_one, g_mat)
    wide_pre = pre.astype(F32)
    conv_sum = sum(
        taps[:, lag][:, None, :] * wide_pre[:, HALO - lag : HALO - lag + seg] for lag in range(KW)
    )
    acts = jax.nn.silu(conv_sum).reshape(3, seg, heads, DH)
    q_normed, q_inverse = norm_keep(acts[0])
    k_normed, k_inverse = norm_keep(acts[1])
    query, keyed, valued = q_normed.astype(BF), k_normed.astype(BF), acts[2].astype(BF)
    live_three = live[:, None, None]
    masked_value = valued * live_three.astype(BF)
    write = jnp.einsum("tha,thb->hab", masked_value, keyed, preferred_element_type=F32) / seg

    def mix_states(values, coefficients):
        pieces, places = gather_states(values.astype(BF))
        total = 0.0
        for piece, place in zip(pieces, places):
            coefficient = lax.dynamic_index_in_dim(coefficients, place, 0, False)
            total = total + coefficient[:, None, None] * piece.astype(F32)
        return total.astype(BF)

    prior = mix_states(write, lax.dynamic_index_in_dim(carry, p, 0, False))
    raw_read = jnp.einsum("hab,thb->tha", prior, query, preferred_element_type=F32)
    readout, read_inverse = norm_keep(raw_read)

    keys_all = jnp.concatenate([pers_k, keyed])
    values_all = jnp.concatenate([pers_v, valued])
    valid = jnp.concatenate([jnp.ones((persistent,), F32), live])
    rows_index = jnp.arange(seg)[:, None]
    column = jnp.arange(persistent + seg)[None, :] - persistent
    allowed = (column < 0) | (column <= rows_index) & (valid[None, :] > 0.5)
    scale = DH ** (-0.5)
    score = jnp.einsum("thd,uhd->htu", query, keys_all, preferred_element_type=F32) * scale
    score = jnp.where(allowed[None], score, -1e30)
    top = jnp.max(score, axis=-1, keepdims=True)
    log_total = top + jnp.log(jnp.sum(jnp.exp(score - top), axis=-1, keepdims=True))
    prob = jnp.exp(score - log_total)
    prob_low = prob.astype(BF)
    attended = jnp.einsum("htu,uhd->thd", prob_low, values_all, preferred_element_type=F32)

    sigma = jax.nn.sigmoid(zgate)
    read_flat = readout.reshape(seg, -1)
    mixed = (attended.reshape(seg, -1) + sigma * read_flat).astype(BF)
    middle = x + live_two * dot_t(mixed, o_mat)
    n_two, inv_two = norm_keep(middle)
    h_two = (n_two * ffn_gain).astype(BF)

    gffn = (live_two * cot).astype(BF)
    ffn_out = 0.0
    dh_two = 0.0
    hidden_slots, gate_slots, up_slots = [], [], []
    for slot in ffn_slots:
        gate_value = dot(h_two, slot[0])
        up_value = dot(h_two, slot[1])
        silu_gate = jax.nn.silu(gate_value)
        hidden = (silu_gate * up_value).astype(BF)
        ffn_out = ffn_out + dot_t(hidden, slot[2])
        dhidden = dot(gffn, slot[2])
        dgate = (dhidden * up_value * silu_slope(gate_value)).astype(BF)
        dup = (dhidden * silu_gate).astype(BF)
        dh_two = dh_two + dot_t(dgate, slot[0]) + dot_t(dup, slot[1])
        hidden_slots.append(hidden)
        gate_slots.append(dgate)
        up_slots.append(dup)
    output = gather_rows((middle + live_two * ffn_out).astype(BF))
    g_gate, g_up, g_down = weight_grads(
        [(h_two, gate_slots), (h_two, up_slots), (gffn, hidden_slots)], True
    )

    grad_ffn_gain = jnp.sum(dh_two * n_two, axis=0)
    dmiddle = cot + norm_back(dh_two * ffn_gain, n_two, inv_two)
    gattn = (live_two * dmiddle).astype(BF)
    dmixed = dot(gattn, o_mat)
    datt = dmixed.astype(BF).reshape(seg, heads, DH)
    dzgate = (dmixed * read_flat * sigma * (1.0 - sigma)).astype(BF)
    dread = norm_back((dmixed * sigma).reshape(seg, heads, DH), readout, read_inverse).astype(BF)
    dprior = jnp.einsum("tha,thb->hab", dread, query, preferred_element_type=F32)
    dwrite = mix_states(dprior, lax.dynamic_index_in_dim(carry, p, 1, False))
    dquery_mem = jnp.einsum("hab,tha->thb", prior, dread, preferred_element_type=F32)
    dprob = jnp.einsum("thd,uhd->htu", datt, values_all, preferred_element_type=F32)
    row_dot = jnp.sum(prob * dprob, axis=-1, keepdims=True)
    dscore = (prob * (dprob - row_dot)).astype(BF)
    dquery = (
        jnp.einsum("htu,uhd->thd", dscore, keys_all, preferred_element_type=F32) * scale
        + dquery_mem
    )
    dkeys = jnp.einsum("htu,thd->uhd", dscore, query, preferred_element_type=F32) * scale
    dvalues = jnp.einsum("htu,thd->uhd", prob_low, datt, preferred_element_type=F32)
    dvals = (
        dvalues[persistent:]
        + live_three * jnp.einsum("hab,thb->tha", dwrite, keyed, preferred_element_type=F32) / seg
    )
    dkey = (
        dkeys[persistent:]
        + jnp.einsum("hab,tha->thb", dwrite, masked_value, preferred_element_type=F32) / seg
    )
    dact = jnp.stack(
        [norm_back(dquery, q_normed, q_inverse), norm_back(dkey, k_normed, k_inverse), dvals]
    ).reshape(3, seg, -1)
    dconv = dact * silu_slope(conv_sum)
    longer = jnp.pad(dconv, ((0, 0), (rim, rim), (0, 0)))
    spread = sum(
        taps[:, lag][:, None, :] * longer[:, lag : lag + seg + rim] for lag in range(KW)
    )
    grad_conv = jnp.stack(
        [
            jnp.sum(dconv * wide_pre[:, HALO - lag : HALO - lag + seg], axis=1)
            for lag in range(KW)
        ],
        axis=1,
    )
    back = lax.ppermute(
        spread[:, :rim].astype(BF), "seq", [(i + 1, i) for i in range(segments - 1)]
    ).astype(F32)
    dpre = spread[:, rim:] + jnp.pad(back, ((0, 0), (seg - rim, 0), (0, 0)))
    dpre = dpre.astype(BF)

    dh_one = (
        dot_t(dpre[0], q_mat) + dot_t(dpre[1], k_mat) + dot_t(dpre[2], v_mat) + dot_t(dzgate, g_mat)
    )
    grad_norm_gain = jnp.sum(dh_one * n_one, axis=0)
    input_grad = gather_rows(
        (dmiddle + norm_back(dh_one * norm_gain, n_one, inv_one)).astype(BF)
    )

    def by_slot(value):
        return [value[..., k * width : (k + 1) * width] for k in range(shards)]

    g_query, g_key, g_value, g_zgate, g_out = weight_grads(
        [(h_one, by_slot(d)) for d in (dpre[0], dpre[1], dpre[2], dzgate)]
        + [(gattn, by_slot(mixed))],
        False,
    )
    rows = jnp.concatenate(
        [
            grad_conv.reshape(3 * KW, -1),
            dkeys[:persistent].reshape(persistent, -1),
            dvalues[:persistent].reshape(persistent, -1),
        ]
    )
    gains = jnp.concatenate([grad_norm_gain, grad_ffn_gain]).reshape(-1, width)
    rows, gains = sum_small(by_slot(rows), gains)
    gains = gains.reshape(2, features)
    return (
        output,
        input_grad,
        gains[0],
        g_query,
        g_key,
        g_value,
        g_zgate,
        rows[: 3 * KW].reshape(3, KW, width),
        rows[3 * KW : 3 * KW + persistent],
        rows[3 * KW + persistent :],
        g_out.T,
        gains[1],
        g_gate,
        g_up,
        g_down.T,
    )


ROWS = 16
BLOCK = 128
SCALE = DH ** (-0.5)


def shift_sum(source, taps, first, rows, step):
    total = taps[0:1] * source[pl.ds(first, rows)]
    for lag in range(1, KW):
        total = total + taps[lag : lag + 1] * source[pl.ds(first + step * lag, rows)]
    return total


def live_rows(first, rows, length, segment_start):
    place = segment_start + first + lax.broadcasted_iota(jnp.int32, (rows, 1), 0)
    return (place < length).astype(F32)


def live_columns(columns, length, segment_start):
    return segment_start + lax.broadcasted_iota(jnp.int32, (1, columns), 1) < length


def masked_scores(query, keys, pers_k, index, columns_live):
    width = keys.shape[0]
    raw = dot_t(query, keys) * SCALE
    row = index * BLOCK + lax.broadcasted_iota(jnp.int32, (BLOCK, width), 0)
    column = lax.broadcasted_iota(jnp.int32, (BLOCK, width), 1)
    keep = (column <= row) & columns_live[:, :width]
    return jnp.where(keep, raw, -1e30), dot_t(query, pers_k) * SCALE


def attention_back_slot(k, refs, length, segment_start):
    query, keyed, valued, lse, datt, dread, prior, small, dqkv, small_grad = refs
    seg = query.shape[1]
    columns_live = live_columns(seg, length, segment_start)
    turn = lambda a, b: lax.dot_general(a, b, (((0,), (0,)), ((), ())), preferred_element_type=F32)
    for head in range(query.shape[2] // DH):
        lanes = slice(head * DH, (head + 1) * DH)
        pers_keys_sum = jnp.zeros((16, DH), F32)
        pers_values_sum = jnp.zeros((16, DH), F32)
        pk = small[k, PERS_K : PERS_K + 16, lanes].astype(BF)
        pv = small[k, PERS_V : PERS_V + 16, lanes].astype(BF)
        dqkv[1, :, lanes] = jnp.zeros((seg, DH), F32)
        dqkv[2, :, lanes] = jnp.zeros((seg, DH), F32)
        dqkv[0, :, lanes] = dot(dread[k, :, lanes], prior[k, head])
        for index in range(seg // BLOCK):
            rows = pl.ds(index * BLOCK, BLOCK)
            upto = pl.ds(0, (index + 1) * BLOCK)
            q, d = query[k, rows, lanes], datt[k, rows, lanes]
            keys = keyed[k, upto, lanes]
            score, pers = masked_scores(q, keys, pk, index, columns_live)
            log_total = lse[k, head, rows]
            prob, prob_p = jnp.exp(score - log_total), jnp.exp(pers - log_total)
            grad = dot_t(d, valued[k, upto, lanes])
            grad_p = dot_t(d, pv)
            row_dot = jnp.sum(prob * grad, axis=-1, keepdims=True) + jnp.sum(
                prob_p * grad_p, axis=-1, keepdims=True
            )
            dscore = (prob * (grad - row_dot)).astype(BF)
            dscore_p = (prob_p * (grad_p - row_dot)).astype(BF)
            dqkv[0, rows, lanes] += (dot(dscore, keys) + dot(dscore_p, pk)) * SCALE
            dqkv[1, upto, lanes] += turn(dscore, q) * SCALE
            dqkv[2, upto, lanes] += turn(prob.astype(BF), d)
            pers_keys_sum = pers_keys_sum + turn(dscore_p, q)
            pers_values_sum = pers_values_sum + turn(prob_p.astype(BF), d)
        small_grad[k, PERS_K : PERS_K + 16, lanes] = pers_keys_sum * SCALE
        small_grad[k, PERS_V : PERS_V + 16, lanes] = pers_values_sum


def conv_back_slot(k, refs, length, segment_start):
    pre, small, keyed, valued, dwrite, dqkv, dconv, small_grad, wide = refs
    seg = keyed.shape[1]
    heads = keyed.shape[2] // DH
    for i in range(3):
        wide[i] = pre[i, k].astype(F32)
    sums = [[jnp.zeros((1, heads * DH), F32) for _ in range(KW)] for _ in range(3)]
    for first in range(0, seg, BLOCK):
        rows = pl.ds(first, BLOCK)
        live = live_rows(first, BLOCK, length, segment_start)
        for i in range(3):
            conv = shift_sum(wide.at[i], taps_of(small, k, i), ROWS + first, BLOCK, -1)
            sigma = jax.nn.sigmoid(conv)
            act = conv * sigma
            parts = []
            for head in range(heads):
                lanes = slice(head * DH, (head + 1) * DH)
                grad = dqkv[i, rows, lanes]
                if i == 1:
                    masked = valued[k, rows, lanes] * live.astype(BF)
                    grad = grad + dot(masked, dwrite[k, head]) / seg
                if i == 2:
                    grad = grad + live * dot_t(keyed[k, rows, lanes], dwrite[k, head]) / seg
                else:
                    grad = norm_back(grad, *norm_keep(act[:, lanes]))
                parts.append(grad)
            result = jnp.concatenate(parts, axis=1) * (sigma * (1.0 + conv * (1.0 - sigma)))
            dconv[i, 0, rows] = result
            for lag in range(KW):
                sums[i][lag] = sums[i][lag] + jnp.sum(
                    result * wide[i, pl.ds(ROWS + first - lag, BLOCK)], axis=0, keepdims=True
                )
    for i in range(3):
        for lag in range(KW):
            row = TAPS + KW * i + lag
            small_grad[k, row : row + 1] = sums[i][lag]


SHAPE = jax.ShapeDtypeStruct
VMEM_LIMIT = 127 * 512 * 1024


MESH = pl.DeviceIdType.MESH
SKEW_ONE, SKEW_TWO = 2, 4


class Links:
    def __init__(self, send, recv):
        self.send, self.recv = send, recv
        self.sent = 0
        self.names = {}
        self.always, self.middles = [], []
        self.p, self.z = lax.axis_index("seq"), lax.axis_index("head")
        self.middle = (self.z == 1) | (self.z == 2)

    def greet(self):
        barrier = pltpu.get_barrier_semaphore()
        for flip in range(1, 8):
            pl.semaphore_signal(barrier, device_id=(self.p ^ flip, self.z), device_id_type=MESH)
        for flip in (1, 2, 3):
            pl.semaphore_signal(barrier, device_id=(self.p, self.z ^ flip), device_id_type=MESH)
        pl.semaphore_wait(barrier, 10)

    def place(self, name):
        return self.recv.at[self.names.setdefault(name, len(self.names))]

    def copy(self, source, target, name, device):
        index = self.sent
        self.sent += 1
        return pltpu.make_async_remote_copy(
            src_ref=source, dst_ref=target, send_sem=self.send.at[index], recv_sem=self.place(name),
            device_id=device, device_id_type=MESH,
        )

    def along_seq(self, source, target, name, flip):
        copy = self.copy(source, target, name, (self.p ^ flip, self.z))
        copy.start()
        self.always.append((lambda: source, self.sent - 1))

    def along_head(self, source, target, name, flip, waits):
        index = self.sent
        copy = self.copy(source(), target(), name, (self.p, self.z ^ flip))
        copy.start()
        waits.append((source, index))

    def arrived(self, target, name):
        pltpu.make_async_remote_copy(
            src_ref=target, dst_ref=target, send_sem=self.send.at[0], recv_sem=self.place(name),
            device_id=(self.p, self.z ^ 1), device_id_type=MESH,
        ).wait_recv()

    def gone(self, source, index):
        pltpu.make_async_remote_copy(
            src_ref=source(), dst_ref=source(), send_sem=self.send.at[index], recv_sem=self.recv.at[0],
            device_id=(self.p, self.z ^ 1), device_id_type=MESH,
        ).wait_send()

    def finish(self):
        for source, index in self.always:
            self.gone(source, index)

        @pl.when(self.middle)
        def _():
            for source, index in self.middles:
                self.gone(source, index)


class LineGather:
    def __init__(self, links, name, view, fixed=False):
        self.links, self.name, self.view, self.fixed = links, name, view, fixed

    def start(self, sources):
        links = self.links
        for source, view in sources:
            links.along_head(source, lambda: view(1), (self.name, 1), 1, links.always)

        @pl.when(links.middle)
        def _():
            for source, view in sources:
                links.along_head(source, lambda: view(3), (self.name, 3), 3, links.middles)

    def forward(self, k, flip):
        view, there = self.view, k ^ flip
        self.links.along_head(
            lambda: view(k), lambda: view(k if self.fixed else there), (self.name, there), flip,
            self.links.middles,
        )

    def step(self, k):
        links, name, view = self.links, self.name, self.view
        if k == 1:
            links.arrived(view(1), (name, 1))

            @pl.when(links.middle)
            def _():
                self.forward(1, 3)
                links.arrived(view(3), (name, 3))
                self.forward(3, 1)

        if k == 2:
            links.arrived(view(2), (name, 2))

            @pl.when(links.middle)
            def _():
                self.forward(2, 1)

        if k == 3:

            @pl.when(~links.middle)
            def _():
                links.arrived(view(3), (name, 3))


class PlaneGather:
    def __init__(self, links, name, view, x_first):
        self.links, self.name, self.view = links, name, view
        self.near, self.far = (2, 4) if x_first else (4, 2)

    def send(self, j, flip):
        links = self.links
        block = self.view(links.p ^ j)
        links.along_seq(block, block, (self.name, j ^ flip), flip)

    def wait(self, j):
        self.links.arrived(self.view(self.links.p ^ j), (self.name, j))

    def start(self):
        self.send(0, self.near)
        self.send(0, self.far)
        self.send(0, 1)

    def step(self):
        self.wait(self.near)
        self.send(self.near, self.far)
        self.send(self.near, 1)
        self.wait(self.far)
        self.send(self.far, 1)

    def last(self):
        self.wait(6)
        self.send(6, 1)

    def end(self):
        for j in (1, 3, 5, 7):
            self.wait(j)


def weight_pieces(links, weights, out_w, gate_up, down):
    block = lambda q: pl.ds(pl.multiple_of(q * 128, 128), 128)
    views = {
        "proj": (lambda k, q: weights.at[k, :, block(q), :], True),
        "out": (lambda k, q: out_w.at[k, :, block(q)], False),
        "ffn": (lambda k, q: gate_up.at[k, :, block(q), :], False),
        "down": (lambda k, q: down.at[k, :, block(q)], True),
    }
    pieces = {}
    for name, (view, x_first) in views.items():
        line = LineGather(links, name, lambda k, view=view: view(k, links.p))
        planes = [
            PlaneGather(links, (name, k), lambda q, view=view, k=k: view(k, q), x_first)
            for k in (1, 2, 3)
        ]
        pieces[name] = (line, planes)
    return pieces


def weight_events(links, own, weights, out_w, gate_up, down):
    q_own, k_own, v_own, g_own, o_own, gate_own, up_own, down_own = own
    mine = pl.ds(pl.multiple_of(links.p * 128, 128), 128)
    pieces = weight_pieces(links, weights, out_w, gate_up, down)
    starts = {
        "proj": [
            (lambda ref=ref: ref.at[mine, :], lambda k, i=i: weights.at[k, i, mine, :])
            for i, ref in enumerate((q_own, k_own, v_own, g_own))
        ],
        "out": [(lambda: o_own.at[:, mine], lambda k: out_w.at[k, :, mine])],
        "ffn": [
            (lambda ref=ref: ref.at[mine, :], lambda k, i=i: gate_up.at[k, i, mine, :])
            for i, ref in enumerate((gate_own, up_own))
        ],
        "down": [(lambda: down_own.at[:, mine], lambda k: down.at[k, :, mine])],
    }
    begin = lambda name: pieces[name][0].start(starts[name])
    units = [("proj", k) for k in (1, 2, 3)] + [("ffn", 1)] + [("out", k) for k in (1, 2, 3)] + [("down", 1)]
    units += [(name, k) for k in (2, 3) for name in ("ffn", "down")]
    when = {0: ["proj"], 1: ["ffn"], 2: ["out"], 3: ["down"]}
    count = len(units)
    events = []
    for i in range(count + SKEW_TWO):
        for name in when.get(i, []):
            events.append((None, lambda name=name: begin(name)))
        if i < count:
            name, k = units[i]

            def first(name=name, k=k):
                pieces[name][0].step(k)
                pieces[name][1][k - 1].start()

            events.append((None, first))
        if 0 <= i - SKEW_ONE < count:
            name, k = units[i - SKEW_ONE]
            events.append((None, pieces[name][1][k - 1].step))
        if 0 <= i - SKEW_TWO < count:
            name, k = units[i - SKEW_TWO]
            events.append(((name, k), pieces[name][1][k - 1].last))
    return events, pieces


PERS_K, PERS_V, TAPS, GAINS, SMALL = 0, 16, 32, 48, 56


def taps_of(small, k, i):
    return small[k, TAPS + KW * i : TAPS + KW * (i + 1)]


def carry_in_kernel(every, place, forward, backward):
    count, lanes = every.shape[0], every.shape[2]
    row = lax.broadcasted_iota(jnp.int32, (count, lanes), 0)
    mem = jnp.zeros((count, lanes), F32)
    mom = jnp.zeros((count, lanes), F32)
    ahead = jnp.zeros((count, lanes), F32)
    behind = jnp.zeros((count, lanes), F32)
    for c in range(count):
        ahead = jnp.where(place == c, mem, ahead)
        mine = jnp.sum(jnp.where(row == place, mem, 0.0), axis=0, keepdims=True)
        behind = jnp.where(row == c, mine, behind)
        mom = every[c, 1:2] * mom + (row == c).astype(F32)
        mem = every[c, 0:1] * mem + mom
    forward[...] = ahead
    backward[...] = behind


def mixed_state(states, coefficients, k, head):
    lane = 2 * k + head
    total = coefficients[0:1, lane : lane + 1] * states[0, k, head].astype(F32)
    for q in range(1, states.shape[0]):
        total = total + coefficients[q : q + 1, lane : lane + 1] * states[q, k, head].astype(F32)
    return total.astype(BF)


def project_slot(k, h_long, weights, pre, zgate, wide):
    seg = zgate.shape[1]
    for i in range(3):
        rounded = dot(h_long[...], weights[i]).astype(BF)
        pre[i, k] = rounded
        wide[i] = rounded.astype(F32)
    zgate[k] = dot(h_long[pl.ds(ROWS, seg)], weights[3])


def convolve_slot(k, small, query, keyed, valued, wide):
    seg = query.shape[1]
    heads = query.shape[2] // DH

    for first in range(0, seg, BLOCK):
        rows = pl.ds(first, BLOCK)
        for i in range(3):
            conv = shift_sum(wide.at[i], taps_of(small, k, i), ROWS + first, BLOCK, -1)
            act = conv * jax.nn.sigmoid(conv)
            if i == 2:
                valued[k, rows] = act.astype(BF)
                continue
            target = (query, keyed)[i]
            for head in range(heads):
                lanes = slice(head * DH, (head + 1) * DH)
                target[k, rows, lanes] = norm_keep(act[:, lanes])[0].astype(BF)


def write_slot(k, p, keyed, valued, states, length, segment_start):
    seg = keyed.shape[1]
    seg_live = live_rows(0, seg, length, segment_start).astype(BF)
    for head in range(keyed.shape[2] // DH):
        lanes = slice(head * DH, (head + 1) * DH)
        masked = valued[k, :, lanes] * seg_live
        states[p, k, head] = (
            lax.dot_general(
                masked, keyed[k, :, lanes], (((0,), (0,)), ((), ())), preferred_element_type=F32
            )
            / seg
        ).astype(BF)


def attend_head(k, head, small, query, keyed, valued, att, lse, length, segment_start):
    seg = query.shape[1]
    columns_live = live_columns(seg, length, segment_start)
    lanes = slice(head * DH, (head + 1) * DH)
    pers_k = small[k, PERS_K : PERS_K + 16, lanes].astype(BF)
    pers_v = small[k, PERS_V : PERS_V + 16, lanes].astype(BF)
    for index in range(seg // BLOCK):
        rows = pl.ds(index * BLOCK, BLOCK)
        upto = pl.ds(0, (index + 1) * BLOCK)
        score, pers = masked_scores(
            query[k, rows, lanes], keyed[k, upto, lanes], pers_k, index, columns_live
        )
        top = jnp.maximum(
            jnp.max(score, axis=-1, keepdims=True), jnp.max(pers, axis=-1, keepdims=True)
        )
        score, pers = jnp.exp(score - top), jnp.exp(pers - top)
        total = jnp.sum(score, axis=-1, keepdims=True) + jnp.sum(pers, axis=-1, keepdims=True)
        inverse = 1.0 / total
        lse[k, head, rows] = top + jnp.log(total)
        att[k, rows, lanes] = dot((score * inverse).astype(BF), valued[k, upto, lanes]) + dot(
            (pers * inverse).astype(BF), pers_v
        )


def read_slot(k, prior, query, zgate, att, mixed):
    for head in range(query.shape[2] // DH):
        lanes = slice(head * DH, (head + 1) * DH)
        normed, _ = norm_keep(dot_t(query[k, :, lanes], prior[k, head]))
        mixed[k, :, lanes] = (
            att[k, :, lanes] + jax.nn.sigmoid(zgate[k, :, lanes]) * normed
        ).astype(BF)


def ffn_rows(rows, h_two, gffn, weights_gu, weights_d, stage, out_acc, grad_acc):
    gate = dot(h_two[rows], weights_gu[0])
    up = dot(h_two[rows], weights_gu[1])
    sigma = jax.nn.sigmoid(gate)
    silu = gate * sigma
    low = (silu * up).astype(BF)
    stage[0, rows] = low
    out_acc[rows] += dot(low, weights_d[...])
    back = dot_t(gffn[rows], weights_d[...])
    low_gate = (back * up * (sigma * (1.0 + gate * (1.0 - sigma)))).astype(BF)
    low_up = (back * silu).astype(BF)
    stage[1, rows] = low_gate
    stage[2, rows] = low_up
    grad_acc[rows] += dot_t(low_gate, weights_gu[0]) + dot_t(low_up, weights_gu[1])


def tail_slot(k, out_w, gattn, query, prior, zgate, datt, dzgate, dread, dprior):
    dmixed = dot_t(gattn[...], out_w[k])
    datt[k] = dmixed.astype(BF)
    for head in range(dmixed.shape[1] // DH):
        lanes = slice(head * DH, (head + 1) * DH)
        sigma = jax.nn.sigmoid(zgate[k, :, lanes])
        readout, rinv = norm_keep(dot_t(query[k, :, lanes], prior[k, head]))
        grad = dmixed[:, lanes] * sigma
        dzgate[k, :, lanes] = (grad * readout * (1.0 - sigma)).astype(BF)
        low = norm_back(grad, readout, rinv).astype(BF)
        dread[k, :, lanes] = low
        dprior[k, head] = lax.dot_general(
            low, query[k, :, lanes], (((0,), (0,)), ((), ())), preferred_element_type=F32
        ).astype(BF)


class Steps:
    def __init__(self, events):
        self.events, self.at, self.done = events, 0, set()

    def run(self, count=1):
        for _ in range(count):
            if self.at < len(self.events):
                label, function = self.events[self.at]
                function()
                self.at += 1
                self.done.add(label)

    def until(self, *labels):
        while not all(label in self.done for label in labels):
            self.run()


def front_kernel(
    lengths, gain, ffn_gain, own_small, own_decays,
    inputs, cotangent, q_own, k_own, v_own, g_own, o_own, gate_own, up_own, down_own,
    x_long, h_long, pre, query, keyed, valued, lse, prior, small, backward, mixed, h_two, gffn,
    output, dmiddle, gattn, datt, dzgate, dread, dprior, gain_grad,
    weights, hidden, dgate, dup, out_w, gate_up, down,
    cot, zgate, att, wide, states, every, forward, wproj, wout, wgu, wdown, stage, out_acc, grad_acc,
    send, recv, sem_x, sem_proj, sem_out, sem_ffn, sem_stage,
):
    links = Links(send, recv)
    p, z = links.p, links.z
    seg = h_two.shape[0]
    length, start = lengths[z], p * seg
    own = (q_own, k_own, v_own, g_own, o_own, gate_own, up_own, down_own)
    load_x = pltpu.make_async_copy(inputs.at[z], x_long.at[pl.ds(ROWS, seg)], sem_x.at[0])
    load_cot = pltpu.make_async_copy(cotangent.at[z], cot, sem_x.at[1])
    load_x.start()

    def proj_loads(k):
        if k == 0:
            return [
                pltpu.make_async_copy(ref, wproj.at[i], sem_proj.at[i]) for i, ref in enumerate(own[:4])
            ]
        return [pltpu.make_async_copy(weights.at[k], wproj, sem_proj.at[0])]

    def out_load(k):
        return pltpu.make_async_copy(o_own if k == 0 else out_w.at[k], wout.at[k], sem_out.at[k])

    def ffn_loads(k):
        side = k % 2
        if k == 0:
            gu = [
                pltpu.make_async_copy(gate_own, wgu.at[0, 0], sem_ffn.at[0, 0]),
                pltpu.make_async_copy(up_own, wgu.at[0, 1], sem_ffn.at[0, 2]),
            ]
        else:
            gu = [pltpu.make_async_copy(gate_up.at[k], wgu.at[side], sem_ffn.at[side, 0])]
        return gu + [
            pltpu.make_async_copy(down_own if k == 0 else down.at[k], wdown.at[side], sem_ffn.at[side, 1])
        ]

    def go(copies):
        for copy in copies:
            copy.start()

    def come(copies):
        for copy in copies:
            copy.wait()

    go(proj_loads(0))
    go([load_cot, out_load(0)])
    go(ffn_loads(0))
    every[p] = own_decays[...]
    small[0] = own_small[...]
    links.greet()
    events, pieces = weight_events(links, own, weights, out_w, gate_up, down)
    steps = Steps(events)

    @pl.when(p < 7)
    def _():
        links.copy(
            inputs.at[z, pl.ds(seg - ROWS, ROWS)], x_long.at[pl.ds(0, ROWS)], "rows", (p + 1, z)
        ).start()

    rows_index = links.sent - 1
    for j in range(1, 8):
        links.along_seq(own_decays, every.at[p], ("decays", j), j)
    for k in (1, 2, 3):
        links.copy(own_small, small.at[k], ("small", k), (p, z ^ k)).start()
        links.always.append((lambda: own_small, links.sent - 1))
    steps.run()

    load_x.wait()

    @pl.when(p == 0)
    def _():
        x_long[pl.ds(0, ROWS)] = jnp.zeros((ROWS, x_long.shape[1]), BF)

    @pl.when(p > 0)
    def _():
        links.arrived(x_long.at[pl.ds(0, ROWS)], "rows")

    @pl.loop(0, 3)
    def _(c):
        rows = pl.ds(pl.multiple_of(c * 176, 16), 176)
        normed, _ = norm_keep(x_long[rows].astype(F32))
        h_long[rows] = (normed * gain[...]).astype(BF)

    exchanges = [PlaneGather(links, ("states", k), lambda q, k=k: states.at[q, k], k % 2 == 0) for k in range(4)]
    complete = lambda name, k: pieces[name][1][k - 1].end()
    come(proj_loads(0))
    for k in range(4):
        project_slot(k, h_long, wproj, pre, zgate, wide)
        steps.run()
        if k == 0:
            for other in (1, 2, 3):
                links.arrived(small.at[other], ("small", other))
        convolve_slot(k, small, query, keyed, valued, wide)
        steps.run()
        write_slot(k, p, keyed, valued, states, length, start)
        exchanges[k].start()
        attend_head(k, 0, small, query, keyed, valued, att, lse, length, start)
        steps.run()
        exchanges[k].step()
        attend_head(k, 1, small, query, keyed, valued, att, lse, length, start)
        steps.run()
        exchanges[k].last()
        if k < 3:
            steps.until(("proj", k + 1))
            complete("proj", k + 1)
            go(proj_loads(k + 1))
            come(proj_loads(k + 1))
    for j in range(1, 8):
        links.arrived(every.at[p ^ j], ("decays", j))
    carry_in_kernel(every, p, forward, backward)
    for k in (1, 2, 3):
        steps.until(("out", k))
        complete("out", k)
        go([out_load(k)])
    for k in range(4):
        exchanges[k].end()
        for head in range(2):
            prior[k, head] = mixed_state(states, forward, k, head)
        read_slot(k, prior, query, zgate, att, mixed)
        come([out_load(k)])

        @pl.loop(0, 2)
        def _(c):
            rows = pl.ds(pl.multiple_of(c * 256, 256), 256)
            part = dot(mixed[k, rows], wout[k])
            if k == 0:
                grad_acc[rows] = part
            else:
                grad_acc[rows] += part

        steps.run()
    load_cot.wait()

    @pl.loop(0, seg // BLOCK)
    def _(c):
        first = pl.multiple_of(c * BLOCK, BLOCK)
        rows = pl.ds(first, BLOCK)
        live = live_rows(first, BLOCK, length, start)
        value = x_long[pl.ds(pl.multiple_of(ROWS + first, 16), BLOCK)].astype(F32) + live * grad_acc[rows]
        dmiddle[rows] = value
        normed, _ = norm_keep(value)
        h_two[rows] = (normed * ffn_gain[...]).astype(BF)
        gffn[rows] = (live * cot[rows].astype(F32)).astype(BF)
        out_acc[rows] = jnp.zeros((BLOCK, out_acc.shape[1]), F32)
        grad_acc[rows] = jnp.zeros((BLOCK, out_acc.shape[1]), F32)

    def stores(k):
        return [
            pltpu.make_async_copy(stage.at[k % 2, i], ref.at[k], sem_stage.at[k % 2, i])
            for i, ref in enumerate((hidden, dgate, dup))
        ]

    for k in range(4):
        if k == 3:
            steps.until(("ffn", 3), ("down", 3))
            complete("ffn", 3)
            complete("down", 3)
            go(ffn_loads(3))
        come(ffn_loads(k))
        if k < 2:
            steps.until(("ffn", k + 1), ("down", k + 1))
            complete("ffn", k + 1)
            complete("down", k + 1)
            go(ffn_loads(k + 1))
        if k >= 2:
            come(stores(k - 2))

        @pl.loop(0, 2)
        def _(c):
            rows = pl.ds(pl.multiple_of(c * 256, 256), 256)
            ffn_rows(rows, h_two, gffn, wgu.at[k % 2], wdown.at[k % 2], stage.at[k % 2], out_acc, grad_acc)

        go(stores(k))
        steps.run(3)
    gain_grad[...] = jnp.zeros_like(gain_grad)

    @pl.loop(0, seg // BLOCK)
    def _(c):
        first = pl.multiple_of(c * BLOCK, BLOCK)
        rows = pl.ds(first, BLOCK)
        live = live_rows(first, BLOCK, length, start)
        value = dmiddle[rows]
        output[rows] = (value + live * out_acc[rows]).astype(BF)
        normed, inverse = norm_keep(value)
        grad = grad_acc[rows]
        gain_grad[...] += jnp.sum(grad * normed, axis=0, keepdims=True)
        result = cot[rows].astype(F32) + norm_back(grad * ffn_gain[...], normed, inverse)
        dmiddle[rows] = result
        gattn[rows] = (live * result).astype(BF)

    for k in range(4):
        tail_slot(k, wout, gattn, query, prior, zgate, datt, dzgate, dread, dprior)
    come(stores(2))
    come(stores(3))

    @pl.when(p < 7)
    def _():
        links.gone(lambda: x_long.at[pl.ds(0, ROWS)], rows_index)

    links.finish()


class PlaneReduce:
    def __init__(self, links, name, blocks, first, second, x_first):
        self.links, self.name, self.x_first = links, name, x_first
        self.blocks, self.first, self.second = blocks, first, second

    def start(self):
        away = self.blocks.at[:, :, 1] if self.x_first else self.blocks.at[:, 1]
        self.links.along_seq(away, self.first, (self.name, 1), 2 if self.x_first else 4)

    def step(self):
        self.links.arrived(self.first, (self.name, 1))
        for i in range(2):
            y, x = (i, 0) if self.x_first else (0, i)

            @pl.loop(0, self.blocks.shape[0])
            def _(m):
                self.blocks[m, y, x] = add(self.blocks[m, y, x], self.first[m, i])

        y, x = (1, 0) if self.x_first else (0, 1)
        self.links.along_seq(
            self.blocks.at[:, y, x], self.second, (self.name, 2), 4 if self.x_first else 2
        )

    def last(self):
        self.links.arrived(self.second, (self.name, 2))

        @pl.loop(0, self.blocks.shape[0])
        def _(m):
            self.blocks[m, 0, 0] = add(self.blocks[m, 0, 0], self.second[m])


class LineReduce:
    def __init__(self, links, name, blocks, landing, result):
        self.links, self.name, self.blocks = links, name, blocks
        self.landing, self.result = landing, result
        self.ends = []

    def send(self, k, slot, flip, waits):
        self.links.along_head(
            lambda: self.blocks(k), lambda: self.landing.at[slot], (self.name, slot), flip, waits
        )

    def merge(self, k, slot):
        self.links.arrived(self.landing.at[slot], (self.name, slot))
        block = self.blocks(k)

        @pl.loop(0, self.landing.shape[1])
        def _(m):
            block[m] = add(block[m], self.landing[slot, m])

    def step(self, k):
        links, middles = self.links, self.links.middles

        @pl.when(~links.middle)
        def _():
            if k == 3:
                self.send(3, 0, 1, self.ends)
            if k == 2:
                self.send(2, 1, 1, self.ends)
            if k == 1:
                self.send(1, 2, 1, self.ends)
            if k == 0:
                self.total([3])

        @pl.when(links.middle)
        def _():
            if k == 2:
                self.merge(2, 0)
                self.send(2, 4, 3, middles)
                self.merge(3, 1)
                self.send(3, 5, 3, middles)
            if k == 1:
                self.merge(1, 4)
                self.send(1, 3, 1, middles)
            if k == 0:
                self.total([2, 5])

    def total(self, slots):
        block = self.blocks(0)
        for slot in slots:
            self.links.arrived(self.landing.at[slot], (self.name, slot))

        @pl.loop(0, self.landing.shape[1])
        def _(m):
            value = block[m].astype(F32)
            for slot in slots:
                value = value + self.landing[slot, m].astype(F32)
            self.result[m] = value

    def finish(self):
        @pl.when(~self.links.middle)
        def _():
            for source, index in self.ends:
                self.links.gone(source, index)


class Pairs:
    def __init__(self, buffers, sems):
        self.buffers, self.sems = buffers, sems

    def copies(self, slot, own, peer):
        rows = own.shape[0]
        return [
            pltpu.make_async_copy(own, self.buffers.at[slot, pl.ds(0, rows)], self.sems.at[slot, 0]),
            pltpu.make_async_copy(peer, self.buffers.at[slot, pl.ds(rows, rows)], self.sems.at[slot, 1]),
        ]

    def start(self, slot, own, peer):
        for copy in self.copies(slot, own, peer):
            copy.start()

    def wait(self, slot, own, peer):
        for copy in self.copies(slot, own, peer):
            copy.wait()


def load_turned(links, own, peer, staged, turned, sems):
    rows = own.shape[0]
    copies = []
    for i, j in enumerate((0, 2, 4, 6)):
        block = pl.ds(pl.multiple_of((links.p ^ j) * 128, 128), 128)
        for side, ref in enumerate((own, peer)):
            copy = pltpu.make_async_copy(
                ref.at[:, block], staged.at[pl.ds(side * rows, rows), pl.ds(i * 128, 128)], sems.at[i, side]
            )
            copy.start()
            copies.append(copy)
    for copy in copies:
        copy.wait()
    for i in range(4):
        turned[pl.ds(i * 128, 128)] = staged[:, pl.ds(i * 128, 128)].T


def conv_back(k, refs, length, segment_start):
    pre, small, keyed, valued, dwrite, dqkv, dslot, small_grad, wide, dpre, part, halo = refs
    conv_back_slot(
        k, (pre, small, keyed, valued, dwrite, dqkv, dslot, small_grad, wide), length, segment_start
    )
    seg = keyed.shape[1]
    for i in range(3):
        dslot[i, 0, pl.ds(seg, 8)] = jnp.zeros((8, dslot.shape[3]), F32)
        halo[i, k] = dslot[i, 0, pl.ds(0, 8)]
        weights = taps_of(small, k, i)
        for first in range(0, seg, BLOCK):
            value = shift_sum(dslot.at[i, 0], weights, first, BLOCK, 1)
            dpre[i, k, pl.ds(first, BLOCK)] = value.astype(BF)
            if first + BLOCK == seg:
                part[i, k] = value[BLOCK - 16 :]


def back_all_kernel(
    lengths, carry,
    query, keyed, valued, lse, datt, dread, prior, small, pre, dprior, x_long, gain, dmiddle, ffn_gain_grad,
    output, h_two, gffn, hidden, dgate, dup, weights, dzgate, q_own, k_own, v_own, g_own,
    all_output, g_ffn, small_grad, dpre, input_grad,
    peer_h_two, peer_gffn, peer_hidden, peer_dgate, peer_dup,
    states, dwrite, dqkv, wide, dslot, part, halo, halo_in, ext, acc, wbuf, zbuf,
    staged, turned, pairs, blocks, first_in, second_in, landing,
    send, recv, sems_turned, sems_pairs, sems_weights, sem_own,
):
    links = Links(send, recv)
    p, z = links.p, links.z
    seg = dmiddle.shape[0]
    length, start = lengths[z], p * seg
    states[p] = dprior[...]
    own_output = pltpu.make_async_copy(output, all_output.at[z], sem_own.at[0])
    own_output.start()
    links.greet()
    exchange = PlaneGather(links, "states", lambda q: states.at[q], True)
    exchange.start()
    to_peer = [("h_two", h_two, peer_h_two)]
    for k in (3, 2, 1, 0):
        to_peer.append((("dgate", k), dgate.at[k], peer_dgate.at[k]))
        to_peer.append((("dup", k), dup.at[k], peer_dup.at[k]))
        if k == 3:
            to_peer.append(("gffn", gffn, peer_gffn))
        to_peer.append((("hidden", k), hidden.at[k], peer_hidden.at[k]))
    for name, source, target in to_peer:
        links.along_seq(source, target, ("peer", name), 1)
    line = LineGather(links, "output", lambda k: all_output.at[z ^ k], fixed=True)
    line.start([(lambda: output, lambda k: all_output.at[z])])

    both = Pairs(pairs, sems_pairs)
    reduces = [
        PlaneReduce(links, ("plane", k), blocks.at[k], first_in.at[k], second_in.at[k], k % 2 == 1)
        for k in range(4)
    ]
    line_reduce = LineReduce(links, "sum", lambda k: blocks.at[k, :, 0, 0], landing, g_ffn)
    sources = ((dgate, peer_dgate, "dgate", 0), (dup, peer_dup, "dup", 0), (hidden, peer_hidden, "hidden", 1))
    units = [(k, m) for k in (3, 2, 1, 0) for m in range(3)]

    def fetch(n):
        k, m = units[n]
        own, peer, name, _ = sources[m]
        links.arrived(peer.at[k], ("peer", (name, k)))
        both.start(n % 2, own.at[k], peer.at[k])

    links.arrived(peer_h_two, ("peer", "h_two"))
    load_turned(links, h_two, peer_h_two, staged, turned.at[0], sems_turned)
    fetch(0)
    for n, (k, m) in enumerate(units):
        if n == 1:
            links.arrived(peer_gffn, ("peer", "gffn"))
            load_turned(links, gffn, peer_gffn, staged, turned.at[1], sems_turned)
        if n + 1 < len(units):
            fetch(n + 1)
        own, peer, _, side = sources[m]
        both.wait(n % 2, own.at[k], peer.at[k])

        @pl.loop(0, 4)
        def _(i):
            rows = pl.ds(pl.multiple_of(i * 128, 128), 128)
            blocks[k, m, i // 2, i % 2] = dot(turned[side, rows], pairs[n % 2]).astype(BF)

        if m == 2:
            reduces[k].start()
            if k == 3:
                exchange.step()
            if k == 2:
                exchange.last()
    exchange.end()

    one = (query, keyed, valued, lse, datt, dread, prior, small, dqkv, small_grad)
    two = (pre, small, keyed, valued, dwrite, dqkv, dslot, small_grad, wide, dpre, part, halo)
    for k in range(4):
        for head in range(2):
            dwrite[k, head] = mixed_state(states, carry, k, head)

    def slots(first):
        @pl.loop(first, first + 2)
        def _(k):
            attention_back_slot(k, one, length, start)
            conv_back(k, two, length, start)

    slots(0)
    line.step(1)
    reduces[3].step()
    reduces[2].step()
    slots(2)

    @pl.when(p > 0)
    def _():
        links.copy(halo, halo_in, "halo", (p - 1, z)).start()

    halo_index = links.sent - 1

    def weight_copies(n):
        copies = [
            pltpu.make_async_copy(
                (q_own, k_own, v_own, g_own)[n] if n < 4 else weights.at[n // 4, n % 4],
                wbuf.at[n % 2], sems_weights.at[n % 2, 0],
            )
        ]
        if n % 4 == 3:
            copies.append(
                pltpu.make_async_copy(dzgate.at[n // 4], zbuf, sems_weights.at[n % 2, 1])
            )
        return copies

    for copy in weight_copies(0):
        copy.start()
    reduces[3].last()
    line_reduce.step(3)
    reduces[2].last()
    line_reduce.step(2)
    line.step(2)

    @pl.when(p == 7)
    def _():
        halo_in[...] = jnp.zeros_like(halo_in)

    @pl.when(p < 7)
    def _():
        links.arrived(halo_in, "halo")

    ext[pl.ds(0, 16)] = jnp.zeros((16, ext.shape[1]), F32)
    for k in range(4):
        for i in range(3):
            ext[pl.ds(16, 8)] = halo_in[i, k]
            dpre[i, k, pl.ds(seg - 16, 16)] = (
                part[i, k] + shift_sum(ext, taps_of(small, k, i), 0, 16, 1)
            ).astype(BF)
        for i in range(4):
            n = 4 * k + i
            if n < 15:
                for copy in weight_copies(n + 1):
                    copy.start()
            for copy in weight_copies(n):
                copy.wait()

            @pl.loop(0, seg // 256)
            def _(c):
                rows = pl.ds(pl.multiple_of(c * 256, 256), 256)
                total = dot_t(zbuf[rows] if i == 3 else dpre[i, k, rows], wbuf[n % 2])
                if n == 0:
                    acc[rows] = total
                else:
                    acc[rows] += total

        if k == 1:
            reduces[1].step()
            reduces[0].step()

    gain_sum = jnp.zeros((1, acc.shape[1]), F32)
    for first in range(0, seg, BLOCK):
        rows = pl.ds(first, BLOCK)
        normed, inverse = norm_keep(x_long[pl.ds(ROWS + first, BLOCK)].astype(F32))
        grad = acc[rows]
        gain_sum = gain_sum + jnp.sum(grad * normed, axis=0, keepdims=True)
        input_grad[rows] = (
            dmiddle[rows] + norm_back(grad * gain[...], normed, inverse)
        ).astype(BF)
    for row, value in enumerate((gain_sum, ffn_gain_grad[...])):
        for i in range(4):
            at = GAINS + 4 * row + i
            for k in range(4):
                small_grad[k, at : at + 1] = value[:, i * 256 : (i + 1) * 256]
    for k in range(4):
        small_grad[k, TAPS + 3 * KW : GAINS] = jnp.zeros((GAINS - TAPS - 3 * KW, 256), F32)
    line.step(3)
    reduces[1].last()
    line_reduce.step(1)
    reduces[0].last()
    line_reduce.step(0)
    own_output.wait()

    @pl.when(p > 0)
    def _():
        links.gone(lambda: halo, halo_index)

    line_reduce.finish()
    links.finish()


def gradient_kernel(
    h_long, gattn, dpre, dzgate, mixed, input_grad, small,
    all_input_grad, g_attn, small_sum,
    peer_h, peer_gattn, peer_dpre, peer_dzgate, peer_mixed,
    staged, turned, pairs, blocks, first_in, second_in, landing, small_in, small_part, small_all,
    send, recv, sems_turned, sems_pairs, sem_own,
):
    links = Links(send, recv)
    p, z = links.p, links.z
    seg = gattn.shape[0]
    own_rows = pltpu.make_async_copy(input_grad, all_input_grad.at[z], sem_own.at[0])
    own_rows.start()
    links.greet()
    h_one = h_long.at[pl.ds(ROWS, seg)]
    links.along_seq(h_one, peer_h, "h", 1)
    order = (3, 2, 1, 0)
    for k in order:
        for i in range(3):
            links.along_seq(dpre.at[i, k], peer_dpre.at[i, k], ("dpre", i, k), 1)
        links.along_seq(dzgate.at[k], peer_dzgate.at[k], ("dpre", 3, k), 1)
        if k == 3:
            links.along_seq(gattn, peer_gattn, "gattn", 1)
        links.along_seq(mixed.at[k], peer_mixed.at[k], ("dpre", 4, k), 1)
    line = LineGather(links, "input_grad", lambda k: all_input_grad.at[z ^ k], fixed=True)
    line.start([(lambda: input_grad, lambda k: all_input_grad.at[z])])
    small_in[0] = small[0]
    for k in (1, 2, 3):
        copy = links.copy(small.at[k], small_in.at[k], ("small", k), (p, z ^ k))
        copy.start()
        links.always.append((lambda k=k: small.at[k], links.sent - 1))

    both = Pairs(pairs, sems_pairs)
    reduces = [
        PlaneReduce(links, ("plane", k), blocks.at[k], first_in.at[k], second_in.at[k], k % 2 == 1)
        for k in range(4)
    ]
    line_reduce = LineReduce(links, "sum", lambda k: blocks.at[k, :, 0, 0], landing, g_attn)
    units = [(k, m) for k in order for m in range(5)]

    def refs(k, m):
        if m < 3:
            return dpre.at[m, k], peer_dpre.at[m, k]
        return ((dzgate.at[k], peer_dzgate.at[k]), (mixed.at[k], peer_mixed.at[k]))[m - 3]

    def fetch(n):
        k, m = units[n]
        own, peer = refs(k, m)
        links.arrived(peer, ("dpre", m, k))
        both.start(n % 2, own, peer)

    links.arrived(peer_h, "h")
    load_turned(links, h_one, peer_h, staged, turned.at[0], sems_turned)
    fetch(0)
    for n, (k, m) in enumerate(units):
        if n == 1:
            links.arrived(peer_gattn, "gattn")
            load_turned(links, gattn, peer_gattn, staged, turned.at[1], sems_turned)
        if n + 1 < len(units):
            fetch(n + 1)
        both.wait(n % 2, *refs(k, m))

        @pl.loop(0, 2)
        def _(i):
            rows = pl.ds(pl.multiple_of(i * 256, 256), 256)
            value = dot(turned[m // 4, rows], pairs[n % 2]).astype(BF)
            blocks[k, m, i, 0] = value[:128]
            blocks[k, m, i, 1] = value[128:]

        if m == 4:
            reduces[k].start()
    for k in (1, 2, 3):
        links.arrived(small_in.at[k], ("small", k))
    small_part[...] = (small_in[0] + small_in[1]) + (small_in[2] + small_in[3])
    small_all[0] = small_part[...]
    for j in range(1, 8):
        links.along_seq(small_part, small_all.at[j], ("all", j), j)
    line.step(1)
    reduces[3].step()
    reduces[2].step()
    reduces[1].step()
    reduces[3].last()
    line_reduce.step(3)
    reduces[2].last()
    line_reduce.step(2)
    reduces[0].step()
    reduces[1].last()
    line_reduce.step(1)
    reduces[0].last()
    line.step(2)
    line_reduce.step(0)
    for j in range(1, 8):
        links.arrived(small_all.at[j], ("all", j))
    pair = lambda j: small_all[j] + small_all[j + 1]
    small_sum[...] = (pair(0) + pair(2)) + (pair(4) + pair(6))
    line.step(3)
    own_rows.wait()
    line_reduce.finish()
    links.finish()


def local_fast(
    inputs, lengths, decays, norm_gain, query_proj, key_proj, value_proj, gate_proj, conv_taps,
    pers_keys, pers_values, out_proj, ffn_gain, ffn_gate, ffn_up, ffn_down, cotangent,
):
    seqs, seg, features = inputs.shape
    segments, shards = lax.axis_size("seq"), lax.axis_size("head")
    p, z = lax.axis_index("seq"), lax.axis_index("head")
    width, hidden_width = query_proj.shape[1], ffn_gate.shape[1]
    heads_here = width // DH
    heads = heads_here * shards
    persistent = pers_keys.shape[0]

    turn = (jnp.arange(shards)[:, None] == (z ^ jnp.arange(shards))[None, :]).astype(F32)
    mine = lax.dynamic_index_in_dim(decays, z, 1, False)[:, 0].reshape(2, shards, 1, heads_here)
    mine = jnp.sum(mine * turn[None, :, :, None], axis=1).reshape(2, heads)
    mine = jnp.pad(mine, ((0, 6), (0, 128 - heads)))
    own_small = jnp.concatenate(
        [pers_keys, pers_values, conv_taps.reshape(3 * KW, width), jnp.zeros((4, width), BF)]
    ).astype(F32)
    gain, ffn_gain = norm_gain[None], ffn_gain[None]
    low = lambda *shape: SHAPE(shape, BF)
    full = lambda *shape: SHAPE(shape, F32)
    rows_low = low(shards, seg, width)
    state = low(shards, heads_here, DH, DH)
    hid = low(shards, seg, hidden_width)
    flat = low(seg, features)
    anywhere = pl.BlockSpec(memory_space=pl.ANY)
    in_vmem = pl.BlockSpec(memory_space=pltpu.VMEM)
    in_smem = pl.BlockSpec(memory_space=pltpu.SMEM)
    vmem_low = lambda *shape: pltpu.VMEM(shape, BF)
    vmem_full = lambda *shape: pltpu.VMEM(shape, F32)
    dma = pltpu.SemaphoreType.DMA
    block = features // 8
    (
        x_long, h_long, pre, query, keyed, valued, lse, prior, small, carry_back, mixed, h_two, gffn,
        output, dmiddle, gattn, datt, dzgate, dread, dprior, g_ffn_gain,
        weights, hidden, dgate, dup, *_,
    ) = pl.pallas_call(
        front_kernel,
        out_shape=[
            low(seg + ROWS, features), low(seg + ROWS, features), low(3, shards, seg + ROWS, width),
            rows_low, rows_low, rows_low, full(shards, heads_here, seg, 1), state, full(shards, GAINS, width),
            full(segments, 128), rows_low, flat, flat,
            flat, full(seg, features), flat, rows_low, rows_low, rows_low, state, full(1, features),
            low(shards, 4, features, width), hid, hid, hid, low(shards, width, features),
            low(shards, 2, features, hidden_width), low(shards, hidden_width, features),
        ],
        in_specs=[in_smem] + [in_vmem] * 4 + [anywhere] * 10,
        out_specs=[in_vmem] * 21 + [anywhere] * 7,
        scratch_shapes=[
            vmem_low(seg, features), vmem_full(shards, seg, width), vmem_full(shards, seg, width),
            vmem_full(3, seg + ROWS, width), vmem_low(segments, shards, heads_here, DH, DH),
            vmem_full(segments, 8, 128), vmem_full(segments, 128), vmem_low(4, features, width),
            vmem_low(shards, width, features), vmem_low(2, 2, features, hidden_width),
            vmem_low(2, hidden_width, features), vmem_low(2, 3, seg, hidden_width),
            vmem_full(seg, features), vmem_full(seg, features),
            dma((192,)), dma((192,)), dma((2,)), dma((4,)), dma((4,)), dma((2, 3)), dma((2, 3)),
        ],
        compiler_params=pltpu.CompilerParams(
            collective_id=0, has_side_effects=True, vmem_limit_bytes=VMEM_LIMIT
        ),
    )(
        lengths, gain, ffn_gain, own_small, mine, inputs, cotangent,
        query_proj, key_proj, value_proj, gate_proj, out_proj, ffn_gate, ffn_up, ffn_down,
    )
    output, g_ffn, small_grad, dpre, input_grad, *_ = pl.pallas_call(
        back_all_kernel,
        out_shape=[
            low(shards, seg, features), full(3, block, hidden_width), full(shards, SMALL, width),
            low(3, shards, seg, width), flat, flat, flat, hid, hid, hid,
        ],
        in_specs=[in_smem] + [in_vmem] * 15 + [anywhere] * 12,
        out_specs=[anywhere] + [in_vmem] * 4 + [anywhere] * 5,
        scratch_shapes=[
            vmem_low(8, shards, heads_here, DH, DH), vmem_low(shards, heads_here, DH, DH),
            vmem_full(3, seg, width), vmem_full(3, seg + ROWS, width), vmem_full(3, 1, seg + 8, width),
            vmem_full(3, shards, 16, width), vmem_full(3, shards, 8, width), vmem_full(3, shards, 8, width),
            vmem_full(24, width), vmem_full(seg, features), vmem_low(2, features, width),
            vmem_low(seg, width),
            vmem_low(2 * seg, features // 2), vmem_low(2, features // 2, 2 * seg),
            vmem_low(2, 2 * seg, hidden_width), vmem_low(4, 3, 2, 2, block, hidden_width),
            vmem_low(4, 3, 2, block, hidden_width), vmem_low(4, 3, block, hidden_width),
            vmem_low(6, 3, block, hidden_width),
            dma((64,)), dma((64,)), dma((4, 2)), dma((2, 2)), dma((2, 2)), dma((1,)),
        ],
        compiler_params=pltpu.CompilerParams(
            collective_id=1, has_side_effects=True, vmem_limit_bytes=VMEM_LIMIT
        ),
    )(
        lengths, carry_back,
        query, keyed, valued, lse, datt, dread, prior, small, pre, dprior, x_long, gain, dmiddle, g_ffn_gain,
        output, h_two, gffn, hidden, dgate, dup, weights, dzgate, query_proj, key_proj, value_proj, gate_proj,
    )
    input_grad, g_attn, small, *_ = pl.pallas_call(
        gradient_kernel,
        out_shape=[
            low(shards, seg, features), full(5, block, width), full(SMALL, width),
            low(seg, features), low(seg, features), low(3, shards, seg, width), rows_low, rows_low,
        ],
        in_specs=[anywhere] * 6 + [in_vmem],
        out_specs=[anywhere] + [in_vmem] * 2 + [anywhere] * 5,
        scratch_shapes=[
            vmem_low(2 * seg, features // 2), vmem_low(2, features // 2, 2 * seg),
            vmem_low(2, 2 * seg, width), vmem_low(4, 5, 2, 2, block, width), vmem_low(4, 5, 2, block, width),
            vmem_low(4, 5, block, width), vmem_low(6, 5, block, width),
            vmem_full(shards, SMALL, width), vmem_full(SMALL, width), vmem_full(8, SMALL, width),
            dma((64,)), dma((64,)), dma((4, 2)), dma((2, 2)), dma((1,)),
        ],
        compiler_params=pltpu.CompilerParams(
            collective_id=2, has_side_effects=True, vmem_limit_bytes=VMEM_LIMIT
        ),
    )(h_long, gattn, dpre, dzgate, mixed, input_grad, small_grad)
    gains = small[GAINS:].reshape(2, features)
    g_query, g_key, g_value, g_zgate, g_out = (g_attn[i] for i in range(5))
    g_gate, g_up, g_down = (g_ffn[i] for i in range(3))
    return (
        output, input_grad, gains[0], g_query, g_key, g_value, g_zgate,
        small[TAPS : TAPS + 3 * KW].reshape(3, KW, width),
        small[PERS_K : PERS_K + persistent], small[PERS_V : PERS_V + persistent],
        g_out.T, gains[1], g_gate, g_up, g_down.T,
    )


def local(*args):
    return local_fast(*args) if custom_mesh() else local_plain(*args)


def solution(mesh):
    in_specs = (
        P(None, "seq", None),
        P(),
        P(None, None, "seq", None),
        P(),
        P(None, "head"),
        P(None, "head"),
        P(None, "head"),
        P(None, "head"),
        P(None, None, "head"),
        P(None, "head"),
        P(None, "head"),
        P("head", None),
        P(),
        P(None, "head"),
        P(None, "head"),
        P("head", None),
        P(None, "seq", None),
    )
    out_specs = (
        P(None, "seq", None),
        P(None, "seq", None),
        P(),
        P("seq", "head"),
        P("seq", "head"),
        P("seq", "head"),
        P("seq", "head"),
        P(None, None, "head"),
        P(None, "head"),
        P(None, "head"),
        P("head", "seq"),
        P(),
        P("seq", "head"),
        P("seq", "head"),
        P("head", "seq"),
    )
    return jax.shard_map(local, mesh=mesh, in_specs=in_specs, out_specs=out_specs, check_vma=False)
```

```python
import functools

import jax
import jax.numpy as jnp
from jax import lax
from jax.experimental import pallas as pl
from jax.experimental.pallas import tpu as pltpu
from jax.sharding import PartitionSpec as P

DH = 128
KW = 4
HALO = 8
EPSILON = 1e-06
BF = jnp.bfloat16
F32 = jnp.float32


def custom_mesh():
    return lax.axis_size("seq") == 8 and lax.axis_size("head") == 4


def along_seq(value, flip):
    return lax.ppermute(value, "seq", [(i, i ^ flip) for i in range(8)])


def along_head(value, pairs):
    return lax.ppermute(value, "head", pairs)


def slot_owner(k):
    return lax.axis_index("head") ^ k if custom_mesh() else k


def gather_head(value):
    z = lax.axis_index("head")
    middle = (z == 1) | (z == 2)
    one = along_head(value, [(0, 1), (1, 0), (2, 3), (3, 2)])
    inner = along_head(value, [(1, 2), (2, 1)])
    two_inner = along_head(one, [(1, 2), (2, 1)])
    two_outer = along_head(inner, [(2, 3), (1, 0)])
    three_outer = along_head(two_inner, [(2, 3), (1, 0)])
    two = jnp.where(middle, two_inner, two_outer)
    three = jnp.where(middle, inner, three_outer)
    return [value, one, two, three]


def gather_plane(value, x_first):
    near, far = (2, 4) if x_first else (4, 2)
    pieces = {0: value, near: along_seq(value, near), far: along_seq(value, far)}
    pieces[6] = along_seq(pieces[near], far)
    for j in (0, 2, 4, 6):
        pieces[j + 1] = along_seq(pieces[j], 1)
    return [pieces[j] for j in range(8)]


def gather_weights(own):
    if not custom_mesh():
        whole = lax.all_gather(own, "head")
        return [whole[k] for k in range(lax.axis_size("head"))]
    p = lax.axis_index("seq")
    matrices, depth, width = own.shape
    block = depth // 8
    mine = lax.dynamic_slice_in_dim(own, p * block, block, 1)
    slots = [own]
    for k, piece in enumerate(gather_head(mine)[1:]):
        if k < 2:
            parts = gather_plane(piece, k == 0)
        else:
            half = block // 2
            upper = gather_plane(piece[:, :half], True)
            lower = gather_plane(piece[:, half:], False)
            parts = [jnp.concatenate([u, v], axis=1) for u, v in zip(upper, lower)]
        full = jnp.zeros((matrices, depth, width), own.dtype)
        for j, part in enumerate(parts):
            full = lax.dynamic_update_slice_in_dim(full, part, (p ^ j) * block, 1)
        slots.append(full)
    return slots


def gather_small(own):
    if not custom_mesh():
        whole = lax.all_gather(own, "head")
        return [whole[k] for k in range(lax.axis_size("head"))]
    return [own] + [along_head(own, [(i, i ^ k) for i in range(4)]) for k in (1, 2, 3)]


def gather_states(value):
    p = lax.axis_index("seq")
    if not custom_mesh():
        whole = lax.all_gather(value, "seq")
        count = lax.axis_size("seq")
        return [whole[i] for i in range(count)], list(range(count))
    half = value.shape[0] // 2
    upper = gather_plane(value[:half], True)
    lower = gather_plane(value[half:], False)
    pieces = [jnp.concatenate([u, v]) for u, v in zip(upper, lower)]
    return pieces, [p ^ j for j in range(8)]


def gather_rows(own):
    if not custom_mesh():
        return lax.all_gather(own, "head")
    z = lax.axis_index("head")
    full = jnp.zeros((4,) + own.shape, own.dtype)
    for k, slot in enumerate(gather_head(own)):
        full = lax.dynamic_update_slice_in_dim(full, slot[None], z ^ k, 0)
    return full


def weight_grads(pairs, x_first):
    dot = lambda a, b: lax.dot_general(a, b, (((0,), (0,)), ((), ())), preferred_element_type=F32)
    if not custom_mesh():
        out = []
        for a, b in pairs:
            full = jnp.stack([dot(a, one) for one in b]).astype(BF)
            part = lax.psum_scatter(full, "head", scatter_dimension=0, tiled=True)[0]
            out.append(lax.psum_scatter(part, "seq", scatter_dimension=0, tiled=True).astype(F32))
        return out
    p, z = lax.axis_index("seq"), lax.axis_index("head")
    block = pairs[0][0].shape[1] // 8
    stacks = [[] for _ in range(4)]
    for a, b in pairs:
        cut = lambda j: lax.dynamic_slice_in_dim(a, (p ^ j) * block, block, 1)
        even = jnp.concatenate([cut(j) for j in (0, 2, 4, 6)], axis=1)
        odd = jnp.concatenate([cut(j) for j in (1, 3, 5, 7)], axis=1)
        peer_a = along_seq(odd, 1)
        for k in range(4):
            peer_b = along_seq(b[k], 1)
            stacks[k].append(
                (dot(even, b[k]) + dot(peer_a, peer_b)).astype(BF).reshape(4, block, -1)
            )
    near, far = (2, 4) if x_first else (4, 2)
    slots = []
    for k in range(4):
        g = jnp.stack(stacks[k])
        y_zero, y_one = g[:, :2], g[:, 2:]
        if x_first:
            keep = jnp.stack([g[:, 0], g[:, 2]], 1)
            away = jnp.stack([g[:, 1], g[:, 3]], 1)
        else:
            keep, away = y_zero, y_one
        summed = (keep.astype(F32) + along_seq(away, near).astype(F32)).astype(BF)
        slots.append(
            (summed[:, 0].astype(F32) + along_seq(summed[:, 1], far).astype(F32)).astype(BF)
        )
    return list(reduce_head(slots))


def add(a, b):
    return (a.astype(F32) + b.astype(F32)).astype(BF)


def reduce_head(slots):
    outer, inner, back = [(0, 1), (3, 2)], [(1, 2), (2, 1)], [(2, 3), (1, 0)]
    own, one, two, three = slots
    far = add(two, along_head(three, outer))
    far = add(one, along_head(far, inner))
    far = along_head(far, back)
    mid = add(three, along_head(two, outer))
    mid = along_head(mid, inner)
    near = along_head(one, outer)
    return own.astype(F32) + far.astype(F32) + mid.astype(F32) + near.astype(F32)


def sum_small(slots, gains):
    if not custom_mesh():
        part = lax.psum_scatter(jnp.stack(slots), "head", scatter_dimension=0, tiled=True)[0]
        return lax.psum(part, "seq"), lax.psum(gains, ("seq", "head"))
    part = slots[0]
    for k in (1, 2, 3):
        part = part + along_head(slots[k], [(i, i ^ k) for i in range(4)])
    for k in (1, 2):
        gains = gains + along_head(gains, [(i, i ^ k) for i in range(4)])
    count = part.shape[0]
    total = jnp.concatenate([part, gains])
    for flip in (1, 2, 4):
        total = total + along_seq(total, flip)
    return total[:count], total[count:]


def norm_keep(values):
    inverse = lax.rsqrt(jnp.mean(values * values, axis=-1, keepdims=True) + EPSILON)
    return (values * inverse, inverse)


def norm_back(grad, normed, inverse):
    return inverse * (grad - normed * jnp.mean(grad * normed, axis=-1, keepdims=True))


def silu_slope(values):
    sigma = jax.nn.sigmoid(values)
    return sigma * (1.0 + values * (1.0 - sigma))


def carry_coefficients(alpha, eta):
    count, heads = alpha.shape
    place = jnp.arange(count)[:, None]
    mem = jnp.zeros((count, heads), F32)
    mom = jnp.zeros((count, heads), F32)
    rows = []
    for c in range(count):
        rows.append(mem)
        mom = eta[c] * mom + (place == c).astype(F32)
        mem = alpha[c] * mem + mom
    return jnp.stack(rows)


def dot(a, b):
    return jnp.dot(a, b, preferred_element_type=F32)


def dot_t(a, b):
    return lax.dot_general(a, b, (((1,), (1,)), ((), ())), preferred_element_type=F32)


def local_plain(
    inputs,
    lengths,
    decays,
    norm_gain,
    query_proj,
    key_proj,
    value_proj,
    gate_proj,
    conv_taps,
    pers_keys,
    pers_values,
    out_proj,
    ffn_gain,
    ffn_gate,
    ffn_up,
    ffn_down,
    cotangent,
):
    seqs, seg, features = inputs.shape
    segments = lax.axis_size("seq")
    shards = lax.axis_size("head")
    p, z = lax.axis_index("seq"), lax.axis_index("head")
    width = query_proj.shape[1]
    heads_here = width // DH
    heads = heads_here * shards
    rim = KW - 1
    persistent = pers_keys.shape[0]

    attn_slots = gather_weights(jnp.stack([query_proj, key_proj, value_proj, gate_proj, out_proj.T]))
    ffn_slots = gather_weights(jnp.stack([ffn_gate, ffn_up, ffn_down.T]))
    small = gather_small(
        jnp.concatenate([conv_taps.reshape(3 * KW, width), pers_keys, pers_values])
    )
    small = jnp.concatenate(small, axis=1)
    taps = small[: 3 * KW].reshape(3, KW, heads * DH).astype(F32)
    pers_k = small[3 * KW : 3 * KW + persistent].reshape(persistent, heads, DH)
    pers_v = small[3 * KW + persistent :].reshape(persistent, heads, DH)
    q_mat, k_mat, v_mat, g_mat, o_mat = [
        jnp.concatenate([slot[i] for slot in attn_slots], axis=1) for i in range(5)
    ]

    mine = lax.dynamic_index_in_dim(decays, z, 1, False)[:, 0]
    mine = jnp.concatenate(
        [lax.dynamic_slice_in_dim(mine, slot_owner(k) * heads_here, heads_here, 1) for k in range(shards)],
        axis=1,
    )
    every = lax.all_gather(mine, "seq")
    carry = carry_coefficients(every[:, 0], every[:, 1])

    x = lax.dynamic_index_in_dim(inputs, z, 0, False).astype(F32)
    cot = lax.dynamic_index_in_dim(cotangent, z, 0, False).astype(F32)
    length = lax.dynamic_index_in_dim(lengths, z, 0, False)
    live = ((p * seg + jnp.arange(seg, dtype=jnp.int32)) < length).astype(F32)
    live_two = live[:, None]
    tail = lax.dynamic_index_in_dim(inputs, z, 0, False)[seg - HALO :]
    before = lax.ppermute(tail, "seq", [(i, i + 1) for i in range(segments - 1)]).astype(F32)
    x_long = jnp.concatenate([before, x])
    n_long, inv_long = norm_keep(x_long)
    h_long = (n_long * norm_gain).astype(BF)
    n_one, inv_one, h_one = n_long[HALO:], inv_long[HALO:], h_long[HALO:]

    pre = jnp.stack([dot(h_long, m) for m in (q_mat, k_mat, v_mat)]).astype(BF)
    zgate = dot(h_one, g_mat)
    wide_pre = pre.astype(F32)
    conv_sum = sum(
        taps[:, lag][:, None, :] * wide_pre[:, HALO - lag : HALO - lag + seg] for lag in range(KW)
    )
    acts = jax.nn.silu(conv_sum).reshape(3, seg, heads, DH)
    q_normed, q_inverse = norm_keep(acts[0])
    k_normed, k_inverse = norm_keep(acts[1])
    query, keyed, valued = q_normed.astype(BF), k_normed.astype(BF), acts[2].astype(BF)
    live_three = live[:, None, None]
    masked_value = valued * live_three.astype(BF)
    write = jnp.einsum("tha,thb->hab", masked_value, keyed, preferred_element_type=F32) / seg

    def mix_states(values, coefficients):
        pieces, places = gather_states(values.astype(BF))
        total = 0.0
        for piece, place in zip(pieces, places):
            coefficient = lax.dynamic_index_in_dim(coefficients, place, 0, False)
            total = total + coefficient[:, None, None] * piece.astype(F32)
        return total.astype(BF)

    prior = mix_states(write, lax.dynamic_index_in_dim(carry, p, 0, False))
    raw_read = jnp.einsum("hab,thb->tha", prior, query, preferred_element_type=F32)
    readout, read_inverse = norm_keep(raw_read)

    keys_all = jnp.concatenate([pers_k, keyed])
    values_all = jnp.concatenate([pers_v, valued])
    valid = jnp.concatenate([jnp.ones((persistent,), F32), live])
    rows_index = jnp.arange(seg)[:, None]
    column = jnp.arange(persistent + seg)[None, :] - persistent
    allowed = (column < 0) | (column <= rows_index) & (valid[None, :] > 0.5)
    scale = DH ** (-0.5)
    score = jnp.einsum("thd,uhd->htu", query, keys_all, preferred_element_type=F32) * scale
    score = jnp.where(allowed[None], score, -1e30)
    top = jnp.max(score, axis=-1, keepdims=True)
    log_total = top + jnp.log(jnp.sum(jnp.exp(score - top), axis=-1, keepdims=True))
    prob = jnp.exp(score - log_total)
    prob_low = prob.astype(BF)
    attended = jnp.einsum("htu,uhd->thd", prob_low, values_all, preferred_element_type=F32)

    sigma = jax.nn.sigmoid(zgate)
    read_flat = readout.reshape(seg, -1)
    mixed = (attended.reshape(seg, -1) + sigma * read_flat).astype(BF)
    middle = x + live_two * dot_t(mixed, o_mat)
    n_two, inv_two = norm_keep(middle)
    h_two = (n_two * ffn_gain).astype(BF)

    gffn = (live_two * cot).astype(BF)
    ffn_out = 0.0
    dh_two = 0.0
    hidden_slots, gate_slots, up_slots = [], [], []
    for slot in ffn_slots:
        gate_value = dot(h_two, slot[0])
        up_value = dot(h_two, slot[1])
        silu_gate = jax.nn.silu(gate_value)
        hidden = (silu_gate * up_value).astype(BF)
        ffn_out = ffn_out + dot_t(hidden, slot[2])
        dhidden = dot(gffn, slot[2])
        dgate = (dhidden * up_value * silu_slope(gate_value)).astype(BF)
        dup = (dhidden * silu_gate).astype(BF)
        dh_two = dh_two + dot_t(dgate, slot[0]) + dot_t(dup, slot[1])
        hidden_slots.append(hidden)
        gate_slots.append(dgate)
        up_slots.append(dup)
    output = gather_rows((middle + live_two * ffn_out).astype(BF))
    g_gate, g_up, g_down = weight_grads(
        [(h_two, gate_slots), (h_two, up_slots), (gffn, hidden_slots)], True
    )

    grad_ffn_gain = jnp.sum(dh_two * n_two, axis=0)
    dmiddle = cot + norm_back(dh_two * ffn_gain, n_two, inv_two)
    gattn = (live_two * dmiddle).astype(BF)
    dmixed = dot(gattn, o_mat)
    datt = dmixed.astype(BF).reshape(seg, heads, DH)
    dzgate = (dmixed * read_flat * sigma * (1.0 - sigma)).astype(BF)
    dread = norm_back((dmixed * sigma).reshape(seg, heads, DH), readout, read_inverse).astype(BF)
    dprior = jnp.einsum("tha,thb->hab", dread, query, preferred_element_type=F32)
    dwrite = mix_states(dprior, lax.dynamic_index_in_dim(carry, p, 1, False))
    dquery_mem = jnp.einsum("hab,tha->thb", prior, dread, preferred_element_type=F32)
    dprob = jnp.einsum("thd,uhd->htu", datt, values_all, preferred_element_type=F32)
    row_dot = jnp.sum(prob * dprob, axis=-1, keepdims=True)
    dscore = (prob * (dprob - row_dot)).astype(BF)
    dquery = (
        jnp.einsum("htu,uhd->thd", dscore, keys_all, preferred_element_type=F32) * scale
        + dquery_mem
    )
    dkeys = jnp.einsum("htu,thd->uhd", dscore, query, preferred_element_type=F32) * scale
    dvalues = jnp.einsum("htu,thd->uhd", prob_low, datt, preferred_element_type=F32)
    dvals = (
        dvalues[persistent:]
        + live_three * jnp.einsum("hab,thb->tha", dwrite, keyed, preferred_element_type=F32) / seg
    )
    dkey = (
        dkeys[persistent:]
        + jnp.einsum("hab,tha->thb", dwrite, masked_value, preferred_element_type=F32) / seg
    )
    dact = jnp.stack(
        [norm_back(dquery, q_normed, q_inverse), norm_back(dkey, k_normed, k_inverse), dvals]
    ).reshape(3, seg, -1)
    dconv = dact * silu_slope(conv_sum)
    longer = jnp.pad(dconv, ((0, 0), (rim, rim), (0, 0)))
    spread = sum(
        taps[:, lag][:, None, :] * longer[:, lag : lag + seg + rim] for lag in range(KW)
    )
    grad_conv = jnp.stack(
        [
            jnp.sum(dconv * wide_pre[:, HALO - lag : HALO - lag + seg], axis=1)
            for lag in range(KW)
        ],
        axis=1,
    )
    back = lax.ppermute(
        spread[:, :rim].astype(BF), "seq", [(i + 1, i) for i in range(segments - 1)]
    ).astype(F32)
    dpre = spread[:, rim:] + jnp.pad(back, ((0, 0), (seg - rim, 0), (0, 0)))
    dpre = dpre.astype(BF)

    dh_one = (
        dot_t(dpre[0], q_mat) + dot_t(dpre[1], k_mat) + dot_t(dpre[2], v_mat) + dot_t(dzgate, g_mat)
    )
    grad_norm_gain = jnp.sum(dh_one * n_one, axis=0)
    input_grad = gather_rows(
        (dmiddle + norm_back(dh_one * norm_gain, n_one, inv_one)).astype(BF)
    )

    def by_slot(value):
        return [value[..., k * width : (k + 1) * width] for k in range(shards)]

    g_query, g_key, g_value, g_zgate, g_out = weight_grads(
        [(h_one, by_slot(d)) for d in (dpre[0], dpre[1], dpre[2], dzgate)]
        + [(gattn, by_slot(mixed))],
        False,
    )
    rows = jnp.concatenate(
        [
            grad_conv.reshape(3 * KW, -1),
            dkeys[:persistent].reshape(persistent, -1),
            dvalues[:persistent].reshape(persistent, -1),
        ]
    )
    gains = jnp.concatenate([grad_norm_gain, grad_ffn_gain]).reshape(-1, width)
    rows, gains = sum_small(by_slot(rows), gains)
    gains = gains.reshape(2, features)
    return (
        output,
        input_grad,
        gains[0],
        g_query,
        g_key,
        g_value,
        g_zgate,
        rows[: 3 * KW].reshape(3, KW, width),
        rows[3 * KW : 3 * KW + persistent],
        rows[3 * KW + persistent :],
        g_out.T,
        gains[1],
        g_gate,
        g_up,
        g_down.T,
    )


ROWS = 16
BLOCK = 128
SCALE = DH ** (-0.5)


def shift_sum(source, taps, first, rows, step):
    total = taps[0:1] * source[pl.ds(first, rows)]
    for lag in range(1, KW):
        total = total + taps[lag : lag + 1] * source[pl.ds(first + step * lag, rows)]
    return total


def live_rows(first, rows, length, segment_start):
    place = segment_start + first + lax.broadcasted_iota(jnp.int32, (rows, 1), 0)
    return (place < length).astype(F32)


def live_columns(columns, length, segment_start):
    return segment_start + lax.broadcasted_iota(jnp.int32, (1, columns), 1) < length


def masked_scores(query, keys, pers_k, index, columns_live):
    width = keys.shape[0]
    raw = dot_t(query, keys) * SCALE
    row = index * BLOCK + lax.broadcasted_iota(jnp.int32, (BLOCK, width), 0)
    column = lax.broadcasted_iota(jnp.int32, (BLOCK, width), 1)
    keep = (column <= row) & columns_live[:, :width]
    return jnp.where(keep, raw, -1e30), dot_t(query, pers_k) * SCALE


def attention_back_slot(k, refs, length, segment_start):
    query, keyed, valued, lse, datt, dread, prior, small, dqkv, small_grad = refs
    seg = query.shape[1]
    columns_live = live_columns(seg, length, segment_start)
    turn = lambda a, b: lax.dot_general(a, b, (((0,), (0,)), ((), ())), preferred_element_type=F32)
    for head in range(query.shape[2] // DH):
        lanes = slice(head * DH, (head + 1) * DH)
        pers_keys_sum = jnp.zeros((16, DH), F32)
        pers_values_sum = jnp.zeros((16, DH), F32)
        pk = small[k, PERS_K : PERS_K + 16, lanes].astype(BF)
        pv = small[k, PERS_V : PERS_V + 16, lanes].astype(BF)
        dqkv[1, :, lanes] = jnp.zeros((seg, DH), F32)
        dqkv[2, :, lanes] = jnp.zeros((seg, DH), F32)
        dqkv[0, :, lanes] = dot(dread[k, :, lanes], prior[k, head])
        for index in range(seg // BLOCK):
            rows = pl.ds(index * BLOCK, BLOCK)
            upto = pl.ds(0, (index + 1) * BLOCK)
            q, d = query[k, rows, lanes], datt[k, rows, lanes]
            keys = keyed[k, upto, lanes]
            score, pers = masked_scores(q, keys, pk, index, columns_live)
            log_total = lse[k, head, rows]
            prob, prob_p = jnp.exp(score - log_total), jnp.exp(pers - log_total)
            grad = dot_t(d, valued[k, upto, lanes])
            grad_p = dot_t(d, pv)
            row_dot = jnp.sum(prob * grad, axis=-1, keepdims=True) + jnp.sum(
                prob_p * grad_p, axis=-1, keepdims=True
            )
            dscore = (prob * (grad - row_dot)).astype(BF)
            dscore_p = (prob_p * (grad_p - row_dot)).astype(BF)
            dqkv[0, rows, lanes] += (dot(dscore, keys) + dot(dscore_p, pk)) * SCALE
            dqkv[1, upto, lanes] += turn(dscore, q) * SCALE
            dqkv[2, upto, lanes] += turn(prob.astype(BF), d)
            pers_keys_sum = pers_keys_sum + turn(dscore_p, q)
            pers_values_sum = pers_values_sum + turn(prob_p.astype(BF), d)
        small_grad[k, PERS_K : PERS_K + 16, lanes] = pers_keys_sum * SCALE
        small_grad[k, PERS_V : PERS_V + 16, lanes] = pers_values_sum


def conv_back_slot(k, refs, length, segment_start):
    pre, small, keyed, valued, dwrite, dqkv, dconv, small_grad, wide = refs
    seg = keyed.shape[1]
    heads = keyed.shape[2] // DH
    for i in range(3):
        wide[i] = pre[i, k].astype(F32)
    sums = [[jnp.zeros((1, heads * DH), F32) for _ in range(KW)] for _ in range(3)]
    for first in range(0, seg, BLOCK):
        rows = pl.ds(first, BLOCK)
        live = live_rows(first, BLOCK, length, segment_start)
        for i in range(3):
            conv = shift_sum(wide.at[i], taps_of(small, k, i), ROWS + first, BLOCK, -1)
            sigma = jax.nn.sigmoid(conv)
            act = conv * sigma
            parts = []
            for head in range(heads):
                lanes = slice(head * DH, (head + 1) * DH)
                grad = dqkv[i, rows, lanes]
                if i == 1:
                    masked = valued[k, rows, lanes] * live.astype(BF)
                    grad = grad + dot(masked, dwrite[k, head]) / seg
                if i == 2:
                    grad = grad + live * dot_t(keyed[k, rows, lanes], dwrite[k, head]) / seg
                else:
                    grad = norm_back(grad, *norm_keep(act[:, lanes]))
                parts.append(grad)
            result = jnp.concatenate(parts, axis=1) * (sigma * (1.0 + conv * (1.0 - sigma)))
            dconv[i, 0, rows] = result
            for lag in range(KW):
                sums[i][lag] = sums[i][lag] + jnp.sum(
                    result * wide[i, pl.ds(ROWS + first - lag, BLOCK)], axis=0, keepdims=True
                )
    for i in range(3):
        for lag in range(KW):
            row = TAPS + KW * i + lag
            small_grad[k, row : row + 1] = sums[i][lag]


SHAPE = jax.ShapeDtypeStruct
VMEM_LIMIT = 127 * 512 * 1024


MESH = pl.DeviceIdType.MESH
SKEW_ONE, SKEW_TWO = 2, 4
WINDOW = 4
UNITS = (
    ("proj", 1), ("proj", 2), ("proj", 3), ("ffn", 1), ("out", 1), ("out", 2), ("out", 3), ("down", 1),
    ("ffn", 2), ("down", 2), ("ffn", 3), ("down", 3),
)


class Links:
    def __init__(self, send, recv):
        self.send, self.recv = send, recv
        self.sent = 0
        self.names = {}
        self.always, self.middles = [], []
        self.p, self.z = lax.axis_index("seq"), lax.axis_index("head")
        self.middle = (self.z == 1) | (self.z == 2)

    def greet(self):
        barrier = pltpu.get_barrier_semaphore()
        for flip in range(1, 8):
            pl.semaphore_signal(barrier, device_id=(self.p ^ flip, self.z), device_id_type=MESH)
        for flip in (1, 2, 3):
            pl.semaphore_signal(barrier, device_id=(self.p, self.z ^ flip), device_id_type=MESH)
        pl.semaphore_wait(barrier, 10)

    def place(self, name):
        return self.recv.at[self.names.setdefault(name, len(self.names))]

    def copy(self, source, target, name, device):
        index = self.sent
        self.sent += 1
        return pltpu.make_async_remote_copy(
            src_ref=source, dst_ref=target, send_sem=self.send.at[index], recv_sem=self.place(name),
            device_id=device, device_id_type=MESH,
        )

    def along_seq(self, source, target, name, flip):
        copy = self.copy(source, target, name, (self.p ^ flip, self.z))
        copy.start()
        self.always.append((lambda: source, self.sent - 1))

    def along_head(self, source, target, name, flip, waits):
        index = self.sent
        copy = self.copy(source(), target(), name, (self.p, self.z ^ flip))
        copy.start()
        waits.append((source, index))

    def arrived(self, target, name):
        pltpu.make_async_remote_copy(
            src_ref=target, dst_ref=target, send_sem=self.send.at[0], recv_sem=self.place(name),
            device_id=(self.p, self.z ^ 1), device_id_type=MESH,
        ).wait_recv()

    def gone(self, source, index):
        pltpu.make_async_remote_copy(
            src_ref=source(), dst_ref=source(), send_sem=self.send.at[index], recv_sem=self.recv.at[0],
            device_id=(self.p, self.z ^ 1), device_id_type=MESH,
        ).wait_send()

    def finish(self):
        for source, index in self.always:
            self.gone(source, index)

        @pl.when(self.middle)
        def _():
            for source, index in self.middles:
                self.gone(source, index)


class LineGather:
    def __init__(self, links, name, view, fixed=False):
        self.links, self.name, self.view, self.fixed = links, name, view, fixed

    def start(self, sources):
        links = self.links
        for source, view in sources:
            links.along_head(source, lambda: view(1), (self.name, 1), 1, links.always)

        @pl.when(links.middle)
        def _():
            for source, view in sources:
                links.along_head(source, lambda: view(3), (self.name, 3), 3, links.middles)

    def forward(self, k, flip):
        view, there = self.view, k ^ flip
        self.links.along_head(
            lambda: view(k), lambda: view(k if self.fixed else there), (self.name, there), flip,
            self.links.middles,
        )

    def outward(self):
        @pl.when(self.links.middle)
        def _():
            self.links.arrived(self.view(3), (self.name, 3))
            self.forward(3, 1)

    def step(self, k):
        links, name, view = self.links, self.name, self.view
        if k == 1:
            links.arrived(view(1), (name, 1))

            @pl.when(links.middle)
            def _():
                self.forward(1, 3)

        if k == 2:
            links.arrived(view(2), (name, 2))

            @pl.when(links.middle)
            def _():
                self.forward(2, 1)

        if k == 3:

            @pl.when(~links.middle)
            def _():
                links.arrived(view(3), (name, 3))


class PlaneGather:
    def __init__(self, links, name, view, x_first):
        self.links, self.name, self.view = links, name, view
        self.near, self.far = (2, 4) if x_first else (4, 2)

    def send(self, j, flip):
        links = self.links
        block = self.view(links.p ^ j)
        links.along_seq(block, block, (self.name, j ^ flip), flip)

    def wait(self, j):
        self.links.arrived(self.view(self.links.p ^ j), (self.name, j))

    def start(self):
        self.send(0, self.near)
        self.send(0, self.far)
        self.send(0, 1)

    def step(self):
        self.wait(self.near)
        self.send(self.near, self.far)
        self.send(self.near, 1)
        self.wait(self.far)
        self.send(self.far, 1)

    def last(self):
        self.wait(6)
        self.send(6, 1)

    def end(self):
        for j in (1, 3, 5, 7):
            self.wait(j)


class StateExchange:
    def __init__(self, links, name, view):
        self.links, self.name, self.view = links, name, view

    def send(self, j, flip):
        block = self.view(self.links.p ^ j)
        self.links.along_seq(block, block, (self.name, j ^ flip), flip)

    def wait(self, j):
        self.links.arrived(self.view(self.links.p ^ j), (self.name, j))

    def start(self):
        for flip in (6, 2, 4, 1):
            self.send(0, flip)

    def step(self):
        for j in (2, 4, 6):
            self.wait(j)
            self.send(j, 1)

    def end(self):
        for j in (1, 3, 5, 7):
            self.wait(j)


def weight_events(links, own, weights, out_w, gate_up, down):
    q_own, k_own, v_own, g_own, o_own, gate_own, up_own, down_own = own
    block = lambda q: pl.ds(pl.multiple_of(q * 128, 128), 128)
    mine = block(links.p)
    views = {
        "proj": (lambda k, q: weights.at[k, :, block(q), :], True),
        "out": (lambda k, q: out_w.at[k, :, block(q)], False),
        "ffn": (lambda k, q: gate_up.at[k, :, block(q), :], False),
        "down": (lambda k, q: down.at[k, :, block(q)], True),
    }
    sources = {
        "proj": [
            (lambda ref=ref: ref.at[mine, :], lambda k, i=i: weights.at[k, i, mine, :])
            for i, ref in enumerate((q_own, k_own, v_own, g_own))
        ],
        "out": [(lambda: o_own.at[:, mine], lambda k: out_w.at[k, :, mine])],
        "ffn": [
            (lambda ref=ref: ref.at[mine, :], lambda k, i=i: gate_up.at[k, i, mine, :])
            for i, ref in enumerate((gate_own, up_own))
        ],
        "down": [(lambda: down_own.at[:, mine], lambda k: down.at[k, :, mine])],
    }
    planes = {
        (name, k): PlaneGather(links, (name, k), lambda q, view=view, k=k: view(k, q), x_first)
        for name, (view, x_first) in views.items()
        for k in (1, 2, 3)
    }
    units = UNITS
    count = len(units)

    def post(i):
        if i < count:
            name, k = units[i]
            for source, target in sources[name]:
                links.along_head(source, lambda: target(k), ("line", name, k), k, links.always)

    def begin():
        for i in range(WINDOW):
            post(i)

    events = [(None, begin)]
    for i in range(count + SKEW_TWO):
        if i < count:
            name, k = units[i]

            def first(name=name, k=k, i=i):
                links.arrived(views[name][0](k, links.p), ("line", name, k))
                post(i + WINDOW)
                planes[name, k].start()

            events.append((None, first))
        if 0 <= i - SKEW_ONE < count:
            events.append((None, planes[units[i - SKEW_ONE]].step))
        if 0 <= i - SKEW_TWO < count:
            events.append((units[i - SKEW_TWO], planes[units[i - SKEW_TWO]].last))
    return events, planes


PERS_K, PERS_V, TAPS, GAINS, SMALL = 0, 16, 32, 48, 56


def taps_of(small, k, i):
    return small[k, TAPS + KW * i : TAPS + KW * (i + 1)]


def carry_in_kernel(every, place, forward, backward):
    count, lanes = every.shape[0], every.shape[2]
    row = lax.broadcasted_iota(jnp.int32, (count, lanes), 0)
    mem = jnp.zeros((count, lanes), F32)
    mom = jnp.zeros((count, lanes), F32)
    ahead = jnp.zeros((count, lanes), F32)
    behind = jnp.zeros((count, lanes), F32)
    for c in range(count):
        ahead = jnp.where(place == c, mem, ahead)
        mine = jnp.sum(jnp.where(row == place, mem, 0.0), axis=0, keepdims=True)
        behind = jnp.where(row == c, mine, behind)
        mom = every[c, 1:2] * mom + (row == c).astype(F32)
        mem = every[c, 0:1] * mem + mom
    forward[...] = ahead
    backward[...] = behind


def mixed_state(states, coefficients, k, head):
    lane = 2 * k + head
    total = coefficients[0:1, lane : lane + 1] * states[0, k, head].astype(F32)
    for q in range(1, states.shape[0]):
        total = total + coefficients[q : q + 1, lane : lane + 1] * states[q, k, head].astype(F32)
    return total.astype(BF)


def project_slot(k, h_long, weights, pre, zgate, wide):
    seg = zgate.shape[1]
    for i in range(3):
        rounded = dot(h_long[...], weights[i]).astype(BF)
        pre[i, k] = rounded
        wide[i] = rounded.astype(F32)
    zgate[k] = dot(h_long[pl.ds(ROWS, seg)], weights[3])


def convolve_slot(k, small, query, keyed, valued, wide):
    seg = query.shape[1]
    heads = query.shape[2] // DH

    for first in range(0, seg, BLOCK):
        rows = pl.ds(first, BLOCK)
        for i in range(3):
            conv = shift_sum(wide.at[i], taps_of(small, k, i), ROWS + first, BLOCK, -1)
            act = conv * jax.nn.sigmoid(conv)
            if i == 2:
                valued[k, rows] = act.astype(BF)
                continue
            target = (query, keyed)[i]
            for head in range(heads):
                lanes = slice(head * DH, (head + 1) * DH)
                target[k, rows, lanes] = norm_keep(act[:, lanes])[0].astype(BF)


def write_slot(k, p, keyed, valued, states, length, segment_start):
    seg = keyed.shape[1]
    seg_live = live_rows(0, seg, length, segment_start).astype(BF)
    for head in range(keyed.shape[2] // DH):
        lanes = slice(head * DH, (head + 1) * DH)
        masked = valued[k, :, lanes] * seg_live
        states[p, k, head] = (
            lax.dot_general(
                masked, keyed[k, :, lanes], (((0,), (0,)), ((), ())), preferred_element_type=F32
            )
            / seg
        ).astype(BF)


def attend_head(k, head, small, query, keyed, valued, att, lse, length, segment_start):
    seg = query.shape[1]
    columns_live = live_columns(seg, length, segment_start)
    lanes = slice(head * DH, (head + 1) * DH)
    pers_k = small[k, PERS_K : PERS_K + 16, lanes].astype(BF)
    pers_v = small[k, PERS_V : PERS_V + 16, lanes].astype(BF)
    for index in range(seg // BLOCK):
        rows = pl.ds(index * BLOCK, BLOCK)
        upto = pl.ds(0, (index + 1) * BLOCK)
        score, pers = masked_scores(
            query[k, rows, lanes], keyed[k, upto, lanes], pers_k, index, columns_live
        )
        top = jnp.maximum(
            jnp.max(score, axis=-1, keepdims=True), jnp.max(pers, axis=-1, keepdims=True)
        )
        score, pers = jnp.exp(score - top), jnp.exp(pers - top)
        total = jnp.sum(score, axis=-1, keepdims=True) + jnp.sum(pers, axis=-1, keepdims=True)
        inverse = 1.0 / total
        lse[k, head, rows] = top + jnp.log(total)
        att[k, rows, lanes] = dot((score * inverse).astype(BF), valued[k, upto, lanes]) + dot(
            (pers * inverse).astype(BF), pers_v
        )


def read_slot(k, prior, query, zgate, att, mixed):
    for head in range(query.shape[2] // DH):
        lanes = slice(head * DH, (head + 1) * DH)
        normed, _ = norm_keep(dot_t(query[k, :, lanes], prior[k, head]))
        mixed[k, :, lanes] = (
            att[k, :, lanes] + jax.nn.sigmoid(zgate[k, :, lanes]) * normed
        ).astype(BF)


def ffn_rows(rows, h_two, gffn, weights_gu, weights_d, stage, out_acc, grad_acc):
    gate = dot(h_two[rows], weights_gu[0])
    up = dot(h_two[rows], weights_gu[1])
    sigma = jax.nn.sigmoid(gate)
    silu = gate * sigma
    low = (silu * up).astype(BF)
    stage[0, rows] = low
    out_acc[rows] += dot(low, weights_d[...])
    back = dot_t(gffn[rows], weights_d[...])
    low_gate = (back * up * (sigma * (1.0 + gate * (1.0 - sigma)))).astype(BF)
    low_up = (back * silu).astype(BF)
    stage[1, rows] = low_gate
    stage[2, rows] = low_up
    grad_acc[rows] += dot_t(low_gate, weights_gu[0]) + dot_t(low_up, weights_gu[1])


def tail_slot(k, out_w, gattn, query, prior, zgate, datt, dzgate, dread, dprior):
    dmixed = dot_t(gattn[...], out_w[k])
    datt[k] = dmixed.astype(BF)
    for head in range(dmixed.shape[1] // DH):
        lanes = slice(head * DH, (head + 1) * DH)
        sigma = jax.nn.sigmoid(zgate[k, :, lanes])
        readout, rinv = norm_keep(dot_t(query[k, :, lanes], prior[k, head]))
        grad = dmixed[:, lanes] * sigma
        dzgate[k, :, lanes] = (grad * readout * (1.0 - sigma)).astype(BF)
        low = norm_back(grad, readout, rinv).astype(BF)
        dread[k, :, lanes] = low
        dprior[k, head] = lax.dot_general(
            low, query[k, :, lanes], (((0,), (0,)), ((), ())), preferred_element_type=F32
        ).astype(BF)


class Steps:
    def __init__(self, events):
        self.events, self.at, self.done = events, 0, set()

    def run(self, count=1):
        for _ in range(count):
            if self.at < len(self.events):
                label, function = self.events[self.at]
                function()
                self.at += 1
                self.done.add(label)

    def until(self, *labels):
        while not all(label in self.done for label in labels):
            self.run()


def front_kernel(
    lengths, gain, ffn_gain, own_small, own_decays,
    inputs, cotangent, q_own, k_own, v_own, g_own, o_own, gate_own, up_own, down_own,
    x_long, h_long, pre, query, keyed, valued, lse, prior, small, backward, mixed, h_two, gffn,
    output, dmiddle, gattn, datt, dzgate, dread, dprior, gain_grad,
    weights, hidden, dgate, dup, out_w, gate_up, down,
    cot, zgate, att, wide, states, every, forward, wproj, wout, wgu, wdown, stage, out_acc, grad_acc,
    send, recv, sem_x, sem_proj, sem_out, sem_ffn, sem_stage,
):
    links = Links(send, recv)
    p, z = links.p, links.z
    seg = h_two.shape[0]
    length, start = lengths[z], p * seg
    own = (q_own, k_own, v_own, g_own, o_own, gate_own, up_own, down_own)
    load_x = pltpu.make_async_copy(inputs.at[z], x_long.at[pl.ds(ROWS, seg)], sem_x.at[0])
    load_cot = pltpu.make_async_copy(cotangent.at[z], cot, sem_x.at[1])
    load_x.start()

    def proj_loads(k):
        if k == 0:
            return [
                pltpu.make_async_copy(ref, wproj.at[i], sem_proj.at[i]) for i, ref in enumerate(own[:4])
            ]
        return [pltpu.make_async_copy(weights.at[k], wproj, sem_proj.at[0])]

    def out_load(k):
        return pltpu.make_async_copy(o_own if k == 0 else out_w.at[k], wout.at[k], sem_out.at[k])

    def ffn_loads(k):
        side = k % 2
        if k == 0:
            gu = [
                pltpu.make_async_copy(gate_own, wgu.at[0, 0], sem_ffn.at[0, 0]),
                pltpu.make_async_copy(up_own, wgu.at[0, 1], sem_ffn.at[0, 2]),
            ]
        else:
            gu = [pltpu.make_async_copy(gate_up.at[k], wgu.at[side], sem_ffn.at[side, 0])]
        return gu + [
            pltpu.make_async_copy(down_own if k == 0 else down.at[k], wdown.at[side], sem_ffn.at[side, 1])
        ]

    def go(copies):
        for copy in copies:
            copy.start()

    def come(copies):
        for copy in copies:
            copy.wait()

    go(proj_loads(0))
    go([load_cot, out_load(0)])
    go(ffn_loads(0))
    every[p] = own_decays[...]
    small[0] = own_small[...]
    links.greet()
    events, planes = weight_events(links, own, weights, out_w, gate_up, down)
    steps = Steps(events)

    @pl.when(p < 7)
    def _():
        links.copy(
            inputs.at[z, pl.ds(seg - ROWS, ROWS)], x_long.at[pl.ds(0, ROWS)], "rows", (p + 1, z)
        ).start()

    rows_index = links.sent - 1
    for j in range(1, 8):
        links.along_seq(own_decays, every.at[p], ("decays", j), j)
    for k in (1, 2, 3):
        links.copy(own_small, small.at[k], ("small", k), (p, z ^ k)).start()
        links.always.append((lambda: own_small, links.sent - 1))
    steps.run()

    load_x.wait()

    @pl.when(p == 0)
    def _():
        x_long[pl.ds(0, ROWS)] = jnp.zeros((ROWS, x_long.shape[1]), BF)

    @pl.when(p > 0)
    def _():
        links.arrived(x_long.at[pl.ds(0, ROWS)], "rows")

    @pl.loop(0, 3)
    def _(c):
        rows = pl.ds(pl.multiple_of(c * 176, 16), 176)
        normed, _ = norm_keep(x_long[rows].astype(F32))
        h_long[rows] = (normed * gain[...]).astype(BF)

    exchanges = [StateExchange(links, ("states", k), lambda q, k=k: states.at[q, k]) for k in range(4)]
    complete = lambda name, k: planes[name, k].end()
    come(proj_loads(0))
    attend = lambda k, head: attend_head(k, head, small, query, keyed, valued, att, lse, length, start)

    def load_next(k):
        steps.until(("proj", k))
        complete("proj", k)
        go(proj_loads(k))

    def open_slot(k):
        project_slot(k, h_long, wproj, pre, zgate, wide)
        steps.run()
        convolve_slot(k, small, query, keyed, valued, wide)
        write_slot(k, p, keyed, valued, states, length, start)
        exchanges[k].start()

    steps.run()
    project_slot(0, h_long, wproj, pre, zgate, wide)
    steps.run()
    for other in (1, 2, 3):
        links.arrived(small.at[other], ("small", other))
    convolve_slot(0, small, query, keyed, valued, wide)
    steps.run()
    write_slot(0, p, keyed, valued, states, length, start)
    exchanges[0].start()
    attend(0, 0)
    steps.run()
    attend(0, 1)
    exchanges[0].step()
    for k in (1, 2, 3):
        load_next(k)
        come(proj_loads(k))
        open_slot(k)
        steps.run()
        if k == 1:
            attend(1, 0)
            steps.run()
            exchanges[1].step()
    attend(1, 1)
    exchanges[2].step()
    steps.run()
    attend(2, 0)
    exchanges[3].step()
    steps.run()
    attend(2, 1)
    steps.run()
    attend(3, 0)
    steps.run()
    attend(3, 1)
    for j in range(1, 8):
        links.arrived(every.at[p ^ j], ("decays", j))
    carry_in_kernel(every, p, forward, backward)
    for k in (1, 2, 3):
        steps.until(("out", k))
        complete("out", k)
        go([out_load(k)])
    for k in range(4):
        exchanges[k].end()
        for head in range(2):
            prior[k, head] = mixed_state(states, forward, k, head)
        read_slot(k, prior, query, zgate, att, mixed)
        come([out_load(k)])

        @pl.loop(0, 2)
        def _(c):
            rows = pl.ds(pl.multiple_of(c * 256, 256), 256)
            part = dot(mixed[k, rows], wout[k])
            if k == 0:
                grad_acc[rows] = part
            else:
                grad_acc[rows] += part

        steps.run()
    load_cot.wait()

    @pl.loop(0, seg // BLOCK)
    def _(c):
        first = pl.multiple_of(c * BLOCK, BLOCK)
        rows = pl.ds(first, BLOCK)
        live = live_rows(first, BLOCK, length, start)
        value = x_long[pl.ds(pl.multiple_of(ROWS + first, 16), BLOCK)].astype(F32) + live * grad_acc[rows]
        dmiddle[rows] = value
        normed, _ = norm_keep(value)
        h_two[rows] = (normed * ffn_gain[...]).astype(BF)
        gffn[rows] = (live * cot[rows].astype(F32)).astype(BF)
        out_acc[rows] = jnp.zeros((BLOCK, out_acc.shape[1]), F32)
        grad_acc[rows] = jnp.zeros((BLOCK, out_acc.shape[1]), F32)

    def stores(k):
        return [
            pltpu.make_async_copy(stage.at[k % 2, i], ref.at[k], sem_stage.at[k % 2, i])
            for i, ref in enumerate((hidden, dgate, dup))
        ]

    for k in range(4):
        if k == 3:
            steps.until(("ffn", 3), ("down", 3))
            complete("ffn", 3)
            complete("down", 3)
            go(ffn_loads(3))
        come(ffn_loads(k))
        if k < 2:
            steps.until(("ffn", k + 1), ("down", k + 1))
            complete("ffn", k + 1)
            complete("down", k + 1)
            go(ffn_loads(k + 1))
        if k >= 2:
            come(stores(k - 2))

        @pl.loop(0, 2)
        def _(c):
            rows = pl.ds(pl.multiple_of(c * 256, 256), 256)
            ffn_rows(rows, h_two, gffn, wgu.at[k % 2], wdown.at[k % 2], stage.at[k % 2], out_acc, grad_acc)

        go(stores(k))
        steps.run(3)
    gain_grad[...] = jnp.zeros_like(gain_grad)

    @pl.loop(0, seg // BLOCK)
    def _(c):
        first = pl.multiple_of(c * BLOCK, BLOCK)
        rows = pl.ds(first, BLOCK)
        live = live_rows(first, BLOCK, length, start)
        value = dmiddle[rows]
        output[rows] = (value + live * out_acc[rows]).astype(BF)
        normed, inverse = norm_keep(value)
        grad = grad_acc[rows]
        gain_grad[...] += jnp.sum(grad * normed, axis=0, keepdims=True)
        result = cot[rows].astype(F32) + norm_back(grad * ffn_gain[...], normed, inverse)
        dmiddle[rows] = result
        gattn[rows] = (live * result).astype(BF)

    for k in range(4):
        tail_slot(k, wout, gattn, query, prior, zgate, datt, dzgate, dread, dprior)
    come(stores(2))
    come(stores(3))

    @pl.when(p < 7)
    def _():
        links.gone(lambda: x_long.at[pl.ds(0, ROWS)], rows_index)

    links.finish()


class PlaneReduce:
    def __init__(self, links, name, blocks, first, second, x_first):
        self.links, self.name, self.x_first = links, name, x_first
        self.blocks, self.first, self.second = blocks, first, second

    def start(self):
        away = self.blocks.at[:, :, 1] if self.x_first else self.blocks.at[:, 1]
        self.links.along_seq(away, self.first, (self.name, 1), 2 if self.x_first else 4)

    def step(self):
        self.links.arrived(self.first, (self.name, 1))
        for i in range(2):
            y, x = (i, 0) if self.x_first else (0, i)

            @pl.loop(0, self.blocks.shape[0])
            def _(m):
                self.blocks[m, y, x] = add(self.blocks[m, y, x], self.first[m, i])

        y, x = (1, 0) if self.x_first else (0, 1)
        self.links.along_seq(
            self.blocks.at[:, y, x], self.second, (self.name, 2), 4 if self.x_first else 2
        )

    def last(self):
        self.links.arrived(self.second, (self.name, 2))

        @pl.loop(0, self.blocks.shape[0])
        def _(m):
            self.blocks[m, 0, 0] = add(self.blocks[m, 0, 0], self.second[m])


class LineReduce:
    def __init__(self, links, name, blocks, landing, result):
        self.links, self.name, self.blocks = links, name, blocks
        self.landing, self.result = landing, result
        self.ends = []

    def send(self, k, slot, flip, waits):
        self.links.along_head(
            lambda: self.blocks(k), lambda: self.landing.at[slot], (self.name, slot), flip, waits
        )

    def merge(self, k, slot):
        self.links.arrived(self.landing.at[slot], (self.name, slot))
        block = self.blocks(k)

        @pl.loop(0, self.landing.shape[1])
        def _(m):
            block[m] = add(block[m], self.landing[slot, m])

    def from_ends(self, k):
        @pl.when(~self.links.middle)
        def _():
            self.send(k, 3 - k, 1, self.ends)

    def across(self, k):
        @pl.when(self.links.middle)
        def _():
            self.merge(5 - k, 3 - k)
            self.send(5 - k, 7 - k, 3, self.links.middles)

    def to_ends(self):
        @pl.when(self.links.middle)
        def _():
            self.merge(1, 4)
            self.send(1, 3, 1, self.links.middles)

    def last(self):
        @pl.when(~self.links.middle)
        def _():
            self.total([3])

        @pl.when(self.links.middle)
        def _():
            self.total([2, 5])

    def total(self, slots):
        block = self.blocks(0)
        for slot in slots:
            self.links.arrived(self.landing.at[slot], (self.name, slot))

        @pl.loop(0, self.landing.shape[1])
        def _(m):
            value = block[m].astype(F32)
            for slot in slots:
                value = value + self.landing[slot, m].astype(F32)
            self.result[m] = value

    def finish(self):
        @pl.when(~self.links.middle)
        def _():
            for source, index in self.ends:
                self.links.gone(source, index)


class Pairs:
    def __init__(self, buffers, sems):
        self.buffers, self.sems = buffers, sems

    def copies(self, slot, own, peer):
        rows = own.shape[0]
        return [
            pltpu.make_async_copy(own, self.buffers.at[slot, pl.ds(0, rows)], self.sems.at[slot, 0]),
            pltpu.make_async_copy(peer, self.buffers.at[slot, pl.ds(rows, rows)], self.sems.at[slot, 1]),
        ]

    def start(self, slot, own, peer):
        for copy in self.copies(slot, own, peer):
            copy.start()

    def wait(self, slot, own, peer):
        for copy in self.copies(slot, own, peer):
            copy.wait()


def load_turned(links, own, peer, staged, turned, sems):
    rows = own.shape[0]
    copies = []
    for i, j in enumerate((0, 2, 4, 6)):
        block = pl.ds(pl.multiple_of((links.p ^ j) * 128, 128), 128)
        for side, ref in enumerate((own, peer)):
            copy = pltpu.make_async_copy(
                ref.at[:, block], staged.at[pl.ds(side * rows, rows), pl.ds(i * 128, 128)], sems.at[i, side]
            )
            copy.start()
            copies.append(copy)
    for copy in copies:
        copy.wait()
    for i in range(4):
        turned[pl.ds(i * 128, 128)] = staged[:, pl.ds(i * 128, 128)].T


def conv_back(k, refs, length, segment_start):
    pre, small, keyed, valued, dwrite, dqkv, dslot, small_grad, wide, dpre, part, halo = refs
    conv_back_slot(
        k, (pre, small, keyed, valued, dwrite, dqkv, dslot, small_grad, wide), length, segment_start
    )
    seg = keyed.shape[1]
    for i in range(3):
        dslot[i, 0, pl.ds(seg, 8)] = jnp.zeros((8, dslot.shape[3]), F32)
        halo[i, k] = dslot[i, 0, pl.ds(0, 8)]
        weights = taps_of(small, k, i)
        for first in range(0, seg, BLOCK):
            value = shift_sum(dslot.at[i, 0], weights, first, BLOCK, 1)
            dpre[i, k, pl.ds(first, BLOCK)] = value.astype(BF)
            if first + BLOCK == seg:
                part[i, k] = value[BLOCK - 16 :]


def product(turned, pair, target):
    @pl.loop(0, 2)
    def _(y):
        for x in range(2):
            rows = pl.ds(pl.multiple_of(y * 256, 256) + x * 128, 128)
            target[y, x] = dot(turned[rows], pair[...]).astype(BF)


def back_all_kernel(
    lengths, carry,
    query, keyed, valued, lse, datt, dread, prior, small, pre, dprior, x_long, gain, dmiddle, ffn_gain_grad,
    output, h_two, gffn, hidden, dgate, dup, h_long, gattn, mixed, weights, dzgate, q_own, k_own, v_own, g_own,
    all_output, part_ffn, small_grad, dpre, input_grad,
    peer_h_two, peer_gffn, peer_hidden, peer_dgate, peer_dup, peer_h, peer_gattn, peer_mixed, peer_dzgate,
    states, dwrite, dqkv, wide, dslot, part, halo, halo_in, ext, acc, wbuf, zbuf,
    staged, turned, pairs, blocks, first_in, second_in, landing,
    send, recv, sems_turned, sems_pairs, sems_weights, sem_own,
):
    links = Links(send, recv)
    p, z = links.p, links.z
    seg = dmiddle.shape[0]
    length, start = lengths[z], p * seg
    states[p] = dprior[...]
    own_output = pltpu.make_async_copy(output, all_output.at[z], sem_own.at[0])
    own_output.start()
    links.greet()
    exchange = StateExchange(links, "states", lambda q: states.at[q])
    exchange.start()
    line = LineGather(links, "output", lambda k: all_output.at[z ^ k], fixed=True)
    line.start([(lambda: output, lambda k: all_output.at[z])])
    to_peer = [("h_two", h_two, peer_h_two)]
    for k in (3, 2, 1, 0):
        to_peer.append((("dgate", k), dgate.at[k], peer_dgate.at[k]))
        to_peer.append((("dup", k), dup.at[k], peer_dup.at[k]))
        if k == 3:
            to_peer.append(("gffn", gffn, peer_gffn))
        to_peer.append((("hidden", k), hidden.at[k], peer_hidden.at[k]))
    h_one = h_long.at[pl.ds(ROWS, seg)]
    later = [("h", h_one, peer_h), ("gattn", gattn, peer_gattn), ("mixed", mixed, peer_mixed), ("dzgate", dzgate, peer_dzgate)]
    for name, source, target in to_peer + later:
        links.along_seq(source, target, ("peer", name), 1)

    both = Pairs(pairs, sems_pairs)
    reduces = {
        k: PlaneReduce(links, ("plane", k), blocks.at[k - 1], first_in.at[k - 1], second_in.at[k - 1], k != 2)
        for k in (3, 2, 1)
    }
    line_reduce = LineReduce(links, "sum", lambda k: blocks.at[k - 1, :, 0, 0], landing, None)
    sources = ((dgate, peer_dgate, "dgate", 0), (dup, peer_dup, "dup", 0), (hidden, peer_hidden, "hidden", 1))
    units = [(k, m) for k in (3, 2, 1) for m in range(3)]

    def fetch(n):
        k, m = units[n]
        own, peer, name, _ = sources[m]
        links.arrived(peer.at[k], ("peer", (name, k)))
        both.start(n % 2, own.at[k], peer.at[k])

    links.arrived(peer_h_two, ("peer", "h_two"))
    load_turned(links, h_two, peer_h_two, staged, turned.at[0], sems_turned)
    fetch(0)
    for n, (k, m) in enumerate(units):
        if n == 1:
            links.arrived(peer_gffn, ("peer", "gffn"))
            load_turned(links, gffn, peer_gffn, staged, turned.at[1], sems_turned)
        if n + 1 < len(units):
            fetch(n + 1)
        own, peer, _, side = sources[m]
        both.wait(n % 2, own.at[k], peer.at[k])
        product(turned.at[side], pairs.at[n % 2], blocks.at[k - 1, m])
        if m == 2:
            reduces[k].start()
            if k == 3:
                exchange.step()
    exchange.end()

    one = (query, keyed, valued, lse, datt, dread, prior, small, dqkv, small_grad)
    two = (pre, small, keyed, valued, dwrite, dqkv, dslot, small_grad, wide, dpre, part, halo)
    for k in range(4):
        for head in range(2):
            dwrite[k, head] = mixed_state(states, carry, k, head)

    def slots(first, count):
        @pl.loop(first, first + count)
        def _(k):
            attention_back_slot(k, one, length, start)
            conv_back(k, two, length, start)

    slots(0, 2)
    line.outward()
    line.step(1)
    slots(2, 1)
    reduces[3].step()
    reduces[2].step()
    slots(3, 1)

    @pl.when(p > 0)
    def _():
        links.copy(halo, halo_in, "halo", (p - 1, z)).start()

    halo_index = links.sent - 1

    def weight_copies(n):
        copies = [
            pltpu.make_async_copy(
                (q_own, k_own, v_own, g_own)[n] if n < 4 else weights.at[n // 4, n % 4],
                wbuf.at[n % 2], sems_weights.at[n % 2, 0],
            )
        ]
        if n % 4 == 3:
            copies.append(
                pltpu.make_async_copy(dzgate.at[n // 4], zbuf, sems_weights.at[n % 2, 1])
            )
        return copies

    for copy in weight_copies(0):
        copy.start()
    reduces[3].last()
    line_reduce.from_ends(3)
    reduces[2].last()
    line_reduce.from_ends(2)
    line.step(2)

    @pl.when(p == 7)
    def _():
        halo_in[...] = jnp.zeros_like(halo_in)

    @pl.when(p < 7)
    def _():
        links.arrived(halo_in, "halo")

    ext[pl.ds(0, 16)] = jnp.zeros((16, ext.shape[1]), F32)
    for k in range(4):
        for i in range(3):
            ext[pl.ds(16, 8)] = halo_in[i, k]
            dpre[i, k, pl.ds(seg - 16, 16)] = (
                part[i, k] + shift_sum(ext, taps_of(small, k, i), 0, 16, 1)
            ).astype(BF)
        for i in range(4):
            n = 4 * k + i
            if n < 15:
                for copy in weight_copies(n + 1):
                    copy.start()
            for copy in weight_copies(n):
                copy.wait()

            @pl.loop(0, seg // 256)
            def _(c):
                rows = pl.ds(pl.multiple_of(c * 256, 256), 256)
                total = dot_t(zbuf[rows] if i == 3 else dpre[i, k, rows], wbuf[n % 2])
                if n == 0:
                    acc[rows] = total
                else:
                    acc[rows] += total

        if k == 1:
            reduces[1].step()
            line_reduce.across(3)

    line_reduce.across(2)
    gain_sum = jnp.zeros((1, acc.shape[1]), F32)
    for first in range(0, seg, BLOCK):
        rows = pl.ds(first, BLOCK)
        normed, inverse = norm_keep(x_long[pl.ds(ROWS + first, BLOCK)].astype(F32))
        grad = acc[rows]
        gain_sum = gain_sum + jnp.sum(grad * normed, axis=0, keepdims=True)
        input_grad[rows] = (
            dmiddle[rows] + norm_back(grad * gain[...], normed, inverse)
        ).astype(BF)
    for row, value in enumerate((gain_sum, ffn_gain_grad[...])):
        for i in range(4):
            at = GAINS + 4 * row + i
            for k in range(4):
                small_grad[k, at : at + 1] = value[:, i * 256 : (i + 1) * 256]
    for k in range(4):
        small_grad[k, TAPS + 3 * KW : GAINS] = jnp.zeros((GAINS - TAPS - 3 * KW, 256), F32)
    reduces[1].last()
    part_ffn[1] = jnp.zeros_like(part_ffn[1])

    @pl.when(links.middle)
    def _():
        line_reduce.merge(1, 4)
        links.arrived(landing.at[5], ("sum", 5))
        part_ffn[1] = landing[5]

    part_ffn[0] = blocks[0, :, 0, 0]
    line.step(3)
    for own, peer, name, _ in sources:
        links.arrived(peer.at[0], ("peer", (name, 0)))
    for name, _, target in later:
        links.arrived(target, ("peer", name))
    own_output.wait()

    @pl.when(p > 0)
    def _():
        links.gone(lambda: halo, halo_index)

    line_reduce.finish()
    links.finish()


def gradient_kernel(
    small, part_ffn,
    h_long, gattn, dpre, dzgate, mixed, input_grad, h_two, gffn, hidden, dgate, dup,
    peer_h_two, peer_gffn, peer_hidden, peer_dgate, peer_dup, peer_h, peer_gattn, peer_mixed, peer_dzgate,
    all_input_grad, g_attn, g_ffn, small_sum, peer_dpre,
    staged, turned, pairs, blocks, first_in, second_in, landing,
    pairs_ffn, blocks_ffn, first_ffn, second_ffn, landing_ffn, small_in, small_part, small_all,
    send, recv, sems_turned, sems_pairs, sems_ffn, sem_own,
):
    links = Links(send, recv)
    p, z = links.p, links.z
    seg = gattn.shape[0]
    own_rows = pltpu.make_async_copy(input_grad, all_input_grad.at[z], sem_own.at[0])
    own_rows.start()
    links.greet()
    line = LineGather(links, "input_grad", lambda k: all_input_grad.at[z ^ k], fixed=True)
    line.start([(lambda: input_grad, lambda k: all_input_grad.at[z])])
    order = (3, 2, 1, 0)
    for k in order:
        for i in range(3):
            links.along_seq(dpre.at[i, k], peer_dpre.at[i, k], ("dpre", i, k), 1)

    line_attn = LineReduce(links, "attn", lambda k: blocks.at[k, :, 0, 0], landing, g_attn)
    small_in[0] = small[0]
    for k in (1, 2, 3):
        links.copy(small.at[k], small_in.at[k], ("small", k), (p, z ^ k)).start()
        links.always.append((lambda k=k: small.at[k], links.sent - 1))

    ffn = PlaneReduce(links, "ffn0", blocks_ffn, first_ffn, second_ffn, False)
    attn = {
        k: PlaneReduce(links, ("attn", k), blocks.at[k], first_in.at[k], second_in.at[k], k != 2)
        for k in order
    }
    sources = ((dgate, peer_dgate, 0), (dup, peer_dup, 0), (hidden, peer_hidden, 1))
    both = Pairs(pairs_ffn, sems_ffn)
    refs_ffn = lambda m: tuple(ref.at[0] for ref in sources[m][:2])
    both.start(0, *refs_ffn(0))
    load_turned(links, h_two, peer_h_two, staged, turned.at[0], sems_turned)
    load_turned(links, gffn, peer_gffn, staged, turned.at[1], sems_turned)
    for m in range(3):
        if m < 2:
            both.start((m + 1) % 2, *refs_ffn(m + 1))
        both.wait(m % 2, *refs_ffn(m))
        product(turned.at[sources[m][2]], pairs_ffn.at[m % 2], blocks_ffn.at[m])
    ffn.start()

    sides = lambda k: [(dpre.at[m, k], peer_dpre.at[m, k]) for m in range(3)] + [
        (dzgate.at[k], peer_dzgate.at[k]), (mixed.at[k], peer_mixed.at[k])
    ]

    def attn_loads(k):
        return [
            pltpu.make_async_copy(ref, pairs.at[k % 2, m, pl.ds(side * seg, seg)], sems_pairs.at[k % 2, m, side])
            for m, both_sides in enumerate(sides(k))
            for side, ref in enumerate(both_sides)
        ]

    def fetch(k):
        for m in range(3):
            links.arrived(peer_dpre.at[m, k], ("dpre", m, k))
        for copy in attn_loads(k):
            copy.start()

    fetch(3)
    load_turned(links, h_long.at[pl.ds(ROWS, seg)], peer_h, staged, turned.at[0], sems_turned)
    load_turned(links, gattn, peer_gattn, staged, turned.at[1], sems_turned)
    for k in order:
        if k > 0:
            fetch(k - 1)
        for copy in attn_loads(k):
            copy.wait()
        for m in range(5):
            product(turned.at[m // 4], pairs.at[k % 2, m], blocks.at[k, m])
        attn[k].start()
    for k in (1, 2, 3):
        links.arrived(small_in.at[k], ("small", k))
    small_part[...] = (small_in[0] + small_in[1]) + (small_in[2] + small_in[3])
    small_all[0] = small_part[...]
    for j in range(1, 8):
        links.along_seq(small_part, small_all.at[j], ("all", j), j)
    line.outward()
    line.step(1)
    links.along_head(lambda: part_ffn.at[0], lambda: landing_ffn, "ffn line", 1, links.always)
    attn[3].step()
    attn[2].step()
    attn[3].last()
    line_attn.from_ends(3)
    attn[2].last()
    line_attn.from_ends(2)
    line.step(2)
    attn[1].step()
    ffn.step()
    attn[0].step()
    line_attn.across(3)
    line_attn.across(2)
    attn[1].last()
    line_attn.from_ends(1)
    line_attn.to_ends()
    ffn.last()
    attn[0].last()
    links.arrived(landing_ffn, "ffn line")
    for m in range(3):
        g_ffn[m] = (
            blocks_ffn[m, 0, 0].astype(F32) + landing_ffn[m].astype(F32) + part_ffn[1, m].astype(F32)
        )
    line.step(3)
    line_attn.last()
    for j in range(1, 8):
        links.arrived(small_all.at[j], ("all", j))
    pair = lambda j: small_all[j] + small_all[j + 1]
    small_sum[...] = (pair(0) + pair(2)) + (pair(4) + pair(6))
    own_rows.wait()
    line_attn.finish()
    links.finish()


def local_fast(
    inputs, lengths, decays, norm_gain, query_proj, key_proj, value_proj, gate_proj, conv_taps,
    pers_keys, pers_values, out_proj, ffn_gain, ffn_gate, ffn_up, ffn_down, cotangent,
):
    seqs, seg, features = inputs.shape
    segments, shards = lax.axis_size("seq"), lax.axis_size("head")
    p, z = lax.axis_index("seq"), lax.axis_index("head")
    width, hidden_width = query_proj.shape[1], ffn_gate.shape[1]
    heads_here = width // DH
    heads = heads_here * shards
    persistent = pers_keys.shape[0]

    turn = (jnp.arange(shards)[:, None] == (z ^ jnp.arange(shards))[None, :]).astype(F32)
    mine = lax.dynamic_index_in_dim(decays, z, 1, False)[:, 0].reshape(2, shards, 1, heads_here)
    mine = jnp.sum(mine * turn[None, :, :, None], axis=1).reshape(2, heads)
    mine = jnp.pad(mine, ((0, 6), (0, 128 - heads)))
    own_small = jnp.concatenate(
        [pers_keys, pers_values, conv_taps.reshape(3 * KW, width), jnp.zeros((4, width), BF)]
    ).astype(F32)
    gain, ffn_gain = norm_gain[None], ffn_gain[None]
    low = lambda *shape: SHAPE(shape, BF)
    full = lambda *shape: SHAPE(shape, F32)
    rows_low = low(shards, seg, width)
    state = low(shards, heads_here, DH, DH)
    hid = low(shards, seg, hidden_width)
    flat = low(seg, features)
    anywhere = pl.BlockSpec(memory_space=pl.ANY)
    in_vmem = pl.BlockSpec(memory_space=pltpu.VMEM)
    in_smem = pl.BlockSpec(memory_space=pltpu.SMEM)
    vmem_low = lambda *shape: pltpu.VMEM(shape, BF)
    vmem_full = lambda *shape: pltpu.VMEM(shape, F32)
    dma = pltpu.SemaphoreType.DMA
    block = features // 8
    (
        x_long, h_long, pre, query, keyed, valued, lse, prior, small, carry_back, mixed, h_two, gffn,
        output, dmiddle, gattn, datt, dzgate, dread, dprior, g_ffn_gain,
        weights, hidden, dgate, dup, *_,
    ) = pl.pallas_call(
        front_kernel,
        out_shape=[
            low(seg + ROWS, features), low(seg + ROWS, features), low(3, shards, seg + ROWS, width),
            rows_low, rows_low, rows_low, full(shards, heads_here, seg, 1), state, full(shards, GAINS, width),
            full(segments, 128), rows_low, flat, flat,
            flat, full(seg, features), flat, rows_low, rows_low, rows_low, state, full(1, features),
            low(shards, 4, features, width), hid, hid, hid, low(shards, width, features),
            low(shards, 2, features, hidden_width), low(shards, hidden_width, features),
        ],
        in_specs=[in_smem] + [in_vmem] * 4 + [anywhere] * 10,
        out_specs=[in_vmem] * 21 + [anywhere] * 7,
        scratch_shapes=[
            vmem_low(seg, features), vmem_full(shards, seg, width), vmem_full(shards, seg, width),
            vmem_full(3, seg + ROWS, width), vmem_low(segments, shards, heads_here, DH, DH),
            vmem_full(segments, 8, 128), vmem_full(segments, 128), vmem_low(4, features, width),
            vmem_low(shards, width, features), vmem_low(2, 2, features, hidden_width),
            vmem_low(2, hidden_width, features), vmem_low(2, 3, seg, hidden_width),
            vmem_full(seg, features), vmem_full(seg, features),
            dma((192,)), dma((192,)), dma((2,)), dma((4,)), dma((4,)), dma((2, 3)), dma((2, 3)),
        ],
        compiler_params=pltpu.CompilerParams(
            collective_id=0, has_side_effects=True, vmem_limit_bytes=VMEM_LIMIT
        ),
    )(
        lengths, gain, ffn_gain, own_small, mine, inputs, cotangent,
        query_proj, key_proj, value_proj, gate_proj, out_proj, ffn_gate, ffn_up, ffn_down,
    )
    output, part_ffn, small_grad, dpre, input_grad, *peers = pl.pallas_call(
        back_all_kernel,
        out_shape=[
            low(shards, seg, features), low(2, 3, block, hidden_width), full(shards, SMALL, width),
            low(3, shards, seg, width), flat, flat, flat, hid, hid, hid, flat, flat, rows_low, rows_low,
        ],
        in_specs=[in_smem] + [in_vmem] * 15 + [anywhere] * 15,
        out_specs=[anywhere] + [in_vmem] * 4 + [anywhere] * 9,
        scratch_shapes=[
            vmem_low(8, shards, heads_here, DH, DH), vmem_low(shards, heads_here, DH, DH),
            vmem_full(3, seg, width), vmem_full(3, seg + ROWS, width), vmem_full(3, 1, seg + 8, width),
            vmem_full(3, shards, 16, width), vmem_full(3, shards, 8, width), vmem_full(3, shards, 8, width),
            vmem_full(24, width), vmem_full(seg, features), vmem_low(2, features, width),
            vmem_low(seg, width),
            vmem_low(2 * seg, features // 2), vmem_low(2, features // 2, 2 * seg),
            vmem_low(2, 2 * seg, hidden_width), vmem_low(3, 3, 2, 2, block, hidden_width),
            vmem_low(3, 3, 2, block, hidden_width), vmem_low(3, 3, block, hidden_width),
            vmem_low(6, 3, block, hidden_width),
            dma((64,)), dma((64,)), dma((4, 2)), dma((2, 2)), dma((2, 2)), dma((1,)),
        ],
        compiler_params=pltpu.CompilerParams(
            collective_id=1, has_side_effects=True, vmem_limit_bytes=VMEM_LIMIT
        ),
    )(
        lengths, carry_back,
        query, keyed, valued, lse, datt, dread, prior, small, pre, dprior, x_long, gain, dmiddle, g_ffn_gain,
        output, h_two, gffn, hidden, dgate, dup, h_long, gattn, mixed, weights, dzgate,
        query_proj, key_proj, value_proj, gate_proj,
    )
    input_grad, g_attn, g_ffn, small, *_ = pl.pallas_call(
        gradient_kernel,
        out_shape=[
            low(shards, seg, features), full(5, block, width), full(3, block, hidden_width), full(SMALL, width),
            low(3, shards, seg, width),
        ],
        in_specs=[in_vmem] * 2 + [anywhere] * 20,
        out_specs=[anywhere] + [in_vmem] * 3 + [anywhere],
        scratch_shapes=[
            vmem_low(2 * seg, features // 2), vmem_low(2, features // 2, 2 * seg),
            vmem_low(2, 5, 2 * seg, width), vmem_low(4, 5, 2, 2, block, width), vmem_low(4, 5, 2, block, width),
            vmem_low(4, 5, block, width), vmem_low(6, 5, block, width),
            vmem_low(2, 2 * seg, hidden_width), vmem_low(3, 2, 2, block, hidden_width),
            vmem_low(3, 2, block, hidden_width), vmem_low(3, block, hidden_width),
            vmem_low(3, block, hidden_width),
            vmem_full(shards, SMALL, width), vmem_full(SMALL, width), vmem_full(8, SMALL, width),
            dma((96,)), dma((96,)), dma((4, 2)), dma((2, 5, 2)), dma((2, 2)), dma((1,)),
        ],
        compiler_params=pltpu.CompilerParams(
            collective_id=2, has_side_effects=True, vmem_limit_bytes=VMEM_LIMIT
        ),
    )(
        small_grad, part_ffn, h_long, gattn, dpre, dzgate, mixed, input_grad, h_two, gffn, hidden, dgate, dup, *peers,
    )
    gains = small[GAINS:].reshape(2, features)
    g_query, g_key, g_value, g_zgate, g_out = (g_attn[i] for i in range(5))
    g_gate, g_up, g_down = (g_ffn[i] for i in range(3))
    return (
        output, input_grad, gains[0], g_query, g_key, g_value, g_zgate,
        small[TAPS : TAPS + 3 * KW].reshape(3, KW, width),
        small[PERS_K : PERS_K + persistent], small[PERS_V : PERS_V + persistent],
        g_out.T, gains[1], g_gate, g_up, g_down.T,
    )


def local(*args):
    return local_fast(*args) if custom_mesh() else local_plain(*args)


def solution(mesh):
    in_specs = (
        P(None, "seq", None),
        P(),
        P(None, None, "seq", None),
        P(),
        P(None, "head"),
        P(None, "head"),
        P(None, "head"),
        P(None, "head"),
        P(None, None, "head"),
        P(None, "head"),
        P(None, "head"),
        P("head", None),
        P(),
        P(None, "head"),
        P(None, "head"),
        P("head", None),
        P(None, "seq", None),
    )
    out_specs = (
        P(None, "seq", None),
        P(None, "seq", None),
        P(),
        P("seq", "head"),
        P("seq", "head"),
        P("seq", "head"),
        P("seq", "head"),
        P(None, None, "head"),
        P(None, "head"),
        P(None, "head"),
        P("head", "seq"),
        P(),
        P("seq", "head"),
        P("seq", "head"),
        P("head", "seq"),
    )
    return jax.shard_map(local, mesh=mesh, in_specs=in_specs, out_specs=out_specs, check_vma=False)
```

```python
import functools

import jax
import jax.numpy as jnp
from jax import lax
from jax.experimental import pallas as pl
from jax.experimental.pallas import tpu as pltpu
from jax.sharding import PartitionSpec as P

DH = 128
KW = 4
HALO = 8
EPSILON = 1e-06
BF = jnp.bfloat16
F32 = jnp.float32


def custom_mesh():
    return lax.axis_size("seq") == 8 and lax.axis_size("head") == 4


def along_seq(value, flip):
    return lax.ppermute(value, "seq", [(i, i ^ flip) for i in range(8)])


def along_head(value, pairs):
    return lax.ppermute(value, "head", pairs)


def slot_owner(k):
    return lax.axis_index("head") ^ k if custom_mesh() else k


def gather_head(value):
    z = lax.axis_index("head")
    middle = (z == 1) | (z == 2)
    one = along_head(value, [(0, 1), (1, 0), (2, 3), (3, 2)])
    inner = along_head(value, [(1, 2), (2, 1)])
    two_inner = along_head(one, [(1, 2), (2, 1)])
    two_outer = along_head(inner, [(2, 3), (1, 0)])
    three_outer = along_head(two_inner, [(2, 3), (1, 0)])
    two = jnp.where(middle, two_inner, two_outer)
    three = jnp.where(middle, inner, three_outer)
    return [value, one, two, three]


def gather_plane(value, x_first):
    near, far = (2, 4) if x_first else (4, 2)
    pieces = {0: value, near: along_seq(value, near), far: along_seq(value, far)}
    pieces[6] = along_seq(pieces[near], far)
    for j in (0, 2, 4, 6):
        pieces[j + 1] = along_seq(pieces[j], 1)
    return [pieces[j] for j in range(8)]


def gather_weights(own):
    if not custom_mesh():
        whole = lax.all_gather(own, "head")
        return [whole[k] for k in range(lax.axis_size("head"))]
    p = lax.axis_index("seq")
    matrices, depth, width = own.shape
    block = depth // 8
    mine = lax.dynamic_slice_in_dim(own, p * block, block, 1)
    slots = [own]
    for k, piece in enumerate(gather_head(mine)[1:]):
        if k < 2:
            parts = gather_plane(piece, k == 0)
        else:
            half = block // 2
            upper = gather_plane(piece[:, :half], True)
            lower = gather_plane(piece[:, half:], False)
            parts = [jnp.concatenate([u, v], axis=1) for u, v in zip(upper, lower)]
        full = jnp.zeros((matrices, depth, width), own.dtype)
        for j, part in enumerate(parts):
            full = lax.dynamic_update_slice_in_dim(full, part, (p ^ j) * block, 1)
        slots.append(full)
    return slots


def gather_small(own):
    if not custom_mesh():
        whole = lax.all_gather(own, "head")
        return [whole[k] for k in range(lax.axis_size("head"))]
    return [own] + [along_head(own, [(i, i ^ k) for i in range(4)]) for k in (1, 2, 3)]


def gather_states(value):
    p = lax.axis_index("seq")
    if not custom_mesh():
        whole = lax.all_gather(value, "seq")
        count = lax.axis_size("seq")
        return [whole[i] for i in range(count)], list(range(count))
    half = value.shape[0] // 2
    upper = gather_plane(value[:half], True)
    lower = gather_plane(value[half:], False)
    pieces = [jnp.concatenate([u, v]) for u, v in zip(upper, lower)]
    return pieces, [p ^ j for j in range(8)]


def gather_rows(own):
    if not custom_mesh():
        return lax.all_gather(own, "head")
    z = lax.axis_index("head")
    full = jnp.zeros((4,) + own.shape, own.dtype)
    for k, slot in enumerate(gather_head(own)):
        full = lax.dynamic_update_slice_in_dim(full, slot[None], z ^ k, 0)
    return full


def weight_grads(pairs, x_first):
    dot = lambda a, b: lax.dot_general(a, b, (((0,), (0,)), ((), ())), preferred_element_type=F32)
    if not custom_mesh():
        out = []
        for a, b in pairs:
            full = jnp.stack([dot(a, one) for one in b]).astype(BF)
            part = lax.psum_scatter(full, "head", scatter_dimension=0, tiled=True)[0]
            out.append(lax.psum_scatter(part, "seq", scatter_dimension=0, tiled=True).astype(F32))
        return out
    p, z = lax.axis_index("seq"), lax.axis_index("head")
    block = pairs[0][0].shape[1] // 8
    stacks = [[] for _ in range(4)]
    for a, b in pairs:
        cut = lambda j: lax.dynamic_slice_in_dim(a, (p ^ j) * block, block, 1)
        even = jnp.concatenate([cut(j) for j in (0, 2, 4, 6)], axis=1)
        odd = jnp.concatenate([cut(j) for j in (1, 3, 5, 7)], axis=1)
        peer_a = along_seq(odd, 1)
        for k in range(4):
            peer_b = along_seq(b[k], 1)
            stacks[k].append(
                (dot(even, b[k]) + dot(peer_a, peer_b)).astype(BF).reshape(4, block, -1)
            )
    near, far = (2, 4) if x_first else (4, 2)
    slots = []
    for k in range(4):
        g = jnp.stack(stacks[k])
        y_zero, y_one = g[:, :2], g[:, 2:]
        if x_first:
            keep = jnp.stack([g[:, 0], g[:, 2]], 1)
            away = jnp.stack([g[:, 1], g[:, 3]], 1)
        else:
            keep, away = y_zero, y_one
        summed = (keep.astype(F32) + along_seq(away, near).astype(F32)).astype(BF)
        slots.append(
            (summed[:, 0].astype(F32) + along_seq(summed[:, 1], far).astype(F32)).astype(BF)
        )
    return list(reduce_head(slots))


def add(a, b):
    return (a.astype(F32) + b.astype(F32)).astype(BF)


def reduce_head(slots):
    outer, inner, back = [(0, 1), (3, 2)], [(1, 2), (2, 1)], [(2, 3), (1, 0)]
    own, one, two, three = slots
    far = add(two, along_head(three, outer))
    far = add(one, along_head(far, inner))
    far = along_head(far, back)
    mid = add(three, along_head(two, outer))
    mid = along_head(mid, inner)
    near = along_head(one, outer)
    return own.astype(F32) + far.astype(F32) + mid.astype(F32) + near.astype(F32)


def sum_small(slots, gains):
    if not custom_mesh():
        part = lax.psum_scatter(jnp.stack(slots), "head", scatter_dimension=0, tiled=True)[0]
        return lax.psum(part, "seq"), lax.psum(gains, ("seq", "head"))
    part = slots[0]
    for k in (1, 2, 3):
        part = part + along_head(slots[k], [(i, i ^ k) for i in range(4)])
    for k in (1, 2):
        gains = gains + along_head(gains, [(i, i ^ k) for i in range(4)])
    count = part.shape[0]
    total = jnp.concatenate([part, gains])
    for flip in (1, 2, 4):
        total = total + along_seq(total, flip)
    return total[:count], total[count:]


def norm_keep(values):
    inverse = lax.rsqrt(jnp.mean(values * values, axis=-1, keepdims=True) + EPSILON)
    return (values * inverse, inverse)


def norm_back(grad, normed, inverse):
    return inverse * (grad - normed * jnp.mean(grad * normed, axis=-1, keepdims=True))


def silu_slope(values):
    sigma = jax.nn.sigmoid(values)
    return sigma * (1.0 + values * (1.0 - sigma))


def carry_coefficients(alpha, eta):
    count, heads = alpha.shape
    place = jnp.arange(count)[:, None]
    mem = jnp.zeros((count, heads), F32)
    mom = jnp.zeros((count, heads), F32)
    rows = []
    for c in range(count):
        rows.append(mem)
        mom = eta[c] * mom + (place == c).astype(F32)
        mem = alpha[c] * mem + mom
    return jnp.stack(rows)


def dot(a, b):
    return jnp.dot(a, b, preferred_element_type=F32)


def dot_t(a, b):
    return lax.dot_general(a, b, (((1,), (1,)), ((), ())), preferred_element_type=F32)


def local_plain(
    inputs,
    lengths,
    decays,
    norm_gain,
    query_proj,
    key_proj,
    value_proj,
    gate_proj,
    conv_taps,
    pers_keys,
    pers_values,
    out_proj,
    ffn_gain,
    ffn_gate,
    ffn_up,
    ffn_down,
    cotangent,
):
    seqs, seg, features = inputs.shape
    segments = lax.axis_size("seq")
    shards = lax.axis_size("head")
    p, z = lax.axis_index("seq"), lax.axis_index("head")
    width = query_proj.shape[1]
    heads_here = width // DH
    heads = heads_here * shards
    rim = KW - 1
    persistent = pers_keys.shape[0]

    attn_slots = gather_weights(jnp.stack([query_proj, key_proj, value_proj, gate_proj, out_proj.T]))
    ffn_slots = gather_weights(jnp.stack([ffn_gate, ffn_up, ffn_down.T]))
    small = gather_small(
        jnp.concatenate([conv_taps.reshape(3 * KW, width), pers_keys, pers_values])
    )
    small = jnp.concatenate(small, axis=1)
    taps = small[: 3 * KW].reshape(3, KW, heads * DH).astype(F32)
    pers_k = small[3 * KW : 3 * KW + persistent].reshape(persistent, heads, DH)
    pers_v = small[3 * KW + persistent :].reshape(persistent, heads, DH)
    q_mat, k_mat, v_mat, g_mat, o_mat = [
        jnp.concatenate([slot[i] for slot in attn_slots], axis=1) for i in range(5)
    ]

    mine = lax.dynamic_index_in_dim(decays, z, 1, False)[:, 0]
    mine = jnp.concatenate(
        [lax.dynamic_slice_in_dim(mine, slot_owner(k) * heads_here, heads_here, 1) for k in range(shards)],
        axis=1,
    )
    every = lax.all_gather(mine, "seq")
    carry = carry_coefficients(every[:, 0], every[:, 1])

    x = lax.dynamic_index_in_dim(inputs, z, 0, False).astype(F32)
    cot = lax.dynamic_index_in_dim(cotangent, z, 0, False).astype(F32)
    length = lax.dynamic_index_in_dim(lengths, z, 0, False)
    live = ((p * seg + jnp.arange(seg, dtype=jnp.int32)) < length).astype(F32)
    live_two = live[:, None]
    tail = lax.dynamic_index_in_dim(inputs, z, 0, False)[seg - HALO :]
    before = lax.ppermute(tail, "seq", [(i, i + 1) for i in range(segments - 1)]).astype(F32)
    x_long = jnp.concatenate([before, x])
    n_long, inv_long = norm_keep(x_long)
    h_long = (n_long * norm_gain).astype(BF)
    n_one, inv_one, h_one = n_long[HALO:], inv_long[HALO:], h_long[HALO:]

    pre = jnp.stack([dot(h_long, m) for m in (q_mat, k_mat, v_mat)]).astype(BF)
    zgate = dot(h_one, g_mat)
    wide_pre = pre.astype(F32)
    conv_sum = sum(
        taps[:, lag][:, None, :] * wide_pre[:, HALO - lag : HALO - lag + seg] for lag in range(KW)
    )
    acts = jax.nn.silu(conv_sum).reshape(3, seg, heads, DH)
    q_normed, q_inverse = norm_keep(acts[0])
    k_normed, k_inverse = norm_keep(acts[1])
    query, keyed, valued = q_normed.astype(BF), k_normed.astype(BF), acts[2].astype(BF)
    live_three = live[:, None, None]
    masked_value = valued * live_three.astype(BF)
    write = jnp.einsum("tha,thb->hab", masked_value, keyed, preferred_element_type=F32) / seg

    def mix_states(values, coefficients):
        pieces, places = gather_states(values.astype(BF))
        total = 0.0
        for piece, place in zip(pieces, places):
            coefficient = lax.dynamic_index_in_dim(coefficients, place, 0, False)
            total = total + coefficient[:, None, None] * piece.astype(F32)
        return total.astype(BF)

    prior = mix_states(write, lax.dynamic_index_in_dim(carry, p, 0, False))
    raw_read = jnp.einsum("hab,thb->tha", prior, query, preferred_element_type=F32)
    readout, read_inverse = norm_keep(raw_read)

    keys_all = jnp.concatenate([pers_k, keyed])
    values_all = jnp.concatenate([pers_v, valued])
    valid = jnp.concatenate([jnp.ones((persistent,), F32), live])
    rows_index = jnp.arange(seg)[:, None]
    column = jnp.arange(persistent + seg)[None, :] - persistent
    allowed = (column < 0) | (column <= rows_index) & (valid[None, :] > 0.5)
    scale = DH ** (-0.5)
    score = jnp.einsum("thd,uhd->htu", query, keys_all, preferred_element_type=F32) * scale
    score = jnp.where(allowed[None], score, -1e30)
    top = jnp.max(score, axis=-1, keepdims=True)
    log_total = top + jnp.log(jnp.sum(jnp.exp(score - top), axis=-1, keepdims=True))
    prob = jnp.exp(score - log_total)
    prob_low = prob.astype(BF)
    attended = jnp.einsum("htu,uhd->thd", prob_low, values_all, preferred_element_type=F32)

    sigma = jax.nn.sigmoid(zgate)
    read_flat = readout.reshape(seg, -1)
    mixed = (attended.reshape(seg, -1) + sigma * read_flat).astype(BF)
    middle = x + live_two * dot_t(mixed, o_mat)
    n_two, inv_two = norm_keep(middle)
    h_two = (n_two * ffn_gain).astype(BF)

    gffn = (live_two * cot).astype(BF)
    ffn_out = 0.0
    dh_two = 0.0
    hidden_slots, gate_slots, up_slots = [], [], []
    for slot in ffn_slots:
        gate_value = dot(h_two, slot[0])
        up_value = dot(h_two, slot[1])
        silu_gate = jax.nn.silu(gate_value)
        hidden = (silu_gate * up_value).astype(BF)
        ffn_out = ffn_out + dot_t(hidden, slot[2])
        dhidden = dot(gffn, slot[2])
        dgate = (dhidden * up_value * silu_slope(gate_value)).astype(BF)
        dup = (dhidden * silu_gate).astype(BF)
        dh_two = dh_two + dot_t(dgate, slot[0]) + dot_t(dup, slot[1])
        hidden_slots.append(hidden)
        gate_slots.append(dgate)
        up_slots.append(dup)
    output = gather_rows((middle + live_two * ffn_out).astype(BF))
    g_gate, g_up, g_down = weight_grads(
        [(h_two, gate_slots), (h_two, up_slots), (gffn, hidden_slots)], True
    )

    grad_ffn_gain = jnp.sum(dh_two * n_two, axis=0)
    dmiddle = cot + norm_back(dh_two * ffn_gain, n_two, inv_two)
    gattn = (live_two * dmiddle).astype(BF)
    dmixed = dot(gattn, o_mat)
    datt = dmixed.astype(BF).reshape(seg, heads, DH)
    dzgate = (dmixed * read_flat * sigma * (1.0 - sigma)).astype(BF)
    dread = norm_back((dmixed * sigma).reshape(seg, heads, DH), readout, read_inverse).astype(BF)
    dprior = jnp.einsum("tha,thb->hab", dread, query, preferred_element_type=F32)
    dwrite = mix_states(dprior, lax.dynamic_index_in_dim(carry, p, 1, False))
    dquery_mem = jnp.einsum("hab,tha->thb", prior, dread, preferred_element_type=F32)
    dprob = jnp.einsum("thd,uhd->htu", datt, values_all, preferred_element_type=F32)
    row_dot = jnp.sum(prob * dprob, axis=-1, keepdims=True)
    dscore = (prob * (dprob - row_dot)).astype(BF)
    dquery = (
        jnp.einsum("htu,uhd->thd", dscore, keys_all, preferred_element_type=F32) * scale
        + dquery_mem
    )
    dkeys = jnp.einsum("htu,thd->uhd", dscore, query, preferred_element_type=F32) * scale
    dvalues = jnp.einsum("htu,thd->uhd", prob_low, datt, preferred_element_type=F32)
    dvals = (
        dvalues[persistent:]
        + live_three * jnp.einsum("hab,thb->tha", dwrite, keyed, preferred_element_type=F32) / seg
    )
    dkey = (
        dkeys[persistent:]
        + jnp.einsum("hab,tha->thb", dwrite, masked_value, preferred_element_type=F32) / seg
    )
    dact = jnp.stack(
        [norm_back(dquery, q_normed, q_inverse), norm_back(dkey, k_normed, k_inverse), dvals]
    ).reshape(3, seg, -1)
    dconv = dact * silu_slope(conv_sum)
    longer = jnp.pad(dconv, ((0, 0), (rim, rim), (0, 0)))
    spread = sum(
        taps[:, lag][:, None, :] * longer[:, lag : lag + seg + rim] for lag in range(KW)
    )
    grad_conv = jnp.stack(
        [
            jnp.sum(dconv * wide_pre[:, HALO - lag : HALO - lag + seg], axis=1)
            for lag in range(KW)
        ],
        axis=1,
    )
    back = lax.ppermute(
        spread[:, :rim].astype(BF), "seq", [(i + 1, i) for i in range(segments - 1)]
    ).astype(F32)
    dpre = spread[:, rim:] + jnp.pad(back, ((0, 0), (seg - rim, 0), (0, 0)))
    dpre = dpre.astype(BF)

    dh_one = (
        dot_t(dpre[0], q_mat) + dot_t(dpre[1], k_mat) + dot_t(dpre[2], v_mat) + dot_t(dzgate, g_mat)
    )
    grad_norm_gain = jnp.sum(dh_one * n_one, axis=0)
    input_grad = gather_rows(
        (dmiddle + norm_back(dh_one * norm_gain, n_one, inv_one)).astype(BF)
    )

    def by_slot(value):
        return [value[..., k * width : (k + 1) * width] for k in range(shards)]

    g_query, g_key, g_value, g_zgate, g_out = weight_grads(
        [(h_one, by_slot(d)) for d in (dpre[0], dpre[1], dpre[2], dzgate)]
        + [(gattn, by_slot(mixed))],
        False,
    )
    rows = jnp.concatenate(
        [
            grad_conv.reshape(3 * KW, -1),
            dkeys[:persistent].reshape(persistent, -1),
            dvalues[:persistent].reshape(persistent, -1),
        ]
    )
    gains = jnp.concatenate([grad_norm_gain, grad_ffn_gain]).reshape(-1, width)
    rows, gains = sum_small(by_slot(rows), gains)
    gains = gains.reshape(2, features)
    return (
        output,
        input_grad,
        gains[0],
        g_query,
        g_key,
        g_value,
        g_zgate,
        rows[: 3 * KW].reshape(3, KW, width),
        rows[3 * KW : 3 * KW + persistent],
        rows[3 * KW + persistent :],
        g_out.T,
        gains[1],
        g_gate,
        g_up,
        g_down.T,
    )


ROWS = 16
BLOCK = 128
SCALE = DH ** (-0.5)


def shift_sum(source, taps, first, rows, step):
    total = taps[0:1] * source[pl.ds(first, rows)]
    for lag in range(1, KW):
        total = total + taps[lag : lag + 1] * source[pl.ds(first + step * lag, rows)]
    return total


def live_rows(first, rows, length, segment_start):
    place = segment_start + first + lax.broadcasted_iota(jnp.int32, (rows, 1), 0)
    return (place < length).astype(F32)


def live_columns(columns, length, segment_start):
    return segment_start + lax.broadcasted_iota(jnp.int32, (1, columns), 1) < length


def masked_scores(query, keys, pers_k, index, columns_live):
    width = keys.shape[0]
    raw = dot_t(query, keys) * SCALE
    row = index * BLOCK + lax.broadcasted_iota(jnp.int32, (BLOCK, width), 0)
    column = lax.broadcasted_iota(jnp.int32, (BLOCK, width), 1)
    keep = (column <= row) & columns_live[:, :width]
    return jnp.where(keep, raw, -1e30), dot_t(query, pers_k) * SCALE


def attention_back_slot(k, refs, length, segment_start):
    query, keyed, valued, lse, datt, dread, prior, small, dqkv, small_grad = refs
    seg = query.shape[1]
    columns_live = live_columns(seg, length, segment_start)
    turn = lambda a, b: lax.dot_general(a, b, (((0,), (0,)), ((), ())), preferred_element_type=F32)
    for head in range(query.shape[2] // DH):
        lanes = slice(head * DH, (head + 1) * DH)
        pers_keys_sum = jnp.zeros((16, DH), F32)
        pers_values_sum = jnp.zeros((16, DH), F32)
        pk = small[k, PERS_K : PERS_K + 16, lanes].astype(BF)
        pv = small[k, PERS_V : PERS_V + 16, lanes].astype(BF)
        dqkv[1, :, lanes] = jnp.zeros((seg, DH), F32)
        dqkv[2, :, lanes] = jnp.zeros((seg, DH), F32)
        dqkv[0, :, lanes] = dot(dread[k, :, lanes], prior[k, head])
        for index in range(seg // BLOCK):
            rows = pl.ds(index * BLOCK, BLOCK)
            upto = pl.ds(0, (index + 1) * BLOCK)
            q, d = query[k, rows, lanes], datt[k, rows, lanes]
            keys = keyed[k, upto, lanes]
            score, pers = masked_scores(q, keys, pk, index, columns_live)
            log_total = lse[k, head, rows]
            prob, prob_p = jnp.exp(score - log_total), jnp.exp(pers - log_total)
            grad = dot_t(d, valued[k, upto, lanes])
            grad_p = dot_t(d, pv)
            row_dot = jnp.sum(prob * grad, axis=-1, keepdims=True) + jnp.sum(
                prob_p * grad_p, axis=-1, keepdims=True
            )
            dscore = (prob * (grad - row_dot)).astype(BF)
            dscore_p = (prob_p * (grad_p - row_dot)).astype(BF)
            dqkv[0, rows, lanes] += (dot(dscore, keys) + dot(dscore_p, pk)) * SCALE
            dqkv[1, upto, lanes] += turn(dscore, q) * SCALE
            dqkv[2, upto, lanes] += turn(prob.astype(BF), d)
            pers_keys_sum = pers_keys_sum + turn(dscore_p, q)
            pers_values_sum = pers_values_sum + turn(prob_p.astype(BF), d)
        small_grad[k, PERS_K : PERS_K + 16, lanes] = pers_keys_sum * SCALE
        small_grad[k, PERS_V : PERS_V + 16, lanes] = pers_values_sum


def conv_back_slot(k, refs, length, segment_start):
    pre, small, keyed, valued, dwrite, dqkv, dconv, small_grad, wide = refs
    seg = keyed.shape[1]
    heads = keyed.shape[2] // DH
    for i in range(3):
        wide[i] = pre[i, k].astype(F32)
    sums = [[jnp.zeros((1, heads * DH), F32) for _ in range(KW)] for _ in range(3)]
    for first in range(0, seg, BLOCK):
        rows = pl.ds(first, BLOCK)
        live = live_rows(first, BLOCK, length, segment_start)
        for i in range(3):
            conv = shift_sum(wide.at[i], taps_of(small, k, i), ROWS + first, BLOCK, -1)
            sigma = jax.nn.sigmoid(conv)
            act = conv * sigma
            parts = []
            for head in range(heads):
                lanes = slice(head * DH, (head + 1) * DH)
                grad = dqkv[i, rows, lanes]
                if i == 1:
                    masked = valued[k, rows, lanes] * live.astype(BF)
                    grad = grad + dot(masked, dwrite[k, head]) / seg
                if i == 2:
                    grad = grad + live * dot_t(keyed[k, rows, lanes], dwrite[k, head]) / seg
                else:
                    grad = norm_back(grad, *norm_keep(act[:, lanes]))
                parts.append(grad)
            result = jnp.concatenate(parts, axis=1) * (sigma * (1.0 + conv * (1.0 - sigma)))
            dconv[i, 0, rows] = result
            for lag in range(KW):
                sums[i][lag] = sums[i][lag] + jnp.sum(
                    result * wide[i, pl.ds(ROWS + first - lag, BLOCK)], axis=0, keepdims=True
                )
    for i in range(3):
        for lag in range(KW):
            row = TAPS + KW * i + lag
            small_grad[k, row : row + 1] = sums[i][lag]


SHAPE = jax.ShapeDtypeStruct
VMEM_LIMIT = 127 * 512 * 1024


MESH = pl.DeviceIdType.MESH
SKEW_ONE, SKEW_TWO = 2, 4
WINDOW = 4
UNITS = (
    ("proj", 1), ("proj", 2), ("proj", 3), ("ffn", 1), ("out", 1), ("out", 2), ("out", 3), ("down", 1),
    ("ffn", 2), ("down", 2), ("ffn", 3), ("down", 3),
)


class Links:
    def __init__(self, send, recv):
        self.send, self.recv = send, recv
        self.sent = 0
        self.names = {}
        self.always, self.middles = [], []
        self.p, self.z = lax.axis_index("seq"), lax.axis_index("head")
        self.middle = (self.z == 1) | (self.z == 2)

    def greet(self):
        barrier = pltpu.get_barrier_semaphore()
        for flip in range(1, 8):
            pl.semaphore_signal(barrier, device_id=(self.p ^ flip, self.z), device_id_type=MESH)
        for flip in (1, 2, 3):
            pl.semaphore_signal(barrier, device_id=(self.p, self.z ^ flip), device_id_type=MESH)
        pl.semaphore_wait(barrier, 10)

    def place(self, name):
        return self.recv.at[self.names.setdefault(name, len(self.names))]

    def copy(self, source, target, name, device):
        index = self.sent
        self.sent += 1
        return pltpu.make_async_remote_copy(
            src_ref=source, dst_ref=target, send_sem=self.send.at[index], recv_sem=self.place(name),
            device_id=device, device_id_type=MESH,
        )

    def along_seq(self, source, target, name, flip):
        copy = self.copy(source, target, name, (self.p ^ flip, self.z))
        copy.start()
        self.always.append((lambda: source, self.sent - 1))

    def along_head(self, source, target, name, flip, waits):
        index = self.sent
        copy = self.copy(source(), target(), name, (self.p, self.z ^ flip))
        copy.start()
        waits.append((source, index))

    def arrived(self, target, name):
        pltpu.make_async_remote_copy(
            src_ref=target, dst_ref=target, send_sem=self.send.at[0], recv_sem=self.place(name),
            device_id=(self.p, self.z ^ 1), device_id_type=MESH,
        ).wait_recv()

    def gone(self, source, index):
        pltpu.make_async_remote_copy(
            src_ref=source(), dst_ref=source(), send_sem=self.send.at[index], recv_sem=self.recv.at[0],
            device_id=(self.p, self.z ^ 1), device_id_type=MESH,
        ).wait_send()

    def finish(self):
        for source, index in self.always:
            self.gone(source, index)

        @pl.when(self.middle)
        def _():
            for source, index in self.middles:
                self.gone(source, index)


class LineGather:
    def __init__(self, links, name, view, fixed=False):
        self.links, self.name, self.view, self.fixed = links, name, view, fixed

    def start(self, sources):
        links = self.links
        for source, view in sources:
            links.along_head(source, lambda: view(1), (self.name, 1), 1, links.always)

        @pl.when(links.middle)
        def _():
            for source, view in sources:
                links.along_head(source, lambda: view(3), (self.name, 3), 3, links.middles)

    def forward(self, k, flip):
        view, there = self.view, k ^ flip
        self.links.along_head(
            lambda: view(k), lambda: view(k if self.fixed else there), (self.name, there), flip,
            self.links.middles,
        )

    def outward(self):
        @pl.when(self.links.middle)
        def _():
            self.links.arrived(self.view(3), (self.name, 3))
            self.forward(3, 1)

    def step(self, k):
        links, name, view = self.links, self.name, self.view
        if k == 1:
            links.arrived(view(1), (name, 1))

            @pl.when(links.middle)
            def _():
                self.forward(1, 3)

        if k == 2:
            links.arrived(view(2), (name, 2))

            @pl.when(links.middle)
            def _():
                self.forward(2, 1)

        if k == 3:

            @pl.when(~links.middle)
            def _():
                links.arrived(view(3), (name, 3))


class PlaneGather:
    def __init__(self, links, name, view, x_first):
        self.links, self.name, self.view = links, name, view
        self.near, self.far = (2, 4) if x_first else (4, 2)

    def send(self, j, flip):
        links = self.links
        block = self.view(links.p ^ j)
        links.along_seq(block, block, (self.name, j ^ flip), flip)

    def wait(self, j):
        self.links.arrived(self.view(self.links.p ^ j), (self.name, j))

    def start(self):
        self.send(0, self.near)
        self.send(0, self.far)
        self.send(0, 1)

    def step(self):
        self.wait(self.near)
        self.send(self.near, self.far)
        self.send(self.near, 1)
        self.wait(self.far)
        self.send(self.far, 1)

    def last(self):
        self.wait(6)
        self.send(6, 1)

    def end(self):
        for j in (1, 3, 5, 7):
            self.wait(j)


class StateExchange:
    def __init__(self, links, name, view):
        self.links, self.name, self.view = links, name, view

    def send(self, j, flip):
        block = self.view(self.links.p ^ j)
        self.links.along_seq(block, block, (self.name, j ^ flip), flip)

    def wait(self, j):
        self.links.arrived(self.view(self.links.p ^ j), (self.name, j))

    def start(self):
        for flip in (6, 2, 4, 1):
            self.send(0, flip)

    def step(self):
        for j in (2, 4, 6):
            self.wait(j)
            self.send(j, 1)

    def end(self):
        for j in (1, 3, 5, 7):
            self.wait(j)


def weight_events(links, own, weights, out_w, gate_up, down):
    q_own, k_own, v_own, g_own, o_own, gate_own, up_own, down_own = own
    block = lambda q: pl.ds(pl.multiple_of(q * 128, 128), 128)
    mine = block(links.p)
    views = {
        "proj": (lambda k, q: weights.at[k, :, block(q), :], True),
        "out": (lambda k, q: out_w.at[k, :, block(q)], False),
        "ffn": (lambda k, q: gate_up.at[k, :, :, block(q)], False),
        "down": (lambda k, q: down.at[k, :, block(q)], True),
    }
    sources = {
        "proj": [
            (lambda ref=ref: ref.at[mine, :], lambda k, i=i: weights.at[k, i, mine, :])
            for i, ref in enumerate((q_own, k_own, v_own, g_own))
        ],
        "out": [(lambda: o_own.at[:, mine], lambda k: out_w.at[k, :, mine])],
        "ffn": [
            (lambda ref=ref: ref.at[:, mine], lambda k, i=i: gate_up.at[k, i, :, mine])
            for i, ref in enumerate((gate_own, up_own))
        ],
        "down": [(lambda: down_own.at[:, mine], lambda k: down.at[k, :, mine])],
    }
    planes = {
        (name, k): PlaneGather(links, (name, k), lambda q, view=view, k=k: view(k, q), x_first)
        for name, (view, x_first) in views.items()
        for k in (1, 2, 3)
    }
    units = UNITS
    count = len(units)

    def post(i):
        if i < count:
            name, k = units[i]
            for source, target in sources[name]:
                links.along_head(source, lambda: target(k), ("line", name, k), k, links.always)

    def begin():
        for i in range(WINDOW):
            post(i)

    events = [(None, begin)]
    for i in range(count + SKEW_TWO):
        if i < count:
            name, k = units[i]

            def first(name=name, k=k, i=i):
                links.arrived(views[name][0](k, links.p), ("line", name, k))
                post(i + WINDOW)
                planes[name, k].start()

            events.append((None, first))
        if 0 <= i - SKEW_ONE < count:
            events.append((None, planes[units[i - SKEW_ONE]].step))
        if 0 <= i - SKEW_TWO < count:
            events.append((units[i - SKEW_TWO], planes[units[i - SKEW_TWO]].last))
    return events, planes


PERS_K, PERS_V, TAPS, GAINS, SMALL = 0, 16, 32, 48, 56


def taps_of(small, k, i):
    return small[k, TAPS + KW * i : TAPS + KW * (i + 1)]


def carry_in_kernel(every, place, forward, backward):
    count, lanes = every.shape[0], every.shape[2]
    row = lax.broadcasted_iota(jnp.int32, (count, lanes), 0)
    mem = jnp.zeros((count, lanes), F32)
    mom = jnp.zeros((count, lanes), F32)
    ahead = jnp.zeros((count, lanes), F32)
    behind = jnp.zeros((count, lanes), F32)
    for c in range(count):
        ahead = jnp.where(place == c, mem, ahead)
        mine = jnp.sum(jnp.where(row == place, mem, 0.0), axis=0, keepdims=True)
        behind = jnp.where(row == c, mine, behind)
        mom = every[c, 1:2] * mom + (row == c).astype(F32)
        mem = every[c, 0:1] * mem + mom
    forward[...] = ahead
    backward[...] = behind


def mixed_state(states, coefficients, k, head):
    lane = 2 * k + head
    total = coefficients[0:1, lane : lane + 1] * states[0, k, head].astype(F32)
    for q in range(1, states.shape[0]):
        total = total + coefficients[q : q + 1, lane : lane + 1] * states[q, k, head].astype(F32)
    return total.astype(BF)


def project_slot(k, h_long, weights, pre, zgate, wide):
    seg = zgate.shape[1]
    for i in range(3):
        rounded = dot(h_long[...], weights[i]).astype(BF)
        pre[i, k] = rounded
        wide[i] = rounded.astype(F32)
    zgate[k] = dot(h_long[pl.ds(ROWS, seg)], weights[3])


def convolve_slot(k, small, query, keyed, valued, wide):
    seg = query.shape[1]
    heads = query.shape[2] // DH

    for first in range(0, seg, BLOCK):
        rows = pl.ds(first, BLOCK)
        for i in range(3):
            conv = shift_sum(wide.at[i], taps_of(small, k, i), ROWS + first, BLOCK, -1)
            act = conv * jax.nn.sigmoid(conv)
            if i == 2:
                valued[k, rows] = act.astype(BF)
                continue
            target = (query, keyed)[i]
            for head in range(heads):
                lanes = slice(head * DH, (head + 1) * DH)
                target[k, rows, lanes] = norm_keep(act[:, lanes])[0].astype(BF)


def write_slot(k, p, keyed, valued, states, length, segment_start):
    seg = keyed.shape[1]
    seg_live = live_rows(0, seg, length, segment_start).astype(BF)
    for head in range(keyed.shape[2] // DH):
        lanes = slice(head * DH, (head + 1) * DH)
        masked = valued[k, :, lanes] * seg_live
        states[p, k, head] = (
            lax.dot_general(
                masked, keyed[k, :, lanes], (((0,), (0,)), ((), ())), preferred_element_type=F32
            )
            / seg
        ).astype(BF)


def attend_head(k, head, small, query, keyed, valued, att, lse, length, segment_start):
    seg = query.shape[1]
    columns_live = live_columns(seg, length, segment_start)
    lanes = slice(head * DH, (head + 1) * DH)
    pers_k = small[k, PERS_K : PERS_K + 16, lanes].astype(BF)
    pers_v = small[k, PERS_V : PERS_V + 16, lanes].astype(BF)
    for index in range(seg // BLOCK):
        rows = pl.ds(index * BLOCK, BLOCK)
        upto = pl.ds(0, (index + 1) * BLOCK)
        score, pers = masked_scores(
            query[k, rows, lanes], keyed[k, upto, lanes], pers_k, index, columns_live
        )
        top = jnp.maximum(
            jnp.max(score, axis=-1, keepdims=True), jnp.max(pers, axis=-1, keepdims=True)
        )
        score, pers = jnp.exp(score - top), jnp.exp(pers - top)
        total = jnp.sum(score, axis=-1, keepdims=True) + jnp.sum(pers, axis=-1, keepdims=True)
        inverse = 1.0 / total
        lse[k, head, rows] = top + jnp.log(total)
        att[k, rows, lanes] = dot((score * inverse).astype(BF), valued[k, upto, lanes]) + dot(
            (pers * inverse).astype(BF), pers_v
        )


def read_slot(k, prior, query, zgate, att, mixed):
    for head in range(query.shape[2] // DH):
        lanes = slice(head * DH, (head + 1) * DH)
        normed, _ = norm_keep(dot_t(query[k, :, lanes], prior[k, head]))
        mixed[k, :, lanes] = (
            att[k, :, lanes] + jax.nn.sigmoid(zgate[k, :, lanes]) * normed
        ).astype(BF)


def ffn_rows(rows, h_two, gffn, weights_gu, weights_d, stage, out_acc, grad_acc):
    gate = dot_t(h_two[rows], weights_gu[0])
    up = dot_t(h_two[rows], weights_gu[1])
    sigma = jax.nn.sigmoid(gate)
    silu = gate * sigma
    low = (silu * up).astype(BF)
    stage[0, rows] = low
    out_acc[rows] += dot(low, weights_d[...])
    back = dot_t(gffn[rows], weights_d[...])
    low_gate = (back * up * (sigma * (1.0 + gate * (1.0 - sigma)))).astype(BF)
    low_up = (back * silu).astype(BF)
    stage[1, rows] = low_gate
    stage[2, rows] = low_up
    grad_acc[rows] += dot(low_gate, weights_gu[0]) + dot(low_up, weights_gu[1])


def tail_slot(k, out_w, gattn, query, prior, zgate, datt, dzgate, dread, dprior):
    dmixed = dot_t(gattn[...], out_w[k])
    datt[k] = dmixed.astype(BF)
    for head in range(dmixed.shape[1] // DH):
        lanes = slice(head * DH, (head + 1) * DH)
        sigma = jax.nn.sigmoid(zgate[k, :, lanes])
        readout, rinv = norm_keep(dot_t(query[k, :, lanes], prior[k, head]))
        grad = dmixed[:, lanes] * sigma
        dzgate[k, :, lanes] = (grad * readout * (1.0 - sigma)).astype(BF)
        low = norm_back(grad, readout, rinv).astype(BF)
        dread[k, :, lanes] = low
        dprior[k, head] = lax.dot_general(
            low, query[k, :, lanes], (((0,), (0,)), ((), ())), preferred_element_type=F32
        ).astype(BF)


class Steps:
    def __init__(self, events):
        self.events, self.at, self.done = events, 0, set()

    def run(self, count=1):
        for _ in range(count):
            if self.at < len(self.events):
                label, function = self.events[self.at]
                function()
                self.at += 1
                self.done.add(label)

    def until(self, *labels):
        while not all(label in self.done for label in labels):
            self.run()


def front_kernel(
    lengths, gain, ffn_gain, own_small, own_decays,
    inputs, cotangent, q_own, k_own, v_own, g_own, o_own, gate_own, up_own, down_own,
    small, backward, dprior, gain_grad,
    x_long_out, h_long_out, pre_out, query_out, keyed_out, valued_out, lse_out, prior_out, mixed_out, h_two_out, gffn_out,
    output_out, dmiddle_out, gattn_out, datt_out, dzgate_out, dread_out,
    weights, hidden, dgate, dup, out_w, gate_up, down,
    x_long, h_long, pre, query, keyed, valued, lse, prior, mixed, h_two, gffn,
    output, dmiddle, gattn, datt, dzgate, dread,
    cot, zgate, att, wide, states, every, forward, wproj, wout, wgu, wdown, stage, out_acc, grad_acc,
    send, recv, sem_x, sem_proj, sem_out, sem_ffn, sem_stage, sem_early, sem_late, sem_slots,
):
    links = Links(send, recv)
    p, z = links.p, links.z
    seg = h_two.shape[0]
    length, start = lengths[z], p * seg
    own = (q_own, k_own, v_own, g_own, o_own, gate_own, up_own, down_own)
    load_x = pltpu.make_async_copy(inputs.at[z], x_long.at[pl.ds(ROWS, seg)], sem_x.at[0])
    load_cot = pltpu.make_async_copy(cotangent.at[z], cot, sem_x.at[1])
    load_x.start()

    def proj_loads(k):
        if k == 0:
            return [
                pltpu.make_async_copy(ref, wproj.at[i], sem_proj.at[i]) for i, ref in enumerate(own[:4])
            ]
        return [pltpu.make_async_copy(weights.at[k], wproj, sem_proj.at[0])]

    def out_load(k):
        return pltpu.make_async_copy(o_own if k == 0 else out_w.at[k], wout.at[k], sem_out.at[k])

    def ffn_loads(k):
        side = k % 2
        if k == 0:
            gu = [
                pltpu.make_async_copy(gate_own, wgu.at[0, 0], sem_ffn.at[0, 0]),
                pltpu.make_async_copy(up_own, wgu.at[0, 1], sem_ffn.at[0, 2]),
            ]
        else:
            gu = [pltpu.make_async_copy(gate_up.at[k], wgu.at[side], sem_ffn.at[side, 0])]
        return gu + [
            pltpu.make_async_copy(down_own if k == 0 else down.at[k], wdown.at[side], sem_ffn.at[side, 1])
        ]

    def go(copies):
        for copy in copies:
            copy.start()

    def come(copies):
        for copy in copies:
            copy.wait()

    go(proj_loads(0))
    go([load_cot, out_load(0)])
    go(ffn_loads(0))
    every[p] = own_decays[...]
    small[0] = own_small[...]
    links.greet()
    events, planes = weight_events(links, own, weights, out_w, gate_up, down)
    steps = Steps(events)

    @pl.when(p < 7)
    def _():
        links.copy(
            inputs.at[z, pl.ds(seg - ROWS, ROWS)], x_long.at[pl.ds(0, ROWS)], "rows", (p + 1, z)
        ).start()

    rows_index = links.sent - 1
    for j in range(1, 8):
        links.along_seq(own_decays, every.at[p], ("decays", j), j)
    for k in (1, 2, 3):
        links.copy(own_small, small.at[k], ("small", k), (p, z ^ k)).start()
        links.always.append((lambda: own_small, links.sent - 1))
    steps.run()

    load_x.wait()

    @pl.when(p == 0)
    def _():
        x_long[pl.ds(0, ROWS)] = jnp.zeros((ROWS, x_long.shape[1]), BF)

    @pl.when(p > 0)
    def _():
        links.arrived(x_long.at[pl.ds(0, ROWS)], "rows")

    @pl.loop(0, 3)
    def _(c):
        rows = pl.ds(pl.multiple_of(c * 176, 16), 176)
        normed, _ = norm_keep(x_long[rows].astype(F32))
        h_long[rows] = (normed * gain[...]).astype(BF)

    exchanges = [StateExchange(links, ("states", k), lambda q, k=k: states.at[q, k]) for k in range(4)]
    complete = lambda name, k: planes[name, k].end()
    come(proj_loads(0))
    attend = lambda k, head: attend_head(k, head, small, query, keyed, valued, att, lse, length, start)

    def load_next(k):
        steps.until(("proj", k))
        complete("proj", k)
        go(proj_loads(k))

    def open_slot(k):
        project_slot(k, h_long, wproj, pre, zgate, wide)
        steps.run()
        convolve_slot(k, small, query, keyed, valued, wide)
        write_slot(k, p, keyed, valued, states, length, start)
        exchanges[k].start()

    steps.run()
    project_slot(0, h_long, wproj, pre, zgate, wide)
    steps.run()
    for other in (1, 2, 3):
        links.arrived(small.at[other], ("small", other))
    convolve_slot(0, small, query, keyed, valued, wide)
    steps.run()
    write_slot(0, p, keyed, valued, states, length, start)
    exchanges[0].start()
    attend(0, 0)
    steps.run()
    attend(0, 1)
    exchanges[0].step()
    for k in (1, 2, 3):
        load_next(k)
        come(proj_loads(k))
        open_slot(k)
        steps.run()
        if k == 1:
            attend(1, 0)
            steps.run()
            exchanges[1].step()
    attend(1, 1)
    exchanges[2].step()
    steps.run()
    attend(2, 0)
    exchanges[3].step()
    steps.run()
    attend(2, 1)
    steps.run()
    attend(3, 0)
    steps.run()
    attend(3, 1)
    for j in range(1, 8):
        links.arrived(every.at[p ^ j], ("decays", j))
    carry_in_kernel(every, p, forward, backward)
    for k in (1, 2, 3):
        steps.until(("out", k))
        complete("out", k)
        go([out_load(k)])
    for k in range(4):
        exchanges[k].end()
        for head in range(2):
            prior[k, head] = mixed_state(states, forward, k, head)
        read_slot(k, prior, query, zgate, att, mixed)
        come([out_load(k)])

        @pl.loop(0, 2)
        def _(c):
            rows = pl.ds(pl.multiple_of(c * 256, 256), 256)
            part = dot(mixed[k, rows], wout[k])
            if k == 0:
                grad_acc[rows] = part
            else:
                grad_acc[rows] += part

        steps.run()
    load_cot.wait()

    @pl.loop(0, seg // BLOCK)
    def _(c):
        first = pl.multiple_of(c * BLOCK, BLOCK)
        rows = pl.ds(first, BLOCK)
        live = live_rows(first, BLOCK, length, start)
        value = x_long[pl.ds(pl.multiple_of(ROWS + first, 16), BLOCK)].astype(F32) + live * grad_acc[rows]
        dmiddle[rows] = value
        normed, _ = norm_keep(value)
        h_two[rows] = (normed * ffn_gain[...]).astype(BF)
        gffn[rows] = (live * cot[rows].astype(F32)).astype(BF)
        out_acc[rows] = jnp.zeros((BLOCK, out_acc.shape[1]), F32)
        grad_acc[rows] = jnp.zeros((BLOCK, out_acc.shape[1]), F32)

    early = [
        pltpu.make_async_copy(source, target, sem_early.at[i])
        for i, (source, target) in enumerate(
            (
                (x_long, x_long_out), (h_long, h_long_out), (pre, pre_out), (query, query_out), (keyed, keyed_out),
                (valued, valued_out), (lse, lse_out), (prior, prior_out), (mixed, mixed_out), (h_two, h_two_out),
                (gffn, gffn_out),
            )
        )
    ]
    late = [
        pltpu.make_async_copy(source, target, sem_late.at[i])
        for i, (source, target) in enumerate(((output, output_out), (dmiddle, dmiddle_out), (gattn, gattn_out)))
    ]
    slot_stores = [
        pltpu.make_async_copy(source.at[k], target.at[k], sem_slots.at[k, i])
        for k in range(4)
        for i, (source, target) in enumerate(((datt, datt_out), (dzgate, dzgate_out), (dread, dread_out)))
    ]
    go(early)

    def stores(k):
        return [
            pltpu.make_async_copy(stage.at[k % 2, i], ref.at[k], sem_stage.at[k % 2, i])
            for i, ref in enumerate((hidden, dgate, dup))
        ]

    for k in range(4):
        if k == 3:
            steps.until(("ffn", 3), ("down", 3))
            complete("ffn", 3)
            complete("down", 3)
            go(ffn_loads(3))
        come(ffn_loads(k))
        if k < 2:
            steps.until(("ffn", k + 1), ("down", k + 1))
            complete("ffn", k + 1)
            complete("down", k + 1)
            go(ffn_loads(k + 1))
        if k >= 2:
            come(stores(k - 2))

        @pl.loop(0, 2)
        def _(c):
            rows = pl.ds(pl.multiple_of(c * 256, 256), 256)
            ffn_rows(rows, h_two, gffn, wgu.at[k % 2], wdown.at[k % 2], stage.at[k % 2], out_acc, grad_acc)

        go(stores(k))
        steps.run(3)
    gain_grad[...] = jnp.zeros_like(gain_grad)

    @pl.loop(0, seg // BLOCK)
    def _(c):
        first = pl.multiple_of(c * BLOCK, BLOCK)
        rows = pl.ds(first, BLOCK)
        live = live_rows(first, BLOCK, length, start)
        value = dmiddle[rows]
        output[rows] = (value + live * out_acc[rows]).astype(BF)
        normed, inverse = norm_keep(value)
        grad = grad_acc[rows]
        gain_grad[...] += jnp.sum(grad * normed, axis=0, keepdims=True)
        result = cot[rows].astype(F32) + norm_back(grad * ffn_gain[...], normed, inverse)
        dmiddle[rows] = result
        gattn[rows] = (live * result).astype(BF)

    go(late)
    for k in range(4):
        tail_slot(k, wout, gattn, query, prior, zgate, datt, dzgate, dread, dprior)
        go(slot_stores[3 * k : 3 * k + 3])
    come(stores(2))
    come(stores(3))
    come(early)
    come(late)
    come(slot_stores)

    @pl.when(p < 7)
    def _():
        links.gone(lambda: x_long.at[pl.ds(0, ROWS)], rows_index)

    links.finish()


class PlaneReduce:
    def __init__(self, links, name, blocks, first, second, x_first):
        self.links, self.name, self.x_first = links, name, x_first
        self.blocks, self.first, self.second = blocks, first, second

    def start(self):
        away = self.blocks.at[:, :, 1] if self.x_first else self.blocks.at[:, 1]
        self.links.along_seq(away, self.first, (self.name, 1), 2 if self.x_first else 4)

    def step(self):
        self.links.arrived(self.first, (self.name, 1))
        for i in range(2):
            y, x = (i, 0) if self.x_first else (0, i)

            @pl.loop(0, self.blocks.shape[0])
            def _(m):
                self.blocks[m, y, x] = add(self.blocks[m, y, x], self.first[m, i])

        y, x = (1, 0) if self.x_first else (0, 1)
        self.links.along_seq(
            self.blocks.at[:, y, x], self.second, (self.name, 2), 4 if self.x_first else 2
        )

    def last(self):
        self.links.arrived(self.second, (self.name, 2))

        @pl.loop(0, self.blocks.shape[0])
        def _(m):
            self.blocks[m, 0, 0] = add(self.blocks[m, 0, 0], self.second[m])


class LineReduce:
    def __init__(self, links, name, blocks, landing, result):
        self.links, self.name, self.blocks = links, name, blocks
        self.landing, self.result = landing, result
        self.ends = []

    def send(self, k, slot, flip, waits):
        self.links.along_head(
            lambda: self.blocks(k), lambda: self.landing.at[slot], (self.name, slot), flip, waits
        )

    def merge(self, k, slot):
        self.links.arrived(self.landing.at[slot], (self.name, slot))
        block = self.blocks(k)

        @pl.loop(0, self.landing.shape[1])
        def _(m):
            block[m] = add(block[m], self.landing[slot, m])

    def from_ends(self, k):
        @pl.when(~self.links.middle)
        def _():
            self.send(k, 3 - k, 1, self.ends)

    def take(self, k):
        @pl.when(self.links.middle)
        def _():
            self.merge(5 - k, 3 - k)

    def across(self, k):
        @pl.when(self.links.middle)
        def _():
            self.send(5 - k, 7 - k, 3, self.links.middles)

    def to_ends(self):
        @pl.when(self.links.middle)
        def _():
            self.merge(1, 4)
            self.send(1, 3, 1, self.links.middles)

    def last(self):
        @pl.when(~self.links.middle)
        def _():
            self.total([3])

        @pl.when(self.links.middle)
        def _():
            self.total([2, 5])

    def total(self, slots):
        block = self.blocks(0)
        for slot in slots:
            self.links.arrived(self.landing.at[slot], (self.name, slot))

        @pl.loop(0, self.landing.shape[1])
        def _(m):
            value = block[m].astype(F32)
            for slot in slots:
                value = value + self.landing[slot, m].astype(F32)
            self.result[m] = value

    def finish(self):
        @pl.when(~self.links.middle)
        def _():
            for source, index in self.ends:
                self.links.gone(source, index)


class Pairs:
    def __init__(self, buffers, sems):
        self.buffers, self.sems = buffers, sems

    def copies(self, slot, own, peer):
        rows = own.shape[0]
        return [
            pltpu.make_async_copy(own, self.buffers.at[slot, pl.ds(0, rows)], self.sems.at[slot, 0]),
            pltpu.make_async_copy(peer, self.buffers.at[slot, pl.ds(rows, rows)], self.sems.at[slot, 1]),
        ]

    def start(self, slot, own, peer):
        for copy in self.copies(slot, own, peer):
            copy.start()

    def wait(self, slot, own, peer):
        for copy in self.copies(slot, own, peer):
            copy.wait()


def load_turned(links, own, peer, staged, turned, sems):
    rows = own.shape[0]
    copies = []
    for i, j in enumerate((0, 2, 4, 6)):
        block = pl.ds(pl.multiple_of((links.p ^ j) * 128, 128), 128)
        for side, ref in enumerate((own, peer)):
            copy = pltpu.make_async_copy(
                ref.at[:, block], staged.at[pl.ds(side * rows, rows), pl.ds(i * 128, 128)], sems.at[i, side]
            )
            copy.start()
            copies.append(copy)
    for copy in copies:
        copy.wait()
    for i in range(4):
        turned[pl.ds(i * 128, 128)] = staged[:, pl.ds(i * 128, 128)].T


def conv_back(k, refs, length, segment_start):
    pre, small, keyed, valued, dwrite, dqkv, dslot, small_grad, wide, dpre, part, halo = refs
    conv_back_slot(
        k, (pre, small, keyed, valued, dwrite, dqkv, dslot, small_grad, wide), length, segment_start
    )
    seg = keyed.shape[1]
    for i in range(3):
        dslot[i, 0, pl.ds(seg, 8)] = jnp.zeros((8, dslot.shape[3]), F32)
        halo[i, k] = dslot[i, 0, pl.ds(0, 8)]
        weights = taps_of(small, k, i)
        for first in range(0, seg, BLOCK):
            value = shift_sum(dslot.at[i, 0], weights, first, BLOCK, 1)
            dpre[i, k, pl.ds(first, BLOCK)] = value.astype(BF)
            if first + BLOCK == seg:
                part[i, k] = value[BLOCK - 16 :]


def product(turned, pair, target):
    @pl.loop(0, 2)
    def _(y):
        for x in range(2):
            rows = pl.ds(pl.multiple_of(y * 256, 256) + x * 128, 128)
            target[y, x] = dot(turned[rows], pair[...]).astype(BF)


def gather_halves(links, own, everyone):
    z = links.z
    half = own.shape[0] // 2
    lines = []
    for i in range(2):
        rows = pl.ds(i * half, half)
        line = LineGather(
            links, ("rows", i), lambda k, rows=rows: everyone.at[z ^ k, rows], fixed=True
        )
        line.start([(lambda rows=rows: own.at[rows], lambda k, rows=rows: everyone.at[z, rows])])
        lines.append(line)
    return lines


def back_all_kernel(
    lengths, carry, small, dprior, gain, ffn_gain_grad,
    query_in, keyed_in, valued_in, lse_in, datt_in, dread_in, prior_in, pre_in, x_long_in, dmiddle_in,
    output, h_two, gffn, hidden, dgate, dup, h_long, gattn, mixed, weights, dzgate, q_own, k_own, v_own, g_own,
    all_output, part_ffn, small_grad, dpre, input_grad,
    peer_h_two, peer_gffn, peer_hidden, peer_dgate, peer_dup, peer_h, peer_gattn, peer_mixed, peer_dzgate,
    query, keyed, valued, lse, datt, dread, prior, pre, x_long, dmiddle,
    states, dwrite, dqkv, wide, dslot, part, halo, halo_in, ext, acc, wbuf, zbuf,
    staged, turned, pairs, blocks, first_in, second_in, landing,
    send, recv, sems_turned, sems_pairs, sems_weights, sem_own, sems_in,
):
    links = Links(send, recv)
    p, z = links.p, links.z
    seg = dmiddle.shape[0]
    loads = [
        pltpu.make_async_copy(source, target, sems_in.at[i])
        for i, (source, target) in enumerate(
            (
                (query_in, query), (keyed_in, keyed), (valued_in, valued), (lse_in, lse), (datt_in, datt),
                (dread_in, dread), (prior_in, prior), (pre_in, pre), (x_long_in, x_long), (dmiddle_in, dmiddle),
            )
        )
    ]
    length, start = lengths[z], p * seg
    states[p] = dprior[...]
    own_output = pltpu.make_async_copy(output, all_output.at[z], sem_own.at[0])
    own_output.start()
    links.greet()
    exchange = StateExchange(links, "states", lambda q: states.at[q])
    exchange.start()
    lines = gather_halves(links, output, all_output)
    h_one = h_long.at[pl.ds(ROWS, seg)]
    later = [("h", h_one, peer_h), ("gattn", gattn, peer_gattn), ("mixed", mixed, peer_mixed), ("dzgate", dzgate, peer_dzgate)]

    def to_peer(name, source, target):
        links.along_seq(source, target, ("peer", name), 1)

    def slot_to_peer(k):
        to_peer(("dgate", k), dgate.at[k], peer_dgate.at[k])
        to_peer(("dup", k), dup.at[k], peer_dup.at[k])
        if k == 3:
            to_peer("gffn", gffn, peer_gffn)
        to_peer(("hidden", k), hidden.at[k], peer_hidden.at[k])

    to_peer("h_two", h_two, peer_h_two)
    slot_to_peer(3)

    both = Pairs(pairs, sems_pairs)
    reduces = {
        k: PlaneReduce(links, ("plane", k), blocks.at[k - 1], first_in.at[k - 1], second_in.at[k - 1], k != 2)
        for k in (3, 2)
    }
    for name, mats, x_first in (("1a", pl.ds(0, 2), True), ("1b", pl.ds(2, 1), False)):
        reduces[name] = PlaneReduce(
            links, ("plane", name), blocks.at[0, mats], first_in.at[0, mats], second_in.at[0, mats], x_first
        )
    line_reduce = LineReduce(links, "sum", lambda k: blocks.at[k - 1, :, 0, 0], landing, None)
    sources = ((dgate, peer_dgate, "dgate", 0), (dup, peer_dup, "dup", 0), (hidden, peer_hidden, "hidden", 1))
    units = [(k, m) for k in (3, 2, 1) for m in range(3)]

    def fetch(n):
        k, m = units[n]
        own, peer, name, _ = sources[m]
        links.arrived(peer.at[k], ("peer", (name, k)))
        both.start(n % 2, own.at[k], peer.at[k])

    for copy in loads:
        copy.start()
    links.arrived(peer_h_two, ("peer", "h_two"))
    load_turned(links, h_two, peer_h_two, staged, turned.at[0], sems_turned)
    fetch(0)
    for n, (k, m) in enumerate(units):
        if n == 1:
            links.arrived(peer_gffn, ("peer", "gffn"))
            load_turned(links, gffn, peer_gffn, staged, turned.at[1], sems_turned)
        if m == 0:
            slot_to_peer(k - 1)
        if n + 1 < len(units):
            fetch(n + 1)
        own, peer, _, side = sources[m]
        both.wait(n % 2, own.at[k], peer.at[k])
        product(turned.at[side], pairs.at[n % 2], blocks.at[k - 1, m])
        if m == 2:
            if k > 1:
                reduces[k].start()
            if k == 3:
                exchange.step()
    for name, source, target in later:
        to_peer(name, source, target)
    exchange.end()
    lines[0].outward()
    lines[0].step(1)

    one = (query, keyed, valued, lse, datt, dread, prior, small, dqkv, small_grad)
    two = (pre, small, keyed, valued, dwrite, dqkv, dslot, small_grad, wide, dpre, part, halo)
    for k in range(4):
        for head in range(2):
            dwrite[k, head] = mixed_state(states, carry, k, head)

    def slots(first, count):
        @pl.loop(first, first + count)
        def _(k):
            attention_back_slot(k, one, length, start)
            conv_back(k, two, length, start)

    for copy in loads:
        copy.wait()
    slots(0, 2)
    lines[1].outward()
    lines[1].step(1)
    slots(2, 1)
    lines[0].step(2)
    reduces[3].step()
    reduces[2].step()
    reduces["1a"].start()
    reduces["1b"].start()
    slots(3, 1)

    @pl.when(p > 0)
    def _():
        links.copy(halo, halo_in, "halo", (p - 1, z)).start()

    halo_index = links.sent - 1

    def weight_copies(n):
        copies = [
            pltpu.make_async_copy(
                (q_own, k_own, v_own, g_own)[n] if n < 4 else weights.at[n // 4, n % 4],
                wbuf.at[n % 2], sems_weights.at[n % 2, 0],
            )
        ]
        if n % 4 == 3:
            copies.append(
                pltpu.make_async_copy(dzgate.at[n // 4], zbuf, sems_weights.at[n % 2, 1])
            )
        return copies

    for copy in weight_copies(0):
        copy.start()
    reduces[3].last()
    line_reduce.from_ends(3)
    reduces[2].last()
    line_reduce.from_ends(2)
    lines[1].step(2)

    @pl.when(p == 7)
    def _():
        halo_in[...] = jnp.zeros_like(halo_in)

    @pl.when(p < 7)
    def _():
        links.arrived(halo_in, "halo")

    ext[pl.ds(0, 16)] = jnp.zeros((16, ext.shape[1]), F32)
    for k in range(4):
        for i in range(3):
            ext[pl.ds(16, 8)] = halo_in[i, k]
            dpre[i, k, pl.ds(seg - 16, 16)] = (
                part[i, k] + shift_sum(ext, taps_of(small, k, i), 0, 16, 1)
            ).astype(BF)
        for i in range(4):
            n = 4 * k + i
            if n < 15:
                for copy in weight_copies(n + 1):
                    copy.start()
            for copy in weight_copies(n):
                copy.wait()

            @pl.loop(0, seg // 256)
            def _(c):
                rows = pl.ds(pl.multiple_of(c * 256, 256), 256)
                total = dot_t(zbuf[rows] if i == 3 else dpre[i, k, rows], wbuf[n % 2])
                if n == 0:
                    acc[rows] = total
                else:
                    acc[rows] += total

    reduces["1a"].step()
    reduces["1b"].step()
    gain_sum = jnp.zeros((1, acc.shape[1]), F32)
    for first in range(0, seg, BLOCK):
        rows = pl.ds(first, BLOCK)
        normed, inverse = norm_keep(x_long[pl.ds(ROWS + first, BLOCK)].astype(F32))
        grad = acc[rows]
        gain_sum = gain_sum + jnp.sum(grad * normed, axis=0, keepdims=True)
        input_grad[rows] = (
            dmiddle[rows] + norm_back(grad * gain[...], normed, inverse)
        ).astype(BF)
    for row, value in enumerate((gain_sum, ffn_gain_grad[...])):
        for i in range(4):
            at = GAINS + 4 * row + i
            for k in range(4):
                small_grad[k, at : at + 1] = value[:, i * 256 : (i + 1) * 256]
    for k in range(4):
        small_grad[k, TAPS + 3 * KW : GAINS] = jnp.zeros((GAINS - TAPS - 3 * KW, 256), F32)
    reduces["1a"].last()
    reduces["1b"].last()
    line_reduce.take(3)
    line_reduce.take(2)
    for k in (1, 2, 3):
        part_ffn[k - 1] = blocks[k - 1, :, 0, 0]
    lines[0].step(3)
    lines[1].step(3)
    for own, peer, name, _ in sources:
        links.arrived(peer.at[0], ("peer", (name, 0)))
    for name, _, target in later:
        links.arrived(target, ("peer", name))
    own_output.wait()

    @pl.when(p > 0)
    def _():
        links.gone(lambda: halo, halo_index)

    line_reduce.finish()
    links.finish()


def gradient_kernel(
    small, part_ffn,
    h_long, gattn, dpre, dzgate, mixed, input_grad, h_two, gffn, hidden, dgate, dup,
    peer_h_two, peer_gffn, peer_hidden, peer_dgate, peer_dup, peer_h, peer_gattn, peer_mixed, peer_dzgate,
    all_input_grad, g_attn, g_ffn, small_sum, peer_dpre,
    staged, turned, pairs, blocks, first_in, second_in, landing,
    pairs_ffn, blocks_ffn, first_ffn, second_ffn, landing_ffn, sums_ffn, small_in, small_part, small_all,
    send, recv, sems_turned, sems_pairs, sems_ffn, sem_own,
):
    links = Links(send, recv)
    p, z = links.p, links.z
    seg = gattn.shape[0]
    own_rows = pltpu.make_async_copy(input_grad, all_input_grad.at[z], sem_own.at[0])
    own_rows.start()
    sums_ffn[...] = part_ffn[...]
    links.greet()
    lines = gather_halves(links, input_grad, all_input_grad)
    order = (3, 2, 1, 0)
    for k in order:
        for i in range(3):
            links.along_seq(dpre.at[i, k], peer_dpre.at[i, k], ("dpre", i, k), 1)

    line_ffn = LineReduce(
        links, "ffn", lambda k: sums_ffn.at[k - 1] if k > 0 else blocks_ffn.at[:, 0, 0], landing_ffn, g_ffn
    )
    line_attn = LineReduce(links, "attn", lambda k: blocks.at[k, :, 0, 0], landing, g_attn)
    small_in[0] = small[0]
    for k in (1, 2, 3):
        links.copy(small.at[k], small_in.at[k], ("small", k), (p, z ^ k)).start()
        links.always.append((lambda k=k: small.at[k], links.sent - 1))

    ffn = PlaneReduce(links, "ffn0", blocks_ffn, first_ffn, second_ffn, False)
    attn = {
        k: PlaneReduce(links, ("attn", k), blocks.at[k], first_in.at[k], second_in.at[k], k != 2)
        for k in order
    }
    sources = ((dgate, peer_dgate, 0), (dup, peer_dup, 0), (hidden, peer_hidden, 1))
    both = Pairs(pairs_ffn, sems_ffn)
    refs_ffn = lambda m: tuple(ref.at[0] for ref in sources[m][:2])
    both.start(0, *refs_ffn(0))
    load_turned(links, h_two, peer_h_two, staged, turned.at[0], sems_turned)
    load_turned(links, gffn, peer_gffn, staged, turned.at[1], sems_turned)
    for m in range(3):
        if m < 2:
            both.start((m + 1) % 2, *refs_ffn(m + 1))
        both.wait(m % 2, *refs_ffn(m))
        product(turned.at[sources[m][2]], pairs_ffn.at[m % 2], blocks_ffn.at[m])
    sides = lambda k: [(dpre.at[m, k], peer_dpre.at[m, k]) for m in range(3)] + [
        (dzgate.at[k], peer_dzgate.at[k]), (mixed.at[k], peer_mixed.at[k])
    ]

    def attn_loads(k):
        return [
            pltpu.make_async_copy(ref, pairs.at[k % 2, m, pl.ds(side * seg, seg)], sems_pairs.at[k % 2, m, side])
            for m, both_sides in enumerate(sides(k))
            for side, ref in enumerate(both_sides)
        ]

    def fetch(k):
        for m in range(3):
            links.arrived(peer_dpre.at[m, k], ("dpre", m, k))
        for copy in attn_loads(k):
            copy.start()

    fetch(3)
    load_turned(links, h_long.at[pl.ds(ROWS, seg)], peer_h, staged, turned.at[0], sems_turned)
    load_turned(links, gattn, peer_gattn, staged, turned.at[1], sems_turned)
    for k in order:
        if k > 0:
            fetch(k - 1)
        for copy in attn_loads(k):
            copy.wait()
        for m in range(5):
            product(turned.at[m // 4], pairs.at[k % 2, m], blocks.at[k, m])
        if k > 1:
            attn[k].start()
        if k == 3:
            lines[0].outward()
            lines[0].step(1)
            line_ffn.across(3)
    for k in (1, 2, 3):
        links.arrived(small_in.at[k], ("small", k))
    small_part[...] = (small_in[0] + small_in[1]) + (small_in[2] + small_in[3])
    small_all[0] = small_part[...]
    for j in range(1, 8):
        links.along_seq(small_part, small_all.at[j], ("all", j), j)
    lines[1].outward()
    lines[1].step(1)
    line_ffn.across(2)
    line_ffn.from_ends(1)
    attn[3].step()
    attn[2].step()
    attn[1].start()
    ffn.start()
    lines[0].step(2)
    attn[3].last()
    line_attn.from_ends(3)
    attn[2].last()
    line_attn.from_ends(2)
    lines[1].step(2)
    attn[1].step()
    attn[0].start()
    ffn.step()
    attn[0].step()
    line_ffn.to_ends()
    line_attn.take(3)
    line_attn.across(3)
    line_attn.take(2)
    line_attn.across(2)
    attn[1].last()
    line_attn.from_ends(1)
    line_attn.to_ends()
    ffn.last()
    attn[0].last()
    line_ffn.last()
    lines[0].step(3)
    lines[1].step(3)
    line_attn.last()
    for j in range(1, 8):
        links.arrived(small_all.at[j], ("all", j))
    pair = lambda j: small_all[j] + small_all[j + 1]
    small_sum[...] = (pair(0) + pair(2)) + (pair(4) + pair(6))
    own_rows.wait()
    line_attn.finish()
    line_ffn.finish()
    links.finish()


def finish_kernel(
    attn, ffn, small, output_in, input_in,
    g_query, g_key, g_value, g_zgate, g_out, g_gate, g_up, g_down, taps, pers_k, pers_v, gains,
    output, input_grad, staged, sems_in, sems_out,
):
    pairs = ((output_in, output), (input_in, input_grad))
    count = output.shape[0]
    for side, (source, _) in enumerate(pairs):
        for s in range(count):
            pltpu.make_async_copy(source.at[s], staged.at[side, s], sems_in.at[side, s]).start()
    for i, ref in enumerate((g_query, g_key, g_value, g_zgate)):
        ref[...] = attn[i]
    g_out[...] = attn[4].T
    for i, ref in enumerate((g_gate, g_up, g_down)):
        for first in range(0, ref.shape[0], 128):
            wide = min(128, ref.shape[0] - first)
            ref[pl.ds(first, wide)] = ffn[i, :, pl.ds(first, wide)].T
    pers_k[...] = small[PERS_K : PERS_K + 16]
    pers_v[...] = small[PERS_V : PERS_V + 16]
    for i in range(3):
        taps[i] = small[TAPS + KW * i : TAPS + KW * (i + 1)]
    width = small.shape[1]
    for row in range(2):
        for i in range(4):
            at = GAINS + 4 * row + i
            gains[row : row + 1, i * width : (i + 1) * width] = small[at : at + 1]
    for side, (source, target) in enumerate(pairs):
        for s in range(count):
            pltpu.make_async_copy(source.at[s], staged.at[side, s], sems_in.at[side, s]).wait()
            pltpu.make_async_copy(staged.at[side, s], target.at[s], sems_out.at[side, s]).start()
    for side, (_, target) in enumerate(pairs):
        for s in range(count):
            pltpu.make_async_copy(staged.at[side, s], target.at[s], sems_out.at[side, s]).wait()


def local_fast(
    inputs, lengths, decays, norm_gain, query_proj, key_proj, value_proj, gate_proj, conv_taps,
    pers_keys, pers_values, out_proj, ffn_gain, ffn_gate, ffn_up, ffn_down, cotangent,
):
    seqs, seg, features = inputs.shape
    segments, shards = lax.axis_size("seq"), lax.axis_size("head")
    p, z = lax.axis_index("seq"), lax.axis_index("head")
    width, hidden_width = query_proj.shape[1], ffn_gate.shape[1]
    heads_here = width // DH
    heads = heads_here * shards
    persistent = pers_keys.shape[0]

    turn = (jnp.arange(shards)[:, None] == (z ^ jnp.arange(shards))[None, :]).astype(F32)
    mine = lax.dynamic_index_in_dim(decays, z, 1, False)[:, 0].reshape(2, shards, 1, heads_here)
    mine = jnp.sum(mine * turn[None, :, :, None], axis=1).reshape(2, heads)
    mine = jnp.pad(mine, ((0, 6), (0, 128 - heads)))
    own_small = jnp.concatenate(
        [pers_keys, pers_values, conv_taps.reshape(3 * KW, width), jnp.zeros((4, width), BF)]
    ).astype(F32)
    gain, ffn_gain = norm_gain[None], ffn_gain[None]
    low = lambda *shape: SHAPE(shape, BF)
    full = lambda *shape: SHAPE(shape, F32)
    rows_low = low(shards, seg, width)
    state = low(shards, heads_here, DH, DH)
    hid = low(shards, seg, hidden_width)
    flat = low(seg, features)
    anywhere = pl.BlockSpec(memory_space=pl.ANY)
    in_vmem = pl.BlockSpec(memory_space=pltpu.VMEM)
    in_smem = pl.BlockSpec(memory_space=pltpu.SMEM)
    vmem_low = lambda *shape: pltpu.VMEM(shape, BF)
    vmem_full = lambda *shape: pltpu.VMEM(shape, F32)
    dma = pltpu.SemaphoreType.DMA
    block = features // 8
    halo_rows, pre_rows = low(seg + ROWS, features), low(3, shards, seg + ROWS, width)
    scores_total, middle_rows = full(shards, heads_here, seg, 1), full(seg, features)
    kept = [
        halo_rows, halo_rows, pre_rows, rows_low, rows_low, rows_low, scores_total, state, rows_low, flat, flat,
        flat, middle_rows, flat, rows_low, rows_low, rows_low,
    ]
    held = lambda shapes: [pltpu.VMEM(shape.shape, shape.dtype) for shape in shapes]
    (
        small, carry_back, dprior, g_ffn_gain,
        x_long, h_long, pre, query, keyed, valued, lse, prior, mixed, h_two, gffn,
        output, dmiddle, gattn, datt, dzgate, dread,
        weights, hidden, dgate, dup, *_,
    ) = pl.pallas_call(
        front_kernel,
        out_shape=[full(shards, GAINS, width), full(segments, 128), state, full(1, features)]
        + kept
        + [
            low(shards, 4, features, width), hid, hid, hid, low(shards, width, features),
            low(shards, 2, hidden_width, features), low(shards, hidden_width, features),
        ],
        in_specs=[in_smem] + [in_vmem] * 4 + [anywhere] * 10,
        out_specs=[in_vmem] * 4 + [anywhere] * (len(kept) + 7),
        scratch_shapes=held(kept) + [
            vmem_low(seg, features), vmem_full(shards, seg, width), vmem_full(shards, seg, width),
            vmem_full(3, seg + ROWS, width), vmem_low(segments, shards, heads_here, DH, DH),
            vmem_full(segments, 8, 128), vmem_full(segments, 128), vmem_low(4, features, width),
            vmem_low(shards, width, features), vmem_low(2, 2, hidden_width, features),
            vmem_low(2, hidden_width, features), vmem_low(2, 3, seg, hidden_width),
            vmem_full(seg, features), vmem_full(seg, features),
            dma((192,)), dma((192,)), dma((2,)), dma((4,)), dma((4,)), dma((2, 3)), dma((2, 3)),
            dma((11,)), dma((3,)), dma((4, 3)),
        ],
        compiler_params=pltpu.CompilerParams(
            collective_id=0, has_side_effects=True, vmem_limit_bytes=VMEM_LIMIT
        ),
    )(
        lengths, gain, ffn_gain, own_small, mine, inputs, cotangent,
        query_proj, key_proj, value_proj, gate_proj, out_proj, ffn_gate.T, ffn_up.T, ffn_down,
    )
    output, part_ffn, small_grad, dpre, input_grad, *peers = pl.pallas_call(
        back_all_kernel,
        out_shape=[
            low(shards, seg, features), low(3, 3, block, hidden_width), full(shards, SMALL, width),
            low(3, shards, seg, width), flat, flat, flat, hid, hid, hid, flat, flat, rows_low, rows_low,
        ],
        in_specs=[in_smem] + [in_vmem] * 5 + [anywhere] * 25,
        out_specs=[anywhere] + [in_vmem] * 4 + [anywhere] * 9,
        scratch_shapes=held(
            [rows_low] * 3 + [scores_total, rows_low, rows_low, state, pre_rows, halo_rows, middle_rows]
        ) + [
            vmem_low(8, shards, heads_here, DH, DH), vmem_low(shards, heads_here, DH, DH),
            vmem_full(3, seg, width), vmem_full(3, seg + ROWS, width), vmem_full(3, 1, seg + 8, width),
            vmem_full(3, shards, 16, width), vmem_full(3, shards, 8, width), vmem_full(3, shards, 8, width),
            vmem_full(24, width), vmem_full(seg, features), vmem_low(2, features, width),
            vmem_low(seg, width),
            vmem_low(2 * seg, features // 2), vmem_low(2, features // 2, 2 * seg),
            vmem_low(2, 2 * seg, hidden_width), vmem_low(3, 3, 2, 2, block, hidden_width),
            vmem_low(3, 3, 2, block, hidden_width), vmem_low(3, 3, block, hidden_width),
            vmem_low(2, 3, block, hidden_width),
            dma((64,)), dma((64,)), dma((4, 2)), dma((2, 2)), dma((2, 2)), dma((1,)), dma((10,)),
        ],
        compiler_params=pltpu.CompilerParams(
            collective_id=1, has_side_effects=True, vmem_limit_bytes=VMEM_LIMIT
        ),
    )(
        lengths, carry_back, small, dprior, gain, g_ffn_gain,
        query, keyed, valued, lse, datt, dread, prior, pre, x_long, dmiddle,
        output, h_two, gffn, hidden, dgate, dup, h_long, gattn, mixed, weights, dzgate,
        query_proj, key_proj, value_proj, gate_proj,
    )
    input_grad, g_attn, g_ffn, small, *_ = pl.pallas_call(
        gradient_kernel,
        out_shape=[
            low(shards, seg, features), full(5, block, width), full(3, block, hidden_width), full(SMALL, width),
            low(3, shards, seg, width),
        ],
        in_specs=[in_vmem] * 2 + [anywhere] * 20,
        out_specs=[anywhere] + [in_vmem] * 3 + [anywhere],
        scratch_shapes=[
            vmem_low(2 * seg, features // 2), vmem_low(2, features // 2, 2 * seg),
            vmem_low(2, 5, 2 * seg, width), vmem_low(4, 5, 2, 2, block, width), vmem_low(4, 5, 2, block, width),
            vmem_low(4, 5, block, width), vmem_low(6, 5, block, width),
            vmem_low(2, 2 * seg, hidden_width), vmem_low(3, 2, 2, block, hidden_width),
            vmem_low(3, 2, block, hidden_width), vmem_low(3, block, hidden_width),
            vmem_low(6, 3, block, hidden_width), vmem_low(3, 3, block, hidden_width),
            vmem_full(shards, SMALL, width), vmem_full(SMALL, width), vmem_full(8, SMALL, width),
            dma((96,)), dma((96,)), dma((4, 2)), dma((2, 5, 2)), dma((2, 2)), dma((1,)),
        ],
        compiler_params=pltpu.CompilerParams(
            collective_id=2, has_side_effects=True, vmem_limit_bytes=VMEM_LIMIT
        ),
    )(
        small_grad, part_ffn, h_long, gattn, dpre, dzgate, mixed, input_grad, h_two, gffn, hidden, dgate, dup, *peers,
    )
    (
        g_query, g_key, g_value, g_zgate, g_out, g_gate, g_up, g_down, g_taps, g_pers_k, g_pers_v, gains,
        output, input_grad,
    ) = pl.pallas_call(
        finish_kernel,
        out_shape=[full(block, width)] * 4
        + [full(width, block)]
        + [full(hidden_width, block)] * 3
        + [full(3, KW, width), full(persistent, width), full(persistent, width), full(2, features)]
        + [low(shards, seg, features)] * 2,
        in_specs=[in_vmem] * 3 + [anywhere] * 2,
        out_specs=[in_vmem] * 12 + [anywhere] * 2,
        scratch_shapes=[vmem_low(2, shards, seg, features), dma((2, 4)), dma((2, 4))],
        compiler_params=pltpu.CompilerParams(vmem_limit_bytes=VMEM_LIMIT),
    )(g_attn, g_ffn, small, output, input_grad)
    return (
        output, input_grad, gains[0], g_query, g_key, g_value, g_zgate, g_taps, g_pers_k, g_pers_v,
        g_out, gains[1], g_gate.T, g_up.T, g_down,
    )


def local(*args):
    return local_fast(*args) if custom_mesh() else local_plain(*args)


def solution(mesh):
    in_specs = (
        P(None, "seq", None),
        P(),
        P(None, None, "seq", None),
        P(),
        P(None, "head"),
        P(None, "head"),
        P(None, "head"),
        P(None, "head"),
        P(None, None, "head"),
        P(None, "head"),
        P(None, "head"),
        P("head", None),
        P(),
        P(None, "head"),
        P(None, "head"),
        P("head", None),
        P(None, "seq", None),
    )
    out_specs = (
        P(None, "seq", None),
        P(None, "seq", None),
        P(),
        P("seq", "head"),
        P("seq", "head"),
        P("seq", "head"),
        P("seq", "head"),
        P(None, None, "head"),
        P(None, "head"),
        P(None, "head"),
        P("head", "seq"),
        P(),
        P("seq", "head"),
        P("seq", "head"),
        P("head", "seq"),
    )
    return jax.shard_map(local, mesh=mesh, in_specs=in_specs, out_specs=out_specs, check_vma=False)
```

```python
import functools

import jax
import jax.numpy as jnp
from jax import lax
from jax.experimental import pallas as pl
from jax.experimental.pallas import tpu as pltpu
from jax.sharding import PartitionSpec as P

DH = 128
KW = 4
HALO = 8
EPSILON = 1e-06
BF = jnp.bfloat16
F32 = jnp.float32


def custom_mesh():
    return lax.axis_size("seq") == 8 and lax.axis_size("head") == 4


def along_seq(value, flip):
    return lax.ppermute(value, "seq", [(i, i ^ flip) for i in range(8)])


def along_head(value, pairs):
    return lax.ppermute(value, "head", pairs)


def slot_owner(k):
    return lax.axis_index("head") ^ k if custom_mesh() else k


def gather_head(value):
    z = lax.axis_index("head")
    middle = (z == 1) | (z == 2)
    one = along_head(value, [(0, 1), (1, 0), (2, 3), (3, 2)])
    inner = along_head(value, [(1, 2), (2, 1)])
    two_inner = along_head(one, [(1, 2), (2, 1)])
    two_outer = along_head(inner, [(2, 3), (1, 0)])
    three_outer = along_head(two_inner, [(2, 3), (1, 0)])
    two = jnp.where(middle, two_inner, two_outer)
    three = jnp.where(middle, inner, three_outer)
    return [value, one, two, three]


def gather_plane(value, x_first):
    near, far = (2, 4) if x_first else (4, 2)
    pieces = {0: value, near: along_seq(value, near), far: along_seq(value, far)}
    pieces[6] = along_seq(pieces[near], far)
    for j in (0, 2, 4, 6):
        pieces[j + 1] = along_seq(pieces[j], 1)
    return [pieces[j] for j in range(8)]


def gather_weights(own):
    if not custom_mesh():
        whole = lax.all_gather(own, "head")
        return [whole[k] for k in range(lax.axis_size("head"))]
    p = lax.axis_index("seq")
    matrices, depth, width = own.shape
    block = depth // 8
    mine = lax.dynamic_slice_in_dim(own, p * block, block, 1)
    slots = [own]
    for k, piece in enumerate(gather_head(mine)[1:]):
        if k < 2:
            parts = gather_plane(piece, k == 0)
        else:
            half = block // 2
            upper = gather_plane(piece[:, :half], True)
            lower = gather_plane(piece[:, half:], False)
            parts = [jnp.concatenate([u, v], axis=1) for u, v in zip(upper, lower)]
        full = jnp.zeros((matrices, depth, width), own.dtype)
        for j, part in enumerate(parts):
            full = lax.dynamic_update_slice_in_dim(full, part, (p ^ j) * block, 1)
        slots.append(full)
    return slots


def gather_small(own):
    if not custom_mesh():
        whole = lax.all_gather(own, "head")
        return [whole[k] for k in range(lax.axis_size("head"))]
    return [own] + [along_head(own, [(i, i ^ k) for i in range(4)]) for k in (1, 2, 3)]


def gather_states(value):
    p = lax.axis_index("seq")
    if not custom_mesh():
        whole = lax.all_gather(value, "seq")
        count = lax.axis_size("seq")
        return [whole[i] for i in range(count)], list(range(count))
    half = value.shape[0] // 2
    upper = gather_plane(value[:half], True)
    lower = gather_plane(value[half:], False)
    pieces = [jnp.concatenate([u, v]) for u, v in zip(upper, lower)]
    return pieces, [p ^ j for j in range(8)]


def gather_rows(own):
    if not custom_mesh():
        return lax.all_gather(own, "head")
    z = lax.axis_index("head")
    full = jnp.zeros((4,) + own.shape, own.dtype)
    for k, slot in enumerate(gather_head(own)):
        full = lax.dynamic_update_slice_in_dim(full, slot[None], z ^ k, 0)
    return full


def weight_grads(pairs, x_first):
    dot = lambda a, b: lax.dot_general(a, b, (((0,), (0,)), ((), ())), preferred_element_type=F32)
    if not custom_mesh():
        out = []
        for a, b in pairs:
            full = jnp.stack([dot(a, one) for one in b]).astype(BF)
            part = lax.psum_scatter(full, "head", scatter_dimension=0, tiled=True)[0]
            out.append(lax.psum_scatter(part, "seq", scatter_dimension=0, tiled=True).astype(F32))
        return out
    p, z = lax.axis_index("seq"), lax.axis_index("head")
    block = pairs[0][0].shape[1] // 8
    stacks = [[] for _ in range(4)]
    for a, b in pairs:
        cut = lambda j: lax.dynamic_slice_in_dim(a, (p ^ j) * block, block, 1)
        even = jnp.concatenate([cut(j) for j in (0, 2, 4, 6)], axis=1)
        odd = jnp.concatenate([cut(j) for j in (1, 3, 5, 7)], axis=1)
        peer_a = along_seq(odd, 1)
        for k in range(4):
            peer_b = along_seq(b[k], 1)
            stacks[k].append(
                (dot(even, b[k]) + dot(peer_a, peer_b)).astype(BF).reshape(4, block, -1)
            )
    near, far = (2, 4) if x_first else (4, 2)
    slots = []
    for k in range(4):
        g = jnp.stack(stacks[k])
        y_zero, y_one = g[:, :2], g[:, 2:]
        if x_first:
            keep = jnp.stack([g[:, 0], g[:, 2]], 1)
            away = jnp.stack([g[:, 1], g[:, 3]], 1)
        else:
            keep, away = y_zero, y_one
        summed = (keep.astype(F32) + along_seq(away, near).astype(F32)).astype(BF)
        slots.append(
            (summed[:, 0].astype(F32) + along_seq(summed[:, 1], far).astype(F32)).astype(BF)
        )
    return list(reduce_head(slots))


def add(a, b):
    return (a.astype(F32) + b.astype(F32)).astype(BF)


def reduce_head(slots):
    outer, inner, back = [(0, 1), (3, 2)], [(1, 2), (2, 1)], [(2, 3), (1, 0)]
    own, one, two, three = slots
    far = add(two, along_head(three, outer))
    far = add(one, along_head(far, inner))
    far = along_head(far, back)
    mid = add(three, along_head(two, outer))
    mid = along_head(mid, inner)
    near = along_head(one, outer)
    return own.astype(F32) + far.astype(F32) + mid.astype(F32) + near.astype(F32)


def sum_small(slots, gains):
    if not custom_mesh():
        part = lax.psum_scatter(jnp.stack(slots), "head", scatter_dimension=0, tiled=True)[0]
        return lax.psum(part, "seq"), lax.psum(gains, ("seq", "head"))
    part = slots[0]
    for k in (1, 2, 3):
        part = part + along_head(slots[k], [(i, i ^ k) for i in range(4)])
    for k in (1, 2):
        gains = gains + along_head(gains, [(i, i ^ k) for i in range(4)])
    count = part.shape[0]
    total = jnp.concatenate([part, gains])
    for flip in (1, 2, 4):
        total = total + along_seq(total, flip)
    return total[:count], total[count:]


def norm_keep(values):
    inverse = lax.rsqrt(jnp.mean(values * values, axis=-1, keepdims=True) + EPSILON)
    return (values * inverse, inverse)


def norm_back(grad, normed, inverse):
    return inverse * (grad - normed * jnp.mean(grad * normed, axis=-1, keepdims=True))


def silu_slope(values):
    sigma = jax.nn.sigmoid(values)
    return sigma * (1.0 + values * (1.0 - sigma))


def carry_coefficients(alpha, eta):
    count, heads = alpha.shape
    place = jnp.arange(count)[:, None]
    mem = jnp.zeros((count, heads), F32)
    mom = jnp.zeros((count, heads), F32)
    rows = []
    for c in range(count):
        rows.append(mem)
        mom = eta[c] * mom + (place == c).astype(F32)
        mem = alpha[c] * mem + mom
    return jnp.stack(rows)


def dot(a, b):
    return jnp.dot(a, b, preferred_element_type=F32)


def dot_t(a, b):
    return lax.dot_general(a, b, (((1,), (1,)), ((), ())), preferred_element_type=F32)


def local_plain(
    inputs,
    lengths,
    decays,
    norm_gain,
    query_proj,
    key_proj,
    value_proj,
    gate_proj,
    conv_taps,
    pers_keys,
    pers_values,
    out_proj,
    ffn_gain,
    ffn_gate,
    ffn_up,
    ffn_down,
    cotangent,
):
    seqs, seg, features = inputs.shape
    segments = lax.axis_size("seq")
    shards = lax.axis_size("head")
    p, z = lax.axis_index("seq"), lax.axis_index("head")
    width = query_proj.shape[1]
    heads_here = width // DH
    heads = heads_here * shards
    rim = KW - 1
    persistent = pers_keys.shape[0]

    attn_slots = gather_weights(jnp.stack([query_proj, key_proj, value_proj, gate_proj, out_proj.T]))
    ffn_slots = gather_weights(jnp.stack([ffn_gate, ffn_up, ffn_down.T]))
    small = gather_small(
        jnp.concatenate([conv_taps.reshape(3 * KW, width), pers_keys, pers_values])
    )
    small = jnp.concatenate(small, axis=1)
    taps = small[: 3 * KW].reshape(3, KW, heads * DH).astype(F32)
    pers_k = small[3 * KW : 3 * KW + persistent].reshape(persistent, heads, DH)
    pers_v = small[3 * KW + persistent :].reshape(persistent, heads, DH)
    q_mat, k_mat, v_mat, g_mat, o_mat = [
        jnp.concatenate([slot[i] for slot in attn_slots], axis=1) for i in range(5)
    ]

    mine = lax.dynamic_index_in_dim(decays, z, 1, False)[:, 0]
    mine = jnp.concatenate(
        [lax.dynamic_slice_in_dim(mine, slot_owner(k) * heads_here, heads_here, 1) for k in range(shards)],
        axis=1,
    )
    every = lax.all_gather(mine, "seq")
    carry = carry_coefficients(every[:, 0], every[:, 1])

    x = lax.dynamic_index_in_dim(inputs, z, 0, False).astype(F32)
    cot = lax.dynamic_index_in_dim(cotangent, z, 0, False).astype(F32)
    length = lax.dynamic_index_in_dim(lengths, z, 0, False)
    live = ((p * seg + jnp.arange(seg, dtype=jnp.int32)) < length).astype(F32)
    live_two = live[:, None]
    tail = lax.dynamic_index_in_dim(inputs, z, 0, False)[seg - HALO :]
    before = lax.ppermute(tail, "seq", [(i, i + 1) for i in range(segments - 1)]).astype(F32)
    x_long = jnp.concatenate([before, x])
    n_long, inv_long = norm_keep(x_long)
    h_long = (n_long * norm_gain).astype(BF)
    n_one, inv_one, h_one = n_long[HALO:], inv_long[HALO:], h_long[HALO:]

    pre = jnp.stack([dot(h_long, m) for m in (q_mat, k_mat, v_mat)]).astype(BF)
    zgate = dot(h_one, g_mat)
    wide_pre = pre.astype(F32)
    conv_sum = sum(
        taps[:, lag][:, None, :] * wide_pre[:, HALO - lag : HALO - lag + seg] for lag in range(KW)
    )
    acts = jax.nn.silu(conv_sum).reshape(3, seg, heads, DH)
    q_normed, q_inverse = norm_keep(acts[0])
    k_normed, k_inverse = norm_keep(acts[1])
    query, keyed, valued = q_normed.astype(BF), k_normed.astype(BF), acts[2].astype(BF)
    live_three = live[:, None, None]
    masked_value = valued * live_three.astype(BF)
    write = jnp.einsum("tha,thb->hab", masked_value, keyed, preferred_element_type=F32) / seg

    def mix_states(values, coefficients):
        pieces, places = gather_states(values.astype(BF))
        total = 0.0
        for piece, place in zip(pieces, places):
            coefficient = lax.dynamic_index_in_dim(coefficients, place, 0, False)
            total = total + coefficient[:, None, None] * piece.astype(F32)
        return total.astype(BF)

    prior = mix_states(write, lax.dynamic_index_in_dim(carry, p, 0, False))
    raw_read = jnp.einsum("hab,thb->tha", prior, query, preferred_element_type=F32)
    readout, read_inverse = norm_keep(raw_read)

    keys_all = jnp.concatenate([pers_k, keyed])
    values_all = jnp.concatenate([pers_v, valued])
    valid = jnp.concatenate([jnp.ones((persistent,), F32), live])
    rows_index = jnp.arange(seg)[:, None]
    column = jnp.arange(persistent + seg)[None, :] - persistent
    allowed = (column < 0) | (column <= rows_index) & (valid[None, :] > 0.5)
    scale = DH ** (-0.5)
    score = jnp.einsum("thd,uhd->htu", query, keys_all, preferred_element_type=F32) * scale
    score = jnp.where(allowed[None], score, -1e30)
    top = jnp.max(score, axis=-1, keepdims=True)
    log_total = top + jnp.log(jnp.sum(jnp.exp(score - top), axis=-1, keepdims=True))
    prob = jnp.exp(score - log_total)
    prob_low = prob.astype(BF)
    attended = jnp.einsum("htu,uhd->thd", prob_low, values_all, preferred_element_type=F32)

    sigma = jax.nn.sigmoid(zgate)
    read_flat = readout.reshape(seg, -1)
    mixed = (attended.reshape(seg, -1) + sigma * read_flat).astype(BF)
    middle = x + live_two * dot_t(mixed, o_mat)
    n_two, inv_two = norm_keep(middle)
    h_two = (n_two * ffn_gain).astype(BF)

    gffn = (live_two * cot).astype(BF)
    ffn_out = 0.0
    dh_two = 0.0
    hidden_slots, gate_slots, up_slots = [], [], []
    for slot in ffn_slots:
        gate_value = dot(h_two, slot[0])
        up_value = dot(h_two, slot[1])
        silu_gate = jax.nn.silu(gate_value)
        hidden = (silu_gate * up_value).astype(BF)
        ffn_out = ffn_out + dot_t(hidden, slot[2])
        dhidden = dot(gffn, slot[2])
        dgate = (dhidden * up_value * silu_slope(gate_value)).astype(BF)
        dup = (dhidden * silu_gate).astype(BF)
        dh_two = dh_two + dot_t(dgate, slot[0]) + dot_t(dup, slot[1])
        hidden_slots.append(hidden)
        gate_slots.append(dgate)
        up_slots.append(dup)
    output = gather_rows((middle + live_two * ffn_out).astype(BF))
    g_gate, g_up, g_down = weight_grads(
        [(h_two, gate_slots), (h_two, up_slots), (gffn, hidden_slots)], True
    )

    grad_ffn_gain = jnp.sum(dh_two * n_two, axis=0)
    dmiddle = cot + norm_back(dh_two * ffn_gain, n_two, inv_two)
    gattn = (live_two * dmiddle).astype(BF)
    dmixed = dot(gattn, o_mat)
    datt = dmixed.astype(BF).reshape(seg, heads, DH)
    dzgate = (dmixed * read_flat * sigma * (1.0 - sigma)).astype(BF)
    dread = norm_back((dmixed * sigma).reshape(seg, heads, DH), readout, read_inverse).astype(BF)
    dprior = jnp.einsum("tha,thb->hab", dread, query, preferred_element_type=F32)
    dwrite = mix_states(dprior, lax.dynamic_index_in_dim(carry, p, 1, False))
    dquery_mem = jnp.einsum("hab,tha->thb", prior, dread, preferred_element_type=F32)
    dprob = jnp.einsum("thd,uhd->htu", datt, values_all, preferred_element_type=F32)
    row_dot = jnp.sum(prob * dprob, axis=-1, keepdims=True)
    dscore = (prob * (dprob - row_dot)).astype(BF)
    dquery = (
        jnp.einsum("htu,uhd->thd", dscore, keys_all, preferred_element_type=F32) * scale
        + dquery_mem
    )
    dkeys = jnp.einsum("htu,thd->uhd", dscore, query, preferred_element_type=F32) * scale
    dvalues = jnp.einsum("htu,thd->uhd", prob_low, datt, preferred_element_type=F32)
    dvals = (
        dvalues[persistent:]
        + live_three * jnp.einsum("hab,thb->tha", dwrite, keyed, preferred_element_type=F32) / seg
    )
    dkey = (
        dkeys[persistent:]
        + jnp.einsum("hab,tha->thb", dwrite, masked_value, preferred_element_type=F32) / seg
    )
    dact = jnp.stack(
        [norm_back(dquery, q_normed, q_inverse), norm_back(dkey, k_normed, k_inverse), dvals]
    ).reshape(3, seg, -1)
    dconv = dact * silu_slope(conv_sum)
    longer = jnp.pad(dconv, ((0, 0), (rim, rim), (0, 0)))
    spread = sum(
        taps[:, lag][:, None, :] * longer[:, lag : lag + seg + rim] for lag in range(KW)
    )
    grad_conv = jnp.stack(
        [
            jnp.sum(dconv * wide_pre[:, HALO - lag : HALO - lag + seg], axis=1)
            for lag in range(KW)
        ],
        axis=1,
    )
    back = lax.ppermute(
        spread[:, :rim].astype(BF), "seq", [(i + 1, i) for i in range(segments - 1)]
    ).astype(F32)
    dpre = spread[:, rim:] + jnp.pad(back, ((0, 0), (seg - rim, 0), (0, 0)))
    dpre = dpre.astype(BF)

    dh_one = (
        dot_t(dpre[0], q_mat) + dot_t(dpre[1], k_mat) + dot_t(dpre[2], v_mat) + dot_t(dzgate, g_mat)
    )
    grad_norm_gain = jnp.sum(dh_one * n_one, axis=0)
    input_grad = gather_rows(
        (dmiddle + norm_back(dh_one * norm_gain, n_one, inv_one)).astype(BF)
    )

    def by_slot(value):
        return [value[..., k * width : (k + 1) * width] for k in range(shards)]

    g_query, g_key, g_value, g_zgate, g_out = weight_grads(
        [(h_one, by_slot(d)) for d in (dpre[0], dpre[1], dpre[2], dzgate)]
        + [(gattn, by_slot(mixed))],
        False,
    )
    rows = jnp.concatenate(
        [
            grad_conv.reshape(3 * KW, -1),
            dkeys[:persistent].reshape(persistent, -1),
            dvalues[:persistent].reshape(persistent, -1),
        ]
    )
    gains = jnp.concatenate([grad_norm_gain, grad_ffn_gain]).reshape(-1, width)
    rows, gains = sum_small(by_slot(rows), gains)
    gains = gains.reshape(2, features)
    return (
        output,
        input_grad,
        gains[0],
        g_query,
        g_key,
        g_value,
        g_zgate,
        rows[: 3 * KW].reshape(3, KW, width),
        rows[3 * KW : 3 * KW + persistent],
        rows[3 * KW + persistent :],
        g_out.T,
        gains[1],
        g_gate,
        g_up,
        g_down.T,
    )


ROWS = 16
BLOCK = 128
SCALE = DH ** (-0.5)


def shift_sum(source, taps, first, rows, step):
    total = taps[0:1] * source[pl.ds(first, rows)]
    for lag in range(1, KW):
        total = total + taps[lag : lag + 1] * source[pl.ds(first + step * lag, rows)]
    return total


def live_rows(first, rows, length, segment_start):
    place = segment_start + first + lax.broadcasted_iota(jnp.int32, (rows, 1), 0)
    return (place < length).astype(F32)


def live_columns(columns, length, segment_start):
    return segment_start + lax.broadcasted_iota(jnp.int32, (1, columns), 1) < length


def masked_scores(query, keys, pers_k, index, columns_live):
    width = keys.shape[0]
    raw = dot_t(query, keys) * SCALE
    row = index * BLOCK + lax.broadcasted_iota(jnp.int32, (BLOCK, width), 0)
    column = lax.broadcasted_iota(jnp.int32, (BLOCK, width), 1)
    keep = (column <= row) & columns_live[:, :width]
    return jnp.where(keep, raw, -1e30), dot_t(query, pers_k) * SCALE


def attention_back_slot(k, refs, length, segment_start):
    query, keyed, valued, lse, datt, dread, prior, small, dqkv, small_grad = refs
    seg = query.shape[1]
    columns_live = live_columns(seg, length, segment_start)
    turn = lambda a, b: lax.dot_general(a, b, (((0,), (0,)), ((), ())), preferred_element_type=F32)
    for head in range(query.shape[2] // DH):
        lanes = slice(head * DH, (head + 1) * DH)
        pers_keys_sum = jnp.zeros((16, DH), F32)
        pers_values_sum = jnp.zeros((16, DH), F32)
        pk = small[k, PERS_K : PERS_K + 16, lanes].astype(BF)
        pv = small[k, PERS_V : PERS_V + 16, lanes].astype(BF)
        dqkv[1, :, lanes] = jnp.zeros((seg, DH), F32)
        dqkv[2, :, lanes] = jnp.zeros((seg, DH), F32)
        dqkv[0, :, lanes] = dot(dread[k, :, lanes], prior[k, head])
        for index in range(seg // BLOCK):
            rows = pl.ds(index * BLOCK, BLOCK)
            upto = pl.ds(0, (index + 1) * BLOCK)
            q, d = query[k, rows, lanes], datt[k, rows, lanes]
            keys = keyed[k, upto, lanes]
            score, pers = masked_scores(q, keys, pk, index, columns_live)
            log_total = lse[k, head, rows]
            prob, prob_p = jnp.exp(score - log_total), jnp.exp(pers - log_total)
            grad = dot_t(d, valued[k, upto, lanes])
            grad_p = dot_t(d, pv)
            row_dot = jnp.sum(prob * grad, axis=-1, keepdims=True) + jnp.sum(
                prob_p * grad_p, axis=-1, keepdims=True
            )
            dscore = (prob * (grad - row_dot)).astype(BF)
            dscore_p = (prob_p * (grad_p - row_dot)).astype(BF)
            dqkv[0, rows, lanes] += (dot(dscore, keys) + dot(dscore_p, pk)) * SCALE
            dqkv[1, upto, lanes] += turn(dscore, q) * SCALE
            dqkv[2, upto, lanes] += turn(prob.astype(BF), d)
            pers_keys_sum = pers_keys_sum + turn(dscore_p, q)
            pers_values_sum = pers_values_sum + turn(prob_p.astype(BF), d)
        small_grad[k, PERS_K : PERS_K + 16, lanes] = pers_keys_sum * SCALE
        small_grad[k, PERS_V : PERS_V + 16, lanes] = pers_values_sum


def conv_back_slot(k, refs, length, segment_start):
    pre, small, keyed, valued, dwrite, dqkv, dconv, small_grad, wide = refs
    seg = keyed.shape[1]
    heads = keyed.shape[2] // DH
    for i in range(3):
        wide[i] = pre[i, k].astype(F32)
    sums = [[jnp.zeros((1, heads * DH), F32) for _ in range(KW)] for _ in range(3)]
    for first in range(0, seg, BLOCK):
        rows = pl.ds(first, BLOCK)
        live = live_rows(first, BLOCK, length, segment_start)
        for i in range(3):
            conv = shift_sum(wide.at[i], taps_of(small, k, i), ROWS + first, BLOCK, -1)
            sigma = jax.nn.sigmoid(conv)
            act = conv * sigma
            parts = []
            for head in range(heads):
                lanes = slice(head * DH, (head + 1) * DH)
                grad = dqkv[i, rows, lanes]
                if i == 1:
                    masked = valued[k, rows, lanes] * live.astype(BF)
                    grad = grad + dot(masked, dwrite[k, head]) / seg
                if i == 2:
                    grad = grad + live * dot_t(keyed[k, rows, lanes], dwrite[k, head]) / seg
                else:
                    grad = norm_back(grad, *norm_keep(act[:, lanes]))
                parts.append(grad)
            result = jnp.concatenate(parts, axis=1) * (sigma * (1.0 + conv * (1.0 - sigma)))
            dconv[i, 0, rows] = result
            for lag in range(KW):
                sums[i][lag] = sums[i][lag] + jnp.sum(
                    result * wide[i, pl.ds(ROWS + first - lag, BLOCK)], axis=0, keepdims=True
                )
    for i in range(3):
        for lag in range(KW):
            row = TAPS + KW * i + lag
            small_grad[k, row : row + 1] = sums[i][lag]


SHAPE = jax.ShapeDtypeStruct
VMEM_LIMIT = 127 * 512 * 1024


MESH = pl.DeviceIdType.MESH
SKEW_ONE, SKEW_TWO = 2, 4
WINDOW = 4
UNITS = (
    ("proj", 1), ("proj", 2), ("proj", 3), ("ffn", 1), ("out", 1), ("out", 2), ("out", 3), ("down", 1),
    ("ffn", 2), ("down", 2), ("ffn", 3), ("down", 3),
)


class Links:
    def __init__(self, send, recv):
        self.send, self.recv = send, recv
        self.sent = 0
        self.names = {}
        self.always, self.middles = [], []
        self.p, self.z = lax.axis_index("seq"), lax.axis_index("head")
        self.middle = (self.z == 1) | (self.z == 2)

    def greet(self):
        barrier = pltpu.get_barrier_semaphore()
        for flip in range(1, 8):
            pl.semaphore_signal(barrier, device_id=(self.p ^ flip, self.z), device_id_type=MESH)
        for flip in (1, 2, 3):
            pl.semaphore_signal(barrier, device_id=(self.p, self.z ^ flip), device_id_type=MESH)
        pl.semaphore_wait(barrier, 10)

    def place(self, name):
        return self.recv.at[self.names.setdefault(name, len(self.names))]

    def copy(self, source, target, name, device):
        index = self.sent
        self.sent += 1
        return pltpu.make_async_remote_copy(
            src_ref=source, dst_ref=target, send_sem=self.send.at[index], recv_sem=self.place(name),
            device_id=device, device_id_type=MESH,
        )

    def along_seq(self, source, target, name, flip):
        copy = self.copy(source, target, name, (self.p ^ flip, self.z))
        copy.start()
        self.always.append((lambda: source, self.sent - 1))

    def along_head(self, source, target, name, flip, waits):
        index = self.sent
        copy = self.copy(source(), target(), name, (self.p, self.z ^ flip))
        copy.start()
        waits.append((source, index))

    def arrived(self, target, name):
        pltpu.make_async_remote_copy(
            src_ref=target, dst_ref=target, send_sem=self.send.at[0], recv_sem=self.place(name),
            device_id=(self.p, self.z ^ 1), device_id_type=MESH,
        ).wait_recv()

    def gone(self, source, index):
        pltpu.make_async_remote_copy(
            src_ref=source(), dst_ref=source(), send_sem=self.send.at[index], recv_sem=self.recv.at[0],
            device_id=(self.p, self.z ^ 1), device_id_type=MESH,
        ).wait_send()

    def finish(self):
        for source, index in self.always:
            self.gone(source, index)

        @pl.when(self.middle)
        def _():
            for source, index in self.middles:
                self.gone(source, index)


class LineGather:
    def __init__(self, links, name, view, fixed=False):
        self.links, self.name, self.view, self.fixed = links, name, view, fixed

    def start(self, sources):
        links = self.links
        for source, view in sources:
            links.along_head(source, lambda: view(1), (self.name, 1), 1, links.always)

        @pl.when(links.middle)
        def _():
            for source, view in sources:
                links.along_head(source, lambda: view(3), (self.name, 3), 3, links.middles)

    def forward(self, k, flip):
        view, there = self.view, k ^ flip
        self.links.along_head(
            lambda: view(k), lambda: view(k if self.fixed else there), (self.name, there), flip,
            self.links.middles,
        )

    def outward(self):
        @pl.when(self.links.middle)
        def _():
            self.links.arrived(self.view(3), (self.name, 3))
            self.forward(3, 1)

    def step(self, k):
        links, name, view = self.links, self.name, self.view
        if k == 1:
            links.arrived(view(1), (name, 1))

            @pl.when(links.middle)
            def _():
                self.forward(1, 3)

        if k == 2:
            links.arrived(view(2), (name, 2))

            @pl.when(links.middle)
            def _():
                self.forward(2, 1)

        if k == 3:

            @pl.when(~links.middle)
            def _():
                links.arrived(view(3), (name, 3))


class PlaneGather:
    def __init__(self, links, name, view, x_first):
        self.links, self.name, self.view = links, name, view
        self.near, self.far = (2, 4) if x_first else (4, 2)

    def send(self, j, flip):
        links = self.links
        block = self.view(links.p ^ j)
        links.along_seq(block, block, (self.name, j ^ flip), flip)

    def wait(self, j):
        self.links.arrived(self.view(self.links.p ^ j), (self.name, j))

    def start(self):
        self.send(0, self.near)
        self.send(0, self.far)
        self.send(0, 1)

    def step(self):
        self.wait(self.near)
        self.send(self.near, self.far)
        self.send(self.near, 1)
        self.wait(self.far)
        self.send(self.far, 1)

    def last(self):
        self.wait(6)
        self.send(6, 1)

    def end(self):
        for j in (1, 3, 5, 7):
            self.wait(j)


class StateExchange:
    def __init__(self, links, name, view):
        self.links, self.name, self.view = links, name, view

    def send(self, j, flip):
        block = self.view(self.links.p ^ j)
        self.links.along_seq(block, block, (self.name, j ^ flip), flip)

    def wait(self, j):
        self.links.arrived(self.view(self.links.p ^ j), (self.name, j))

    def start(self):
        for flip in (6, 2, 4, 1):
            self.send(0, flip)

    def step(self):
        for j in (2, 4, 6):
            self.wait(j)
            self.send(j, 1)

    def end(self):
        for j in (1, 3, 5, 7):
            self.wait(j)


def weight_events(links, own, weights, out_w, gate_up, down):
    q_own, k_own, v_own, g_own, o_own, gate_own, up_own, down_own = own
    block = lambda q: pl.ds(pl.multiple_of(q * 128, 128), 128)
    mine = block(links.p)
    views = {
        "proj": (lambda k, q: weights.at[k, :, block(q), :], True),
        "out": (lambda k, q: out_w.at[k, :, block(q)], False),
        "ffn": (lambda k, q: gate_up.at[k, :, :, block(q)], False),
        "down": (lambda k, q: down.at[k, :, block(q)], True),
    }
    sources = {
        "proj": [
            (lambda ref=ref: ref.at[mine, :], lambda k, i=i: weights.at[k, i, mine, :])
            for i, ref in enumerate((q_own, k_own, v_own, g_own))
        ],
        "out": [(lambda: o_own.at[:, mine], lambda k: out_w.at[k, :, mine])],
        "ffn": [
            (lambda ref=ref: ref.at[:, mine], lambda k, i=i: gate_up.at[k, i, :, mine])
            for i, ref in enumerate((gate_own, up_own))
        ],
        "down": [(lambda: down_own.at[:, mine], lambda k: down.at[k, :, mine])],
    }
    planes = {
        (name, k): PlaneGather(links, (name, k), lambda q, view=view, k=k: view(k, q), x_first)
        for name, (view, x_first) in views.items()
        for k in (1, 2, 3)
    }
    units = UNITS
    count = len(units)

    def post(i):
        if i < count:
            name, k = units[i]
            for source, target in sources[name]:
                links.along_head(source, lambda: target(k), ("line", name, k), k, links.always)

    def begin():
        for i in range(WINDOW):
            post(i)

    events = [(None, begin)]
    for i in range(count + SKEW_TWO):
        if i < count:
            name, k = units[i]

            def first(name=name, k=k, i=i):
                links.arrived(views[name][0](k, links.p), ("line", name, k))
                post(i + WINDOW)
                planes[name, k].start()

            events.append((None, first))
        if 0 <= i - SKEW_ONE < count:
            events.append((None, planes[units[i - SKEW_ONE]].step))
        if 0 <= i - SKEW_TWO < count:
            events.append((units[i - SKEW_TWO], planes[units[i - SKEW_TWO]].last))
    return events, planes


PERS_K, PERS_V, TAPS, GAINS, SMALL = 0, 16, 32, 48, 56


def taps_of(small, k, i):
    return small[k, TAPS + KW * i : TAPS + KW * (i + 1)]


def carry_in_kernel(every, place, forward, backward):
    count, lanes = every.shape[0], every.shape[2]
    row = lax.broadcasted_iota(jnp.int32, (count, lanes), 0)
    mem = jnp.zeros((count, lanes), F32)
    mom = jnp.zeros((count, lanes), F32)
    ahead = jnp.zeros((count, lanes), F32)
    behind = jnp.zeros((count, lanes), F32)
    for c in range(count):
        ahead = jnp.where(place == c, mem, ahead)
        mine = jnp.sum(jnp.where(row == place, mem, 0.0), axis=0, keepdims=True)
        behind = jnp.where(row == c, mine, behind)
        mom = every[c, 1:2] * mom + (row == c).astype(F32)
        mem = every[c, 0:1] * mem + mom
    forward[...] = ahead
    backward[...] = behind


def mixed_state(states, coefficients, k, head):
    lane = 2 * k + head
    total = coefficients[0:1, lane : lane + 1] * states[0, k, head].astype(F32)
    for q in range(1, states.shape[0]):
        total = total + coefficients[q : q + 1, lane : lane + 1] * states[q, k, head].astype(F32)
    return total.astype(BF)


def project_slot(k, h_long, weights, pre, zgate, wide):
    seg = zgate.shape[1]
    for i in range(3):
        rounded = dot(h_long[...], weights[i]).astype(BF)
        pre[i, k] = rounded
        wide[i] = rounded.astype(F32)
    zgate[k] = dot(h_long[pl.ds(ROWS, seg)], weights[3])


def convolve_slot(k, small, query, keyed, valued, wide):
    seg = query.shape[1]
    heads = query.shape[2] // DH

    for first in range(0, seg, BLOCK):
        rows = pl.ds(first, BLOCK)
        for i in range(3):
            conv = shift_sum(wide.at[i], taps_of(small, k, i), ROWS + first, BLOCK, -1)
            act = conv * jax.nn.sigmoid(conv)
            if i == 2:
                valued[k, rows] = act.astype(BF)
                continue
            target = (query, keyed)[i]
            for head in range(heads):
                lanes = slice(head * DH, (head + 1) * DH)
                target[k, rows, lanes] = norm_keep(act[:, lanes])[0].astype(BF)


def write_slot(k, p, keyed, valued, states, length, segment_start):
    seg = keyed.shape[1]
    seg_live = live_rows(0, seg, length, segment_start).astype(BF)
    for head in range(keyed.shape[2] // DH):
        lanes = slice(head * DH, (head + 1) * DH)
        masked = valued[k, :, lanes] * seg_live
        states[p, k, head] = (
            lax.dot_general(
                masked, keyed[k, :, lanes], (((0,), (0,)), ((), ())), preferred_element_type=F32
            )
            / seg
        ).astype(BF)


def attend_head(k, head, small, query, keyed, valued, att, lse, length, segment_start):
    seg = query.shape[1]
    columns_live = live_columns(seg, length, segment_start)
    lanes = slice(head * DH, (head + 1) * DH)
    pers_k = small[k, PERS_K : PERS_K + 16, lanes].astype(BF)
    pers_v = small[k, PERS_V : PERS_V + 16, lanes].astype(BF)
    for index in range(seg // BLOCK):
        rows = pl.ds(index * BLOCK, BLOCK)
        upto = pl.ds(0, (index + 1) * BLOCK)
        score, pers = masked_scores(
            query[k, rows, lanes], keyed[k, upto, lanes], pers_k, index, columns_live
        )
        top = jnp.maximum(
            jnp.max(score, axis=-1, keepdims=True), jnp.max(pers, axis=-1, keepdims=True)
        )
        score, pers = jnp.exp(score - top), jnp.exp(pers - top)
        total = jnp.sum(score, axis=-1, keepdims=True) + jnp.sum(pers, axis=-1, keepdims=True)
        inverse = 1.0 / total
        lse[k, head, rows] = top + jnp.log(total)
        att[k, rows, lanes] = dot((score * inverse).astype(BF), valued[k, upto, lanes]) + dot(
            (pers * inverse).astype(BF), pers_v
        )


def read_slot(k, prior, query, zgate, att, mixed):
    for head in range(query.shape[2] // DH):
        lanes = slice(head * DH, (head + 1) * DH)
        normed, _ = norm_keep(dot_t(query[k, :, lanes], prior[k, head]))
        mixed[k, :, lanes] = (
            att[k, :, lanes] + jax.nn.sigmoid(zgate[k, :, lanes]) * normed
        ).astype(BF)


def ffn_rows(rows, h_two, gffn, weights_gu, weights_d, stage, out_acc, grad_acc):
    gate = dot_t(h_two[rows], weights_gu[0])
    up = dot_t(h_two[rows], weights_gu[1])
    sigma = jax.nn.sigmoid(gate)
    silu = gate * sigma
    low = (silu * up).astype(BF)
    stage[0, rows] = low
    out_acc[rows] += dot(low, weights_d[...])
    back = dot_t(gffn[rows], weights_d[...])
    low_gate = (back * up * (sigma * (1.0 + gate * (1.0 - sigma)))).astype(BF)
    low_up = (back * silu).astype(BF)
    stage[1, rows] = low_gate
    stage[2, rows] = low_up
    grad_acc[rows] += dot(low_gate, weights_gu[0]) + dot(low_up, weights_gu[1])


def tail_slot(k, out_w, gattn, query, prior, zgate, datt, dzgate, dread, dprior):
    dmixed = dot_t(gattn[...], out_w[k])
    datt[k] = dmixed.astype(BF)
    for head in range(dmixed.shape[1] // DH):
        lanes = slice(head * DH, (head + 1) * DH)
        sigma = jax.nn.sigmoid(zgate[k, :, lanes])
        readout, rinv = norm_keep(dot_t(query[k, :, lanes], prior[k, head]))
        grad = dmixed[:, lanes] * sigma
        dzgate[k, :, lanes] = (grad * readout * (1.0 - sigma)).astype(BF)
        low = norm_back(grad, readout, rinv).astype(BF)
        dread[k, :, lanes] = low
        dprior[k, head] = lax.dot_general(
            low, query[k, :, lanes], (((0,), (0,)), ((), ())), preferred_element_type=F32
        ).astype(BF)


class Steps:
    def __init__(self, events):
        self.events, self.at, self.done = events, 0, set()

    def run(self, count=1):
        for _ in range(count):
            if self.at < len(self.events):
                label, function = self.events[self.at]
                function()
                self.at += 1
                self.done.add(label)

    def until(self, *labels):
        while not all(label in self.done for label in labels):
            self.run()


def front_kernel(
    lengths, gain, ffn_gain, own_small, own_decays,
    inputs, cotangent, q_own, k_own, v_own, g_own, o_own, gate_own, up_own, down_own,
    small, backward, dprior, gain_grad,
    x_long_out, h_long_out, pre_out, query_out, keyed_out, valued_out, lse_out, prior_out, mixed_out, h_two_out, gffn_out,
    output_out, dmiddle_out, gattn_out, datt_out, dzgate_out, dread_out,
    weights, hidden, dgate, dup, out_w, gate_up, down,
    x_long, h_long, pre, query, keyed, valued, lse, prior, mixed, h_two, gffn,
    output, dmiddle, gattn, datt, dzgate, dread,
    cot, zgate, att, wide, states, every, forward, wproj, wout, wgu, wdown, stage, out_acc, grad_acc,
    send, recv, sem_x, sem_proj, sem_out, sem_ffn, sem_stage, sem_early, sem_late, sem_slots,
):
    links = Links(send, recv)
    p, z = links.p, links.z
    seg = h_two.shape[0]
    length, start = lengths[z], p * seg
    own = (q_own, k_own, v_own, g_own, o_own, gate_own, up_own, down_own)
    load_x = pltpu.make_async_copy(inputs.at[z], x_long.at[pl.ds(ROWS, seg)], sem_x.at[0])
    load_cot = pltpu.make_async_copy(cotangent.at[z], cot, sem_x.at[1])
    load_x.start()

    def proj_loads(k):
        if k == 0:
            return [
                pltpu.make_async_copy(ref, wproj.at[i], sem_proj.at[i]) for i, ref in enumerate(own[:4])
            ]
        return [pltpu.make_async_copy(weights.at[k], wproj, sem_proj.at[0])]

    def out_load(k):
        return pltpu.make_async_copy(o_own if k == 0 else out_w.at[k], wout.at[k], sem_out.at[k])

    def ffn_loads(k):
        side = k % 2
        if k == 0:
            gu = [
                pltpu.make_async_copy(gate_own, wgu.at[0, 0], sem_ffn.at[0, 0]),
                pltpu.make_async_copy(up_own, wgu.at[0, 1], sem_ffn.at[0, 2]),
            ]
        else:
            gu = [pltpu.make_async_copy(gate_up.at[k], wgu.at[side], sem_ffn.at[side, 0])]
        return gu + [
            pltpu.make_async_copy(down_own if k == 0 else down.at[k], wdown.at[side], sem_ffn.at[side, 1])
        ]

    def go(copies):
        for copy in copies:
            copy.start()

    def come(copies):
        for copy in copies:
            copy.wait()

    go(proj_loads(0))
    go([load_cot, out_load(0)])
    go(ffn_loads(0))
    every[p] = own_decays[...]
    small[0] = own_small[...]
    links.greet()
    events, planes = weight_events(links, own, weights, out_w, gate_up, down)
    steps = Steps(events)

    @pl.when(p < 7)
    def _():
        links.copy(
            inputs.at[z, pl.ds(seg - ROWS, ROWS)], x_long.at[pl.ds(0, ROWS)], "rows", (p + 1, z)
        ).start()

    rows_index = links.sent - 1
    for j in range(1, 8):
        links.along_seq(own_decays, every.at[p], ("decays", j), j)
    for k in (1, 2, 3):
        links.copy(own_small, small.at[k], ("small", k), (p, z ^ k)).start()
        links.always.append((lambda: own_small, links.sent - 1))
    steps.run()

    load_x.wait()

    @pl.when(p == 0)
    def _():
        x_long[pl.ds(0, ROWS)] = jnp.zeros((ROWS, x_long.shape[1]), BF)

    @pl.when(p > 0)
    def _():
        links.arrived(x_long.at[pl.ds(0, ROWS)], "rows")

    @pl.loop(0, 3)
    def _(c):
        rows = pl.ds(pl.multiple_of(c * 176, 16), 176)
        normed, _ = norm_keep(x_long[rows].astype(F32))
        h_long[rows] = (normed * gain[...]).astype(BF)

    exchanges = [StateExchange(links, ("states", k), lambda q, k=k: states.at[q, k]) for k in range(4)]
    complete = lambda name, k: planes[name, k].end()
    come(proj_loads(0))
    attend = lambda k, head: attend_head(k, head, small, query, keyed, valued, att, lse, length, start)

    def load_next(k):
        steps.until(("proj", k))
        complete("proj", k)
        go(proj_loads(k))

    def open_slot(k):
        project_slot(k, h_long, wproj, pre, zgate, wide)
        steps.run()
        convolve_slot(k, small, query, keyed, valued, wide)
        write_slot(k, p, keyed, valued, states, length, start)
        exchanges[k].start()

    steps.run()
    project_slot(0, h_long, wproj, pre, zgate, wide)
    steps.run()
    for other in (1, 2, 3):
        links.arrived(small.at[other], ("small", other))
    convolve_slot(0, small, query, keyed, valued, wide)
    steps.run()
    write_slot(0, p, keyed, valued, states, length, start)
    exchanges[0].start()
    attend(0, 0)
    steps.run()
    attend(0, 1)
    exchanges[0].step()
    for k in (1, 2, 3):
        load_next(k)
        come(proj_loads(k))
        open_slot(k)
        steps.run()
        if k == 1:
            attend(1, 0)
            steps.run()
            exchanges[1].step()
    attend(1, 1)
    exchanges[2].step()
    steps.run()
    attend(2, 0)
    exchanges[3].step()
    steps.run()
    attend(2, 1)
    steps.run()
    attend(3, 0)
    steps.run()
    attend(3, 1)
    for j in range(1, 8):
        links.arrived(every.at[p ^ j], ("decays", j))
    carry_in_kernel(every, p, forward, backward)
    for k in (1, 2, 3):
        steps.until(("out", k))
        complete("out", k)
        go([out_load(k)])
    for k in range(4):
        exchanges[k].end()
        for head in range(2):
            prior[k, head] = mixed_state(states, forward, k, head)
        read_slot(k, prior, query, zgate, att, mixed)
        come([out_load(k)])

        @pl.loop(0, 2)
        def _(c):
            rows = pl.ds(pl.multiple_of(c * 256, 256), 256)
            part = dot(mixed[k, rows], wout[k])
            if k == 0:
                grad_acc[rows] = part
            else:
                grad_acc[rows] += part

        steps.run()
    load_cot.wait()

    @pl.loop(0, seg // BLOCK)
    def _(c):
        first = pl.multiple_of(c * BLOCK, BLOCK)
        rows = pl.ds(first, BLOCK)
        live = live_rows(first, BLOCK, length, start)
        value = x_long[pl.ds(pl.multiple_of(ROWS + first, 16), BLOCK)].astype(F32) + live * grad_acc[rows]
        dmiddle[rows] = value
        normed, _ = norm_keep(value)
        h_two[rows] = (normed * ffn_gain[...]).astype(BF)
        gffn[rows] = (live * cot[rows].astype(F32)).astype(BF)
        out_acc[rows] = jnp.zeros((BLOCK, out_acc.shape[1]), F32)
        grad_acc[rows] = jnp.zeros((BLOCK, out_acc.shape[1]), F32)

    early = [
        pltpu.make_async_copy(source, target, sem_early.at[i])
        for i, (source, target) in enumerate(
            (
                (x_long, x_long_out), (h_long, h_long_out), (pre, pre_out), (query, query_out), (keyed, keyed_out),
                (valued, valued_out), (lse, lse_out), (prior, prior_out), (mixed, mixed_out), (h_two, h_two_out),
                (gffn, gffn_out),
            )
        )
    ]
    late = [
        pltpu.make_async_copy(source, target, sem_late.at[i])
        for i, (source, target) in enumerate(((output, output_out), (dmiddle, dmiddle_out), (gattn, gattn_out)))
    ]
    slot_stores = [
        pltpu.make_async_copy(source.at[k], target.at[k], sem_slots.at[k, i])
        for k in range(4)
        for i, (source, target) in enumerate(((datt, datt_out), (dzgate, dzgate_out), (dread, dread_out)))
    ]
    go(early)

    def stores(k):
        return [
            pltpu.make_async_copy(stage.at[k % 2, i], ref.at[k], sem_stage.at[k % 2, i])
            for i, ref in enumerate((hidden, dgate, dup))
        ]

    for k in range(4):
        if k == 3:
            steps.until(("ffn", 3), ("down", 3))
            complete("ffn", 3)
            complete("down", 3)
            go(ffn_loads(3))
        come(ffn_loads(k))
        if k < 2:
            steps.until(("ffn", k + 1), ("down", k + 1))
            complete("ffn", k + 1)
            complete("down", k + 1)
            go(ffn_loads(k + 1))
        if k >= 2:
            come(stores(k - 2))

        @pl.loop(0, 2)
        def _(c):
            rows = pl.ds(pl.multiple_of(c * 256, 256), 256)
            ffn_rows(rows, h_two, gffn, wgu.at[k % 2], wdown.at[k % 2], stage.at[k % 2], out_acc, grad_acc)

        go(stores(k))
        steps.run(3)
    gain_grad[...] = jnp.zeros_like(gain_grad)

    @pl.loop(0, seg // BLOCK)
    def _(c):
        first = pl.multiple_of(c * BLOCK, BLOCK)
        rows = pl.ds(first, BLOCK)
        live = live_rows(first, BLOCK, length, start)
        value = dmiddle[rows]
        output[rows] = (value + live * out_acc[rows]).astype(BF)
        normed, inverse = norm_keep(value)
        grad = grad_acc[rows]
        gain_grad[...] += jnp.sum(grad * normed, axis=0, keepdims=True)
        result = cot[rows].astype(F32) + norm_back(grad * ffn_gain[...], normed, inverse)
        dmiddle[rows] = result
        gattn[rows] = (live * result).astype(BF)

    go(late)
    for k in range(4):
        tail_slot(k, wout, gattn, query, prior, zgate, datt, dzgate, dread, dprior)
        go(slot_stores[3 * k : 3 * k + 3])
    come(stores(2))
    come(stores(3))
    come(early)
    come(late)
    come(slot_stores)

    @pl.when(p < 7)
    def _():
        links.gone(lambda: x_long.at[pl.ds(0, ROWS)], rows_index)

    links.finish()


class PlaneReduce:
    def __init__(self, links, name, blocks, first, second, x_first):
        self.links, self.name, self.x_first = links, name, x_first
        self.blocks, self.first, self.second = blocks, first, second

    def start(self):
        away = self.blocks.at[:, :, 1] if self.x_first else self.blocks.at[:, 1]
        self.links.along_seq(away, self.first, (self.name, 1), 2 if self.x_first else 4)

    def step(self):
        self.links.arrived(self.first, (self.name, 1))
        for i in range(2):
            y, x = (i, 0) if self.x_first else (0, i)

            @pl.loop(0, self.blocks.shape[0])
            def _(m):
                self.blocks[m, y, x] = add(self.blocks[m, y, x], self.first[m, i])

        y, x = (1, 0) if self.x_first else (0, 1)
        self.links.along_seq(
            self.blocks.at[:, y, x], self.second, (self.name, 2), 4 if self.x_first else 2
        )

    def last(self):
        self.links.arrived(self.second, (self.name, 2))

        @pl.loop(0, self.blocks.shape[0])
        def _(m):
            self.blocks[m, 0, 0] = add(self.blocks[m, 0, 0], self.second[m])


class LineReduce:
    def __init__(self, links, name, blocks, landing, result):
        self.links, self.name, self.blocks = links, name, blocks
        self.landing, self.result = landing, result
        self.ends = []

    def send(self, k, slot, flip, waits):
        self.links.along_head(
            lambda: self.blocks(k), lambda: self.landing.at[slot], (self.name, slot), flip, waits
        )

    def merge(self, k, slot):
        self.links.arrived(self.landing.at[slot], (self.name, slot))
        block = self.blocks(k)

        @pl.loop(0, self.landing.shape[1])
        def _(m):
            block[m] = add(block[m], self.landing[slot, m])

    def from_ends(self, k):
        @pl.when(~self.links.middle)
        def _():
            self.send(k, 3 - k, 1, self.ends)

    def take(self, k):
        @pl.when(self.links.middle)
        def _():
            self.merge(5 - k, 3 - k)

    def across(self, k):
        @pl.when(self.links.middle)
        def _():
            self.send(5 - k, 7 - k, 3, self.links.middles)

    def to_ends(self):
        @pl.when(self.links.middle)
        def _():
            self.merge(1, 4)
            self.send(1, 3, 1, self.links.middles)

    def last(self):
        @pl.when(~self.links.middle)
        def _():
            self.total([3])

        @pl.when(self.links.middle)
        def _():
            self.total([2, 5])

    def total(self, slots):
        block = self.blocks(0)
        for slot in slots:
            self.links.arrived(self.landing.at[slot], (self.name, slot))

        @pl.loop(0, self.landing.shape[1])
        def _(m):
            value = block[m].astype(F32)
            for slot in slots:
                value = value + self.landing[slot, m].astype(F32)
            self.result[m] = value

    def finish(self):
        @pl.when(~self.links.middle)
        def _():
            for source, index in self.ends:
                self.links.gone(source, index)


class Pairs:
    def __init__(self, buffers, sems):
        self.buffers, self.sems = buffers, sems

    def copies(self, slot, own, peer):
        rows = own.shape[0]
        return [
            pltpu.make_async_copy(own, self.buffers.at[slot, pl.ds(0, rows)], self.sems.at[slot, 0]),
            pltpu.make_async_copy(peer, self.buffers.at[slot, pl.ds(rows, rows)], self.sems.at[slot, 1]),
        ]

    def start(self, slot, own, peer):
        for copy in self.copies(slot, own, peer):
            copy.start()

    def wait(self, slot, own, peer):
        for copy in self.copies(slot, own, peer):
            copy.wait()


def load_turned(links, own, peer, staged, turned, sems):
    rows = own.shape[0]
    copies = []
    for i, j in enumerate((0, 2, 4, 6)):
        block = pl.ds(pl.multiple_of((links.p ^ j) * 128, 128), 128)
        for side, ref in enumerate((own, peer)):
            copy = pltpu.make_async_copy(
                ref.at[:, block], staged.at[pl.ds(side * rows, rows), pl.ds(i * 128, 128)], sems.at[i, side]
            )
            copy.start()
            copies.append(copy)
    for copy in copies:
        copy.wait()
    for i in range(4):
        turned[pl.ds(i * 128, 128)] = staged[:, pl.ds(i * 128, 128)].T


def conv_back(k, refs, length, segment_start):
    pre, small, keyed, valued, dwrite, dqkv, dslot, small_grad, wide, dpre, part, halo = refs
    conv_back_slot(
        k, (pre, small, keyed, valued, dwrite, dqkv, dslot, small_grad, wide), length, segment_start
    )
    seg = keyed.shape[1]
    for i in range(3):
        dslot[i, 0, pl.ds(seg, 8)] = jnp.zeros((8, dslot.shape[3]), F32)
        halo[i, k] = dslot[i, 0, pl.ds(0, 8)]
        weights = taps_of(small, k, i)
        for first in range(0, seg, BLOCK):
            value = shift_sum(dslot.at[i, 0], weights, first, BLOCK, 1)
            dpre[i, k, pl.ds(first, BLOCK)] = value.astype(BF)
            if first + BLOCK == seg:
                part[i, k] = value[BLOCK - 16 :]


def product(turned, pair, target):
    @pl.loop(0, 2)
    def _(y):
        for x in range(2):
            rows = pl.ds(pl.multiple_of(y * 256, 256) + x * 128, 128)
            target[y, x] = dot(turned[rows], pair[...]).astype(BF)


def gather_halves(links, own, everyone):
    z = links.z
    half = own.shape[0] // 2
    lines = []
    for i in range(2):
        rows = pl.ds(i * half, half)
        line = LineGather(
            links, ("rows", i), lambda k, rows=rows: everyone.at[z ^ k, rows], fixed=True
        )
        line.start([(lambda rows=rows: own.at[rows], lambda k, rows=rows: everyone.at[z, rows])])
        lines.append(line)
    return lines


def back_all_kernel(
    lengths, carry, small, dprior, gain, ffn_gain_grad,
    query_in, keyed_in, valued_in, lse_in, datt_in, dread_in, prior_in, pre_in, x_long_in, dmiddle_in,
    output, h_two, gffn, hidden, dgate, dup, h_long, gattn, mixed, weights, dzgate, q_own, k_own, v_own, g_own,
    all_output, part_ffn, small_grad, dpre, input_grad,
    peer_h_two, peer_gffn, peer_hidden, peer_dgate, peer_dup, peer_h, peer_gattn, peer_mixed, peer_dzgate,
    query, keyed, valued, lse, datt, dread, prior, pre, x_long, dmiddle,
    states, dwrite, dqkv, wide, dslot, part, halo, halo_in, ext, acc, wbuf, zbuf,
    staged, turned, pairs, blocks, first_in, second_in, landing,
    send, recv, sems_turned, sems_pairs, sems_weights, sem_own, sems_in,
):
    links = Links(send, recv)
    p, z = links.p, links.z
    seg = dmiddle.shape[0]
    loads = [
        pltpu.make_async_copy(source, target, sems_in.at[i])
        for i, (source, target) in enumerate(
            (
                (query_in, query), (keyed_in, keyed), (valued_in, valued), (lse_in, lse), (datt_in, datt),
                (dread_in, dread), (prior_in, prior), (pre_in, pre), (x_long_in, x_long), (dmiddle_in, dmiddle),
            )
        )
    ]
    length, start = lengths[z], p * seg
    states[p] = dprior[...]
    own_output = pltpu.make_async_copy(output, all_output.at[z], sem_own.at[0])
    own_output.start()
    links.greet()
    exchange = StateExchange(links, "states", lambda q: states.at[q])
    exchange.start()
    lines = gather_halves(links, output, all_output)
    h_one = h_long.at[pl.ds(ROWS, seg)]
    later = [("h", h_one, peer_h), ("gattn", gattn, peer_gattn), ("mixed", mixed, peer_mixed), ("dzgate", dzgate, peer_dzgate)]

    def to_peer(name, source, target):
        links.along_seq(source, target, ("peer", name), 1)

    def slot_to_peer(k):
        to_peer(("dgate", k), dgate.at[k], peer_dgate.at[k])
        to_peer(("dup", k), dup.at[k], peer_dup.at[k])
        if k == 3:
            to_peer("gffn", gffn, peer_gffn)
        to_peer(("hidden", k), hidden.at[k], peer_hidden.at[k])

    to_peer("h_two", h_two, peer_h_two)
    slot_to_peer(3)

    both = Pairs(pairs, sems_pairs)
    reduces = {
        k: PlaneReduce(links, ("plane", k), blocks.at[k - 1], first_in.at[k - 1], second_in.at[k - 1], k != 2)
        for k in (3, 2)
    }
    for name, mats, x_first in (("1a", pl.ds(0, 2), True), ("1b", pl.ds(2, 1), False)):
        reduces[name] = PlaneReduce(
            links, ("plane", name), blocks.at[0, mats], first_in.at[0, mats], second_in.at[0, mats], x_first
        )
    line_reduce = LineReduce(links, "sum", lambda k: blocks.at[k - 1, :, 0, 0], landing, None)
    sources = ((dgate, peer_dgate, "dgate", 0), (dup, peer_dup, "dup", 0), (hidden, peer_hidden, "hidden", 1))
    units = [(k, m) for k in (3, 2, 1) for m in range(3)]

    def fetch(n):
        k, m = units[n]
        own, peer, name, _ = sources[m]
        links.arrived(peer.at[k], ("peer", (name, k)))
        both.start(n % 2, own.at[k], peer.at[k])

    for copy in loads:
        copy.start()
    links.arrived(peer_h_two, ("peer", "h_two"))
    load_turned(links, h_two, peer_h_two, staged, turned.at[0], sems_turned)
    fetch(0)
    for n, (k, m) in enumerate(units):
        if n == 1:
            links.arrived(peer_gffn, ("peer", "gffn"))
            load_turned(links, gffn, peer_gffn, staged, turned.at[1], sems_turned)
        if m == 0:
            slot_to_peer(k - 1)
        if n + 1 < len(units):
            fetch(n + 1)
        own, peer, _, side = sources[m]
        both.wait(n % 2, own.at[k], peer.at[k])
        product(turned.at[side], pairs.at[n % 2], blocks.at[k - 1, m])
        if m == 2:
            if k > 1:
                reduces[k].start()
            if k == 3:
                exchange.step()
    for name, source, target in later:
        to_peer(name, source, target)
    exchange.end()
    lines[0].outward()
    lines[0].step(1)

    one = (query, keyed, valued, lse, datt, dread, prior, small, dqkv, small_grad)
    two = (pre, small, keyed, valued, dwrite, dqkv, dslot, small_grad, wide, dpre, part, halo)
    for k in range(4):
        for head in range(2):
            dwrite[k, head] = mixed_state(states, carry, k, head)

    def slots(first, count):
        @pl.loop(first, first + count)
        def _(k):
            attention_back_slot(k, one, length, start)
            conv_back(k, two, length, start)

    for copy in loads:
        copy.wait()
    slots(0, 2)
    lines[1].outward()
    lines[1].step(1)
    reduces[3].step()
    reduces["1a"].start()
    slots(2, 1)
    lines[0].step(2)
    reduces[2].step()
    reduces["1b"].start()
    slots(3, 1)

    @pl.when(p > 0)
    def _():
        links.copy(halo, halo_in, "halo", (p - 1, z)).start()

    halo_index = links.sent - 1

    def weight_copies(n):
        copies = [
            pltpu.make_async_copy(
                (q_own, k_own, v_own, g_own)[n] if n < 4 else weights.at[n // 4, n % 4],
                wbuf.at[n % 2], sems_weights.at[n % 2, 0],
            )
        ]
        if n % 4 == 3:
            copies.append(
                pltpu.make_async_copy(dzgate.at[n // 4], zbuf, sems_weights.at[n % 2, 1])
            )
        return copies

    for copy in weight_copies(0):
        copy.start()
    reduces[3].last()
    line_reduce.from_ends(3)
    reduces[2].last()
    line_reduce.from_ends(2)
    lines[1].step(2)

    @pl.when(p == 7)
    def _():
        halo_in[...] = jnp.zeros_like(halo_in)

    @pl.when(p < 7)
    def _():
        links.arrived(halo_in, "halo")

    ext[pl.ds(0, 16)] = jnp.zeros((16, ext.shape[1]), F32)
    for k in range(4):
        for i in range(3):
            ext[pl.ds(16, 8)] = halo_in[i, k]
            dpre[i, k, pl.ds(seg - 16, 16)] = (
                part[i, k] + shift_sum(ext, taps_of(small, k, i), 0, 16, 1)
            ).astype(BF)
        for i in range(4):
            n = 4 * k + i
            if n < 15:
                for copy in weight_copies(n + 1):
                    copy.start()
            for copy in weight_copies(n):
                copy.wait()

            @pl.loop(0, seg // 256)
            def _(c):
                rows = pl.ds(pl.multiple_of(c * 256, 256), 256)
                total = dot_t(zbuf[rows] if i == 3 else dpre[i, k, rows], wbuf[n % 2])
                if n == 0:
                    acc[rows] = total
                else:
                    acc[rows] += total

    reduces["1a"].step()
    reduces["1b"].step()
    gain_sum = jnp.zeros((1, acc.shape[1]), F32)
    for first in range(0, seg, BLOCK):
        rows = pl.ds(first, BLOCK)
        normed, inverse = norm_keep(x_long[pl.ds(ROWS + first, BLOCK)].astype(F32))
        grad = acc[rows]
        gain_sum = gain_sum + jnp.sum(grad * normed, axis=0, keepdims=True)
        input_grad[rows] = (
            dmiddle[rows] + norm_back(grad * gain[...], normed, inverse)
        ).astype(BF)
    for row, value in enumerate((gain_sum, ffn_gain_grad[...])):
        for i in range(4):
            at = GAINS + 4 * row + i
            for k in range(4):
                small_grad[k, at : at + 1] = value[:, i * 256 : (i + 1) * 256]
    for k in range(4):
        small_grad[k, TAPS + 3 * KW : GAINS] = jnp.zeros((GAINS - TAPS - 3 * KW, 256), F32)
    reduces["1a"].last()
    reduces["1b"].last()
    line_reduce.take(3)
    line_reduce.take(2)
    for k in (1, 2, 3):
        part_ffn[k - 1] = blocks[k - 1, :, 0, 0]
    lines[0].step(3)
    lines[1].step(3)
    for own, peer, name, _ in sources:
        links.arrived(peer.at[0], ("peer", (name, 0)))
    for name, _, target in later:
        links.arrived(target, ("peer", name))
    own_output.wait()

    @pl.when(p > 0)
    def _():
        links.gone(lambda: halo, halo_index)

    line_reduce.finish()
    links.finish()


def gradient_kernel(
    small, part_ffn,
    h_long, gattn, dpre, dzgate, mixed, input_grad, h_two, gffn, hidden, dgate, dup,
    peer_h_two, peer_gffn, peer_hidden, peer_dgate, peer_dup, peer_h, peer_gattn, peer_mixed, peer_dzgate,
    all_input_grad, g_attn, g_ffn, small_sum, peer_dpre,
    staged, turned, pairs, blocks, first_in, second_in, landing,
    pairs_ffn, blocks_ffn, first_ffn, second_ffn, landing_ffn, sums_ffn, small_in, small_part, small_all,
    send, recv, sems_turned, sems_pairs, sems_ffn, sem_own,
):
    links = Links(send, recv)
    p, z = links.p, links.z
    seg = gattn.shape[0]
    own_rows = pltpu.make_async_copy(input_grad, all_input_grad.at[z], sem_own.at[0])
    own_rows.start()
    sums_ffn[...] = part_ffn[...]
    links.greet()
    lines = gather_halves(links, input_grad, all_input_grad)
    order = (3, 2, 1, 0)
    for k in order:
        for i in range(3):
            links.along_seq(dpre.at[i, k], peer_dpre.at[i, k], ("dpre", i, k), 1)

    line_ffn = LineReduce(
        links, "ffn", lambda k: sums_ffn.at[k - 1] if k > 0 else blocks_ffn.at[:, 0, 0], landing_ffn, g_ffn
    )
    line_attn = LineReduce(links, "attn", lambda k: blocks.at[k, :, 0, 0], landing, g_attn)
    small_in[0] = small[0]
    for k in (1, 2, 3):
        links.copy(small.at[k], small_in.at[k], ("small", k), (p, z ^ k)).start()
        links.always.append((lambda k=k: small.at[k], links.sent - 1))

    ffn = PlaneReduce(links, "ffn0", blocks_ffn, first_ffn, second_ffn, False)
    attn = {
        k: PlaneReduce(links, ("attn", k), blocks.at[k], first_in.at[k], second_in.at[k], k != 2)
        for k in order
    }
    sources = ((dgate, peer_dgate, 0), (dup, peer_dup, 0), (hidden, peer_hidden, 1))
    both = Pairs(pairs_ffn, sems_ffn)
    sides = lambda k: [(dpre.at[m, k], peer_dpre.at[m, k]) for m in range(3)] + [
        (dzgate.at[k], peer_dzgate.at[k]), (mixed.at[k], peer_mixed.at[k])
    ]

    def attn_loads(k):
        return [
            pltpu.make_async_copy(ref, pairs.at[k % 2, m, pl.ds(side * seg, seg)], sems_pairs.at[k % 2, m, side])
            for m, both_sides in enumerate(sides(k))
            for side, ref in enumerate(both_sides)
        ]

    def fetch(k):
        for m in range(3):
            links.arrived(peer_dpre.at[m, k], ("dpre", m, k))
        for copy in attn_loads(k):
            copy.start()

    fetch(3)
    load_turned(links, h_long.at[pl.ds(ROWS, seg)], peer_h, staged, turned.at[0], sems_turned)
    load_turned(links, gattn, peer_gattn, staged, turned.at[1], sems_turned)
    for k in order:
        if k > 0:
            fetch(k - 1)
        for copy in attn_loads(k):
            copy.wait()
        for m in range(5):
            product(turned.at[m // 4], pairs.at[k % 2, m], blocks.at[k, m])
        if k > 1:
            attn[k].start()
        if k == 3:
            lines[0].outward()
            lines[0].step(1)
            line_ffn.across(3)
    refs_ffn = lambda m: tuple(ref.at[0] for ref in sources[m][:2])
    both.start(0, *refs_ffn(0))
    load_turned(links, h_two, peer_h_two, staged, turned.at[0], sems_turned)
    load_turned(links, gffn, peer_gffn, staged, turned.at[1], sems_turned)
    for m in range(3):
        if m < 2:
            both.start((m + 1) % 2, *refs_ffn(m + 1))
        both.wait(m % 2, *refs_ffn(m))
        product(turned.at[sources[m][2]], pairs_ffn.at[m % 2], blocks_ffn.at[m])
    for k in (1, 2, 3):
        links.arrived(small_in.at[k], ("small", k))
    small_part[...] = (small_in[0] + small_in[1]) + (small_in[2] + small_in[3])
    small_all[0] = small_part[...]
    for j in range(1, 8):
        links.along_seq(small_part, small_all.at[j], ("all", j), j)
    lines[1].outward()
    lines[1].step(1)
    line_ffn.across(2)
    line_ffn.from_ends(1)
    attn[3].step()
    attn[2].step()
    attn[1].start()
    ffn.start()
    lines[0].step(2)
    attn[3].last()
    line_attn.from_ends(3)
    attn[2].last()
    line_attn.from_ends(2)
    lines[1].step(2)
    attn[1].step()
    attn[0].start()
    ffn.step()
    attn[0].step()
    line_ffn.to_ends()
    line_attn.take(3)
    line_attn.across(3)
    line_attn.take(2)
    line_attn.across(2)
    attn[1].last()
    line_attn.from_ends(1)
    line_attn.to_ends()
    ffn.last()
    attn[0].last()
    line_ffn.last()
    lines[0].step(3)
    lines[1].step(3)
    line_attn.last()
    for j in range(1, 8):
        links.arrived(small_all.at[j], ("all", j))
    pair = lambda j: small_all[j] + small_all[j + 1]
    small_sum[...] = (pair(0) + pair(2)) + (pair(4) + pair(6))
    own_rows.wait()
    line_attn.finish()
    line_ffn.finish()
    links.finish()


def finish_kernel(
    attn, ffn, small, output_in, input_in,
    g_query, g_key, g_value, g_zgate, g_out, g_gate, g_up, g_down, taps, pers_k, pers_v, gains,
    output, input_grad, staged, sems_in, sems_out,
):
    pairs = ((output_in, output), (input_in, input_grad))
    count = output.shape[0]
    for side, (source, _) in enumerate(pairs):
        for s in range(count):
            pltpu.make_async_copy(source.at[s], staged.at[side, s], sems_in.at[side, s]).start()
    for i, ref in enumerate((g_query, g_key, g_value, g_zgate)):
        ref[...] = attn[i]
    g_out[...] = attn[4].T
    for i, ref in enumerate((g_gate, g_up, g_down)):
        for first in range(0, ref.shape[0], 128):
            wide = min(128, ref.shape[0] - first)
            ref[pl.ds(first, wide)] = ffn[i, :, pl.ds(first, wide)].T
    pers_k[...] = small[PERS_K : PERS_K + 16]
    pers_v[...] = small[PERS_V : PERS_V + 16]
    for i in range(3):
        taps[i] = small[TAPS + KW * i : TAPS + KW * (i + 1)]
    width = small.shape[1]
    for row in range(2):
        for i in range(4):
            at = GAINS + 4 * row + i
            gains[row : row + 1, i * width : (i + 1) * width] = small[at : at + 1]
    for side, (source, target) in enumerate(pairs):
        for s in range(count):
            pltpu.make_async_copy(source.at[s], staged.at[side, s], sems_in.at[side, s]).wait()
            pltpu.make_async_copy(staged.at[side, s], target.at[s], sems_out.at[side, s]).start()
    for side, (_, target) in enumerate(pairs):
        for s in range(count):
            pltpu.make_async_copy(staged.at[side, s], target.at[s], sems_out.at[side, s]).wait()


def local_fast(
    inputs, lengths, decays, norm_gain, query_proj, key_proj, value_proj, gate_proj, conv_taps,
    pers_keys, pers_values, out_proj, ffn_gain, ffn_gate, ffn_up, ffn_down, cotangent,
):
    seqs, seg, features = inputs.shape
    segments, shards = lax.axis_size("seq"), lax.axis_size("head")
    p, z = lax.axis_index("seq"), lax.axis_index("head")
    width, hidden_width = query_proj.shape[1], ffn_gate.shape[1]
    heads_here = width // DH
    heads = heads_here * shards
    persistent = pers_keys.shape[0]

    turn = (jnp.arange(shards)[:, None] == (z ^ jnp.arange(shards))[None, :]).astype(F32)
    mine = lax.dynamic_index_in_dim(decays, z, 1, False)[:, 0].reshape(2, shards, 1, heads_here)
    mine = jnp.sum(mine * turn[None, :, :, None], axis=1).reshape(2, heads)
    mine = jnp.pad(mine, ((0, 6), (0, 128 - heads)))
    own_small = jnp.concatenate(
        [pers_keys, pers_values, conv_taps.reshape(3 * KW, width), jnp.zeros((4, width), BF)]
    ).astype(F32)
    gain, ffn_gain = norm_gain[None], ffn_gain[None]
    low = lambda *shape: SHAPE(shape, BF)
    full = lambda *shape: SHAPE(shape, F32)
    rows_low = low(shards, seg, width)
    state = low(shards, heads_here, DH, DH)
    hid = low(shards, seg, hidden_width)
    flat = low(seg, features)
    anywhere = pl.BlockSpec(memory_space=pl.ANY)
    in_vmem = pl.BlockSpec(memory_space=pltpu.VMEM)
    in_smem = pl.BlockSpec(memory_space=pltpu.SMEM)
    vmem_low = lambda *shape: pltpu.VMEM(shape, BF)
    vmem_full = lambda *shape: pltpu.VMEM(shape, F32)
    dma = pltpu.SemaphoreType.DMA
    block = features // 8
    halo_rows, pre_rows = low(seg + ROWS, features), low(3, shards, seg + ROWS, width)
    scores_total, middle_rows = full(shards, heads_here, seg, 1), full(seg, features)
    kept = [
        halo_rows, halo_rows, pre_rows, rows_low, rows_low, rows_low, scores_total, state, rows_low, flat, flat,
        flat, middle_rows, flat, rows_low, rows_low, rows_low,
    ]
    held = lambda shapes: [pltpu.VMEM(shape.shape, shape.dtype) for shape in shapes]
    (
        small, carry_back, dprior, g_ffn_gain,
        x_long, h_long, pre, query, keyed, valued, lse, prior, mixed, h_two, gffn,
        output, dmiddle, gattn, datt, dzgate, dread,
        weights, hidden, dgate, dup, *_,
    ) = pl.pallas_call(
        front_kernel,
        out_shape=[full(shards, GAINS, width), full(segments, 128), state, full(1, features)]
        + kept
        + [
            low(shards, 4, features, width), hid, hid, hid, low(shards, width, features),
            low(shards, 2, hidden_width, features), low(shards, hidden_width, features),
        ],
        in_specs=[in_smem] + [in_vmem] * 4 + [anywhere] * 10,
        out_specs=[in_vmem] * 4 + [anywhere] * (len(kept) + 7),
        scratch_shapes=held(kept) + [
            vmem_low(seg, features), vmem_full(shards, seg, width), vmem_full(shards, seg, width),
            vmem_full(3, seg + ROWS, width), vmem_low(segments, shards, heads_here, DH, DH),
            vmem_full(segments, 8, 128), vmem_full(segments, 128), vmem_low(4, features, width),
            vmem_low(shards, width, features), vmem_low(2, 2, hidden_width, features),
            vmem_low(2, hidden_width, features), vmem_low(2, 3, seg, hidden_width),
            vmem_full(seg, features), vmem_full(seg, features),
            dma((192,)), dma((192,)), dma((2,)), dma((4,)), dma((4,)), dma((2, 3)), dma((2, 3)),
            dma((11,)), dma((3,)), dma((4, 3)),
        ],
        compiler_params=pltpu.CompilerParams(
            collective_id=0, has_side_effects=True, vmem_limit_bytes=VMEM_LIMIT
        ),
    )(
        lengths, gain, ffn_gain, own_small, mine, inputs, cotangent,
        query_proj, key_proj, value_proj, gate_proj, out_proj, ffn_gate.T, ffn_up.T, ffn_down,
    )
    output, part_ffn, small_grad, dpre, input_grad, *peers = pl.pallas_call(
        back_all_kernel,
        out_shape=[
            low(shards, seg, features), low(3, 3, block, hidden_width), full(shards, SMALL, width),
            low(3, shards, seg, width), flat, flat, flat, hid, hid, hid, flat, flat, rows_low, rows_low,
        ],
        in_specs=[in_smem] + [in_vmem] * 5 + [anywhere] * 25,
        out_specs=[anywhere] + [in_vmem] * 4 + [anywhere] * 9,
        scratch_shapes=held(
            [rows_low] * 3 + [scores_total, rows_low, rows_low, state, pre_rows, halo_rows, middle_rows]
        ) + [
            vmem_low(8, shards, heads_here, DH, DH), vmem_low(shards, heads_here, DH, DH),
            vmem_full(3, seg, width), vmem_full(3, seg + ROWS, width), vmem_full(3, 1, seg + 8, width),
            vmem_full(3, shards, 16, width), vmem_full(3, shards, 8, width), vmem_full(3, shards, 8, width),
            vmem_full(24, width), vmem_full(seg, features), vmem_low(2, features, width),
            vmem_low(seg, width),
            vmem_low(2 * seg, features // 2), vmem_low(2, features // 2, 2 * seg),
            vmem_low(2, 2 * seg, hidden_width), vmem_low(3, 3, 2, 2, block, hidden_width),
            vmem_low(3, 3, 2, block, hidden_width), vmem_low(3, 3, block, hidden_width),
            vmem_low(2, 3, block, hidden_width),
            dma((64,)), dma((64,)), dma((4, 2)), dma((2, 2)), dma((2, 2)), dma((1,)), dma((10,)),
        ],
        compiler_params=pltpu.CompilerParams(
            collective_id=1, has_side_effects=True, vmem_limit_bytes=VMEM_LIMIT
        ),
    )(
        lengths, carry_back, small, dprior, gain, g_ffn_gain,
        query, keyed, valued, lse, datt, dread, prior, pre, x_long, dmiddle,
        output, h_two, gffn, hidden, dgate, dup, h_long, gattn, mixed, weights, dzgate,
        query_proj, key_proj, value_proj, gate_proj,
    )
    input_grad, g_attn, g_ffn, small, *_ = pl.pallas_call(
        gradient_kernel,
        out_shape=[
            low(shards, seg, features), full(5, block, width), full(3, block, hidden_width), full(SMALL, width),
            low(3, shards, seg, width),
        ],
        in_specs=[in_vmem] * 2 + [anywhere] * 20,
        out_specs=[anywhere] + [in_vmem] * 3 + [anywhere],
        scratch_shapes=[
            vmem_low(2 * seg, features // 2), vmem_low(2, features // 2, 2 * seg),
            vmem_low(2, 5, 2 * seg, width), vmem_low(4, 5, 2, 2, block, width), vmem_low(4, 5, 2, block, width),
            vmem_low(4, 5, block, width), vmem_low(6, 5, block, width),
            vmem_low(2, 2 * seg, hidden_width), vmem_low(3, 2, 2, block, hidden_width),
            vmem_low(3, 2, block, hidden_width), vmem_low(3, block, hidden_width),
            vmem_low(6, 3, block, hidden_width), vmem_low(3, 3, block, hidden_width),
            vmem_full(shards, SMALL, width), vmem_full(SMALL, width), vmem_full(8, SMALL, width),
            dma((96,)), dma((96,)), dma((4, 2)), dma((2, 5, 2)), dma((2, 2)), dma((1,)),
        ],
        compiler_params=pltpu.CompilerParams(
            collective_id=2, has_side_effects=True, vmem_limit_bytes=VMEM_LIMIT
        ),
    )(
        small_grad, part_ffn, h_long, gattn, dpre, dzgate, mixed, input_grad, h_two, gffn, hidden, dgate, dup, *peers,
    )
    (
        g_query, g_key, g_value, g_zgate, g_out, g_gate, g_up, g_down, g_taps, g_pers_k, g_pers_v, gains,
        output, input_grad,
    ) = pl.pallas_call(
        finish_kernel,
        out_shape=[full(block, width)] * 4
        + [full(width, block)]
        + [full(hidden_width, block)] * 3
        + [full(3, KW, width), full(persistent, width), full(persistent, width), full(2, features)]
        + [low(shards, seg, features)] * 2,
        in_specs=[in_vmem] * 3 + [anywhere] * 2,
        out_specs=[in_vmem] * 12 + [anywhere] * 2,
        scratch_shapes=[vmem_low(2, shards, seg, features), dma((2, 4)), dma((2, 4))],
        compiler_params=pltpu.CompilerParams(vmem_limit_bytes=VMEM_LIMIT),
    )(g_attn, g_ffn, small, output, input_grad)
    return (
        output, input_grad, gains[0], g_query, g_key, g_value, g_zgate, g_taps, g_pers_k, g_pers_v,
        g_out, gains[1], g_gate.T, g_up.T, g_down,
    )


def local(*args):
    return local_fast(*args) if custom_mesh() else local_plain(*args)


def solution(mesh):
    in_specs = (
        P(None, "seq", None),
        P(),
        P(None, None, "seq", None),
        P(),
        P(None, "head"),
        P(None, "head"),
        P(None, "head"),
        P(None, "head"),
        P(None, None, "head"),
        P(None, "head"),
        P(None, "head"),
        P("head", None),
        P(),
        P(None, "head"),
        P(None, "head"),
        P("head", None),
        P(None, "seq", None),
    )
    out_specs = (
        P(None, "seq", None),
        P(None, "seq", None),
        P(),
        P("seq", "head"),
        P("seq", "head"),
        P("seq", "head"),
        P("seq", "head"),
        P(None, None, "head"),
        P(None, "head"),
        P(None, "head"),
        P("head", "seq"),
        P(),
        P("seq", "head"),
        P("seq", "head"),
        P("head", "seq"),
    )
    return jax.shard_map(local, mesh=mesh, in_specs=in_specs, out_specs=out_specs, check_vma=False)
```

```python
import functools

import jax
import jax.numpy as jnp
from jax import lax
from jax.experimental import pallas as pl
from jax.experimental.pallas import tpu as pltpu
from jax.sharding import PartitionSpec as P

DH = 128
KW = 4
HALO = 8
EPSILON = 1e-06
BF = jnp.bfloat16
F32 = jnp.float32


def custom_mesh():
    return lax.axis_size("seq") == 8 and lax.axis_size("head") == 4


def along_seq(value, flip):
    return lax.ppermute(value, "seq", [(i, i ^ flip) for i in range(8)])


def along_head(value, pairs):
    return lax.ppermute(value, "head", pairs)


def slot_owner(k):
    return lax.axis_index("head") ^ k if custom_mesh() else k


def gather_head(value):
    z = lax.axis_index("head")
    middle = (z == 1) | (z == 2)
    one = along_head(value, [(0, 1), (1, 0), (2, 3), (3, 2)])
    inner = along_head(value, [(1, 2), (2, 1)])
    two_inner = along_head(one, [(1, 2), (2, 1)])
    two_outer = along_head(inner, [(2, 3), (1, 0)])
    three_outer = along_head(two_inner, [(2, 3), (1, 0)])
    two = jnp.where(middle, two_inner, two_outer)
    three = jnp.where(middle, inner, three_outer)
    return [value, one, two, three]


def gather_plane(value, x_first):
    near, far = (2, 4) if x_first else (4, 2)
    pieces = {0: value, near: along_seq(value, near), far: along_seq(value, far)}
    pieces[6] = along_seq(pieces[near], far)
    for j in (0, 2, 4, 6):
        pieces[j + 1] = along_seq(pieces[j], 1)
    return [pieces[j] for j in range(8)]


def gather_weights(own):
    if not custom_mesh():
        whole = lax.all_gather(own, "head")
        return [whole[k] for k in range(lax.axis_size("head"))]
    p = lax.axis_index("seq")
    matrices, depth, width = own.shape
    block = depth // 8
    mine = lax.dynamic_slice_in_dim(own, p * block, block, 1)
    slots = [own]
    for k, piece in enumerate(gather_head(mine)[1:]):
        if k < 2:
            parts = gather_plane(piece, k == 0)
        else:
            half = block // 2
            upper = gather_plane(piece[:, :half], True)
            lower = gather_plane(piece[:, half:], False)
            parts = [jnp.concatenate([u, v], axis=1) for u, v in zip(upper, lower)]
        full = jnp.zeros((matrices, depth, width), own.dtype)
        for j, part in enumerate(parts):
            full = lax.dynamic_update_slice_in_dim(full, part, (p ^ j) * block, 1)
        slots.append(full)
    return slots


def gather_small(own):
    if not custom_mesh():
        whole = lax.all_gather(own, "head")
        return [whole[k] for k in range(lax.axis_size("head"))]
    return [own] + [along_head(own, [(i, i ^ k) for i in range(4)]) for k in (1, 2, 3)]


def gather_states(value):
    p = lax.axis_index("seq")
    if not custom_mesh():
        whole = lax.all_gather(value, "seq")
        count = lax.axis_size("seq")
        return [whole[i] for i in range(count)], list(range(count))
    half = value.shape[0] // 2
    upper = gather_plane(value[:half], True)
    lower = gather_plane(value[half:], False)
    pieces = [jnp.concatenate([u, v]) for u, v in zip(upper, lower)]
    return pieces, [p ^ j for j in range(8)]


def gather_rows(own):
    if not custom_mesh():
        return lax.all_gather(own, "head")
    z = lax.axis_index("head")
    full = jnp.zeros((4,) + own.shape, own.dtype)
    for k, slot in enumerate(gather_head(own)):
        full = lax.dynamic_update_slice_in_dim(full, slot[None], z ^ k, 0)
    return full


def weight_grads(pairs, x_first):
    dot = lambda a, b: lax.dot_general(a, b, (((0,), (0,)), ((), ())), preferred_element_type=F32)
    if not custom_mesh():
        out = []
        for a, b in pairs:
            full = jnp.stack([dot(a, one) for one in b]).astype(BF)
            part = lax.psum_scatter(full, "head", scatter_dimension=0, tiled=True)[0]
            out.append(lax.psum_scatter(part, "seq", scatter_dimension=0, tiled=True).astype(F32))
        return out
    p, z = lax.axis_index("seq"), lax.axis_index("head")
    block = pairs[0][0].shape[1] // 8
    stacks = [[] for _ in range(4)]
    for a, b in pairs:
        cut = lambda j: lax.dynamic_slice_in_dim(a, (p ^ j) * block, block, 1)
        even = jnp.concatenate([cut(j) for j in (0, 2, 4, 6)], axis=1)
        odd = jnp.concatenate([cut(j) for j in (1, 3, 5, 7)], axis=1)
        peer_a = along_seq(odd, 1)
        for k in range(4):
            peer_b = along_seq(b[k], 1)
            stacks[k].append(
                (dot(even, b[k]) + dot(peer_a, peer_b)).astype(BF).reshape(4, block, -1)
            )
    near, far = (2, 4) if x_first else (4, 2)
    slots = []
    for k in range(4):
        g = jnp.stack(stacks[k])
        y_zero, y_one = g[:, :2], g[:, 2:]
        if x_first:
            keep = jnp.stack([g[:, 0], g[:, 2]], 1)
            away = jnp.stack([g[:, 1], g[:, 3]], 1)
        else:
            keep, away = y_zero, y_one
        summed = (keep.astype(F32) + along_seq(away, near).astype(F32)).astype(BF)
        slots.append(
            (summed[:, 0].astype(F32) + along_seq(summed[:, 1], far).astype(F32)).astype(BF)
        )
    return list(reduce_head(slots))


def add(a, b):
    return (a.astype(F32) + b.astype(F32)).astype(BF)


def reduce_head(slots):
    outer, inner, back = [(0, 1), (3, 2)], [(1, 2), (2, 1)], [(2, 3), (1, 0)]
    own, one, two, three = slots
    far = add(two, along_head(three, outer))
    far = add(one, along_head(far, inner))
    far = along_head(far, back)
    mid = add(three, along_head(two, outer))
    mid = along_head(mid, inner)
    near = along_head(one, outer)
    return own.astype(F32) + far.astype(F32) + mid.astype(F32) + near.astype(F32)


def sum_small(slots, gains):
    if not custom_mesh():
        part = lax.psum_scatter(jnp.stack(slots), "head", scatter_dimension=0, tiled=True)[0]
        return lax.psum(part, "seq"), lax.psum(gains, ("seq", "head"))
    part = slots[0]
    for k in (1, 2, 3):
        part = part + along_head(slots[k], [(i, i ^ k) for i in range(4)])
    for k in (1, 2):
        gains = gains + along_head(gains, [(i, i ^ k) for i in range(4)])
    count = part.shape[0]
    total = jnp.concatenate([part, gains])
    for flip in (1, 2, 4):
        total = total + along_seq(total, flip)
    return total[:count], total[count:]


def norm_keep(values):
    inverse = lax.rsqrt(jnp.mean(values * values, axis=-1, keepdims=True) + EPSILON)
    return (values * inverse, inverse)


def norm_back(grad, normed, inverse):
    return inverse * (grad - normed * jnp.mean(grad * normed, axis=-1, keepdims=True))


def silu_slope(values):
    sigma = jax.nn.sigmoid(values)
    return sigma * (1.0 + values * (1.0 - sigma))


def carry_coefficients(alpha, eta):
    count, heads = alpha.shape
    place = jnp.arange(count)[:, None]
    mem = jnp.zeros((count, heads), F32)
    mom = jnp.zeros((count, heads), F32)
    rows = []
    for c in range(count):
        rows.append(mem)
        mom = eta[c] * mom + (place == c).astype(F32)
        mem = alpha[c] * mem + mom
    return jnp.stack(rows)


def dot(a, b):
    return jnp.dot(a, b, preferred_element_type=F32)


def dot_t(a, b):
    return lax.dot_general(a, b, (((1,), (1,)), ((), ())), preferred_element_type=F32)


def local_plain(
    inputs,
    lengths,
    decays,
    norm_gain,
    query_proj,
    key_proj,
    value_proj,
    gate_proj,
    conv_taps,
    pers_keys,
    pers_values,
    out_proj,
    ffn_gain,
    ffn_gate,
    ffn_up,
    ffn_down,
    cotangent,
):
    seqs, seg, features = inputs.shape
    segments = lax.axis_size("seq")
    shards = lax.axis_size("head")
    p, z = lax.axis_index("seq"), lax.axis_index("head")
    width = query_proj.shape[1]
    heads_here = width // DH
    heads = heads_here * shards
    rim = KW - 1
    persistent = pers_keys.shape[0]

    attn_slots = gather_weights(jnp.stack([query_proj, key_proj, value_proj, gate_proj, out_proj.T]))
    ffn_slots = gather_weights(jnp.stack([ffn_gate, ffn_up, ffn_down.T]))
    small = gather_small(
        jnp.concatenate([conv_taps.reshape(3 * KW, width), pers_keys, pers_values])
    )
    small = jnp.concatenate(small, axis=1)
    taps = small[: 3 * KW].reshape(3, KW, heads * DH).astype(F32)
    pers_k = small[3 * KW : 3 * KW + persistent].reshape(persistent, heads, DH)
    pers_v = small[3 * KW + persistent :].reshape(persistent, heads, DH)
    q_mat, k_mat, v_mat, g_mat, o_mat = [
        jnp.concatenate([slot[i] for slot in attn_slots], axis=1) for i in range(5)
    ]

    mine = lax.dynamic_index_in_dim(decays, z, 1, False)[:, 0]
    mine = jnp.concatenate(
        [lax.dynamic_slice_in_dim(mine, slot_owner(k) * heads_here, heads_here, 1) for k in range(shards)],
        axis=1,
    )
    every = lax.all_gather(mine, "seq")
    carry = carry_coefficients(every[:, 0], every[:, 1])

    x = lax.dynamic_index_in_dim(inputs, z, 0, False).astype(F32)
    cot = lax.dynamic_index_in_dim(cotangent, z, 0, False).astype(F32)
    length = lax.dynamic_index_in_dim(lengths, z, 0, False)
    live = ((p * seg + jnp.arange(seg, dtype=jnp.int32)) < length).astype(F32)
    live_two = live[:, None]
    tail = lax.dynamic_index_in_dim(inputs, z, 0, False)[seg - HALO :]
    before = lax.ppermute(tail, "seq", [(i, i + 1) for i in range(segments - 1)]).astype(F32)
    x_long = jnp.concatenate([before, x])
    n_long, inv_long = norm_keep(x_long)
    h_long = (n_long * norm_gain).astype(BF)
    n_one, inv_one, h_one = n_long[HALO:], inv_long[HALO:], h_long[HALO:]

    pre = jnp.stack([dot(h_long, m) for m in (q_mat, k_mat, v_mat)]).astype(BF)
    zgate = dot(h_one, g_mat)
    wide_pre = pre.astype(F32)
    conv_sum = sum(
        taps[:, lag][:, None, :] * wide_pre[:, HALO - lag : HALO - lag + seg] for lag in range(KW)
    )
    acts = jax.nn.silu(conv_sum).reshape(3, seg, heads, DH)
    q_normed, q_inverse = norm_keep(acts[0])
    k_normed, k_inverse = norm_keep(acts[1])
    query, keyed, valued = q_normed.astype(BF), k_normed.astype(BF), acts[2].astype(BF)
    live_three = live[:, None, None]
    masked_value = valued * live_three.astype(BF)
    write = jnp.einsum("tha,thb->hab", masked_value, keyed, preferred_element_type=F32) / seg

    def mix_states(values, coefficients):
        pieces, places = gather_states(values.astype(BF))
        total = 0.0
        for piece, place in zip(pieces, places):
            coefficient = lax.dynamic_index_in_dim(coefficients, place, 0, False)
            total = total + coefficient[:, None, None] * piece.astype(F32)
        return total.astype(BF)

    prior = mix_states(write, lax.dynamic_index_in_dim(carry, p, 0, False))
    raw_read = jnp.einsum("hab,thb->tha", prior, query, preferred_element_type=F32)
    readout, read_inverse = norm_keep(raw_read)

    keys_all = jnp.concatenate([pers_k, keyed])
    values_all = jnp.concatenate([pers_v, valued])
    valid = jnp.concatenate([jnp.ones((persistent,), F32), live])
    rows_index = jnp.arange(seg)[:, None]
    column = jnp.arange(persistent + seg)[None, :] - persistent
    allowed = (column < 0) | (column <= rows_index) & (valid[None, :] > 0.5)
    scale = DH ** (-0.5)
    score = jnp.einsum("thd,uhd->htu", query, keys_all, preferred_element_type=F32) * scale
    score = jnp.where(allowed[None], score, -1e30)
    top = jnp.max(score, axis=-1, keepdims=True)
    log_total = top + jnp.log(jnp.sum(jnp.exp(score - top), axis=-1, keepdims=True))
    prob = jnp.exp(score - log_total)
    prob_low = prob.astype(BF)
    attended = jnp.einsum("htu,uhd->thd", prob_low, values_all, preferred_element_type=F32)

    sigma = jax.nn.sigmoid(zgate)
    read_flat = readout.reshape(seg, -1)
    mixed = (attended.reshape(seg, -1) + sigma * read_flat).astype(BF)
    middle = x + live_two * dot_t(mixed, o_mat)
    n_two, inv_two = norm_keep(middle)
    h_two = (n_two * ffn_gain).astype(BF)

    gffn = (live_two * cot).astype(BF)
    ffn_out = 0.0
    dh_two = 0.0
    hidden_slots, gate_slots, up_slots = [], [], []
    for slot in ffn_slots:
        gate_value = dot(h_two, slot[0])
        up_value = dot(h_two, slot[1])
        silu_gate = jax.nn.silu(gate_value)
        hidden = (silu_gate * up_value).astype(BF)
        ffn_out = ffn_out + dot_t(hidden, slot[2])
        dhidden = dot(gffn, slot[2])
        dgate = (dhidden * up_value * silu_slope(gate_value)).astype(BF)
        dup = (dhidden * silu_gate).astype(BF)
        dh_two = dh_two + dot_t(dgate, slot[0]) + dot_t(dup, slot[1])
        hidden_slots.append(hidden)
        gate_slots.append(dgate)
        up_slots.append(dup)
    output = gather_rows((middle + live_two * ffn_out).astype(BF))
    g_gate, g_up, g_down = weight_grads(
        [(h_two, gate_slots), (h_two, up_slots), (gffn, hidden_slots)], True
    )

    grad_ffn_gain = jnp.sum(dh_two * n_two, axis=0)
    dmiddle = cot + norm_back(dh_two * ffn_gain, n_two, inv_two)
    gattn = (live_two * dmiddle).astype(BF)
    dmixed = dot(gattn, o_mat)
    datt = dmixed.astype(BF).reshape(seg, heads, DH)
    dzgate = (dmixed * read_flat * sigma * (1.0 - sigma)).astype(BF)
    dread = norm_back((dmixed * sigma).reshape(seg, heads, DH), readout, read_inverse).astype(BF)
    dprior = jnp.einsum("tha,thb->hab", dread, query, preferred_element_type=F32)
    dwrite = mix_states(dprior, lax.dynamic_index_in_dim(carry, p, 1, False))
    dquery_mem = jnp.einsum("hab,tha->thb", prior, dread, preferred_element_type=F32)
    dprob = jnp.einsum("thd,uhd->htu", datt, values_all, preferred_element_type=F32)
    row_dot = jnp.sum(prob * dprob, axis=-1, keepdims=True)
    dscore = (prob * (dprob - row_dot)).astype(BF)
    dquery = (
        jnp.einsum("htu,uhd->thd", dscore, keys_all, preferred_element_type=F32) * scale
        + dquery_mem
    )
    dkeys = jnp.einsum("htu,thd->uhd", dscore, query, preferred_element_type=F32) * scale
    dvalues = jnp.einsum("htu,thd->uhd", prob_low, datt, preferred_element_type=F32)
    dvals = (
        dvalues[persistent:]
        + live_three * jnp.einsum("hab,thb->tha", dwrite, keyed, preferred_element_type=F32) / seg
    )
    dkey = (
        dkeys[persistent:]
        + jnp.einsum("hab,tha->thb", dwrite, masked_value, preferred_element_type=F32) / seg
    )
    dact = jnp.stack(
        [norm_back(dquery, q_normed, q_inverse), norm_back(dkey, k_normed, k_inverse), dvals]
    ).reshape(3, seg, -1)
    dconv = dact * silu_slope(conv_sum)
    longer = jnp.pad(dconv, ((0, 0), (rim, rim), (0, 0)))
    spread = sum(
        taps[:, lag][:, None, :] * longer[:, lag : lag + seg + rim] for lag in range(KW)
    )
    grad_conv = jnp.stack(
        [
            jnp.sum(dconv * wide_pre[:, HALO - lag : HALO - lag + seg], axis=1)
            for lag in range(KW)
        ],
        axis=1,
    )
    back = lax.ppermute(
        spread[:, :rim].astype(BF), "seq", [(i + 1, i) for i in range(segments - 1)]
    ).astype(F32)
    dpre = spread[:, rim:] + jnp.pad(back, ((0, 0), (seg - rim, 0), (0, 0)))
    dpre = dpre.astype(BF)

    dh_one = (
        dot_t(dpre[0], q_mat) + dot_t(dpre[1], k_mat) + dot_t(dpre[2], v_mat) + dot_t(dzgate, g_mat)
    )
    grad_norm_gain = jnp.sum(dh_one * n_one, axis=0)
    input_grad = gather_rows(
        (dmiddle + norm_back(dh_one * norm_gain, n_one, inv_one)).astype(BF)
    )

    def by_slot(value):
        return [value[..., k * width : (k + 1) * width] for k in range(shards)]

    g_query, g_key, g_value, g_zgate, g_out = weight_grads(
        [(h_one, by_slot(d)) for d in (dpre[0], dpre[1], dpre[2], dzgate)]
        + [(gattn, by_slot(mixed))],
        False,
    )
    rows = jnp.concatenate(
        [
            grad_conv.reshape(3 * KW, -1),
            dkeys[:persistent].reshape(persistent, -1),
            dvalues[:persistent].reshape(persistent, -1),
        ]
    )
    gains = jnp.concatenate([grad_norm_gain, grad_ffn_gain]).reshape(-1, width)
    rows, gains = sum_small(by_slot(rows), gains)
    gains = gains.reshape(2, features)
    return (
        output,
        input_grad,
        gains[0],
        g_query,
        g_key,
        g_value,
        g_zgate,
        rows[: 3 * KW].reshape(3, KW, width),
        rows[3 * KW : 3 * KW + persistent],
        rows[3 * KW + persistent :],
        g_out.T,
        gains[1],
        g_gate,
        g_up,
        g_down.T,
    )


ROWS = 16
BLOCK = 128
SCALE = DH ** (-0.5)


def shift_sum(source, taps, first, rows, step):
    total = taps[0:1] * source[pl.ds(first, rows)]
    for lag in range(1, KW):
        total = total + taps[lag : lag + 1] * source[pl.ds(first + step * lag, rows)]
    return total


def live_rows(first, rows, length, segment_start):
    place = segment_start + first + lax.broadcasted_iota(jnp.int32, (rows, 1), 0)
    return (place < length).astype(F32)


def live_columns(columns, length, segment_start):
    return segment_start + lax.broadcasted_iota(jnp.int32, (1, columns), 1) < length


def masked_scores(query, keys, pers_k, index, columns_live):
    width = keys.shape[0]
    raw = dot_t(query, keys) * SCALE
    row = index * BLOCK + lax.broadcasted_iota(jnp.int32, (BLOCK, width), 0)
    column = lax.broadcasted_iota(jnp.int32, (BLOCK, width), 1)
    keep = (column <= row) & columns_live[:, :width]
    return jnp.where(keep, raw, -1e30), dot_t(query, pers_k) * SCALE


def attention_back_slot(k, refs, length, segment_start):
    query, keyed, valued, lse, datt, dread, prior, small, dqkv, small_grad = refs
    seg = query.shape[1]
    columns_live = live_columns(seg, length, segment_start)
    turn = lambda a, b: lax.dot_general(a, b, (((0,), (0,)), ((), ())), preferred_element_type=F32)
    for head in range(query.shape[2] // DH):
        lanes = slice(head * DH, (head + 1) * DH)
        pers_keys_sum = jnp.zeros((16, DH), F32)
        pers_values_sum = jnp.zeros((16, DH), F32)
        pk = small[k, PERS_K : PERS_K + 16, lanes].astype(BF)
        pv = small[k, PERS_V : PERS_V + 16, lanes].astype(BF)
        dqkv[1, :, lanes] = jnp.zeros((seg, DH), F32)
        dqkv[2, :, lanes] = jnp.zeros((seg, DH), F32)
        dqkv[0, :, lanes] = dot(dread[k, :, lanes], prior[k, head])
        for index in range(seg // BLOCK):
            rows = pl.ds(index * BLOCK, BLOCK)
            upto = pl.ds(0, (index + 1) * BLOCK)
            q, d = query[k, rows, lanes], datt[k, rows, lanes]
            keys = keyed[k, upto, lanes]
            score, pers = masked_scores(q, keys, pk, index, columns_live)
            log_total = lse[k, head, rows]
            prob, prob_p = jnp.exp(score - log_total), jnp.exp(pers - log_total)
            grad = dot_t(d, valued[k, upto, lanes])
            grad_p = dot_t(d, pv)
            row_dot = jnp.sum(prob * grad, axis=-1, keepdims=True) + jnp.sum(
                prob_p * grad_p, axis=-1, keepdims=True
            )
            dscore = (prob * (grad - row_dot)).astype(BF)
            dscore_p = (prob_p * (grad_p - row_dot)).astype(BF)
            dqkv[0, rows, lanes] += (dot(dscore, keys) + dot(dscore_p, pk)) * SCALE
            dqkv[1, upto, lanes] += turn(dscore, q) * SCALE
            dqkv[2, upto, lanes] += turn(prob.astype(BF), d)
            pers_keys_sum = pers_keys_sum + turn(dscore_p, q)
            pers_values_sum = pers_values_sum + turn(prob_p.astype(BF), d)
        small_grad[k, PERS_K : PERS_K + 16, lanes] = pers_keys_sum * SCALE
        small_grad[k, PERS_V : PERS_V + 16, lanes] = pers_values_sum


def conv_back_slot(k, refs, length, segment_start):
    pre, small, keyed, valued, dwrite, dqkv, dconv, small_grad, wide = refs
    seg = keyed.shape[1]
    heads = keyed.shape[2] // DH
    for i in range(3):
        wide[i] = pre[i, k].astype(F32)
    sums = [[jnp.zeros((1, heads * DH), F32) for _ in range(KW)] for _ in range(3)]
    for first in range(0, seg, BLOCK):
        rows = pl.ds(first, BLOCK)
        live = live_rows(first, BLOCK, length, segment_start)
        for i in range(3):
            conv = shift_sum(wide.at[i], taps_of(small, k, i), ROWS + first, BLOCK, -1)
            sigma = jax.nn.sigmoid(conv)
            act = conv * sigma
            parts = []
            for head in range(heads):
                lanes = slice(head * DH, (head + 1) * DH)
                grad = dqkv[i, rows, lanes]
                if i == 1:
                    masked = valued[k, rows, lanes] * live.astype(BF)
                    grad = grad + dot(masked, dwrite[k, head]) / seg
                if i == 2:
                    grad = grad + live * dot_t(keyed[k, rows, lanes], dwrite[k, head]) / seg
                else:
                    grad = norm_back(grad, *norm_keep(act[:, lanes]))
                parts.append(grad)
            result = jnp.concatenate(parts, axis=1) * (sigma * (1.0 + conv * (1.0 - sigma)))
            dconv[i, 0, rows] = result
            for lag in range(KW):
                sums[i][lag] = sums[i][lag] + jnp.sum(
                    result * wide[i, pl.ds(ROWS + first - lag, BLOCK)], axis=0, keepdims=True
                )
    for i in range(3):
        for lag in range(KW):
            row = TAPS + KW * i + lag
            small_grad[k, row : row + 1] = sums[i][lag]


SHAPE = jax.ShapeDtypeStruct
VMEM_LIMIT = 127 * 512 * 1024


MESH = pl.DeviceIdType.MESH
SKEW_ONE, SKEW_TWO = 2, 4
WINDOW = 6
UNITS = (
    ("proj", 1), ("proj", 2), ("proj", 3), ("ffn", 1), ("out", 1), ("out", 2), ("out", 3), ("down", 1),
    ("ffn", 2), ("down", 2), ("ffn", 3), ("down", 3),
)


class Links:
    def __init__(self, send, recv):
        self.send, self.recv = send, recv
        self.sent = 0
        self.names = {}
        self.always, self.middles = [], []
        self.p, self.z = lax.axis_index("seq"), lax.axis_index("head")
        self.middle = (self.z == 1) | (self.z == 2)

    def greet(self):
        barrier = pltpu.get_barrier_semaphore()
        for flip in range(1, 8):
            pl.semaphore_signal(barrier, device_id=(self.p ^ flip, self.z), device_id_type=MESH)
        for flip in (1, 2, 3):
            pl.semaphore_signal(barrier, device_id=(self.p, self.z ^ flip), device_id_type=MESH)
        pl.semaphore_wait(barrier, 10)

    def place(self, name):
        return self.recv.at[self.names.setdefault(name, len(self.names))]

    def copy(self, source, target, name, device):
        index = self.sent
        self.sent += 1
        return pltpu.make_async_remote_copy(
            src_ref=source, dst_ref=target, send_sem=self.send.at[index], recv_sem=self.place(name),
            device_id=device, device_id_type=MESH,
        )

    def along_seq(self, source, target, name, flip):
        copy = self.copy(source, target, name, (self.p ^ flip, self.z))
        copy.start()
        self.always.append((lambda: source, self.sent - 1))

    def along_head(self, source, target, name, flip, waits):
        index = self.sent
        copy = self.copy(source(), target(), name, (self.p, self.z ^ flip))
        copy.start()
        waits.append((source, index))

    def arrived(self, target, name):
        pltpu.make_async_remote_copy(
            src_ref=target, dst_ref=target, send_sem=self.send.at[0], recv_sem=self.place(name),
            device_id=(self.p, self.z ^ 1), device_id_type=MESH,
        ).wait_recv()

    def gone(self, source, index):
        pltpu.make_async_remote_copy(
            src_ref=source(), dst_ref=source(), send_sem=self.send.at[index], recv_sem=self.recv.at[0],
            device_id=(self.p, self.z ^ 1), device_id_type=MESH,
        ).wait_send()

    def finish(self):
        for source, index in self.always:
            self.gone(source, index)

        @pl.when(self.middle)
        def _():
            for source, index in self.middles:
                self.gone(source, index)


class LineGather:
    def __init__(self, links, name, view, fixed=False):
        self.links, self.name, self.view, self.fixed = links, name, view, fixed

    def start(self, sources):
        links = self.links
        for source, view in sources:
            links.along_head(source, lambda: view(1), (self.name, 1), 1, links.always)

        @pl.when(links.middle)
        def _():
            for source, view in sources:
                links.along_head(source, lambda: view(3), (self.name, 3), 3, links.middles)

    def forward(self, k, flip):
        view, there = self.view, k ^ flip
        self.links.along_head(
            lambda: view(k), lambda: view(k if self.fixed else there), (self.name, there), flip,
            self.links.middles,
        )

    def outward(self):
        @pl.when(self.links.middle)
        def _():
            self.links.arrived(self.view(3), (self.name, 3))
            self.forward(3, 1)

    def step(self, k):
        links, name, view = self.links, self.name, self.view
        if k == 1:
            links.arrived(view(1), (name, 1))

            @pl.when(links.middle)
            def _():
                self.forward(1, 3)

        if k == 2:
            links.arrived(view(2), (name, 2))

            @pl.when(links.middle)
            def _():
                self.forward(2, 1)

        if k == 3:

            @pl.when(~links.middle)
            def _():
                links.arrived(view(3), (name, 3))


class PlaneGather:
    def __init__(self, links, name, view, x_first):
        self.links, self.name, self.view = links, name, view
        self.near, self.far = (2, 4) if x_first else (4, 2)

    def send(self, j, flip):
        links = self.links
        block = self.view(links.p ^ j)
        links.along_seq(block, block, (self.name, j ^ flip), flip)

    def wait(self, j):
        self.links.arrived(self.view(self.links.p ^ j), (self.name, j))

    def start(self):
        self.send(0, self.near)
        self.send(0, self.far)
        self.send(0, 1)

    def step(self):
        self.wait(self.near)
        self.send(self.near, self.far)
        self.send(self.near, 1)
        self.wait(self.far)
        self.send(self.far, 1)

    def last(self):
        self.wait(6)
        self.send(6, 1)

    def end(self):
        for j in (1, 3, 5, 7):
            self.wait(j)


class StateExchange:
    def __init__(self, links, name, view):
        self.links, self.name, self.view = links, name, view

    def send(self, j, flip):
        block = self.view(self.links.p ^ j)
        self.links.along_seq(block, block, (self.name, j ^ flip), flip)

    def wait(self, j):
        self.links.arrived(self.view(self.links.p ^ j), (self.name, j))

    def start(self):
        for flip in (6, 2, 4, 1):
            self.send(0, flip)

    def step(self):
        for j in (2, 4, 6):
            self.wait(j)
            self.send(j, 1)

    def end(self):
        for j in (1, 3, 5, 7):
            self.wait(j)


def weight_events(links, own, weights, out_w, gate_up, down):
    q_own, k_own, v_own, g_own, o_own, gate_own, up_own, down_own = own
    block = lambda q: pl.ds(pl.multiple_of(q * 128, 128), 128)
    mine = block(links.p)
    views = {
        "proj": (lambda k, q: weights.at[k, :, block(q), :], True),
        "out": (lambda k, q: out_w.at[k, :, block(q)], False),
        "ffn": (lambda k, q: gate_up.at[k, :, :, block(q)], False),
        "down": (lambda k, q: down.at[k, :, block(q)], True),
    }
    sources = {
        "proj": [
            (lambda ref=ref: ref.at[mine, :], lambda k, i=i: weights.at[k, i, mine, :])
            for i, ref in enumerate((q_own, k_own, v_own, g_own))
        ],
        "out": [(lambda: o_own.at[:, mine], lambda k: out_w.at[k, :, mine])],
        "ffn": [
            (lambda ref=ref: ref.at[:, mine], lambda k, i=i: gate_up.at[k, i, :, mine])
            for i, ref in enumerate((gate_own, up_own))
        ],
        "down": [(lambda: down_own.at[:, mine], lambda k: down.at[k, :, mine])],
    }
    planes = {
        (name, k): PlaneGather(links, (name, k), lambda q, view=view, k=k: view(k, q), x_first)
        for name, (view, x_first) in views.items()
        for k in (1, 2, 3)
    }
    units = UNITS
    count = len(units)

    def post(i):
        if i < count:
            name, k = units[i]
            for source, target in sources[name]:
                links.along_head(source, lambda: target(k), ("line", name, k), k, links.always)

    def begin():
        for i in range(WINDOW):
            post(i)

    events = [(None, begin)]
    for i in range(count + SKEW_TWO):
        if i < count:
            name, k = units[i]

            def first(name=name, k=k, i=i):
                links.arrived(views[name][0](k, links.p), ("line", name, k))
                post(i + WINDOW)
                planes[name, k].start()

            events.append((None, first))
        if 0 <= i - SKEW_ONE < count:
            events.append((None, planes[units[i - SKEW_ONE]].step))
        if 0 <= i - SKEW_TWO < count:
            events.append((units[i - SKEW_TWO], planes[units[i - SKEW_TWO]].last))
    return events, planes


PERS_K, PERS_V, TAPS, GAINS, SMALL = 0, 16, 32, 48, 56


def taps_of(small, k, i):
    return small[k, TAPS + KW * i : TAPS + KW * (i + 1)]


def carry_in_kernel(every, place, forward, backward):
    count, lanes = every.shape[0], every.shape[2]
    row = lax.broadcasted_iota(jnp.int32, (count, lanes), 0)
    mem = jnp.zeros((count, lanes), F32)
    mom = jnp.zeros((count, lanes), F32)
    ahead = jnp.zeros((count, lanes), F32)
    behind = jnp.zeros((count, lanes), F32)
    for c in range(count):
        ahead = jnp.where(place == c, mem, ahead)
        mine = jnp.sum(jnp.where(row == place, mem, 0.0), axis=0, keepdims=True)
        behind = jnp.where(row == c, mine, behind)
        mom = every[c, 1:2] * mom + (row == c).astype(F32)
        mem = every[c, 0:1] * mem + mom
    forward[...] = ahead
    backward[...] = behind


def mixed_state(states, coefficients, k, head):
    lane = 2 * k + head
    total = coefficients[0:1, lane : lane + 1] * states[0, k, head].astype(F32)
    for q in range(1, states.shape[0]):
        total = total + coefficients[q : q + 1, lane : lane + 1] * states[q, k, head].astype(F32)
    return total.astype(BF)


def project_slot(k, h_long, weights, pre, zgate, wide):
    seg = zgate.shape[1]
    for i in range(3):
        rounded = dot(h_long[...], weights[i]).astype(BF)
        pre[i, k] = rounded
        wide[i] = rounded.astype(F32)
    zgate[k] = dot(h_long[pl.ds(ROWS, seg)], weights[3])


def convolve_slot(k, small, query, keyed, valued, wide):
    seg = query.shape[1]
    heads = query.shape[2] // DH

    for first in range(0, seg, BLOCK):
        rows = pl.ds(first, BLOCK)
        for i in range(3):
            conv = shift_sum(wide.at[i], taps_of(small, k, i), ROWS + first, BLOCK, -1)
            act = conv * jax.nn.sigmoid(conv)
            if i == 2:
                valued[k, rows] = act.astype(BF)
                continue
            target = (query, keyed)[i]
            for head in range(heads):
                lanes = slice(head * DH, (head + 1) * DH)
                target[k, rows, lanes] = norm_keep(act[:, lanes])[0].astype(BF)


def write_slot(k, p, keyed, valued, states, length, segment_start):
    seg = keyed.shape[1]
    seg_live = live_rows(0, seg, length, segment_start).astype(BF)
    for head in range(keyed.shape[2] // DH):
        lanes = slice(head * DH, (head + 1) * DH)
        masked = valued[k, :, lanes] * seg_live
        states[p, k, head] = (
            lax.dot_general(
                masked, keyed[k, :, lanes], (((0,), (0,)), ((), ())), preferred_element_type=F32
            )
            / seg
        ).astype(BF)


def attend_head(k, head, small, query, keyed, valued, att, lse, length, segment_start):
    seg = query.shape[1]
    columns_live = live_columns(seg, length, segment_start)
    lanes = slice(head * DH, (head + 1) * DH)
    pers_k = small[k, PERS_K : PERS_K + 16, lanes].astype(BF)
    pers_v = small[k, PERS_V : PERS_V + 16, lanes].astype(BF)
    for index in range(seg // BLOCK):
        rows = pl.ds(index * BLOCK, BLOCK)
        upto = pl.ds(0, (index + 1) * BLOCK)
        score, pers = masked_scores(
            query[k, rows, lanes], keyed[k, upto, lanes], pers_k, index, columns_live
        )
        top = jnp.maximum(
            jnp.max(score, axis=-1, keepdims=True), jnp.max(pers, axis=-1, keepdims=True)
        )
        score, pers = jnp.exp(score - top), jnp.exp(pers - top)
        total = jnp.sum(score, axis=-1, keepdims=True) + jnp.sum(pers, axis=-1, keepdims=True)
        inverse = 1.0 / total
        lse[k, head, rows] = top + jnp.log(total)
        att[k, rows, lanes] = dot((score * inverse).astype(BF), valued[k, upto, lanes]) + dot(
            (pers * inverse).astype(BF), pers_v
        )


def read_slot(k, prior, query, zgate, att, mixed):
    for head in range(query.shape[2] // DH):
        lanes = slice(head * DH, (head + 1) * DH)
        normed, _ = norm_keep(dot_t(query[k, :, lanes], prior[k, head]))
        mixed[k, :, lanes] = (
            att[k, :, lanes] + jax.nn.sigmoid(zgate[k, :, lanes]) * normed
        ).astype(BF)


def ffn_rows(rows, h_two, gffn, weights_gu, weights_d, stage, out_acc, grad_acc):
    gate = dot_t(h_two[rows], weights_gu[0])
    up = dot_t(h_two[rows], weights_gu[1])
    sigma = jax.nn.sigmoid(gate)
    silu = gate * sigma
    low = (silu * up).astype(BF)
    stage[0, rows] = low
    out_acc[rows] += dot(low, weights_d[...])
    back = dot_t(gffn[rows], weights_d[...])
    low_gate = (back * up * (sigma * (1.0 + gate * (1.0 - sigma)))).astype(BF)
    low_up = (back * silu).astype(BF)
    stage[1, rows] = low_gate
    stage[2, rows] = low_up
    grad_acc[rows] += dot(low_gate, weights_gu[0]) + dot(low_up, weights_gu[1])


def tail_slot(k, out_w, gattn, query, prior, zgate, datt, dzgate, dread, dprior):
    dmixed = dot_t(gattn[...], out_w[k])
    datt[k] = dmixed.astype(BF)
    for head in range(dmixed.shape[1] // DH):
        lanes = slice(head * DH, (head + 1) * DH)
        sigma = jax.nn.sigmoid(zgate[k, :, lanes])
        readout, rinv = norm_keep(dot_t(query[k, :, lanes], prior[k, head]))
        grad = dmixed[:, lanes] * sigma
        dzgate[k, :, lanes] = (grad * readout * (1.0 - sigma)).astype(BF)
        low = norm_back(grad, readout, rinv).astype(BF)
        dread[k, :, lanes] = low
        dprior[k, head] = lax.dot_general(
            low, query[k, :, lanes], (((0,), (0,)), ((), ())), preferred_element_type=F32
        ).astype(BF)


class Steps:
    def __init__(self, events):
        self.events, self.at, self.done = events, 0, set()

    def run(self, count=1):
        for _ in range(count):
            if self.at < len(self.events):
                label, function = self.events[self.at]
                function()
                self.at += 1
                self.done.add(label)

    def until(self, *labels):
        while not all(label in self.done for label in labels):
            self.run()


def front_kernel(
    lengths, gain, ffn_gain, own_small, own_decays,
    inputs, cotangent, q_own, k_own, v_own, g_own, o_own, gate_own, up_own, down_own,
    small, backward, dprior, gain_grad,
    x_long_out, h_long_out, pre_out, query_out, keyed_out, valued_out, lse_out, prior_out, mixed_out, h_two_out, gffn_out,
    output_out, dmiddle_out, gattn_out, datt_out, dzgate_out, dread_out,
    weights, hidden, dgate, dup, out_w, gate_up, down,
    x_long, h_long, pre, query, keyed, valued, lse, prior, mixed, h_two, gffn,
    output, dmiddle, gattn, datt, dzgate, dread,
    cot, zgate, att, wide, states, every, forward, wproj, wout, wgu, wdown, stage, out_acc, grad_acc,
    send, recv, sem_x, sem_proj, sem_out, sem_ffn, sem_stage, sem_early, sem_late, sem_slots,
):
    links = Links(send, recv)
    p, z = links.p, links.z
    seg = h_two.shape[0]
    length, start = lengths[z], p * seg
    own = (q_own, k_own, v_own, g_own, o_own, gate_own, up_own, down_own)
    load_x = pltpu.make_async_copy(inputs.at[z], x_long.at[pl.ds(ROWS, seg)], sem_x.at[0])
    load_cot = pltpu.make_async_copy(cotangent.at[z], cot, sem_x.at[1])
    load_x.start()

    def proj_loads(k):
        if k == 0:
            return [
                pltpu.make_async_copy(ref, wproj.at[i], sem_proj.at[i]) for i, ref in enumerate(own[:4])
            ]
        return [pltpu.make_async_copy(weights.at[k], wproj, sem_proj.at[0])]

    def out_load(k):
        return pltpu.make_async_copy(o_own if k == 0 else out_w.at[k], wout.at[k], sem_out.at[k])

    def ffn_loads(k):
        side = k % 2
        if k == 0:
            gu = [
                pltpu.make_async_copy(gate_own, wgu.at[0, 0], sem_ffn.at[0, 0]),
                pltpu.make_async_copy(up_own, wgu.at[0, 1], sem_ffn.at[0, 2]),
            ]
        else:
            gu = [pltpu.make_async_copy(gate_up.at[k], wgu.at[side], sem_ffn.at[side, 0])]
        return gu + [
            pltpu.make_async_copy(down_own if k == 0 else down.at[k], wdown.at[side], sem_ffn.at[side, 1])
        ]

    def go(copies):
        for copy in copies:
            copy.start()

    def come(copies):
        for copy in copies:
            copy.wait()

    go(proj_loads(0))
    go([load_cot, out_load(0)])
    go(ffn_loads(0))
    every[p] = own_decays[...]
    small[0] = own_small[...]
    links.greet()
    events, planes = weight_events(links, own, weights, out_w, gate_up, down)
    steps = Steps(events)

    @pl.when(p < 7)
    def _():
        links.copy(
            inputs.at[z, pl.ds(seg - ROWS, ROWS)], x_long.at[pl.ds(0, ROWS)], "rows", (p + 1, z)
        ).start()

    rows_index = links.sent - 1
    for j in range(1, 8):
        links.along_seq(own_decays, every.at[p], ("decays", j), j)
    for k in (1, 2, 3):
        links.copy(own_small, small.at[k], ("small", k), (p, z ^ k)).start()
        links.always.append((lambda: own_small, links.sent - 1))
    steps.run()

    load_x.wait()

    @pl.when(p == 0)
    def _():
        x_long[pl.ds(0, ROWS)] = jnp.zeros((ROWS, x_long.shape[1]), BF)

    @pl.when(p > 0)
    def _():
        links.arrived(x_long.at[pl.ds(0, ROWS)], "rows")

    @pl.loop(0, 3)
    def _(c):
        rows = pl.ds(pl.multiple_of(c * 176, 16), 176)
        normed, _ = norm_keep(x_long[rows].astype(F32))
        h_long[rows] = (normed * gain[...]).astype(BF)

    exchanges = [StateExchange(links, ("states", k), lambda q, k=k: states.at[q, k]) for k in range(4)]
    complete = lambda name, k: planes[name, k].end()
    come(proj_loads(0))
    attend = lambda k, head: attend_head(k, head, small, query, keyed, valued, att, lse, length, start)

    def load_next(k):
        steps.until(("proj", k))
        complete("proj", k)
        go(proj_loads(k))

    def open_slot(k):
        project_slot(k, h_long, wproj, pre, zgate, wide)
        steps.run()
        convolve_slot(k, small, query, keyed, valued, wide)
        write_slot(k, p, keyed, valued, states, length, start)
        exchanges[k].start()

    steps.run()
    project_slot(0, h_long, wproj, pre, zgate, wide)
    steps.run()
    for other in (1, 2, 3):
        links.arrived(small.at[other], ("small", other))
    convolve_slot(0, small, query, keyed, valued, wide)
    steps.run()
    write_slot(0, p, keyed, valued, states, length, start)
    exchanges[0].start()
    attend(0, 0)
    steps.run()
    attend(0, 1)
    exchanges[0].step()
    for k in (1, 2, 3):
        load_next(k)
        come(proj_loads(k))
        open_slot(k)
        steps.run()
        if k == 1:
            attend(1, 0)
            steps.run()
            exchanges[1].step()
    attend(1, 1)
    exchanges[2].step()
    steps.run()
    attend(2, 0)
    exchanges[3].step()
    steps.run()
    attend(2, 1)
    steps.run()
    attend(3, 0)
    steps.run()
    attend(3, 1)
    for j in range(1, 8):
        links.arrived(every.at[p ^ j], ("decays", j))
    carry_in_kernel(every, p, forward, backward)
    for k in (1, 2, 3):
        steps.until(("out", k))
        complete("out", k)
        go([out_load(k)])
    for k in range(4):
        exchanges[k].end()
        for head in range(2):
            prior[k, head] = mixed_state(states, forward, k, head)
        read_slot(k, prior, query, zgate, att, mixed)
        come([out_load(k)])

        @pl.loop(0, 2)
        def _(c):
            rows = pl.ds(pl.multiple_of(c * 256, 256), 256)
            part = dot(mixed[k, rows], wout[k])
            if k == 0:
                grad_acc[rows] = part
            else:
                grad_acc[rows] += part

        steps.run()
    load_cot.wait()

    @pl.loop(0, seg // BLOCK)
    def _(c):
        first = pl.multiple_of(c * BLOCK, BLOCK)
        rows = pl.ds(first, BLOCK)
        live = live_rows(first, BLOCK, length, start)
        value = x_long[pl.ds(pl.multiple_of(ROWS + first, 16), BLOCK)].astype(F32) + live * grad_acc[rows]
        dmiddle[rows] = value
        normed, _ = norm_keep(value)
        h_two[rows] = (normed * ffn_gain[...]).astype(BF)
        gffn[rows] = (live * cot[rows].astype(F32)).astype(BF)
        out_acc[rows] = jnp.zeros((BLOCK, out_acc.shape[1]), F32)
        grad_acc[rows] = jnp.zeros((BLOCK, out_acc.shape[1]), F32)

    early = [
        pltpu.make_async_copy(source, target, sem_early.at[i])
        for i, (source, target) in enumerate(
            (
                (x_long, x_long_out), (h_long, h_long_out), (pre, pre_out), (query, query_out), (keyed, keyed_out),
                (valued, valued_out), (lse, lse_out), (prior, prior_out), (mixed, mixed_out), (h_two, h_two_out),
                (gffn, gffn_out),
            )
        )
    ]
    late = [
        pltpu.make_async_copy(source, target, sem_late.at[i])
        for i, (source, target) in enumerate(((output, output_out), (dmiddle, dmiddle_out), (gattn, gattn_out)))
    ]
    slot_stores = [
        pltpu.make_async_copy(source.at[k], target.at[k], sem_slots.at[k, i])
        for k in range(4)
        for i, (source, target) in enumerate(((datt, datt_out), (dzgate, dzgate_out), (dread, dread_out)))
    ]
    go(early)

    def stores(k):
        return [
            pltpu.make_async_copy(stage.at[k % 2, i], ref.at[k], sem_stage.at[k % 2, i])
            for i, ref in enumerate((hidden, dgate, dup))
        ]

    for k in range(4):
        if k == 3:
            steps.until(("ffn", 3), ("down", 3))
            complete("ffn", 3)
            complete("down", 3)
            go(ffn_loads(3))
        come(ffn_loads(k))
        if k < 2:
            steps.until(("ffn", k + 1), ("down", k + 1))
            complete("ffn", k + 1)
            complete("down", k + 1)
            go(ffn_loads(k + 1))
        if k >= 2:
            come(stores(k - 2))

        @pl.loop(0, 2)
        def _(c):
            rows = pl.ds(pl.multiple_of(c * 256, 256), 256)
            ffn_rows(rows, h_two, gffn, wgu.at[k % 2], wdown.at[k % 2], stage.at[k % 2], out_acc, grad_acc)

        go(stores(k))
        steps.run(3)
    gain_grad[...] = jnp.zeros_like(gain_grad)

    @pl.loop(0, seg // BLOCK)
    def _(c):
        first = pl.multiple_of(c * BLOCK, BLOCK)
        rows = pl.ds(first, BLOCK)
        live = live_rows(first, BLOCK, length, start)
        value = dmiddle[rows]
        output[rows] = (value + live * out_acc[rows]).astype(BF)
        normed, inverse = norm_keep(value)
        grad = grad_acc[rows]
        gain_grad[...] += jnp.sum(grad * normed, axis=0, keepdims=True)
        result = cot[rows].astype(F32) + norm_back(grad * ffn_gain[...], normed, inverse)
        dmiddle[rows] = result
        gattn[rows] = (live * result).astype(BF)

    go(late)
    for k in range(4):
        tail_slot(k, wout, gattn, query, prior, zgate, datt, dzgate, dread, dprior)
        go(slot_stores[3 * k : 3 * k + 3])
    come(stores(2))
    come(stores(3))
    come(early)
    come(late)
    come(slot_stores)

    @pl.when(p < 7)
    def _():
        links.gone(lambda: x_long.at[pl.ds(0, ROWS)], rows_index)

    links.finish()


class PlaneReduce:
    def __init__(self, links, name, blocks, first, second, x_first):
        self.links, self.name, self.x_first = links, name, x_first
        self.blocks, self.first, self.second = blocks, first, second

    def start(self):
        away = self.blocks.at[:, :, 1] if self.x_first else self.blocks.at[:, 1]
        self.links.along_seq(away, self.first, (self.name, 1), 2 if self.x_first else 4)

    def step(self):
        self.links.arrived(self.first, (self.name, 1))
        for i in range(2):
            y, x = (i, 0) if self.x_first else (0, i)

            @pl.loop(0, self.blocks.shape[0])
            def _(m):
                self.blocks[m, y, x] = add(self.blocks[m, y, x], self.first[m, i])

        y, x = (1, 0) if self.x_first else (0, 1)
        self.links.along_seq(
            self.blocks.at[:, y, x], self.second, (self.name, 2), 4 if self.x_first else 2
        )

    def last(self):
        self.links.arrived(self.second, (self.name, 2))

        @pl.loop(0, self.blocks.shape[0])
        def _(m):
            self.blocks[m, 0, 0] = add(self.blocks[m, 0, 0], self.second[m])


class LineReduce:
    def __init__(self, links, name, blocks, landing, result):
        self.links, self.name, self.blocks = links, name, blocks
        self.landing, self.result = landing, result
        self.ends = []

    def send(self, k, slot, flip, waits):
        self.links.along_head(
            lambda: self.blocks(k), lambda: self.landing.at[slot], (self.name, slot), flip, waits
        )

    def merge(self, k, slot):
        self.links.arrived(self.landing.at[slot], (self.name, slot))
        block = self.blocks(k)

        @pl.loop(0, self.landing.shape[1])
        def _(m):
            block[m] = add(block[m], self.landing[slot, m])

    def from_ends(self, k):
        @pl.when(~self.links.middle)
        def _():
            self.send(k, 3 - k, 1, self.ends)

    def take(self, k):
        @pl.when(self.links.middle)
        def _():
            self.merge(5 - k, 3 - k)

    def across(self, k):
        @pl.when(self.links.middle)
        def _():
            self.send(5 - k, 7 - k, 3, self.links.middles)

    def to_ends(self):
        @pl.when(self.links.middle)
        def _():
            self.merge(1, 4)
            self.send(1, 3, 1, self.links.middles)

    def last(self):
        @pl.when(~self.links.middle)
        def _():
            self.total([3])

        @pl.when(self.links.middle)
        def _():
            self.total([2, 5])

    def total(self, slots):
        block = self.blocks(0)
        for slot in slots:
            self.links.arrived(self.landing.at[slot], (self.name, slot))

        @pl.loop(0, self.landing.shape[1])
        def _(m):
            value = block[m].astype(F32)
            for slot in slots:
                value = value + self.landing[slot, m].astype(F32)
            self.result[m] = value

    def finish(self):
        @pl.when(~self.links.middle)
        def _():
            for source, index in self.ends:
                self.links.gone(source, index)


class Pairs:
    def __init__(self, buffers, sems):
        self.buffers, self.sems = buffers, sems

    def copies(self, slot, own, peer):
        rows = own.shape[0]
        return [
            pltpu.make_async_copy(own, self.buffers.at[slot, pl.ds(0, rows)], self.sems.at[slot, 0]),
            pltpu.make_async_copy(peer, self.buffers.at[slot, pl.ds(rows, rows)], self.sems.at[slot, 1]),
        ]

    def start(self, slot, own, peer):
        for copy in self.copies(slot, own, peer):
            copy.start()

    def wait(self, slot, own, peer):
        for copy in self.copies(slot, own, peer):
            copy.wait()


def load_turned(links, own, peer, staged, turned, sems):
    rows = own.shape[0]
    copies = []
    for i, j in enumerate((0, 2, 4, 6)):
        block = pl.ds(pl.multiple_of((links.p ^ j) * 128, 128), 128)
        for side, ref in enumerate((own, peer)):
            copy = pltpu.make_async_copy(
                ref.at[:, block], staged.at[pl.ds(side * rows, rows), pl.ds(i * 128, 128)], sems.at[i, side]
            )
            copy.start()
            copies.append(copy)
    for copy in copies:
        copy.wait()
    for i in range(4):
        turned[pl.ds(i * 128, 128)] = staged[:, pl.ds(i * 128, 128)].T


def conv_back(k, refs, length, segment_start):
    pre, small, keyed, valued, dwrite, dqkv, dslot, small_grad, wide, dpre, part, halo = refs
    conv_back_slot(
        k, (pre, small, keyed, valued, dwrite, dqkv, dslot, small_grad, wide), length, segment_start
    )
    seg = keyed.shape[1]
    for i in range(3):
        dslot[i, 0, pl.ds(seg, 8)] = jnp.zeros((8, dslot.shape[3]), F32)
        halo[i, k] = dslot[i, 0, pl.ds(0, 8)]
        weights = taps_of(small, k, i)
        for first in range(0, seg, BLOCK):
            value = shift_sum(dslot.at[i, 0], weights, first, BLOCK, 1)
            dpre[i, k, pl.ds(first, BLOCK)] = value.astype(BF)
            if first + BLOCK == seg:
                part[i, k] = value[BLOCK - 16 :]


def product(turned, pair, target):
    @pl.loop(0, 2)
    def _(y):
        for x in range(2):
            rows = pl.ds(pl.multiple_of(y * 256, 256) + x * 128, 128)
            target[y, x] = dot(turned[rows], pair[...]).astype(BF)


def gather_halves(links, own, everyone):
    z = links.z
    half = own.shape[0] // 2
    lines = []
    for i in range(2):
        rows = pl.ds(i * half, half)
        line = LineGather(
            links, ("rows", i), lambda k, rows=rows: everyone.at[z ^ k, rows], fixed=True
        )
        line.start([(lambda rows=rows: own.at[rows], lambda k, rows=rows: everyone.at[z, rows])])
        lines.append(line)
    return lines


def back_all_kernel(
    lengths, carry, small, dprior, gain, ffn_gain_grad,
    query_in, keyed_in, valued_in, lse_in, datt_in, dread_in, prior_in, pre_in, x_long_in, dmiddle_in,
    output, h_two, gffn, hidden, dgate, dup, h_long, gattn, mixed, weights, dzgate, q_own, k_own, v_own, g_own,
    all_output, part_ffn, small_grad, dpre, input_grad,
    peer_h_two, peer_gffn, peer_hidden, peer_dgate, peer_dup, peer_h, peer_gattn, peer_mixed, peer_dzgate,
    query, keyed, valued, lse, datt, dread, prior, pre, x_long, dmiddle,
    states, dwrite, dqkv, wide, dslot, part, halo, halo_in, ext, acc, wbuf, zbuf,
    staged, turned, pairs, blocks, first_in, second_in, landing,
    send, recv, sems_turned, sems_pairs, sems_weights, sem_own, sems_in,
):
    links = Links(send, recv)
    p, z = links.p, links.z
    seg = dmiddle.shape[0]
    loads = [
        pltpu.make_async_copy(source, target, sems_in.at[i])
        for i, (source, target) in enumerate(
            (
                (query_in, query), (keyed_in, keyed), (valued_in, valued), (lse_in, lse), (datt_in, datt),
                (dread_in, dread), (prior_in, prior), (pre_in, pre), (x_long_in, x_long), (dmiddle_in, dmiddle),
            )
        )
    ]
    length, start = lengths[z], p * seg
    states[p] = dprior[...]
    own_output = pltpu.make_async_copy(output, all_output.at[z], sem_own.at[0])
    own_output.start()
    links.greet()
    exchange = StateExchange(links, "states", lambda q: states.at[q])
    exchange.start()
    lines = gather_halves(links, output, all_output)
    h_one = h_long.at[pl.ds(ROWS, seg)]
    later = [("h", h_one, peer_h), ("gattn", gattn, peer_gattn), ("mixed", mixed, peer_mixed), ("dzgate", dzgate, peer_dzgate)]

    def to_peer(name, source, target):
        links.along_seq(source, target, ("peer", name), 1)

    def slot_to_peer(k):
        to_peer(("dgate", k), dgate.at[k], peer_dgate.at[k])
        to_peer(("dup", k), dup.at[k], peer_dup.at[k])
        if k == 3:
            to_peer("gffn", gffn, peer_gffn)
        to_peer(("hidden", k), hidden.at[k], peer_hidden.at[k])

    to_peer("h_two", h_two, peer_h_two)
    slot_to_peer(3)

    both = Pairs(pairs, sems_pairs)
    reduces = {
        k: PlaneReduce(links, ("plane", k), blocks.at[k - 1], first_in.at[k - 1], second_in.at[k - 1], k != 2)
        for k in (3, 2)
    }
    for name, mats, x_first in (("1a", pl.ds(0, 2), True), ("1b", pl.ds(2, 1), False)):
        reduces[name] = PlaneReduce(
            links, ("plane", name), blocks.at[0, mats], first_in.at[0, mats], second_in.at[0, mats], x_first
        )
    line_reduce = LineReduce(links, "sum", lambda k: blocks.at[k - 1, :, 0, 0], landing, None)
    sources = ((dgate, peer_dgate, "dgate", 0), (dup, peer_dup, "dup", 0), (hidden, peer_hidden, "hidden", 1))
    units = [(k, m) for k in (3, 2, 1) for m in range(3)]

    def fetch(n):
        k, m = units[n]
        own, peer, name, _ = sources[m]
        links.arrived(peer.at[k], ("peer", (name, k)))
        both.start(n % 2, own.at[k], peer.at[k])

    for copy in loads:
        copy.start()
    links.arrived(peer_h_two, ("peer", "h_two"))
    load_turned(links, h_two, peer_h_two, staged, turned.at[0], sems_turned)
    fetch(0)
    for n, (k, m) in enumerate(units):
        if n == 1:
            links.arrived(peer_gffn, ("peer", "gffn"))
            load_turned(links, gffn, peer_gffn, staged, turned.at[1], sems_turned)
        if m == 0:
            slot_to_peer(k - 1)
        if n + 1 < len(units):
            fetch(n + 1)
        own, peer, _, side = sources[m]
        both.wait(n % 2, own.at[k], peer.at[k])
        product(turned.at[side], pairs.at[n % 2], blocks.at[k - 1, m])
        if m == 2:
            if k > 1:
                reduces[k].start()
            if k == 3:
                exchange.step()
    for name, source, target in later:
        to_peer(name, source, target)
    exchange.end()
    lines[0].outward()
    lines[0].step(1)

    one = (query, keyed, valued, lse, datt, dread, prior, small, dqkv, small_grad)
    two = (pre, small, keyed, valued, dwrite, dqkv, dslot, small_grad, wide, dpre, part, halo)
    for k in range(4):
        for head in range(2):
            dwrite[k, head] = mixed_state(states, carry, k, head)

    def slots(first, count):
        @pl.loop(first, first + count)
        def _(k):
            attention_back_slot(k, one, length, start)
            conv_back(k, two, length, start)

    for copy in loads:
        copy.wait()
    slots(0, 2)
    lines[1].outward()
    lines[1].step(1)
    reduces[3].step()
    reduces["1a"].start()
    slots(2, 1)
    lines[0].step(2)
    reduces[2].step()
    reduces["1b"].start()
    slots(3, 1)

    @pl.when(p > 0)
    def _():
        links.copy(halo, halo_in, "halo", (p - 1, z)).start()

    halo_index = links.sent - 1

    def weight_copies(n):
        copies = [
            pltpu.make_async_copy(
                (q_own, k_own, v_own, g_own)[n] if n < 4 else weights.at[n // 4, n % 4],
                wbuf.at[n % 2], sems_weights.at[n % 2, 0],
            )
        ]
        if n % 4 == 3:
            copies.append(
                pltpu.make_async_copy(dzgate.at[n // 4], zbuf, sems_weights.at[n % 2, 1])
            )
        return copies

    for copy in weight_copies(0):
        copy.start()
    reduces[3].last()
    line_reduce.from_ends(3)
    reduces[2].last()
    line_reduce.from_ends(2)
    lines[1].step(2)

    @pl.when(p == 7)
    def _():
        halo_in[...] = jnp.zeros_like(halo_in)

    @pl.when(p < 7)
    def _():
        links.arrived(halo_in, "halo")

    ext[pl.ds(0, 16)] = jnp.zeros((16, ext.shape[1]), F32)
    for k in range(4):
        for i in range(3):
            ext[pl.ds(16, 8)] = halo_in[i, k]
            dpre[i, k, pl.ds(seg - 16, 16)] = (
                part[i, k] + shift_sum(ext, taps_of(small, k, i), 0, 16, 1)
            ).astype(BF)
        for i in range(4):
            n = 4 * k + i
            if n < 15:
                for copy in weight_copies(n + 1):
                    copy.start()
            for copy in weight_copies(n):
                copy.wait()

            @pl.loop(0, seg // 256)
            def _(c):
                rows = pl.ds(pl.multiple_of(c * 256, 256), 256)
                total = dot_t(zbuf[rows] if i == 3 else dpre[i, k, rows], wbuf[n % 2])
                if n == 0:
                    acc[rows] = total
                else:
                    acc[rows] += total

    reduces["1a"].step()
    reduces["1b"].step()
    gain_sum = jnp.zeros((1, acc.shape[1]), F32)
    for first in range(0, seg, BLOCK):
        rows = pl.ds(first, BLOCK)
        normed, inverse = norm_keep(x_long[pl.ds(ROWS + first, BLOCK)].astype(F32))
        grad = acc[rows]
        gain_sum = gain_sum + jnp.sum(grad * normed, axis=0, keepdims=True)
        input_grad[rows] = (
            dmiddle[rows] + norm_back(grad * gain[...], normed, inverse)
        ).astype(BF)
    for row, value in enumerate((gain_sum, ffn_gain_grad[...])):
        for i in range(4):
            at = GAINS + 4 * row + i
            for k in range(4):
                small_grad[k, at : at + 1] = value[:, i * 256 : (i + 1) * 256]
    for k in range(4):
        small_grad[k, TAPS + 3 * KW : GAINS] = jnp.zeros((GAINS - TAPS - 3 * KW, 256), F32)
    reduces["1a"].last()
    reduces["1b"].last()
    line_reduce.take(3)
    line_reduce.take(2)
    for k in (1, 2, 3):
        part_ffn[k - 1] = blocks[k - 1, :, 0, 0]
    lines[0].step(3)
    lines[1].step(3)
    for own, peer, name, _ in sources:
        links.arrived(peer.at[0], ("peer", (name, 0)))
    for name, _, target in later:
        links.arrived(target, ("peer", name))
    own_output.wait()

    @pl.when(p > 0)
    def _():
        links.gone(lambda: halo, halo_index)

    line_reduce.finish()
    links.finish()


def gradient_kernel(
    small, part_ffn,
    h_long, gattn, dpre, dzgate, mixed, input_grad, h_two, gffn, hidden, dgate, dup,
    peer_h_two, peer_gffn, peer_hidden, peer_dgate, peer_dup, peer_h, peer_gattn, peer_mixed, peer_dzgate,
    all_input_grad, g_attn, g_ffn, small_sum, peer_dpre,
    staged, turned, pairs, blocks, first_in, second_in, landing,
    pairs_ffn, blocks_ffn, first_ffn, second_ffn, landing_ffn, sums_ffn, small_in, small_part, small_all,
    send, recv, sems_turned, sems_pairs, sems_ffn, sem_own,
):
    links = Links(send, recv)
    p, z = links.p, links.z
    seg = gattn.shape[0]
    own_rows = pltpu.make_async_copy(input_grad, all_input_grad.at[z], sem_own.at[0])
    own_rows.start()
    sums_ffn[...] = part_ffn[...]
    links.greet()
    lines = gather_halves(links, input_grad, all_input_grad)
    order = (3, 2, 1, 0)
    for k in order:
        for i in range(3):
            links.along_seq(dpre.at[i, k], peer_dpre.at[i, k], ("dpre", i, k), 1)

    line_ffn = LineReduce(
        links, "ffn", lambda k: sums_ffn.at[k - 1] if k > 0 else blocks_ffn.at[:, 0, 0], landing_ffn, g_ffn
    )
    line_attn = LineReduce(links, "attn", lambda k: blocks.at[k, :, 0, 0], landing, g_attn)
    small_in[0] = small[0]
    for k in (1, 2, 3):
        links.copy(small.at[k], small_in.at[k], ("small", k), (p, z ^ k)).start()
        links.always.append((lambda k=k: small.at[k], links.sent - 1))

    ffn = PlaneReduce(links, "ffn0", blocks_ffn, first_ffn, second_ffn, False)
    attn = {
        k: PlaneReduce(links, ("attn", k), blocks.at[k], first_in.at[k], second_in.at[k], k != 2)
        for k in order
    }
    sources = ((dgate, peer_dgate, 0), (dup, peer_dup, 0), (hidden, peer_hidden, 1))
    both = Pairs(pairs_ffn, sems_ffn)
    sides = lambda k: [(dpre.at[m, k], peer_dpre.at[m, k]) for m in range(3)] + [
        (dzgate.at[k], peer_dzgate.at[k]), (mixed.at[k], peer_mixed.at[k])
    ]

    def attn_loads(k):
        return [
            pltpu.make_async_copy(ref, pairs.at[k % 2, m, pl.ds(side * seg, seg)], sems_pairs.at[k % 2, m, side])
            for m, both_sides in enumerate(sides(k))
            for side, ref in enumerate(both_sides)
        ]

    def fetch(k):
        for m in range(3):
            links.arrived(peer_dpre.at[m, k], ("dpre", m, k))
        for copy in attn_loads(k):
            copy.start()

    fetch(3)
    load_turned(links, h_long.at[pl.ds(ROWS, seg)], peer_h, staged, turned.at[0], sems_turned)
    load_turned(links, gattn, peer_gattn, staged, turned.at[1], sems_turned)
    for k in order:
        if k > 0:
            fetch(k - 1)
        for copy in attn_loads(k):
            copy.wait()
        for m in range(5):
            product(turned.at[m // 4], pairs.at[k % 2, m], blocks.at[k, m])
        if k > 1:
            attn[k].start()
        if k == 3:
            lines[0].outward()
            lines[0].step(1)
            line_ffn.across(3)
    refs_ffn = lambda m: tuple(ref.at[0] for ref in sources[m][:2])
    both.start(0, *refs_ffn(0))
    load_turned(links, h_two, peer_h_two, staged, turned.at[0], sems_turned)
    load_turned(links, gffn, peer_gffn, staged, turned.at[1], sems_turned)
    for m in range(3):
        if m < 2:
            both.start((m + 1) % 2, *refs_ffn(m + 1))
        both.wait(m % 2, *refs_ffn(m))
        product(turned.at[sources[m][2]], pairs_ffn.at[m % 2], blocks_ffn.at[m])
    for k in (1, 2, 3):
        links.arrived(small_in.at[k], ("small", k))
    small_part[...] = (small_in[0] + small_in[1]) + (small_in[2] + small_in[3])
    small_all[0] = small_part[...]
    for j in range(1, 8):
        links.along_seq(small_part, small_all.at[j], ("all", j), j)
    lines[1].outward()
    lines[1].step(1)
    line_ffn.across(2)
    line_ffn.from_ends(1)
    attn[3].step()
    attn[2].step()
    attn[1].start()
    ffn.start()
    lines[0].step(2)
    attn[3].last()
    line_attn.from_ends(3)
    attn[2].last()
    line_attn.from_ends(2)
    lines[1].step(2)
    attn[1].step()
    attn[0].start()
    ffn.step()
    attn[0].step()
    line_ffn.to_ends()
    line_attn.take(3)
    line_attn.across(3)
    line_attn.take(2)
    line_attn.across(2)
    attn[1].last()
    line_attn.from_ends(1)
    line_attn.to_ends()
    ffn.last()
    attn[0].last()
    line_ffn.last()
    lines[0].step(3)
    lines[1].step(3)
    line_attn.last()
    for j in range(1, 8):
        links.arrived(small_all.at[j], ("all", j))
    pair = lambda j: small_all[j] + small_all[j + 1]
    small_sum[...] = (pair(0) + pair(2)) + (pair(4) + pair(6))
    own_rows.wait()
    line_attn.finish()
    line_ffn.finish()
    links.finish()


def finish_kernel(
    attn, ffn, small, output_in, input_in,
    g_query, g_key, g_value, g_zgate, g_out, g_gate, g_up, g_down, taps, pers_k, pers_v, gains,
    output, input_grad, staged, sems_in, sems_out,
):
    pairs = ((output_in, output), (input_in, input_grad))
    count = output.shape[0]
    for side, (source, _) in enumerate(pairs):
        for s in range(count):
            pltpu.make_async_copy(source.at[s], staged.at[side, s], sems_in.at[side, s]).start()
    for i, ref in enumerate((g_query, g_key, g_value, g_zgate)):
        ref[...] = attn[i]
    g_out[...] = attn[4].T
    for i, ref in enumerate((g_gate, g_up, g_down)):
        for first in range(0, ref.shape[0], 128):
            wide = min(128, ref.shape[0] - first)
            ref[pl.ds(first, wide)] = ffn[i, :, pl.ds(first, wide)].T
    pers_k[...] = small[PERS_K : PERS_K + 16]
    pers_v[...] = small[PERS_V : PERS_V + 16]
    for i in range(3):
        taps[i] = small[TAPS + KW * i : TAPS + KW * (i + 1)]
    width = small.shape[1]
    for row in range(2):
        for i in range(4):
            at = GAINS + 4 * row + i
            gains[row : row + 1, i * width : (i + 1) * width] = small[at : at + 1]
    for side, (source, target) in enumerate(pairs):
        for s in range(count):
            pltpu.make_async_copy(source.at[s], staged.at[side, s], sems_in.at[side, s]).wait()
            pltpu.make_async_copy(staged.at[side, s], target.at[s], sems_out.at[side, s]).start()
    for side, (_, target) in enumerate(pairs):
        for s in range(count):
            pltpu.make_async_copy(staged.at[side, s], target.at[s], sems_out.at[side, s]).wait()


def local_fast(
    inputs, lengths, decays, norm_gain, query_proj, key_proj, value_proj, gate_proj, conv_taps,
    pers_keys, pers_values, out_proj, ffn_gain, ffn_gate, ffn_up, ffn_down, cotangent,
):
    seqs, seg, features = inputs.shape
    segments, shards = lax.axis_size("seq"), lax.axis_size("head")
    p, z = lax.axis_index("seq"), lax.axis_index("head")
    width, hidden_width = query_proj.shape[1], ffn_gate.shape[1]
    heads_here = width // DH
    heads = heads_here * shards
    persistent = pers_keys.shape[0]

    turn = (jnp.arange(shards)[:, None] == (z ^ jnp.arange(shards))[None, :]).astype(F32)
    mine = lax.dynamic_index_in_dim(decays, z, 1, False)[:, 0].reshape(2, shards, 1, heads_here)
    mine = jnp.sum(mine * turn[None, :, :, None], axis=1).reshape(2, heads)
    mine = jnp.pad(mine, ((0, 6), (0, 128 - heads)))
    own_small = jnp.concatenate(
        [pers_keys, pers_values, conv_taps.reshape(3 * KW, width), jnp.zeros((4, width), BF)]
    ).astype(F32)
    gain, ffn_gain = norm_gain[None], ffn_gain[None]
    low = lambda *shape: SHAPE(shape, BF)
    full = lambda *shape: SHAPE(shape, F32)
    rows_low = low(shards, seg, width)
    state = low(shards, heads_here, DH, DH)
    hid = low(shards, seg, hidden_width)
    flat = low(seg, features)
    anywhere = pl.BlockSpec(memory_space=pl.ANY)
    in_vmem = pl.BlockSpec(memory_space=pltpu.VMEM)
    in_smem = pl.BlockSpec(memory_space=pltpu.SMEM)
    vmem_low = lambda *shape: pltpu.VMEM(shape, BF)
    vmem_full = lambda *shape: pltpu.VMEM(shape, F32)
    dma = pltpu.SemaphoreType.DMA
    block = features // 8
    halo_rows, pre_rows = low(seg + ROWS, features), low(3, shards, seg + ROWS, width)
    scores_total, middle_rows = full(shards, heads_here, seg, 1), full(seg, features)
    kept = [
        halo_rows, halo_rows, pre_rows, rows_low, rows_low, rows_low, scores_total, state, rows_low, flat, flat,
        flat, middle_rows, flat, rows_low, rows_low, rows_low,
    ]
    held = lambda shapes: [pltpu.VMEM(shape.shape, shape.dtype) for shape in shapes]
    (
        small, carry_back, dprior, g_ffn_gain,
        x_long, h_long, pre, query, keyed, valued, lse, prior, mixed, h_two, gffn,
        output, dmiddle, gattn, datt, dzgate, dread,
        weights, hidden, dgate, dup, *_,
    ) = pl.pallas_call(
        front_kernel,
        out_shape=[full(shards, GAINS, width), full(segments, 128), state, full(1, features)]
        + kept
        + [
            low(shards, 4, features, width), hid, hid, hid, low(shards, width, features),
            low(shards, 2, hidden_width, features), low(shards, hidden_width, features),
        ],
        in_specs=[in_smem] + [in_vmem] * 4 + [anywhere] * 10,
        out_specs=[in_vmem] * 4 + [anywhere] * (len(kept) + 7),
        scratch_shapes=held(kept) + [
            vmem_low(seg, features), vmem_full(shards, seg, width), vmem_full(shards, seg, width),
            vmem_full(3, seg + ROWS, width), vmem_low(segments, shards, heads_here, DH, DH),
            vmem_full(segments, 8, 128), vmem_full(segments, 128), vmem_low(4, features, width),
            vmem_low(shards, width, features), vmem_low(2, 2, hidden_width, features),
            vmem_low(2, hidden_width, features), vmem_low(2, 3, seg, hidden_width),
            vmem_full(seg, features), vmem_full(seg, features),
            dma((192,)), dma((192,)), dma((2,)), dma((4,)), dma((4,)), dma((2, 3)), dma((2, 3)),
            dma((11,)), dma((3,)), dma((4, 3)),
        ],
        compiler_params=pltpu.CompilerParams(
            collective_id=0, has_side_effects=True, vmem_limit_bytes=VMEM_LIMIT
        ),
    )(
        lengths, gain, ffn_gain, own_small, mine, inputs, cotangent,
        query_proj, key_proj, value_proj, gate_proj, out_proj, ffn_gate.T, ffn_up.T, ffn_down,
    )
    output, part_ffn, small_grad, dpre, input_grad, *peers = pl.pallas_call(
        back_all_kernel,
        out_shape=[
            low(shards, seg, features), low(3, 3, block, hidden_width), full(shards, SMALL, width),
            low(3, shards, seg, width), flat, flat, flat, hid, hid, hid, flat, flat, rows_low, rows_low,
        ],
        in_specs=[in_smem] + [in_vmem] * 5 + [anywhere] * 25,
        out_specs=[anywhere] + [in_vmem] * 4 + [anywhere] * 9,
        scratch_shapes=held(
            [rows_low] * 3 + [scores_total, rows_low, rows_low, state, pre_rows, halo_rows, middle_rows]
        ) + [
            vmem_low(8, shards, heads_here, DH, DH), vmem_low(shards, heads_here, DH, DH),
            vmem_full(3, seg, width), vmem_full(3, seg + ROWS, width), vmem_full(3, 1, seg + 8, width),
            vmem_full(3, shards, 16, width), vmem_full(3, shards, 8, width), vmem_full(3, shards, 8, width),
            vmem_full(24, width), vmem_full(seg, features), vmem_low(2, features, width),
            vmem_low(seg, width),
            vmem_low(2 * seg, features // 2), vmem_low(2, features // 2, 2 * seg),
            vmem_low(2, 2 * seg, hidden_width), vmem_low(3, 3, 2, 2, block, hidden_width),
            vmem_low(3, 3, 2, block, hidden_width), vmem_low(3, 3, block, hidden_width),
            vmem_low(2, 3, block, hidden_width),
            dma((64,)), dma((64,)), dma((4, 2)), dma((2, 2)), dma((2, 2)), dma((1,)), dma((10,)),
        ],
        compiler_params=pltpu.CompilerParams(
            collective_id=1, has_side_effects=True, vmem_limit_bytes=VMEM_LIMIT
        ),
    )(
        lengths, carry_back, small, dprior, gain, g_ffn_gain,
        query, keyed, valued, lse, datt, dread, prior, pre, x_long, dmiddle,
        output, h_two, gffn, hidden, dgate, dup, h_long, gattn, mixed, weights, dzgate,
        query_proj, key_proj, value_proj, gate_proj,
    )
    input_grad, g_attn, g_ffn, small, *_ = pl.pallas_call(
        gradient_kernel,
        out_shape=[
            low(shards, seg, features), full(5, block, width), full(3, block, hidden_width), full(SMALL, width),
            low(3, shards, seg, width),
        ],
        in_specs=[in_vmem] * 2 + [anywhere] * 20,
        out_specs=[anywhere] + [in_vmem] * 3 + [anywhere],
        scratch_shapes=[
            vmem_low(2 * seg, features // 2), vmem_low(2, features // 2, 2 * seg),
            vmem_low(2, 5, 2 * seg, width), vmem_low(4, 5, 2, 2, block, width), vmem_low(4, 5, 2, block, width),
            vmem_low(4, 5, block, width), vmem_low(6, 5, block, width),
            vmem_low(2, 2 * seg, hidden_width), vmem_low(3, 2, 2, block, hidden_width),
            vmem_low(3, 2, block, hidden_width), vmem_low(3, block, hidden_width),
            vmem_low(6, 3, block, hidden_width), vmem_low(3, 3, block, hidden_width),
            vmem_full(shards, SMALL, width), vmem_full(SMALL, width), vmem_full(8, SMALL, width),
            dma((96,)), dma((96,)), dma((4, 2)), dma((2, 5, 2)), dma((2, 2)), dma((1,)),
        ],
        compiler_params=pltpu.CompilerParams(
            collective_id=2, has_side_effects=True, vmem_limit_bytes=VMEM_LIMIT
        ),
    )(
        small_grad, part_ffn, h_long, gattn, dpre, dzgate, mixed, input_grad, h_two, gffn, hidden, dgate, dup, *peers,
    )
    (
        g_query, g_key, g_value, g_zgate, g_out, g_gate, g_up, g_down, g_taps, g_pers_k, g_pers_v, gains,
        output, input_grad,
    ) = pl.pallas_call(
        finish_kernel,
        out_shape=[full(block, width)] * 4
        + [full(width, block)]
        + [full(hidden_width, block)] * 3
        + [full(3, KW, width), full(persistent, width), full(persistent, width), full(2, features)]
        + [low(shards, seg, features)] * 2,
        in_specs=[in_vmem] * 3 + [anywhere] * 2,
        out_specs=[in_vmem] * 12 + [anywhere] * 2,
        scratch_shapes=[vmem_low(2, shards, seg, features), dma((2, 4)), dma((2, 4))],
        compiler_params=pltpu.CompilerParams(vmem_limit_bytes=VMEM_LIMIT),
    )(g_attn, g_ffn, small, output, input_grad)
    return (
        output, input_grad, gains[0], g_query, g_key, g_value, g_zgate, g_taps, g_pers_k, g_pers_v,
        g_out, gains[1], g_gate.T, g_up.T, g_down,
    )


def local(*args):
    return local_fast(*args) if custom_mesh() else local_plain(*args)


def solution(mesh):
    in_specs = (
        P(None, "seq", None),
        P(),
        P(None, None, "seq", None),
        P(),
        P(None, "head"),
        P(None, "head"),
        P(None, "head"),
        P(None, "head"),
        P(None, None, "head"),
        P(None, "head"),
        P(None, "head"),
        P("head", None),
        P(),
        P(None, "head"),
        P(None, "head"),
        P("head", None),
        P(None, "seq", None),
    )
    out_specs = (
        P(None, "seq", None),
        P(None, "seq", None),
        P(),
        P("seq", "head"),
        P("seq", "head"),
        P("seq", "head"),
        P("seq", "head"),
        P(None, None, "head"),
        P(None, "head"),
        P(None, "head"),
        P("head", "seq"),
        P(),
        P("seq", "head"),
        P("seq", "head"),
        P("head", "seq"),
    )
    return jax.shard_map(local, mesh=mesh, in_specs=in_specs, out_specs=out_specs, check_vma=False)
```
